32 devices in a mesh: rep: 1, ga: 32 (over z, y, x, core).
Axes of the slice: x: 2, y: 2, z: 4, core: 2. Of those that a mesh axis runs over, the one named last changes fastest.
Arguments:
- orbitals: float32 [8, 2, 128, 128, 128], P('rep', None, 'ga'), as said below
- plane_order: int32 [128], P('rep'), may hold values from 0 to 127, as said below
- potential: float32 [128, 128, 128], P('rep', 'ga'), may hold values from -1.5 to 0.5
- projectors: float32 [256, 8, 2, 8192], P(('rep', 'ga')), may hold values from -0.25 to 0.25
- slot_owner: int32 [256, 8], P(('rep', 'ga')), may hold values from 0 to 127
- strengths: float32 [32, 4], P('rep'), may hold values from 0.5 to 2
Outputs:
- residual: float32 [8, 2, 128, 128, 128], P('rep', None, 'ga')
- lagrange: float32 [2, 8, 8], P(None, 'rep')
The draws below stay inside these ranges and needn't reach their ends.
Inputs may be any that keep to these rules, and one draw needn't show every extreme that they name: `plane_order`: A permutation: every frequency index appears at exactly one stored x-plane. `orbitals`: every band is the transform of a real field: its coefficient at frequencies (kx, ky, kz) is the complex conjugate of its coefficient at (-kx, -ky, -kz) modulo the lengths, where stored x-plane p has kx = plane_order[p].
All inputs are finite; a program needn't handle non-finite values.
Results may differ from the reference program's by a relative error of at most 0.011.
Values sent between devices are 32-bit elements; how exact they have to be, the bound alone decides.
No kernel may reach another device: no remote copies, remote signals or barrier semaphores. Data moves between devices by JAX's collectives and lax.ppermute only.
A program may use at most 128 MiB of HBM per device.

```python
import math
import jax
import jax.numpy as jnp
from jax import lax

NF = 128
NFZ = 128
NB = 8
ATOMS = 32
NPROJ = 4
BROWS = 64
SLOTS = 8
NBLK = 256


def plane_table(key):
    return jax.random.permutation(jax.random.fold_in(key, 11), NF).astype(jnp.int32)


def mirrored(values):
    flipped = jnp.flip(values, axis=(-3, -2, -1))
    return jnp.roll(flipped, 1, axis=(-3, -2, -1))


def draw_plane_order(key, part):
    return plane_table(key)


def draw_orbitals(key, part):
    ordering = plane_table(key)
    key = jax.random.fold_in(key, 5)
    key_base, key_rows, key_bands = jax.random.split(key, 3)
    full_shape = (NB, 2, NF, NF, NFZ)
    base_draw = jax.random.normal(key_base, full_shape, jnp.float32)
    spread = math.log(3.0)
    real_part = (base_draw[:, 0] + mirrored(base_draw[:, 0])) * 0.7071
    imag_part = (base_draw[:, 1] - mirrored(base_draw[:, 1])) * 0.7071
    roughness = jax.random.uniform(key_rows, (NF, NF), jnp.float32)
    roughness = 0.5 * (roughness + jnp.roll(jnp.flip(roughness, axis=(0, 1)), 1, axis=(0, 1)))
    frequency = jnp.arange(NF)
    distance = jnp.minimum(frequency, NF - frequency).astype(jnp.float32)
    rising = 1.0 + 2.0 * distance / (NF // 2)
    envelope = rising[:, None] * jnp.exp(spread * roughness)
    fields = jnp.stack([real_part, imag_part], axis=1) * envelope[None, None, :, :, None]
    fields = fields + 0.5 * jnp.roll(fields, -1, axis=0) + 0.3 * jnp.roll(fields, -3, axis=0)
    scales = 0.4 * jnp.exp(spread * jax.random.uniform(key_bands, (NB,), jnp.float32))
    fields = fields * scales[:, None, None, None, None]
    return jnp.take(fields, ordering, axis=2)


def set_ends(result, stream_key, low, largest):
    shape = result.shape
    index_at = [jax.random.randint(jax.random.fold_in(stream_key, axis), (), 0, shape[axis]) for axis in range(len(shape))]
    result = result.at[tuple(index_at)].set(low)
    longest = shape.index(max(shape))
    index_at[longest] = (index_at[longest] + 1) % shape[longest]
    return result.at[tuple(index_at)].set(largest)


def level_of(key, dims, pieces, low, high):
    def one(dim, parts):
        steps = jax.random.uniform(jax.random.fold_in(jax.random.fold_in(key, 6), dim), (parts,), jnp.float32, low / len(pieces), high / len(pieces))
        return jnp.repeat(jnp.exp(steps), dims[dim] // parts).reshape((-1,) + (1,) * (len(dims) - dim - 1))

    factor_of = one(*pieces[0])
    for cut in pieces[1:]:
        factor_of = factor_of * one(*cut)
    return factor_of


def scatter_about(own_key, dims, scale, most, cuts=(), kind=jnp.bfloat16):
    result = jax.random.normal(own_key, dims, jnp.float32) * scale
    if len(cuts) > 0:
        result = level_of(own_key, dims, cuts, -0.22, 0.18) * result
    return jnp.clip(result, min=-most, max=most).astype(kind)


def setup_inputs(seed: int = 0, part: int = 0) -> dict:
    key_list = jax.random.split(jax.random.key(seed), 7)
    part_splits = jax.random.split(jax.random.fold_in(key_list[6], part), 7)
    return {
        "orbitals": draw_orbitals(jax.random.fold_in(jax.random.fold_in(key_list[6], part), 71), part),
        "plane_order": draw_plane_order(jax.random.fold_in(jax.random.fold_in(key_list[6], part), 71), part),
        "potential": jnp.clip(-1.5 + 2.0 * jax.random.uniform(part_splits[2], (NF, NF, NFZ), jnp.float32) ** level_of(part_splits[2], (NF, NF, NFZ), ((1, 32),), -0.2, 0.2), -1.5, 0.5),
        "projectors": scatter_about(part_splits[3], (NBLK, SLOTS, 2, BROWS * NFZ), (1.7 / (BROWS * NFZ) ** 0.5), 0.25, ((0, 32),), jnp.float32),
        "slot_owner": set_ends(jax.random.randint(part_splits[4], (NBLK, SLOTS), 0, ATOMS * NPROJ), jax.random.fold_in(part_splits[4], 1), 0, (ATOMS * NPROJ) - 1).astype(jnp.int32),
        "strengths": jnp.clip(jnp.exp(jax.random.uniform(part_splits[5], (ATOMS, NPROJ), jnp.float32, math.log(0.5), math.log(2.0))), 0.5, 2.0),
    }


highest = lax.Precision.HIGHEST

def signed_index(values, length):
    return jnp.where(values < length // 2, values, values - length)

def inner_sum(first_rows, second_rows):
    return jnp.einsum('ag,bg->ab', first_rows.astype(jnp.float32), second_rows.astype(jnp.float32), precision=highest, preferred_element_type=jnp.float32)

def correlation_real(bands):
    return inner_sum(bands[:, 0], bands[:, 0]) + inner_sum(bands[:, 1], bands[:, 1])

def gram_matrix(left_side, right_side):
    real_part = inner_sum(left_side[:, 0], right_side[:, 0]) + inner_sum(left_side[:, 1], right_side[:, 1])
    imag_part = inner_sum(left_side[:, 0], right_side[:, 1]) - inner_sum(left_side[:, 1], right_side[:, 0])
    return (real_part, imag_part)

def subspace_solve(s_real, h_real, h_imag):
    factor = jnp.linalg.cholesky(s_real)
    solved = jax.scipy.linalg.cho_solve((factor, True), jnp.concatenate([h_real, h_imag], axis=1))
    order_size = s_real.shape[0]
    return (solved[:, :order_size], solved[:, order_size:])

def project_blocks(blocks, projectors):

    def contract(operand, weights):
        return jnp.einsum('bge,gse->gsb', operand.astype(jnp.float32), weights.astype(jnp.float32), precision=highest, preferred_element_type=jnp.float32)
    beta_real = projectors[:, :, 0]
    beta_imag = projectors[:, :, 1]
    proj_real = contract(blocks[:, 0], beta_real) + contract(blocks[:, 1], beta_imag)
    proj_imag = contract(blocks[:, 1], beta_real) - contract(blocks[:, 0], beta_imag)
    return (proj_real, proj_imag)

def expand_blocks(coef_real, coef_imag, projectors):

    def spread(coeffs, weights):
        return jnp.einsum('gsb,gse->bge', coeffs.astype(jnp.float32), weights.astype(jnp.float32), precision=highest, preferred_element_type=jnp.float32)
    beta_real = projectors[:, :, 0]
    beta_imag = projectors[:, :, 1]
    out_real = spread(coef_real, beta_real) - spread(coef_imag, beta_imag)
    out_imag = spread(coef_imag, beta_real) + spread(coef_real, beta_imag)
    return jnp.stack([out_real, out_imag], axis=1)

def band_potential(one_band, potential, position, plane_order):
    ordered = jnp.take(one_band, position, axis=1)
    values = lax.complex(ordered[0], ordered[1])
    spatial = jnp.fft.ifftn(values, norm='ortho')
    spectra = jnp.fft.fftn(spatial * potential, norm='ortho')
    stacked = jnp.stack([jnp.real(spectra), jnp.imag(spectra)]).astype(one_band.dtype)
    return jnp.take(stacked, plane_order, axis=1)

def reference(orbitals, plane_order, potential, projectors, slot_owner, strengths):
    grid_x = jnp.arange(NF, dtype=jnp.int32)
    grid_z = jnp.arange(NFZ, dtype=jnp.int32)
    matches = plane_order[:, None] == grid_x[None, :]
    position = jnp.sum(jnp.where(matches, grid_x[:, None], 0), axis=0).astype(jnp.int32)

    def per_band(one_band):
        return band_potential(one_band, potential, position, plane_order)
    local_part = lax.map(per_band, orbitals)
    freq_x = signed_index(plane_order, NF).astype(jnp.float32) / NF
    freq_y = signed_index(grid_x, NF).astype(jnp.float32) / NF
    freq_z = signed_index(grid_z, NFZ).astype(jnp.float32) / NFZ
    kinetic = 2.0 * (freq_x[:, None, None] ** 2 + freq_y[None, :, None] ** 2 + freq_z[None, None, :] ** 2)
    local_part = local_part + kinetic[None, None] * orbitals
    blocks = orbitals.reshape(NB, 2, NBLK, BROWS * NFZ)
    proj_real, proj_imag = project_blocks(blocks, projectors)
    owners = slot_owner.reshape(-1)
    sum_real = jax.ops.segment_sum(proj_real.reshape(-1, NB), owners, num_segments=ATOMS * NPROJ)
    sum_imag = jax.ops.segment_sum(proj_imag.reshape(-1, NB), owners, num_segments=ATOMS * NPROJ)
    weights_flat = strengths.reshape(-1)
    coef_real = jnp.take(weights_flat[:, None] * sum_real, slot_owner, axis=0)
    coef_imag = jnp.take(weights_flat[:, None] * sum_imag, slot_owner, axis=0)
    applied = local_part + expand_blocks(coef_real, coef_imag, projectors).reshape(orbitals.shape)
    flat_orbitals = orbitals.reshape(NB, 2, -1)
    flat_applied = applied.reshape(NB, 2, -1)
    s_real = correlation_real(flat_orbitals)
    h_real, h_imag = gram_matrix(flat_orbitals, flat_applied)
    m_real, m_imag = subspace_solve(s_real, h_real, h_imag)

    def combine(coeffs, operand):
        return jnp.einsum('ab,ag->bg', coeffs.astype(jnp.float32), operand.astype(jnp.float32), precision=highest, preferred_element_type=jnp.float32)
    mix_real = combine(m_real, flat_orbitals[:, 0]) - combine(m_imag, flat_orbitals[:, 1])
    mix_imag = combine(m_real, flat_orbitals[:, 1]) + combine(m_imag, flat_orbitals[:, 0])
    residual = applied - jnp.stack([mix_real, mix_imag], axis=1).reshape(orbitals.shape)
    return (residual, jnp.stack([m_real, m_imag]))
```

```python
import functools
import math

import jax
import jax.numpy as jnp
import numpy as np
from jax import lax
from jax.experimental import pallas as pl
from jax.experimental.pallas import tpu as pltpu
from jax.sharding import PartitionSpec as P

highest = lax.Precision.HIGHEST
f32 = jnp.float32
bf16 = jnp.bfloat16
vmem_limit = 48 * 1024 * 1024


def signed_index(values, length):
    return jnp.where(values < length // 2, values, values - length)


def dft(length, orient):
    index = np.arange(length)
    angles = (index[:, None] * index[None, :] % length) * (2.0 * math.pi / length)
    factor = 1.0 / math.sqrt(length)
    return np.cos(angles) * factor, orient * np.sin(angles) * factor


def left_table(length, orient, row_order=None, col_order=None):
    cosine, sine = dft(length, orient)
    if row_order is not None:
        cosine, sine = cosine[row_order], sine[row_order]
    if col_order is not None:
        cosine, sine = cosine[:, col_order], sine[:, col_order]
    return np.block([[cosine, -sine], [sine, cosine]])


def right_table(length, orient):
    cosine, sine = dft(length, orient)
    return np.block([[cosine, sine], [-sine, cosine]])


def split_const(table):
    high = np.asarray(table, np.float32).astype(jnp.bfloat16)
    low = (np.asarray(table, np.float32) - high.astype(np.float32)).astype(jnp.bfloat16)
    return jnp.asarray(high), jnp.asarray(low)


def split(values):
    high = values.astype(bf16)
    low = (values - high.astype(f32)).astype(bf16)
    return high, low


def split_outside(values):
    high = lax.reduce_precision(values, exponent_bits=8, mantissa_bits=7)
    return high.astype(bf16), (values - high).astype(bf16)


def mm(left, right):
    return jnp.dot(left, right, preferred_element_type=f32)


def dot_left(w_high, w_low, values):
    high, low = split(values)
    return mm(w_high, high) + (mm(w_high, low) + mm(w_low, high))


def dot_right(values, w_high, w_low):
    high, low = split(values)
    return mm(high, w_high) + (mm(low, w_high) + mm(high, w_low))


def to_rows_kernel(devices, rows, planes, psi, yh, yl, zh, zl, out):
    real = jnp.concatenate([psi[0, 0, p] - psi[1, 1, p] for p in range(planes)], axis=1)
    imag = jnp.concatenate([psi[0, 1, p] + psi[1, 0, p] for p in range(planes)], axis=1)
    span_y, span_z = psi.shape[3], psi.shape[4]
    along_y = dot_left(yh[...], yl[...], jnp.concatenate([real, imag], axis=0))
    for p in range(planes):
        cols = slice(p * span_z, (p + 1) * span_z)
        plane = jnp.concatenate([along_y[:span_y, cols], along_y[span_y:, cols]], axis=1)
        values = dot_right(plane, zh[...], zl[...])
        for part in range(2):
            for r in range(rows):
                start = (r * planes + p) * 2 + part
                out[pl.ds(start, devices, stride=2 * planes * rows), :] = values[
                    r * devices : (r + 1) * devices, part * span_z : (part + 1) * span_z
                ]


def real_space_kernel(devices, rows, planes, recv, pot, ih, il, fh, fl, back, field):
    span_x = pot.shape[0]
    block = 2 * planes
    columns = [
        recv[:, r * block : (r + 1) * block, :].reshape(devices * block, recv.shape[2])
        for r in range(rows)
    ]
    spatial = dot_left(ih[...], il[...], jnp.concatenate(columns, axis=1))
    for band in range(2):
        one = spatial[band * span_x : (band + 1) * span_x]
        field[band] = one
        spectral = dot_left(fh[...], fl[...], one * pot[...])
        for r in range(rows):
            cols = spectral[:, r * recv.shape[2] : (r + 1) * recv.shape[2]]
            back[:, band, r * block : (r + 1) * block] = cols.reshape(devices, block, recv.shape[2])


def gram_kernel(bands, f0, f1, f2, f3, pot, out):
    fields = [f0, f1, f2, f3]
    pairs = [(a, b) for a in range(bands) for b in range(a, bands)]
    for weighted in range(2):

        def step(i, sums):
            rows = pl.ds(pl.multiple_of(i * 8, 8), 8)
            values = [fields[a // 2][a % 2, rows, :] for a in range(bands)]
            other = [v * pot[rows, :] for v in values] if weighted else values
            result = []
            for (a, b), total in zip(pairs, sums):
                product = values[a] * other[b]
                lanes = product[:, :128]
                for c in range(128, product.shape[1], 128):
                    lanes = lanes + product[:, c : c + 128]
                result.append(total + lanes)
            return tuple(result)

        sums = lax.fori_loop(
            0, pot.shape[0] // 8, step, tuple(jnp.zeros((8, 128), f32) for _ in pairs)
        )
        for (a, b), total in zip(pairs, sums):
            line = jnp.sum(total, axis=0, keepdims=True)
            out[weighted, a, b : b + 1, :] = line
            out[weighted, b, a : a + 1, :] = line


def to_planes_kernel(devices, rows, planes, recv, base, yh, yl, zh, zl, out):
    span_y, span_z = base.shape[3], base.shape[4]
    flat = recv.reshape(devices * 2 * planes * rows, span_z)
    columns = []
    for p in range(planes):
        columns.append(
            jnp.concatenate(
                [
                    flat[pl.ds((r * planes + p) * 2 + part, devices, stride=2 * planes * rows), :]
                    for part in range(2)
                    for r in range(rows)
                ],
                axis=0,
            )
        )
    along_y = dot_left(yh[...], yl[...], jnp.concatenate(columns, axis=1))
    for p in range(planes):
        cols = slice(p * span_z, (p + 1) * span_z)
        plane = jnp.concatenate([along_y[:span_y, cols], along_y[span_y:, cols]], axis=1)
        values = dot_right(plane, zh[...], zl[...])
        for part in range(2):
            out[0, part, p] = base[0, part, p] + values[:, part * span_z : (part + 1) * span_z]


def whole(shape):
    return pl.BlockSpec(shape, lambda *_: (0,) * len(shape))


def inner_sum(first_rows, second_rows):
    return jnp.einsum(
        "ag,bg->ab", first_rows, second_rows, precision=highest, preferred_element_type=jnp.float32
    )


def subspace_solve(s_real, h_real, h_imag):
    factor = jnp.linalg.cholesky(s_real)
    solved = jax.scipy.linalg.cho_solve((factor, True), jnp.concatenate([h_real, h_imag], axis=1))
    order_size = s_real.shape[0]
    return (solved[:, :order_size], solved[:, order_size:])


def project_blocks(blocks, projectors):
    def contract(operand, weights):
        return jnp.einsum(
            "bge,gse->gsb", operand, weights, precision=highest, preferred_element_type=jnp.float32
        )

    beta_real = projectors[:, :, 0]
    beta_imag = projectors[:, :, 1]
    proj_real = contract(blocks[:, 0], beta_real) + contract(blocks[:, 1], beta_imag)
    proj_imag = contract(blocks[:, 1], beta_real) - contract(blocks[:, 0], beta_imag)
    return (proj_real, proj_imag)


def expand_blocks(coef_real, coef_imag, projectors):
    def spread(coeffs, weights):
        return jnp.einsum(
            "gsb,gse->bge", coeffs, weights, precision=highest, preferred_element_type=jnp.float32
        )

    beta_real = projectors[:, :, 0]
    beta_imag = projectors[:, :, 1]
    out_real = spread(coef_real, beta_real) - spread(coef_imag, beta_imag)
    out_imag = spread(coef_imag, beta_real) + spread(coef_real, beta_imag)
    return jnp.stack([out_real, out_imag], axis=1)


def tdot(pattern, left, right):
    return jnp.einsum(pattern, left, right, precision=highest, preferred_element_type=jnp.float32)


def on_device(devices, orbitals, plane_order, potential, projectors, slot_owner, strengths):
    band_count = orbitals.shape[0]
    planes = orbitals.shape[2]
    span_y = orbitals.shape[3]
    span_z = orbitals.shape[4]
    span_x = plane_order.shape[0]
    rows = span_y // devices
    pair_count = band_count // 2
    grid_x = jnp.arange(span_x, dtype=jnp.int32)
    grid_y = jnp.arange(span_y, dtype=jnp.int32)
    grid_z = jnp.arange(span_z, dtype=jnp.int32)
    params = pltpu.CompilerParams(vmem_limit_bytes=vmem_limit)

    row_major = (np.arange(devices)[None, :] * rows + np.arange(rows)[:, None]).reshape(-1)
    inv_y = split_const(left_table(span_y, 1.0, row_order=row_major))
    inv_z = split_const(right_table(span_z, 1.0))
    fwd_y = split_const(left_table(span_y, -1.0, col_order=row_major))
    fwd_z = split_const(right_table(span_z, -1.0))

    phases = (plane_order[:, None] * grid_x[None, :]) % span_x
    angles = phases.astype(f32) * (2.0 * math.pi / span_x)
    factor = 1.0 / math.sqrt(span_x)
    cosine, sine = jnp.cos(angles) * factor, jnp.sin(angles) * factor
    fwd_x = jnp.stack([cosine, -sine], axis=1).reshape(2 * span_x, span_x)
    other = jnp.stack([sine, cosine], axis=1).reshape(2 * span_x, span_x)
    inv_x = jnp.concatenate([fwd_x.T, other.T], axis=0)
    fwd_x = split_outside(fwd_x)
    inv_x = split_outside(inv_x)
    pot = potential.reshape(span_x, rows * span_z)

    lanes = rows * span_z
    block_rows = 2 * planes * rows
    to_rows = [
        pl.pallas_call(
            functools.partial(to_rows_kernel, devices, rows, planes),
            out_shape=jax.ShapeDtypeStruct((devices * block_rows, span_z), f32),
            grid=(1,),
            in_specs=[
                pl.BlockSpec((2, 2, planes, span_y, span_z), lambda i, j=j: (j, 0, 0, 0, 0)),
                whole((2 * span_y, 2 * span_y)),
                whole((2 * span_y, 2 * span_y)),
                whole((2 * span_z, 2 * span_z)),
                whole((2 * span_z, 2 * span_z)),
            ],
            out_specs=whole((devices * block_rows, span_z)),
            compiler_params=params,
            cost_estimate=pl.CostEstimate(flops=10**9, bytes_accessed=2 * 10**6, transcendentals=0),
            name="to_rows",
        )
        for j in range(pair_count)
    ]
    real_space = pl.pallas_call(
        functools.partial(real_space_kernel, devices, rows, planes),
        out_shape=(
            jax.ShapeDtypeStruct((devices, 2, block_rows, span_z), f32),
            jax.ShapeDtypeStruct((2, span_x, lanes), f32),
        ),
        grid=(1,),
        in_specs=[
            whole((devices, block_rows, span_z)),
            whole((span_x, lanes)),
            whole((2 * span_x, 2 * span_x)),
            whole((2 * span_x, 2 * span_x)),
            whole((2 * span_x, span_x)),
            whole((2 * span_x, span_x)),
        ],
        out_specs=(whole((devices, 2, block_rows, span_z)), whole((2, span_x, lanes))),
        compiler_params=params,
        cost_estimate=pl.CostEstimate(flops=10**9, bytes_accessed=2 * 10**6, transcendentals=0),
        name="real_space",
    )

    sent = [to_rows[j](orbitals, *inv_y, *inv_z) for j in range(pair_count)]
    arrived = [
        lax.all_to_all(
            one.reshape(devices, block_rows, span_z), "ga", split_axis=0, concat_axis=0, tiled=True
        )
        for one in sent
    ]

    local_order = lax.dynamic_slice_in_dim(plane_order, lax.axis_index("ga") * planes, planes)
    freq_x = signed_index(local_order, span_x).astype(f32) / span_x
    freq_y = signed_index(grid_y, span_y).astype(f32) / span_y
    freq_z = signed_index(grid_z, span_z).astype(f32) / span_z
    kinetic = 2.0 * (
        freq_x[:, None, None] ** 2 + freq_y[None, :, None] ** 2 + freq_z[None, None, :] ** 2
    )
    local_blocks = slot_owner.shape[0]
    order_size = strengths.shape[0] * strengths.shape[1]
    blocks = orbitals.reshape(band_count, 2, local_blocks, -1)
    proj_real, proj_imag = project_blocks(blocks, projectors)
    selector = (
        slot_owner[:, :, None] == jnp.arange(order_size, dtype=jnp.int32)[None, None, :]
    ).astype(f32)
    partial = tdot("gsj,gsb->jb", selector, jnp.concatenate([proj_real, proj_imag], axis=2))
    proj = jnp.sum(lax.all_gather(partial, "ga"), axis=0)
    weights_flat = strengths.reshape(-1)
    weighted = weights_flat[:, None] * proj
    coefs = jnp.take(weighted, slot_owner, axis=0)
    coef_real, coef_imag = coefs[..., :band_count], coefs[..., band_count:]
    p_real, p_imag = proj[:, :band_count], proj[:, band_count:]
    w_real, w_imag = weighted[:, :band_count], weighted[:, band_count:]
    h_real = tdot("ja,jb->ab", p_real, w_real) + tdot("ja,jb->ab", p_imag, w_imag)
    h_imag = tdot("ja,jb->ab", p_real, w_imag) - tdot("ja,jb->ab", p_imag, w_real)
    flat_orbitals = orbitals.reshape(band_count, 2, -1)
    kin_orbitals = kinetic[None, None] * orbitals
    flat_kin = kin_orbitals.reshape(band_count, 2, -1)
    kin_gram = inner_sum(flat_orbitals[:, 0], flat_kin[:, 0]) + inner_sum(
        flat_orbitals[:, 1], flat_kin[:, 1]
    )

    back, fields = [], []
    for j in range(pair_count):
        one_back, one_field = real_space(arrived[j], pot, *inv_x, *fwd_x)
        back.append(one_back)
        fields.append(one_field)
    returned = [
        lax.all_to_all(one, "ga", split_axis=0, concat_axis=0, tiled=True) for one in back
    ]
    sums = pl.pallas_call(
        functools.partial(gram_kernel, band_count),
        out_shape=jax.ShapeDtypeStruct((2, band_count, band_count, 128), f32),
        compiler_params=params,
        cost_estimate=pl.CostEstimate(flops=10**7, bytes_accessed=2 * 10**6, transcendentals=0),
        name="real_gram",
    )(*fields, pot)
    sums = jnp.sum(sums, axis=-1)
    first = lax.axis_index("ga") == 0
    sums = jnp.stack([sums[0], sums[1] + kin_gram + jnp.where(first, h_real, 0.0)])
    sums = jnp.sum(lax.all_gather(sums, "ga"), axis=0)
    m_real, m_imag = subspace_solve(sums[0], sums[1], h_imag)

    def combine(coeffs, operand):
        return tdot("ab,ag->bg", coeffs, operand)

    mix_real = combine(m_real, flat_orbitals[:, 0]) - combine(m_imag, flat_orbitals[:, 1])
    mix_imag = combine(m_real, flat_orbitals[:, 1]) + combine(m_imag, flat_orbitals[:, 0])
    residual = (
        kin_orbitals
        + expand_blocks(coef_real, coef_imag, projectors).reshape(orbitals.shape)
        - jnp.stack([mix_real, mix_imag], axis=1).reshape(orbitals.shape)
    )
    for j in range(pair_count):
        block = pl.BlockSpec(
            (1, 2, planes, span_y, span_z), lambda i, j=j: (2 * j + i, 0, 0, 0, 0)
        )
        residual = pl.pallas_call(
            functools.partial(to_planes_kernel, devices, rows, planes),
            out_shape=jax.ShapeDtypeStruct(residual.shape, f32),
            grid=(2,),
            in_specs=[
                pl.BlockSpec((devices, None, block_rows, span_z), lambda i: (0, i, 0, 0)),
                block,
                whole((2 * span_y, 2 * span_y)),
                whole((2 * span_y, 2 * span_y)),
                whole((2 * span_z, 2 * span_z)),
                whole((2 * span_z, 2 * span_z)),
            ],
            out_specs=block,
            input_output_aliases={1: 0},
            compiler_params=params,
            cost_estimate=pl.CostEstimate(flops=10**9, bytes_accessed=3 * 10**6, transcendentals=0),
            name="to_planes",
        )(returned[j], residual, *fwd_y, *fwd_z)
    return (residual, jnp.stack([m_real, m_imag]))


def solution(mesh):
    return jax.shard_map(
        functools.partial(on_device, mesh.shape["ga"]),
        mesh=mesh,
        in_specs=(
            P("rep", None, "ga", None, None),
            P("rep"),
            P("rep", "ga", None),
            P(("rep", "ga"), None, None, None),
            P(("rep", "ga"), None),
            P("rep", None),
        ),
        out_specs=(P("rep", None, "ga", None, None), P(None, "rep", None)),
        check_vma=False,
    )
```

```python
import functools
import math

import jax
import jax.numpy as jnp
import numpy as np
from jax import lax
from jax.experimental import pallas as pl
from jax.experimental.pallas import tpu as pltpu
from jax.sharding import PartitionSpec as P

highest = lax.Precision.HIGHEST
f32 = jnp.float32
bf16 = jnp.bfloat16
vmem_limit = 48 * 1024 * 1024


def signed_index(values, length):
    return jnp.where(values < length // 2, values, values - length)


def dft(length, orient):
    index = np.arange(length)
    angles = (index[:, None] * index[None, :] % length) * (2.0 * math.pi / length)
    factor = 1.0 / math.sqrt(length)
    return np.cos(angles) * factor, orient * np.sin(angles) * factor


def left_table(length, orient, row_order=None, col_order=None):
    cosine, sine = dft(length, orient)
    if row_order is not None:
        cosine, sine = cosine[row_order], sine[row_order]
    if col_order is not None:
        cosine, sine = cosine[:, col_order], sine[:, col_order]
    return np.block([[cosine, -sine], [sine, cosine]])


def right_table(length, orient):
    cosine, sine = dft(length, orient)
    return np.block([[cosine, sine], [-sine, cosine]])


def split(values):
    high = values.astype(bf16)
    low = (values - high.astype(f32)).astype(bf16)
    return high, low


def split_outside(values):
    high = lax.reduce_precision(values, exponent_bits=8, mantissa_bits=7)
    return high.astype(bf16), (values - high).astype(bf16)


def const_parts(table):
    table = np.asarray(table, np.float32)
    high = table.astype(jnp.bfloat16)
    low = (table - high.astype(np.float32)).astype(jnp.bfloat16)
    return high, low


def left_const(table):
    high, low = const_parts(table)
    return jnp.asarray(np.concatenate([high, high, low], axis=1))


def right_const(table):
    high, low = const_parts(table)
    return jnp.asarray(np.concatenate([high, high, low], axis=0))


def dot_left(table, values):
    high, low = split(values)
    return jnp.dot(
        table, jnp.concatenate([high, low, high], axis=0), preferred_element_type=f32
    )


def dot_right(values, table):
    high, low = split(values)
    return jnp.dot(
        jnp.concatenate([high, low, high], axis=1), table, preferred_element_type=f32
    )


def to_rows_kernel(devices, rows, planes, psi, y_table, z_table, out):
    real = jnp.concatenate([psi[0, 0, p] - psi[1, 1, p] for p in range(planes)], axis=1)
    imag = jnp.concatenate([psi[0, 1, p] + psi[1, 0, p] for p in range(planes)], axis=1)
    span_y, span_z = psi.shape[3], psi.shape[4]
    along_y = dot_left(y_table[...], jnp.concatenate([real, imag], axis=0))
    flat = out.reshape(devices * 2 * planes * rows, span_z)
    for p in range(planes):
        cols = slice(p * span_z, (p + 1) * span_z)
        plane = jnp.concatenate([along_y[:span_y, cols], along_y[span_y:, cols]], axis=1)
        values = dot_right(plane, z_table[...])
        for part in range(2):
            for r in range(rows):
                start = (r * planes + p) * 2 + part
                flat[pl.ds(start, devices, stride=2 * planes * rows), :] = values[
                    r * devices : (r + 1) * devices, part * span_z : (part + 1) * span_z
                ]


def real_space_kernel(devices, rows, planes, recv, pot, inverse, forward, back, field):
    span_x = pot.shape[0]
    block = 2 * planes
    columns = [
        recv[:, r * block : (r + 1) * block, :].reshape(devices * block, recv.shape[2])
        for r in range(rows)
    ]
    spatial = dot_left(inverse[...], jnp.concatenate(columns, axis=1))
    for band in range(2):
        one = spatial[band * span_x : (band + 1) * span_x]
        field[band] = one
        spectral = dot_left(forward[...], one * pot[...])
        for r in range(rows):
            cols = spectral[:, r * recv.shape[2] : (r + 1) * recv.shape[2]]
            back[:, band, r * block : (r + 1) * block] = cols.reshape(devices, block, recv.shape[2])


def real_gram_kernel(bands, field, pot, out):
    pairs = [(a, b) for a in range(bands) for b in range(a, bands)]
    for weighted in range(2):

        def step(i, sums):
            rows = pl.ds(pl.multiple_of(i * 8, 8), 8)
            values = [field[a, rows, :] for a in range(bands)]
            other = [v * pot[rows, :] for v in values] if weighted else values
            result = []
            for (a, b), total in zip(pairs, sums):
                product = values[a] * other[b]
                lanes = product[:, :128]
                for c in range(128, product.shape[1], 128):
                    lanes = lanes + product[:, c : c + 128]
                result.append(total + lanes)
            return tuple(result)

        sums = lax.fori_loop(
            0, pot.shape[0] // 8, step, tuple(jnp.zeros((8, 128), f32) for _ in pairs)
        )
        for (a, b), total in zip(pairs, sums):
            line = jnp.sum(total, axis=0, keepdims=True)
            out[weighted, a, b : b + 1, :] = line
            out[weighted, b, a : a + 1, :] = line


def to_planes_kernel(devices, rows, planes, recv, base, y_table, z_table, out):
    span_y, span_z = base.shape[3], base.shape[4]
    flat = recv.reshape(devices * 2 * planes * rows, span_z)
    columns = []
    for p in range(planes):
        columns.append(
            jnp.concatenate(
                [
                    flat[pl.ds((r * planes + p) * 2 + part, devices, stride=2 * planes * rows), :]
                    for part in range(2)
                    for r in range(rows)
                ],
                axis=0,
            )
        )
    along_y = dot_left(y_table[...], jnp.concatenate(columns, axis=1))
    for p in range(planes):
        cols = slice(p * span_z, (p + 1) * span_z)
        plane = jnp.concatenate([along_y[:span_y, cols], along_y[span_y:, cols]], axis=1)
        values = dot_right(plane, z_table[...])
        for part in range(2):
            out[0, part, p] = base[0, part, p] + values[:, part * span_z : (part + 1) * span_z]


def block_rows_of(psi, beta, slots):
    bands, _, span, span_z = psi.shape
    psi_flat = psi.reshape(bands * 2 * span, span_z)
    psi_rows = [psi_flat[pl.ds(y, 2 * bands, stride=span), :] for y in range(span)]
    beta_rows = [
        jnp.concatenate(
            [beta[pl.ds(2 * y + part, slots, stride=2 * span), :] for part in range(2)], axis=0
        )
        for y in range(span)
    ]
    return psi_rows, beta_rows


def project_kernel(slots, psi, beta, kinetic, out):
    bands, _, span, span_z = psi.shape
    psi_rows, beta_rows = block_rows_of(psi, beta, slots)
    kin_rows = [psi_rows[y] * kinetic[y : y + 1, :] for y in range(span)]
    right = jnp.concatenate(split(jnp.concatenate(psi_rows, axis=1)), axis=0)
    left = jnp.concatenate(
        split(jnp.concatenate(beta_rows, axis=1)) + split(jnp.concatenate(kin_rows, axis=1)), axis=0
    )
    full = lax.dot_general(left, right, (((1,), (1,)), ((), ())), preferred_element_type=f32)
    width, height = 2 * bands, 2 * slots
    full = full[:, :width] + full[:, width:]
    out[0:height] = full[0:height] + full[height : 2 * height]
    rest = full[2 * height :]
    out[height:] = rest[0:width] + rest[width:]


def base_kernel(slots, psi, beta, kinetic, coefs, out):
    bands, _, span, span_z = psi.shape
    psi_rows, beta_rows = block_rows_of(psi, beta, slots)
    values = jnp.concatenate(
        [jnp.concatenate(psi_rows, axis=1), jnp.concatenate(beta_rows, axis=1)], axis=0
    )
    high, low = split(coefs[...])
    summed = dot_left(jnp.concatenate([high, high, low], axis=1), values)
    flat = out.reshape(bands * 2 * span, span_z)
    for y in range(span):
        flat[pl.ds(y, 2 * bands, stride=span), :] = (
            psi_rows[y] * kinetic[y : y + 1, :] + summed[:, y * span_z : (y + 1) * span_z]
        )


def whole(shape):
    return pl.BlockSpec(shape, lambda *_: (0,) * len(shape))


def subspace_solve(s_real, h_real, h_imag):
    factor = jnp.linalg.cholesky(s_real)
    solved = jax.scipy.linalg.cho_solve((factor, True), jnp.concatenate([h_real, h_imag], axis=1))
    order_size = s_real.shape[0]
    return (solved[:, :order_size], solved[:, order_size:])


def tdot(pattern, left, right):
    return jnp.einsum(pattern, left, right, precision=highest, preferred_element_type=jnp.float32)


def sum_over(values, devices):
    if devices & (devices - 1):
        return lax.psum(values, "ga")
    step = 1
    while step < devices:
        values = values + lax.ppermute(values, "ga", [(d, d ^ step) for d in range(devices)])
        step *= 2
    return values


def on_device(devices, orbitals, plane_order, potential, projectors, slot_owner, strengths):
    bands = orbitals.shape[0]
    planes = orbitals.shape[2]
    span_y = orbitals.shape[3]
    span_z = orbitals.shape[4]
    span_x = plane_order.shape[0]
    blocks, slots = slot_owner.shape
    owners = strengths.shape[0] * strengths.shape[1]
    rows = span_y // devices
    block_rows = 2 * planes * rows
    lanes = rows * span_z
    pairs = bands // 2
    block_span = projectors.shape[3] // span_z
    per_plane = span_y // block_span
    grid_x = jnp.arange(span_x, dtype=jnp.int32)
    grid_y = jnp.arange(span_y, dtype=jnp.int32)
    grid_z = jnp.arange(span_z, dtype=jnp.int32)
    params = pltpu.CompilerParams(vmem_limit_bytes=vmem_limit)

    def cost(flops, moved):
        return pl.CostEstimate(flops=flops, bytes_accessed=moved, transcendentals=0)

    row_major = (np.arange(devices)[None, :] * rows + np.arange(rows)[:, None]).reshape(-1)
    inv_y = left_const(left_table(span_y, 1.0, row_order=row_major))
    inv_z = right_const(right_table(span_z, 1.0))
    fwd_y = left_const(left_table(span_y, -1.0, col_order=row_major))
    fwd_z = right_const(right_table(span_z, -1.0))

    sent = pl.pallas_call(
        functools.partial(to_rows_kernel, devices, rows, planes),
        out_shape=jax.ShapeDtypeStruct((devices, pairs, block_rows, span_z), f32),
        grid=(pairs,),
        in_specs=[
            pl.BlockSpec((2, 2, planes, span_y, span_z), lambda j: (j, 0, 0, 0, 0)),
            whole(inv_y.shape),
            whole(inv_z.shape),
        ],
        out_specs=pl.BlockSpec((devices, None, block_rows, span_z), lambda j: (0, j, 0, 0)),
        compiler_params=params,
        cost_estimate=cost(4 * 10**9, 6 * 10**6),
        name="to_rows",
    )(orbitals, inv_y, inv_z)
    arrived = lax.all_to_all(sent, "ga", split_axis=0, concat_axis=0, tiled=True)

    phases = (plane_order[:, None] * grid_x[None, :]) % span_x
    angles = phases.astype(f32) * (2.0 * math.pi / span_x)
    factor = 1.0 / math.sqrt(span_x)
    cosine, sine = jnp.cos(angles) * factor, jnp.sin(angles) * factor
    fwd_x = jnp.stack([cosine, -sine], axis=1).reshape(2 * span_x, span_x)
    other = jnp.stack([sine, cosine], axis=1).reshape(2 * span_x, span_x)
    inv_x = jnp.concatenate([fwd_x.T, other.T], axis=0)
    high, low = split_outside(fwd_x)
    fwd_x = jnp.concatenate([high, high, low], axis=1)
    high, low = split_outside(inv_x)
    inv_x = jnp.concatenate([high, high, low], axis=1)
    pot = potential.reshape(span_x, lanes)

    local_order = lax.dynamic_slice_in_dim(plane_order, lax.axis_index("ga") * planes, planes)
    freq_x = signed_index(local_order, span_x).astype(f32) / span_x
    freq_y = signed_index(grid_y, span_y).astype(f32) / span_y
    freq_z = signed_index(grid_z, span_z).astype(f32) / span_z
    kinetic = 2.0 * (
        freq_x[:, None, None] ** 2 + freq_y[None, :, None] ** 2 + freq_z[None, None, :] ** 2
    )
    beta = projectors.reshape(blocks, slots, 2, block_span, span_z)
    beta = beta.transpose(0, 1, 3, 2, 4).reshape(blocks, slots * block_span * 2, span_z)
    block_specs = [
        pl.BlockSpec(
            (bands, 2, None, block_span, span_z),
            lambda g: (0, 0, g // per_plane, g % per_plane, 0),
        ),
        pl.BlockSpec((None, slots * block_span * 2, span_z), lambda g: (g, 0, 0)),
        pl.BlockSpec((None, block_span, span_z), lambda g: (g // per_plane, g % per_plane, 0)),
    ]
    products = pl.pallas_call(
        functools.partial(project_kernel, slots),
        out_shape=jax.ShapeDtypeStruct((blocks, 2 * slots + 2 * bands, 2 * bands), f32),
        grid=(blocks,),
        in_specs=block_specs,
        out_specs=pl.BlockSpec((None, 2 * slots + 2 * bands, 2 * bands), lambda g: (g, 0, 0)),
        compiler_params=params,
        cost_estimate=cost(8 * 10**9, 8 * 10**6),
        name="project",
    )(orbitals, beta, kinetic)
    with_real = products[:, :slots].reshape(blocks, slots, bands, 2)
    with_imag = products[:, slots : 2 * slots].reshape(blocks, slots, bands, 2)
    proj = jnp.concatenate(
        [
            with_real[..., 0] + with_imag[..., 1],
            with_real[..., 1] - with_imag[..., 0],
        ],
        axis=-1,
    )
    owned = (
        slot_owner[:, :, None] == jnp.arange(owners, dtype=jnp.int32)[None, None, :]
    ).astype(f32)
    proj = tdot("gsj,gsc->jc", owned, proj)
    kin = jnp.sum(products[:, 2 * slots :], axis=0).reshape(bands, 2, bands, 2)
    kin = kin[:, 0, :, 0] + kin[:, 1, :, 1]

    back, field = pl.pallas_call(
        functools.partial(real_space_kernel, devices, rows, planes),
        out_shape=(
            jax.ShapeDtypeStruct((devices, bands, block_rows, span_z), f32),
            jax.ShapeDtypeStruct((bands, span_x, lanes), f32),
        ),
        grid=(pairs,),
        in_specs=[
            pl.BlockSpec((devices, None, block_rows, span_z), lambda j: (0, j, 0, 0)),
            whole(pot.shape),
            whole(inv_x.shape),
            whole(fwd_x.shape),
        ],
        out_specs=(
            pl.BlockSpec((devices, 2, block_rows, span_z), lambda j: (0, j, 0, 0)),
            pl.BlockSpec((2, span_x, lanes), lambda j: (j, 0, 0)),
        ),
        compiler_params=params,
        cost_estimate=cost(4 * 10**9, 8 * 10**6),
        name="real_space",
    )(arrived, pot, inv_x, fwd_x)
    returned = lax.all_to_all(back, "ga", split_axis=0, concat_axis=0, tiled=True)

    grams = pl.pallas_call(
        functools.partial(real_gram_kernel, bands),
        out_shape=jax.ShapeDtypeStruct((2, bands, bands, 128), f32),
        compiler_params=params,
        cost_estimate=cost(10**7, 2 * 10**6),
        name="real_gram",
    )(field, pot)
    grams = jnp.sum(grams, axis=-1)
    own = jnp.concatenate([proj, jnp.concatenate([grams[0], grams[1] + kin], axis=1)], axis=0)
    total = sum_over(own, devices)
    proj, s_real, h_real = total[:owners], total[owners:, :bands], total[owners:, bands:]
    weighted = strengths.reshape(-1)[:, None] * proj
    p_real, p_imag = proj[:, :bands], proj[:, bands:]
    w_real, w_imag = weighted[:, :bands], weighted[:, bands:]
    h_real = h_real + tdot("ja,jb->ab", p_real, w_real) + tdot("ja,jb->ab", p_imag, w_imag)
    h_imag = tdot("ja,jb->ab", p_real, w_imag) - tdot("ja,jb->ab", p_imag, w_real)
    m_real, m_imag = subspace_solve(s_real, h_real, h_imag)

    coefs = tdot("gsj,jc->gcs", owned, weighted)
    c_real, c_imag = coefs[:, :bands], coefs[:, bands:]
    from_beta = jnp.stack(
        [
            jnp.concatenate([c_real, -c_imag], axis=2),
            jnp.concatenate([c_imag, c_real], axis=2),
        ],
        axis=2,
    ).reshape(blocks, 2 * bands, 2 * slots)
    from_psi = jnp.stack(
        [
            jnp.stack([-m_real.T, m_imag.T], axis=-1),
            jnp.stack([-m_imag.T, -m_real.T], axis=-1),
        ],
        axis=1,
    ).reshape(1, 2 * bands, 2 * bands)
    coefs = jnp.concatenate(
        [jnp.broadcast_to(from_psi, (blocks, 2 * bands, 2 * bands)), from_beta], axis=2
    )
    base = pl.pallas_call(
        functools.partial(base_kernel, slots),
        out_shape=jax.ShapeDtypeStruct(orbitals.shape, f32),
        grid=(blocks,),
        in_specs=block_specs
        + [pl.BlockSpec((None, 2 * bands, 2 * bands + 2 * slots), lambda g: (g, 0, 0))],
        out_specs=block_specs[0],
        compiler_params=params,
        cost_estimate=cost(8 * 10**9, 12 * 10**6),
        name="base",
    )(orbitals, beta, kinetic, coefs)

    one_band = pl.BlockSpec((1, 2, planes, span_y, span_z), lambda b: (b, 0, 0, 0, 0))
    residual = pl.pallas_call(
        functools.partial(to_planes_kernel, devices, rows, planes),
        out_shape=jax.ShapeDtypeStruct(orbitals.shape, f32),
        grid=(bands,),
        in_specs=[
            pl.BlockSpec((devices, None, block_rows, span_z), lambda b: (0, b, 0, 0)),
            one_band,
            whole(fwd_y.shape),
            whole(fwd_z.shape),
        ],
        out_specs=one_band,
        compiler_params=params,
        cost_estimate=cost(8 * 10**9, 12 * 10**6),
        name="to_planes",
    )(returned, base, fwd_y, fwd_z)
    return (residual, jnp.stack([m_real, m_imag]))


def solution(mesh):
    return jax.shard_map(
        functools.partial(on_device, mesh.shape["ga"]),
        mesh=mesh,
        in_specs=(
            P("rep", None, "ga", None, None),
            P("rep"),
            P("rep", "ga", None),
            P(("rep", "ga"), None, None, None),
            P(("rep", "ga"), None),
            P("rep", None),
        ),
        out_specs=(P("rep", None, "ga", None, None), P(None, "rep", None)),
        check_vma=False,
    )
```

```python
import functools
import math

import jax
import jax.numpy as jnp
import numpy as np
from jax import lax
from jax.experimental import pallas as pl
from jax.experimental.pallas import tpu as pltpu
from jax.sharding import PartitionSpec as P

highest = lax.Precision.HIGHEST
f32 = jnp.float32
bf16 = jnp.bfloat16
vmem_limit = 48 * 1024 * 1024


def signed_index(values, length):
    return jnp.where(values < length // 2, values, values - length)


def dft(length, orient):
    index = np.arange(length)
    angles = (index[:, None] * index[None, :] % length) * (2.0 * math.pi / length)
    factor = 1.0 / math.sqrt(length)
    return np.cos(angles) * factor, orient * np.sin(angles) * factor


def left_table(length, orient, row_order=None, col_order=None):
    cosine, sine = dft(length, orient)
    if row_order is not None:
        cosine, sine = cosine[row_order], sine[row_order]
    if col_order is not None:
        cosine, sine = cosine[:, col_order], sine[:, col_order]
    return np.block([[cosine, -sine], [sine, cosine]])


def right_table(length, orient):
    cosine, sine = dft(length, orient)
    return np.block([[cosine, sine], [-sine, cosine]])


def split(values):
    high = values.astype(bf16)
    low = (values - high.astype(f32)).astype(bf16)
    return high, low


def split_outside(values):
    high = lax.reduce_precision(values, exponent_bits=8, mantissa_bits=7)
    return high.astype(bf16), (values - high).astype(bf16)


def const_parts(table):
    table = np.asarray(table, np.float32)
    high = table.astype(jnp.bfloat16)
    low = (table - high.astype(np.float32)).astype(jnp.bfloat16)
    return high, low


def left_const(table):
    high, low = const_parts(table)
    return jnp.asarray(np.concatenate([high, high, low], axis=1))


def right_const(table):
    high, low = const_parts(table)
    return jnp.asarray(np.concatenate([high, high, low], axis=0))


def dot_left(table, values):
    high, low = split(values)
    return jnp.dot(
        table, jnp.concatenate([high, low, high], axis=0), preferred_element_type=f32
    )


def dot_right(values, table):
    high, low = split(values)
    return jnp.dot(
        jnp.concatenate([high, low, high], axis=1), table, preferred_element_type=f32
    )


def to_rows_kernel(devices, rows, planes, psi, y_table, z_table, out):
    real = jnp.concatenate([psi[0, 0, p] - psi[1, 1, p] for p in range(planes)], axis=1)
    imag = jnp.concatenate([psi[0, 1, p] + psi[1, 0, p] for p in range(planes)], axis=1)
    span_y, span_z = psi.shape[3], psi.shape[4]
    along_y = dot_left(y_table[...], jnp.concatenate([real, imag], axis=0))
    flat = out.reshape(devices * 2 * planes * rows, span_z)
    for p in range(planes):
        cols = slice(p * span_z, (p + 1) * span_z)
        plane = jnp.concatenate([along_y[:span_y, cols], along_y[span_y:, cols]], axis=1)
        values = dot_right(plane, z_table[...])
        for part in range(2):
            for r in range(rows):
                start = (r * planes + p) * 2 + part
                flat[pl.ds(start, devices, stride=2 * planes * rows), :] = values[
                    r * devices : (r + 1) * devices, part * span_z : (part + 1) * span_z
                ]


def real_space_kernel(devices, rows, planes, recv, pot, inverse, forward, _, field, *rest):
    back, staged = rest[:-1], rest[-1]
    span_x = pot.shape[0]
    span_z = recv.shape[2]
    block = 2 * planes
    size = block * rows
    columns = [
        recv[:, r * block : (r + 1) * block, :].reshape(devices * block, span_z)
        for r in range(rows)
    ]
    spatial = dot_left(inverse[...], jnp.concatenate(columns, axis=1))
    for band in range(2):
        one = spatial[band * span_x : (band + 1) * span_x]
        field[band] = one
        spectral = dot_left(forward[...], one * pot[...])
        for part in range(2):
            for p in range(planes):
                first = (part * planes + p) * devices
                for r in range(rows):
                    staged[band, pl.ds((p * rows + r) * 2 + part, devices, stride=size), :] = (
                        spectral[first : first + devices, r * span_z : (r + 1) * span_z]
                    )
        for k in range(devices):
            back[k][band] = staged[band, k * size : (k + 1) * size, :]


def real_gram_kernel(bands, field, pot, out):
    pairs = [(a, b) for a in range(bands) for b in range(a, bands)]
    for weighted in range(2):

        def step(i, sums):
            rows = pl.ds(pl.multiple_of(i * 8, 8), 8)
            values = [field[a, rows, :] for a in range(bands)]
            other = [v * pot[rows, :] for v in values] if weighted else values
            result = []
            for (a, b), total in zip(pairs, sums):
                product = values[a] * other[b]
                lanes = product[:, :128]
                for c in range(128, product.shape[1], 128):
                    lanes = lanes + product[:, c : c + 128]
                result.append(total + lanes)
            return tuple(result)

        sums = lax.fori_loop(
            0, pot.shape[0] // 8, step, tuple(jnp.zeros((8, 128), f32) for _ in pairs)
        )
        for (a, b), total in zip(pairs, sums):
            line = jnp.sum(total, axis=0, keepdims=True)
            out[weighted, a, b : b + 1, :] = line
            out[weighted, b, a : a + 1, :] = line


def to_planes_kernel(rows, planes, *refs):
    recv, (base, y_table, z_table, out) = refs[:-4], refs[-4:]
    span_y, span_z = base.shape[3], base.shape[4]
    columns = []
    for p in range(planes):
        part_rows = slice(2 * rows * p, 2 * rows * (p + 1))
        columns.append(jnp.concatenate([one[part_rows, :] for one in recv], axis=0))
    along_y = dot_left(y_table[...], jnp.concatenate(columns, axis=1))
    for p in range(planes):
        cols = slice(p * span_z, (p + 1) * span_z)
        plane = jnp.concatenate([along_y[:span_y, cols], along_y[span_y:, cols]], axis=1)
        values = dot_right(plane, z_table[...])
        for part in range(2):
            out[0, part, p] = base[0, part, p] + values[:, part * span_z : (part + 1) * span_z]


def block_rows_of(psi, beta, slots):
    bands, _, span, span_z = psi.shape
    psi_flat = psi.reshape(bands * 2 * span, span_z)
    psi_rows = [psi_flat[pl.ds(y, 2 * bands, stride=span), :] for y in range(span)]
    beta_rows = [
        jnp.concatenate(
            [beta[pl.ds(2 * y + part, slots, stride=2 * span), :] for part in range(2)], axis=0
        )
        for y in range(span)
    ]
    return psi_rows, beta_rows


def project_kernel(slots, psi, beta, kinetic, out):
    bands, _, span, span_z = psi.shape
    psi_rows, beta_rows = block_rows_of(psi, beta, slots)
    kin_rows = [psi_rows[y] * kinetic[y : y + 1, :] for y in range(span)]
    right = jnp.concatenate(split(jnp.concatenate(psi_rows, axis=1)), axis=0)
    left = jnp.concatenate(
        split(jnp.concatenate(beta_rows, axis=1)) + split(jnp.concatenate(kin_rows, axis=1)), axis=0
    )
    full = lax.dot_general(left, right, (((1,), (1,)), ((), ())), preferred_element_type=f32)
    width, height = 2 * bands, 2 * slots
    full = full[:, :width] + full[:, width:]
    out[0:height] = full[0:height] + full[height : 2 * height]
    rest = full[2 * height :]
    out[height:] = rest[0:width] + rest[width:]


def base_kernel(slots, psi, beta, kinetic, coefs, out):
    bands, _, span, span_z = psi.shape
    psi_rows, beta_rows = block_rows_of(psi, beta, slots)
    values = jnp.concatenate(
        [jnp.concatenate(psi_rows, axis=1), jnp.concatenate(beta_rows, axis=1)], axis=0
    )
    high, low = split(coefs[...])
    summed = dot_left(jnp.concatenate([high, high, low], axis=1), values)
    flat = out.reshape(bands * 2 * span, span_z)
    for y in range(span):
        flat[pl.ds(y, 2 * bands, stride=span), :] = (
            psi_rows[y] * kinetic[y : y + 1, :] + summed[:, y * span_z : (y + 1) * span_z]
        )


def whole(shape):
    return pl.BlockSpec(shape, lambda *_: (0,) * len(shape))


def subspace_solve(s_real, h_real, h_imag):
    factor = jnp.linalg.cholesky(s_real)
    solved = jax.scipy.linalg.cho_solve((factor, True), jnp.concatenate([h_real, h_imag], axis=1))
    order_size = s_real.shape[0]
    return (solved[:, :order_size], solved[:, order_size:])


def tdot(pattern, left, right):
    return jnp.einsum(pattern, left, right, precision=highest, preferred_element_type=jnp.float32)


def partner(values, devices, k):
    return lax.ppermute(values, "ga", [(d, d ^ k) for d in range(devices)])


def sum_over(values, devices):
    step = devices // 4
    others = [partner(values, devices, k * step) for k in (1, 2, 3)]
    values = (values + others[0]) + (others[1] + others[2])
    while step > 1:
        step //= 2
        values = values + partner(values, devices, step)
    return values


def on_device(devices, orbitals, plane_order, potential, projectors, slot_owner, strengths):
    bands = orbitals.shape[0]
    planes = orbitals.shape[2]
    span_y = orbitals.shape[3]
    span_z = orbitals.shape[4]
    span_x = plane_order.shape[0]
    blocks, slots = slot_owner.shape
    owners = strengths.shape[0] * strengths.shape[1]
    rows = span_y // devices
    block_rows = 2 * planes * rows
    lanes = rows * span_z
    pairs = bands // 2
    block_span = projectors.shape[3] // span_z
    per_plane = span_y // block_span
    grid_x = jnp.arange(span_x, dtype=jnp.int32)
    grid_y = jnp.arange(span_y, dtype=jnp.int32)
    grid_z = jnp.arange(span_z, dtype=jnp.int32)
    params = pltpu.CompilerParams(vmem_limit_bytes=vmem_limit)

    def cost(flops, moved):
        return pl.CostEstimate(flops=flops, bytes_accessed=moved, transcendentals=0)

    row_major = (np.arange(devices)[None, :] * rows + np.arange(rows)[:, None]).reshape(-1)
    inv_y = left_const(left_table(span_y, 1.0, row_order=row_major))
    inv_z = right_const(right_table(span_z, 1.0))
    mine = lax.axis_index("ga")
    source = np.arange(2 * span_y) // (2 * rows)
    inner = np.arange(2 * span_y) % (2 * rows)
    columns = (inner % 2) * span_y + source * rows + inner // 2
    fwd_y = left_table(span_y, -1.0)[:, columns]
    fwd_y = jnp.asarray(np.concatenate(const_parts(fwd_y), axis=0))
    swap = jnp.arange(2 * span_y, dtype=jnp.int32)
    swap = (swap[:, None] == (swap[None, :] ^ (mine * 2 * rows))).astype(bf16)
    fwd_y = jnp.dot(fwd_y, swap, preferred_element_type=f32).astype(bf16)
    high, low = fwd_y[: 2 * span_y], fwd_y[2 * span_y :]
    fwd_y = jnp.concatenate([high, high, low], axis=1)
    fwd_z = right_const(right_table(span_z, -1.0))

    sent = pl.pallas_call(
        functools.partial(to_rows_kernel, devices, rows, planes),
        out_shape=jax.ShapeDtypeStruct((devices, pairs, block_rows, span_z), f32),
        grid=(pairs,),
        in_specs=[
            pl.BlockSpec((2, 2, planes, span_y, span_z), lambda j: (j, 0, 0, 0, 0)),
            whole(inv_y.shape),
            whole(inv_z.shape),
        ],
        out_specs=pl.BlockSpec((devices, None, block_rows, span_z), lambda j: (0, j, 0, 0)),
        compiler_params=params,
        cost_estimate=cost(4 * 10**9, 6 * 10**6),
        name="to_rows",
    )(orbitals, inv_y, inv_z)
    arrived = lax.all_to_all(sent, "ga", split_axis=0, concat_axis=0, tiled=True)

    def along_x(order):
        phases = (order[:, None] * grid_x[None, :]) % span_x
        angles = phases.astype(f32) * (2.0 * math.pi / span_x)
        factor = 1.0 / math.sqrt(span_x)
        return jnp.cos(angles) * factor, jnp.sin(angles) * factor

    members = jnp.arange(devices, dtype=jnp.int32) ^ mine
    partner_order = jnp.take(plane_order.reshape(devices, planes), members, axis=0).T.reshape(-1)
    cosine, sine = along_x(partner_order)
    fwd_x = jnp.concatenate([cosine, -sine], axis=0)
    cosine, sine = along_x(plane_order)
    inv_x = jnp.concatenate(
        [
            jnp.stack([cosine, -sine], axis=1).reshape(2 * span_x, span_x).T,
            jnp.stack([sine, cosine], axis=1).reshape(2 * span_x, span_x).T,
        ],
        axis=0,
    )
    high, low = split_outside(fwd_x)
    fwd_x = jnp.concatenate([high, high, low], axis=1)
    high, low = split_outside(inv_x)
    inv_x = jnp.concatenate([high, high, low], axis=1)
    pot = potential.reshape(span_x, lanes)

    local_order = lax.dynamic_slice_in_dim(plane_order, lax.axis_index("ga") * planes, planes)
    freq_x = signed_index(local_order, span_x).astype(f32) / span_x
    freq_y = signed_index(grid_y, span_y).astype(f32) / span_y
    freq_z = signed_index(grid_z, span_z).astype(f32) / span_z
    kinetic = 2.0 * (
        freq_x[:, None, None] ** 2 + freq_y[None, :, None] ** 2 + freq_z[None, None, :] ** 2
    )
    beta = projectors.reshape(blocks, slots, 2, block_span, span_z)
    beta = beta.transpose(0, 1, 3, 2, 4).reshape(blocks, slots * block_span * 2, span_z)
    block_specs = [
        pl.BlockSpec(
            (bands, 2, None, block_span, span_z),
            lambda g: (0, 0, g // per_plane, g % per_plane, 0),
        ),
        pl.BlockSpec((None, slots * block_span * 2, span_z), lambda g: (g, 0, 0)),
        pl.BlockSpec((None, block_span, span_z), lambda g: (g // per_plane, g % per_plane, 0)),
    ]
    products = pl.pallas_call(
        functools.partial(project_kernel, slots),
        out_shape=jax.ShapeDtypeStruct((blocks, 2 * slots + 2 * bands, 2 * bands), f32),
        grid=(blocks,),
        in_specs=block_specs,
        out_specs=pl.BlockSpec((None, 2 * slots + 2 * bands, 2 * bands), lambda g: (g, 0, 0)),
        compiler_params=params,
        cost_estimate=cost(8 * 10**9, 8 * 10**6),
        name="project",
    )(orbitals, beta, kinetic)
    with_real = products[:, :slots].reshape(blocks, slots, bands, 2)
    with_imag = products[:, slots : 2 * slots].reshape(blocks, slots, bands, 2)
    proj = jnp.concatenate(
        [
            with_real[..., 0] + with_imag[..., 1],
            with_real[..., 1] - with_imag[..., 0],
        ],
        axis=-1,
    )
    owned = (
        slot_owner[:, :, None] == jnp.arange(owners, dtype=jnp.int32)[None, None, :]
    ).astype(f32)
    proj = tdot("gsj,gsc->jc", owned, proj)
    kin = jnp.sum(products[:, 2 * slots :], axis=0).reshape(bands, 2, bands, 2)
    kin = kin[:, 0, :, 0] + kin[:, 1, :, 1]

    field, *back = pl.pallas_call(
        functools.partial(real_space_kernel, devices, rows, planes),
        out_shape=[jax.ShapeDtypeStruct((bands, span_x, lanes), f32)]
        + [jax.ShapeDtypeStruct((bands, block_rows, span_z), f32)] * devices,
        grid=(pairs,),
        in_specs=[
            pl.BlockSpec((devices, None, block_rows, span_z), lambda j: (0, j, 0, 0)),
            whole(pot.shape),
            whole(inv_x.shape),
            whole(fwd_x.shape),
            whole(proj.shape),
        ],
        out_specs=[pl.BlockSpec((2, span_x, lanes), lambda j: (j, 0, 0))]
        + [pl.BlockSpec((2, block_rows, span_z), lambda j: (j, 0, 0))] * devices,
        scratch_shapes=[pltpu.VMEM((2, devices * block_rows, span_z), f32)],
        compiler_params=params,
        cost_estimate=cost(4 * 10**9, 8 * 10**6),
        name="real_space",
    )(arrived, pot, inv_x, fwd_x, proj)
    returned = {k: partner(back[k], devices, k) for k in range(devices - 1, 0, -1)}
    returned = [back[0]] + [returned[k] for k in range(1, devices)]

    grams = pl.pallas_call(
        functools.partial(real_gram_kernel, bands),
        out_shape=jax.ShapeDtypeStruct((2, bands, bands, 128), f32),
        compiler_params=params,
        cost_estimate=cost(10**7, 2 * 10**6),
        name="real_gram",
    )(field, pot)
    grams = jnp.sum(grams, axis=-1)
    own = jnp.concatenate([proj, jnp.concatenate([grams[0], grams[1] + kin], axis=1)], axis=0)
    total = sum_over(own, devices)
    proj, s_real, h_real = total[:owners], total[owners:, :bands], total[owners:, bands:]
    weighted = strengths.reshape(-1)[:, None] * proj
    p_real, p_imag = proj[:, :bands], proj[:, bands:]
    w_real, w_imag = weighted[:, :bands], weighted[:, bands:]
    h_real = h_real + tdot("ja,jb->ab", p_real, w_real) + tdot("ja,jb->ab", p_imag, w_imag)
    h_imag = tdot("ja,jb->ab", p_real, w_imag) - tdot("ja,jb->ab", p_imag, w_real)
    m_real, m_imag = subspace_solve(s_real, h_real, h_imag)

    coefs = tdot("gsj,jc->gcs", owned, weighted)
    c_real, c_imag = coefs[:, :bands], coefs[:, bands:]
    from_beta = jnp.stack(
        [
            jnp.concatenate([c_real, -c_imag], axis=2),
            jnp.concatenate([c_imag, c_real], axis=2),
        ],
        axis=2,
    ).reshape(blocks, 2 * bands, 2 * slots)
    from_psi = jnp.stack(
        [
            jnp.stack([-m_real.T, m_imag.T], axis=-1),
            jnp.stack([-m_imag.T, -m_real.T], axis=-1),
        ],
        axis=1,
    ).reshape(1, 2 * bands, 2 * bands)
    coefs = jnp.concatenate(
        [jnp.broadcast_to(from_psi, (blocks, 2 * bands, 2 * bands)), from_beta], axis=2
    )
    base = pl.pallas_call(
        functools.partial(base_kernel, slots),
        out_shape=jax.ShapeDtypeStruct(orbitals.shape, f32),
        grid=(blocks,),
        in_specs=block_specs
        + [pl.BlockSpec((None, 2 * bands, 2 * bands + 2 * slots), lambda g: (g, 0, 0))],
        out_specs=block_specs[0],
        compiler_params=params,
        cost_estimate=cost(8 * 10**9, 12 * 10**6),
        name="base",
    )(orbitals, beta, kinetic, coefs)

    one_band = pl.BlockSpec((1, 2, planes, span_y, span_z), lambda b: (b, 0, 0, 0, 0))
    residual = pl.pallas_call(
        functools.partial(to_planes_kernel, rows, planes),
        out_shape=jax.ShapeDtypeStruct(orbitals.shape, f32),
        grid=(bands,),
        in_specs=[pl.BlockSpec((None, block_rows, span_z), lambda b: (b, 0, 0))] * devices
        + [
            one_band,
            whole(fwd_y.shape),
            whole(fwd_z.shape),
        ],
        out_specs=one_band,
        compiler_params=params,
        cost_estimate=cost(8 * 10**9, 12 * 10**6),
        name="to_planes",
    )(*returned, base, fwd_y, fwd_z)
    return (residual, jnp.stack([m_real, m_imag]))


def solution(mesh):
    return jax.shard_map(
        functools.partial(on_device, mesh.shape["ga"]),
        mesh=mesh,
        in_specs=(
            P("rep", None, "ga", None, None),
            P("rep"),
            P("rep", "ga", None),
            P(("rep", "ga"), None, None, None),
            P(("rep", "ga"), None),
            P("rep", None),
        ),
        out_specs=(P("rep", None, "ga", None, None), P(None, "rep", None)),
        check_vma=False,
    )
```

```python
import functools
import math

import jax
import jax.numpy as jnp
import numpy as np
from jax import lax
from jax.experimental import pallas as pl
from jax.experimental.pallas import tpu as pltpu
from jax.sharding import PartitionSpec as P

highest = lax.Precision.HIGHEST
f32 = jnp.float32
bf16 = jnp.bfloat16
vmem_limit = 60 * 1024 * 1024


def signed_index(values, length):
    return jnp.where(values < length // 2, values, values - length)


def dft(length, orient):
    index = np.arange(length)
    angles = (index[:, None] * index[None, :] % length) * (2.0 * math.pi / length)
    factor = 1.0 / math.sqrt(length)
    return np.cos(angles) * factor, orient * np.sin(angles) * factor


def left_table(length, orient, row_order=None, col_order=None):
    cosine, sine = dft(length, orient)
    if row_order is not None:
        cosine, sine = cosine[row_order], sine[row_order]
    if col_order is not None:
        cosine, sine = cosine[:, col_order], sine[:, col_order]
    return np.block([[cosine, -sine], [sine, cosine]])


def right_table(length, orient):
    cosine, sine = dft(length, orient)
    return np.block([[cosine, sine], [-sine, cosine]])


def split(values):
    high = values.astype(bf16)
    low = (values - high.astype(f32)).astype(bf16)
    return high, low


def split_outside(values):
    high = lax.reduce_precision(values, exponent_bits=8, mantissa_bits=7)
    return high.astype(bf16), (values - high).astype(bf16)


def const_parts(table):
    table = np.asarray(table, np.float32)
    high = table.astype(jnp.bfloat16)
    low = (table - high.astype(np.float32)).astype(jnp.bfloat16)
    return high, low


def left_const(table):
    high, low = const_parts(table)
    return jnp.asarray(np.concatenate([high, high, low], axis=1))


def right_const(table):
    high, low = const_parts(table)
    return jnp.asarray(np.concatenate([high, high, low], axis=0))


def dot_left(table, values):
    high, low = split(values)
    return jnp.dot(
        table, jnp.concatenate([high, low, high], axis=0), preferred_element_type=f32
    )


def dot_right(values, table):
    high, low = split(values)
    return jnp.dot(
        jnp.concatenate([high, low, high], axis=1), table, preferred_element_type=f32
    )


def groups(count, width):
    size = max(1, 256 // width)
    return [list(range(i, min(i + size, count))) for i in range(0, count, size)]


def parts_in_lanes(values, span, width):
    items = values.shape[1] // width
    return jnp.concatenate(
        [
            jnp.concatenate(
                [values[:span, i * width : (i + 1) * width], values[span:, i * width : (i + 1) * width]],
                axis=1,
            )
            for i in range(items)
        ],
        axis=0,
    )


def to_rows_kernel(devices, rows, planes, psi, y_table, z_table, out):
    span_y, span_z = psi.shape[3], psi.shape[4]
    flat = out.reshape(devices * 2 * planes * rows, span_z)
    for group in groups(planes, span_z):
        real = jnp.concatenate([psi[0, 0, p] - psi[1, 1, p] for p in group], axis=1)
        imag = jnp.concatenate([psi[0, 1, p] + psi[1, 0, p] for p in group], axis=1)
        along_y = dot_left(y_table[...], jnp.concatenate([real, imag], axis=0))
        values = dot_right(parts_in_lanes(along_y, span_y, span_z), z_table[...])
        for i, p in enumerate(group):
            for part in range(2):
                for r in range(rows):
                    first = i * span_y + r * devices
                    start = (r * planes + p) * 2 + part
                    flat[pl.ds(start, devices, stride=2 * planes * rows), :] = values[
                        first : first + devices, part * span_z : (part + 1) * span_z
                    ]


def real_space_kernel(devices, rows, planes, recv, pot, inverse, forward, _, back, field):
    span_x = pot.shape[0]
    block = 2 * planes
    span_z = recv.shape[2]
    for group in groups(rows, span_z):
        columns = [
            recv[:, r * block : (r + 1) * block, :].reshape(devices * block, span_z) for r in group
        ]
        spatial = dot_left(inverse[...], jnp.concatenate(columns, axis=1))
        lanes = slice(group[0] * span_z, (group[-1] + 1) * span_z)
        for band in range(2):
            one = spatial[band * span_x : (band + 1) * span_x]
            field[band, :, lanes] = one
            spectral = dot_left(forward[...], one * pot[:, lanes])
            for i, r in enumerate(group):
                cols = spectral[:, i * span_z : (i + 1) * span_z]
                back[:, band, r * block : (r + 1) * block] = cols.reshape(devices, block, span_z)


def real_gram_kernel(bands, field, pot, out):
    pairs = [(a, b) for a in range(bands) for b in range(a, bands)]
    for weighted in range(2):

        def step(i, sums):
            rows = pl.ds(pl.multiple_of(i * 8, 8), 8)
            values = [field[a, rows, :] for a in range(bands)]
            other = [v * pot[rows, :] for v in values] if weighted else values
            result = []
            for (a, b), total in zip(pairs, sums):
                product = values[a] * other[b]
                lanes = product[:, :128]
                for c in range(128, product.shape[1], 128):
                    lanes = lanes + product[:, c : c + 128]
                result.append(total + lanes)
            return tuple(result)

        sums = lax.fori_loop(
            0, pot.shape[0] // 8, step, tuple(jnp.zeros((8, 128), f32) for _ in pairs)
        )
        for (a, b), total in zip(pairs, sums):
            line = jnp.sum(total, axis=0, keepdims=True)
            out[weighted, a, b : b + 1, :] = line
            out[weighted, b, a : a + 1, :] = line


def to_planes_kernel(devices, rows, planes, recv, base, y_table, z_table, out):
    span_y, span_z = base.shape[3], base.shape[4]
    flat = recv.reshape(devices * 2 * planes * rows, span_z)
    for group in groups(planes, span_z):
        columns = [
            jnp.concatenate(
                [
                    flat[pl.ds((r * planes + p) * 2 + part, devices, stride=2 * planes * rows), :]
                    for part in range(2)
                    for r in range(rows)
                ],
                axis=0,
            )
            for p in group
        ]
        along_y = dot_left(y_table[...], jnp.concatenate(columns, axis=1))
        values = dot_right(parts_in_lanes(along_y, span_y, span_z), z_table[...])
        for i, p in enumerate(group):
            for part in range(2):
                out[0, part, p] = base[0, part, p] + (
                    values[i * span_y : (i + 1) * span_y, part * span_z : (part + 1) * span_z]
                )


def block_rows_of(psi, beta, slots):
    bands, _, span, span_z = psi.shape
    psi_flat = psi.reshape(bands * 2 * span, span_z)
    psi_rows = [psi_flat[pl.ds(y, 2 * bands, stride=span), :] for y in range(span)]
    beta_rows = [
        jnp.concatenate(
            [beta[pl.ds(2 * y + part, slots, stride=2 * span), :] for part in range(2)], axis=0
        )
        for y in range(span)
    ]
    return psi_rows, beta_rows


def project_kernel(slots, psi, beta, kinetic, out):
    bands, _, span, span_z = psi.shape
    psi_rows, beta_rows = block_rows_of(psi, beta, slots)
    kin_rows = [psi_rows[y] * kinetic[y : y + 1, :] for y in range(span)]
    right = jnp.concatenate(split(jnp.concatenate(psi_rows, axis=1)), axis=0)
    left = jnp.concatenate(
        split(jnp.concatenate(beta_rows, axis=1)) + split(jnp.concatenate(kin_rows, axis=1)), axis=0
    )
    full = lax.dot_general(left, right, (((1,), (1,)), ((), ())), preferred_element_type=f32)
    width, height = 2 * bands, 2 * slots
    full = full[:, :width] + full[:, width:]
    out[0:height] = full[0:height] + full[height : 2 * height]
    rest = full[2 * height :]
    out[height:] = rest[0:width] + rest[width:]


def base_kernel(slots, psi, beta, kinetic, coefs, out):
    bands, _, span, span_z = psi.shape
    psi_rows, beta_rows = block_rows_of(psi, beta, slots)
    values = jnp.concatenate(
        [jnp.concatenate(psi_rows, axis=1), jnp.concatenate(beta_rows, axis=1)], axis=0
    )
    high, low = split(coefs[...])
    summed = dot_left(jnp.concatenate([high, high, low], axis=1), values)
    flat = out.reshape(bands * 2 * span, span_z)
    for y in range(span):
        flat[pl.ds(y, 2 * bands, stride=span), :] = (
            psi_rows[y] * kinetic[y : y + 1, :] + summed[:, y * span_z : (y + 1) * span_z]
        )


def whole(shape):
    return pl.BlockSpec(shape, lambda *_: (0,) * len(shape))


def subspace_solve(s_real, h_real, h_imag):
    factor = jnp.linalg.cholesky(s_real)
    solved = jax.scipy.linalg.cho_solve((factor, True), jnp.concatenate([h_real, h_imag], axis=1))
    order_size = s_real.shape[0]
    return (solved[:, :order_size], solved[:, order_size:])


def tdot(pattern, left, right):
    return jnp.einsum(pattern, left, right, precision=highest, preferred_element_type=jnp.float32)


def partner(values, devices, k):
    return lax.ppermute(values, "ga", [(d, d ^ k) for d in range(devices)])


def sum_over(values, devices):
    if devices & (devices - 1) or devices < 4:
        return lax.psum(values, "ga")
    step = devices // 4
    others = [partner(values, devices, k * step) for k in (1, 2, 3)]
    values = (values + others[0]) + (others[1] + others[2])
    while step > 1:
        step //= 2
        values = values + partner(values, devices, step)
    return values


def on_device(devices, orbitals, plane_order, potential, projectors, slot_owner, strengths):
    bands = orbitals.shape[0]
    planes = orbitals.shape[2]
    span_y = orbitals.shape[3]
    span_z = orbitals.shape[4]
    span_x = plane_order.shape[0]
    blocks, slots = slot_owner.shape
    owners = strengths.shape[0] * strengths.shape[1]
    rows = span_y // devices
    block_rows = 2 * planes * rows
    lanes = rows * span_z
    pairs = bands // 2
    block_span = projectors.shape[3] // span_z
    per_plane = span_y // block_span
    grid_x = jnp.arange(span_x, dtype=jnp.int32)
    grid_y = jnp.arange(span_y, dtype=jnp.int32)
    grid_z = jnp.arange(span_z, dtype=jnp.int32)
    params = pltpu.CompilerParams(vmem_limit_bytes=vmem_limit)

    def cost(flops, moved):
        return pl.CostEstimate(flops=flops, bytes_accessed=moved, transcendentals=0)

    row_major = (np.arange(devices)[None, :] * rows + np.arange(rows)[:, None]).reshape(-1)
    inv_y = left_const(left_table(span_y, 1.0, row_order=row_major))
    inv_z = right_const(right_table(span_z, 1.0))
    fwd_y = left_const(left_table(span_y, -1.0, col_order=row_major))
    fwd_z = right_const(right_table(span_z, -1.0))

    sent = pl.pallas_call(
        functools.partial(to_rows_kernel, devices, rows, planes),
        out_shape=jax.ShapeDtypeStruct((devices, pairs, block_rows, span_z), f32),
        grid=(pairs,),
        in_specs=[
            pl.BlockSpec((2, 2, planes, span_y, span_z), lambda j: (j, 0, 0, 0, 0)),
            whole(inv_y.shape),
            whole(inv_z.shape),
        ],
        out_specs=pl.BlockSpec((devices, None, block_rows, span_z), lambda j: (0, j, 0, 0)),
        compiler_params=params,
        cost_estimate=cost(4 * 10**9, 6 * 10**6),
        name="to_rows",
    )(orbitals, inv_y, inv_z)
    arrived = lax.all_to_all(sent, "ga", split_axis=0, concat_axis=0, tiled=True)

    phases = (plane_order[:, None] * grid_x[None, :]) % span_x
    angles = phases.astype(f32) * (2.0 * math.pi / span_x)
    factor = 1.0 / math.sqrt(span_x)
    cosine, sine = jnp.cos(angles) * factor, jnp.sin(angles) * factor
    fwd_x = jnp.stack([cosine, -sine], axis=1).reshape(2 * span_x, span_x)
    other = jnp.stack([sine, cosine], axis=1).reshape(2 * span_x, span_x)
    inv_x = jnp.concatenate([fwd_x.T, other.T], axis=0)
    high, low = split_outside(fwd_x)
    fwd_x = jnp.concatenate([high, high, low], axis=1)
    high, low = split_outside(inv_x)
    inv_x = jnp.concatenate([high, high, low], axis=1)
    pot = potential.reshape(span_x, lanes)

    local_order = lax.dynamic_slice_in_dim(plane_order, lax.axis_index("ga") * planes, planes)
    freq_x = signed_index(local_order, span_x).astype(f32) / span_x
    freq_y = signed_index(grid_y, span_y).astype(f32) / span_y
    freq_z = signed_index(grid_z, span_z).astype(f32) / span_z
    kinetic = 2.0 * (
        freq_x[:, None, None] ** 2 + freq_y[None, :, None] ** 2 + freq_z[None, None, :] ** 2
    )
    beta = projectors.reshape(blocks, slots, 2, block_span, span_z)
    beta = beta.transpose(0, 1, 3, 2, 4).reshape(blocks, slots * block_span * 2, span_z)
    block_specs = [
        pl.BlockSpec(
            (bands, 2, None, block_span, span_z),
            lambda g: (0, 0, g // per_plane, g % per_plane, 0),
        ),
        pl.BlockSpec((None, slots * block_span * 2, span_z), lambda g: (g, 0, 0)),
        pl.BlockSpec((None, block_span, span_z), lambda g: (g // per_plane, g % per_plane, 0)),
    ]
    products = pl.pallas_call(
        functools.partial(project_kernel, slots),
        out_shape=jax.ShapeDtypeStruct((blocks, 2 * slots + 2 * bands, 2 * bands), f32),
        grid=(blocks,),
        in_specs=block_specs,
        out_specs=pl.BlockSpec((None, 2 * slots + 2 * bands, 2 * bands), lambda g: (g, 0, 0)),
        compiler_params=params,
        cost_estimate=cost(8 * 10**9, 8 * 10**6),
        name="project",
    )(orbitals, beta, kinetic)
    with_real = products[:, :slots].reshape(blocks, slots, bands, 2)
    with_imag = products[:, slots : 2 * slots].reshape(blocks, slots, bands, 2)
    proj = jnp.concatenate(
        [
            with_real[..., 0] + with_imag[..., 1],
            with_real[..., 1] - with_imag[..., 0],
        ],
        axis=-1,
    )
    owned = (
        slot_owner[:, :, None] == jnp.arange(owners, dtype=jnp.int32)[None, None, :]
    ).astype(f32)
    proj = tdot("gsj,gsc->jc", owned, proj)
    kin = jnp.sum(products[:, 2 * slots :], axis=0).reshape(bands, 2, bands, 2)
    kin = kin[:, 0, :, 0] + kin[:, 1, :, 1]

    back, field = pl.pallas_call(
        functools.partial(real_space_kernel, devices, rows, planes),
        out_shape=(
            jax.ShapeDtypeStruct((devices, bands, block_rows, span_z), f32),
            jax.ShapeDtypeStruct((bands, span_x, lanes), f32),
        ),
        grid=(pairs,),
        in_specs=[
            pl.BlockSpec((devices, None, block_rows, span_z), lambda j: (0, j, 0, 0)),
            whole(pot.shape),
            whole(inv_x.shape),
            whole(fwd_x.shape),
            whole(proj.shape),
        ],
        out_specs=(
            pl.BlockSpec((devices, 2, block_rows, span_z), lambda j: (0, j, 0, 0)),
            pl.BlockSpec((2, span_x, lanes), lambda j: (j, 0, 0)),
        ),
        compiler_params=params,
        cost_estimate=cost(4 * 10**9, 8 * 10**6),
        name="real_space",
    )(arrived, pot, inv_x, fwd_x, proj)
    returned = lax.all_to_all(back, "ga", split_axis=0, concat_axis=0, tiled=True)

    grams = pl.pallas_call(
        functools.partial(real_gram_kernel, bands),
        out_shape=jax.ShapeDtypeStruct((2, bands, bands, 128), f32),
        compiler_params=params,
        cost_estimate=cost(10**7, 2 * 10**6),
        name="real_gram",
    )(field, pot)
    grams = jnp.sum(grams, axis=-1)
    own = jnp.concatenate([proj, jnp.concatenate([grams[0], grams[1] + kin], axis=1)], axis=0)
    total = sum_over(own, devices)
    proj, s_real, h_real = total[:owners], total[owners:, :bands], total[owners:, bands:]
    weighted = strengths.reshape(-1)[:, None] * proj
    p_real, p_imag = proj[:, :bands], proj[:, bands:]
    w_real, w_imag = weighted[:, :bands], weighted[:, bands:]
    h_real = h_real + tdot("ja,jb->ab", p_real, w_real) + tdot("ja,jb->ab", p_imag, w_imag)
    h_imag = tdot("ja,jb->ab", p_real, w_imag) - tdot("ja,jb->ab", p_imag, w_real)
    m_real, m_imag = subspace_solve(s_real, h_real, h_imag)

    coefs = tdot("gsj,jc->gcs", owned, weighted)
    c_real, c_imag = coefs[:, :bands], coefs[:, bands:]
    from_beta = jnp.stack(
        [
            jnp.concatenate([c_real, -c_imag], axis=2),
            jnp.concatenate([c_imag, c_real], axis=2),
        ],
        axis=2,
    ).reshape(blocks, 2 * bands, 2 * slots)
    from_psi = jnp.stack(
        [
            jnp.stack([-m_real.T, m_imag.T], axis=-1),
            jnp.stack([-m_imag.T, -m_real.T], axis=-1),
        ],
        axis=1,
    ).reshape(1, 2 * bands, 2 * bands)
    coefs = jnp.concatenate(
        [jnp.broadcast_to(from_psi, (blocks, 2 * bands, 2 * bands)), from_beta], axis=2
    )
    base = pl.pallas_call(
        functools.partial(base_kernel, slots),
        out_shape=jax.ShapeDtypeStruct(orbitals.shape, f32),
        grid=(blocks,),
        in_specs=block_specs
        + [pl.BlockSpec((None, 2 * bands, 2 * bands + 2 * slots), lambda g: (g, 0, 0))],
        out_specs=block_specs[0],
        compiler_params=params,
        cost_estimate=cost(8 * 10**9, 12 * 10**6),
        name="base",
    )(orbitals, beta, kinetic, coefs)

    one_band = pl.BlockSpec((1, 2, planes, span_y, span_z), lambda b: (b, 0, 0, 0, 0))
    residual = pl.pallas_call(
        functools.partial(to_planes_kernel, devices, rows, planes),
        out_shape=jax.ShapeDtypeStruct(orbitals.shape, f32),
        grid=(bands,),
        in_specs=[
            pl.BlockSpec((devices, None, block_rows, span_z), lambda b: (0, b, 0, 0)),
            one_band,
            whole(fwd_y.shape),
            whole(fwd_z.shape),
        ],
        out_specs=one_band,
        compiler_params=params,
        cost_estimate=cost(8 * 10**9, 12 * 10**6),
        name="to_planes",
    )(returned, base, fwd_y, fwd_z)
    return (residual, jnp.stack([m_real, m_imag]))


def solution(mesh):
    return jax.shard_map(
        functools.partial(on_device, mesh.shape["ga"]),
        mesh=mesh,
        in_specs=(
            P("rep", None, "ga", None, None),
            P("rep"),
            P("rep", "ga", None),
            P(("rep", "ga"), None, None, None),
            P(("rep", "ga"), None),
            P("rep", None),
        ),
        out_specs=(P("rep", None, "ga", None, None), P(None, "rep", None)),
        check_vma=False,
    )
```

```python
import functools
import math

import jax
import jax.numpy as jnp
import numpy as np
from jax import lax
from jax.experimental import pallas as pl
from jax.experimental.pallas import tpu as pltpu
from jax.sharding import PartitionSpec as P

highest = lax.Precision.HIGHEST
f32 = jnp.float32
bf16 = jnp.bfloat16
vmem_limit = 60 * 1024 * 1024


def signed_index(values, length):
    return jnp.where(values < length // 2, values, values - length)


def dft(length, orient):
    index = np.arange(length)
    angles = (index[:, None] * index[None, :] % length) * (2.0 * math.pi / length)
    factor = 1.0 / math.sqrt(length)
    return np.cos(angles) * factor, orient * np.sin(angles) * factor


def left_table(length, orient, row_order=None, col_order=None):
    cosine, sine = dft(length, orient)
    if row_order is not None:
        cosine, sine = cosine[row_order], sine[row_order]
    if col_order is not None:
        cosine, sine = cosine[:, col_order], sine[:, col_order]
    return np.block([[cosine, -sine], [sine, cosine]])


def right_table(length, orient):
    cosine, sine = dft(length, orient)
    return np.block([[cosine, sine], [-sine, cosine]])


def split(values):
    high = values.astype(bf16)
    low = (values - high.astype(f32)).astype(bf16)
    return high, low


def split_outside(values):
    high = lax.reduce_precision(values, exponent_bits=8, mantissa_bits=7)
    return high.astype(bf16), (values - high).astype(bf16)


def const_parts(table):
    table = np.asarray(table, np.float32)
    high = table.astype(jnp.bfloat16)
    low = (table - high.astype(np.float32)).astype(jnp.bfloat16)
    return high, low


def left_const(table):
    high, low = const_parts(table)
    return jnp.asarray(np.concatenate([high, high, low], axis=1))


def right_const(table):
    high, low = const_parts(table)
    return jnp.asarray(np.concatenate([high, high, low], axis=0))


def dot_left(table, values):
    high, low = split(values)
    return jnp.dot(
        table, jnp.concatenate([high, low, high], axis=0), preferred_element_type=f32
    )


def dot_right(values, table):
    high, low = split(values)
    return jnp.dot(
        jnp.concatenate([high, low, high], axis=1), table, preferred_element_type=f32
    )


def groups(count, width):
    size = max(1, 256 // width)
    return [list(range(i, min(i + size, count))) for i in range(0, count, size)]


def parts_in_lanes(values, span, width):
    items = values.shape[1] // width
    return jnp.concatenate(
        [
            jnp.concatenate(
                [values[:span, i * width : (i + 1) * width], values[span:, i * width : (i + 1) * width]],
                axis=1,
            )
            for i in range(items)
        ],
        axis=0,
    )


def to_rows_kernel(devices, rows, planes, psi, y_table, z_table, out):
    span_y, span_z = psi.shape[3], psi.shape[4]
    flat = out.reshape(devices * 2 * planes * rows, span_z)
    for group in groups(planes, span_z):
        real = jnp.concatenate([psi[0, 0, p] - psi[1, 1, p] for p in group], axis=1)
        imag = jnp.concatenate([psi[0, 1, p] + psi[1, 0, p] for p in group], axis=1)
        along_y = dot_left(y_table[...], jnp.concatenate([real, imag], axis=0))
        values = dot_right(parts_in_lanes(along_y, span_y, span_z), z_table[...])
        for i, p in enumerate(group):
            for part in range(2):
                for r in range(rows):
                    first = i * span_y + r * devices
                    start = (r * planes + p) * 2 + part
                    flat[pl.ds(start, devices, stride=2 * planes * rows), :] = values[
                        first : first + devices, part * span_z : (part + 1) * span_z
                    ]


def real_space_kernel(devices, rows, planes, recv, pot, inverse, forward, _, back, field):
    span_x = pot.shape[0]
    block = 2 * planes
    span_z = recv.shape[2]
    for group in groups(rows, span_z):
        columns = [
            recv[:, r * block : (r + 1) * block, :].reshape(devices * block, span_z) for r in group
        ]
        spatial = dot_left(inverse[...], jnp.concatenate(columns, axis=1))
        lanes = slice(group[0] * span_z, (group[-1] + 1) * span_z)
        for band in range(2):
            one = spatial[band * span_x : (band + 1) * span_x]
            field[band, :, lanes] = one
            spectral = dot_left(forward[...], one * pot[:, lanes])
            for i, r in enumerate(group):
                cols = spectral[:, i * span_z : (i + 1) * span_z]
                back[:, band, r * block : (r + 1) * block] = cols.reshape(devices, block, span_z)


def real_gram_kernel(bands, *refs):
    fields, (pot, out) = refs[:-2], refs[-2:]
    held = fields[0].shape[0]
    pairs = [(a, b) for a in range(bands) for b in range(a, bands)]
    for weighted in range(2):

        def step(i, sums):
            rows = pl.ds(pl.multiple_of(i * 8, 8), 8)
            values = [fields[a // held][a % held, rows, :] for a in range(bands)]
            other = [v * pot[rows, :] for v in values] if weighted else values
            result = []
            for (a, b), total in zip(pairs, sums):
                product = values[a] * other[b]
                lanes = product[:, :128]
                for c in range(128, product.shape[1], 128):
                    lanes = lanes + product[:, c : c + 128]
                result.append(total + lanes)
            return tuple(result)

        sums = lax.fori_loop(
            0, pot.shape[0] // 8, step, tuple(jnp.zeros((8, 128), f32) for _ in pairs)
        )
        for (a, b), total in zip(pairs, sums):
            line = jnp.sum(total, axis=0, keepdims=True)
            out[weighted, a, b : b + 1, :] = line
            out[weighted, b, a : a + 1, :] = line


def to_planes_kernel(devices, rows, planes, recv, base, y_table, z_table, out):
    span_y, span_z = base.shape[3], base.shape[4]
    flat = recv.reshape(devices * 2 * planes * rows, span_z)
    for group in groups(planes, span_z):
        columns = [
            jnp.concatenate(
                [
                    flat[pl.ds((r * planes + p) * 2 + part, devices, stride=2 * planes * rows), :]
                    for part in range(2)
                    for r in range(rows)
                ],
                axis=0,
            )
            for p in group
        ]
        along_y = dot_left(y_table[...], jnp.concatenate(columns, axis=1))
        values = dot_right(parts_in_lanes(along_y, span_y, span_z), z_table[...])
        for i, p in enumerate(group):
            for part in range(2):
                out[0, part, p] = base[0, part, p] + (
                    values[i * span_y : (i + 1) * span_y, part * span_z : (part + 1) * span_z]
                )


def block_rows_of(psi, beta, slots):
    bands, _, span, span_z = psi.shape
    psi_flat = psi.reshape(bands * 2 * span, span_z)
    psi_rows = [psi_flat[pl.ds(y, 2 * bands, stride=span), :] for y in range(span)]
    beta_rows = [
        jnp.concatenate(
            [beta[pl.ds(2 * y + part, slots, stride=2 * span), :] for part in range(2)], axis=0
        )
        for y in range(span)
    ]
    return psi_rows, beta_rows


def project_kernel(slots, psi, beta, kinetic, out):
    bands, _, span, span_z = psi.shape
    psi_rows, beta_rows = block_rows_of(psi, beta, slots)
    kin_rows = [psi_rows[y] * kinetic[y : y + 1, :] for y in range(span)]
    right = jnp.concatenate(split(jnp.concatenate(psi_rows, axis=1)), axis=0)
    left = jnp.concatenate(
        split(jnp.concatenate(beta_rows, axis=1)) + split(jnp.concatenate(kin_rows, axis=1)), axis=0
    )
    full = lax.dot_general(left, right, (((1,), (1,)), ((), ())), preferred_element_type=f32)
    width, height = 2 * bands, 2 * slots
    full = full[:, :width] + full[:, width:]
    out[0:height] = full[0:height] + full[height : 2 * height]
    rest = full[2 * height :]
    out[height:] = rest[0:width] + rest[width:]


def base_kernel(slots, psi, beta, kinetic, coefs, out):
    bands, _, span, span_z = psi.shape
    psi_rows, beta_rows = block_rows_of(psi, beta, slots)
    values = jnp.concatenate(
        [jnp.concatenate(psi_rows, axis=1), jnp.concatenate(beta_rows, axis=1)], axis=0
    )
    high, low = split(coefs[...])
    summed = dot_left(jnp.concatenate([high, high, low], axis=1), values)
    flat = out.reshape(bands * 2 * span, span_z)
    for y in range(span):
        flat[pl.ds(y, 2 * bands, stride=span), :] = (
            psi_rows[y] * kinetic[y : y + 1, :] + summed[:, y * span_z : (y + 1) * span_z]
        )


def whole(shape):
    return pl.BlockSpec(shape, lambda *_: (0,) * len(shape))


def subspace_solve(s_real, h_real, h_imag):
    factor = jnp.linalg.cholesky(s_real)
    solved = jax.scipy.linalg.cho_solve((factor, True), jnp.concatenate([h_real, h_imag], axis=1))
    order_size = s_real.shape[0]
    return (solved[:, :order_size], solved[:, order_size:])


def tdot(pattern, left, right):
    return jnp.einsum(pattern, left, right, precision=highest, preferred_element_type=jnp.float32)


def partner(values, devices, k):
    return lax.ppermute(values, "ga", [(d, d ^ k) for d in range(devices)])


def sum_over(values, devices):
    if devices & (devices - 1) or devices < 4:
        return lax.psum(values, "ga")
    step = 1
    while step < devices // 4:
        values = values + partner(values, devices, step)
        step *= 2
    others = [partner(values, devices, k * step) for k in (1, 2, 3)]
    return (values + others[0]) + (others[1] + others[2])


def on_device(devices, orbitals, plane_order, potential, projectors, slot_owner, strengths):
    bands = orbitals.shape[0]
    planes = orbitals.shape[2]
    span_y = orbitals.shape[3]
    span_z = orbitals.shape[4]
    span_x = plane_order.shape[0]
    blocks, slots = slot_owner.shape
    owners = strengths.shape[0] * strengths.shape[1]
    rows = span_y // devices
    block_rows = 2 * planes * rows
    lanes = rows * span_z
    pairs = bands // 2
    block_span = projectors.shape[3] // span_z
    per_plane = span_y // block_span
    grid_x = jnp.arange(span_x, dtype=jnp.int32)
    grid_y = jnp.arange(span_y, dtype=jnp.int32)
    grid_z = jnp.arange(span_z, dtype=jnp.int32)
    params = pltpu.CompilerParams(vmem_limit_bytes=vmem_limit)

    def cost(flops, moved):
        return pl.CostEstimate(flops=flops, bytes_accessed=moved, transcendentals=0)

    row_major = (np.arange(devices)[None, :] * rows + np.arange(rows)[:, None]).reshape(-1)
    inv_y = left_const(left_table(span_y, 1.0, row_order=row_major))
    inv_z = right_const(right_table(span_z, 1.0))
    fwd_y = left_const(left_table(span_y, -1.0, col_order=row_major))
    fwd_z = right_const(right_table(span_z, -1.0))

    sent = pl.pallas_call(
        functools.partial(to_rows_kernel, devices, rows, planes),
        out_shape=jax.ShapeDtypeStruct((devices, pairs, block_rows, span_z), f32),
        grid=(pairs,),
        in_specs=[
            pl.BlockSpec((2, 2, planes, span_y, span_z), lambda j: (j, 0, 0, 0, 0)),
            whole(inv_y.shape),
            whole(inv_z.shape),
        ],
        out_specs=pl.BlockSpec((devices, None, block_rows, span_z), lambda j: (0, j, 0, 0)),
        compiler_params=params,
        cost_estimate=cost(4 * 10**9, 6 * 10**6),
        name="to_rows",
    )(orbitals, inv_y, inv_z)
    arrived = lax.all_to_all(sent, "ga", split_axis=0, concat_axis=0, tiled=True)

    phases = (plane_order[:, None] * grid_x[None, :]) % span_x
    angles = phases.astype(f32) * (2.0 * math.pi / span_x)
    factor = 1.0 / math.sqrt(span_x)
    cosine, sine = jnp.cos(angles) * factor, jnp.sin(angles) * factor
    fwd_x = jnp.stack([cosine, -sine], axis=1).reshape(2 * span_x, span_x)
    other = jnp.stack([sine, cosine], axis=1).reshape(2 * span_x, span_x)
    inv_x = jnp.concatenate([fwd_x.T, other.T], axis=0)
    high, low = split_outside(fwd_x)
    fwd_x = jnp.concatenate([high, high, low], axis=1)
    high, low = split_outside(inv_x)
    inv_x = jnp.concatenate([high, high, low], axis=1)
    pot = potential.reshape(span_x, lanes)

    local_order = lax.dynamic_slice_in_dim(plane_order, lax.axis_index("ga") * planes, planes)
    freq_x = signed_index(local_order, span_x).astype(f32) / span_x
    freq_y = signed_index(grid_y, span_y).astype(f32) / span_y
    freq_z = signed_index(grid_z, span_z).astype(f32) / span_z
    kinetic = 2.0 * (
        freq_x[:, None, None] ** 2 + freq_y[None, :, None] ** 2 + freq_z[None, None, :] ** 2
    )
    beta = projectors.reshape(blocks, slots, 2, block_span, span_z)
    beta = beta.transpose(0, 1, 3, 2, 4).reshape(blocks, slots * block_span * 2, span_z)
    block_specs = [
        pl.BlockSpec(
            (bands, 2, None, block_span, span_z),
            lambda g: (0, 0, g // per_plane, g % per_plane, 0),
        ),
        pl.BlockSpec((None, slots * block_span * 2, span_z), lambda g: (g, 0, 0)),
        pl.BlockSpec((None, block_span, span_z), lambda g: (g // per_plane, g % per_plane, 0)),
    ]
    products = pl.pallas_call(
        functools.partial(project_kernel, slots),
        out_shape=jax.ShapeDtypeStruct((blocks, 2 * slots + 2 * bands, 2 * bands), f32),
        grid=(blocks,),
        in_specs=block_specs,
        out_specs=pl.BlockSpec((None, 2 * slots + 2 * bands, 2 * bands), lambda g: (g, 0, 0)),
        compiler_params=params,
        cost_estimate=cost(8 * 10**9, 8 * 10**6),
        name="project",
    )(orbitals, beta, kinetic)
    with_real = products[:, :slots].reshape(blocks, slots, bands, 2)
    with_imag = products[:, slots : 2 * slots].reshape(blocks, slots, bands, 2)
    proj = jnp.concatenate(
        [
            with_real[..., 0] + with_imag[..., 1],
            with_real[..., 1] - with_imag[..., 0],
        ],
        axis=-1,
    )
    owned = (
        slot_owner[:, :, None] == jnp.arange(owners, dtype=jnp.int32)[None, None, :]
    ).astype(f32)
    proj = tdot("gsj,gsc->jc", owned, proj)
    kin = jnp.sum(products[:, 2 * slots :], axis=0).reshape(bands, 2, bands, 2)
    kin = kin[:, 0, :, 0] + kin[:, 1, :, 1]

    parts = 2 if pairs % 2 == 0 else 1
    share = pairs // parts
    returned, fields = [], []
    for c in range(parts):
        back, field = pl.pallas_call(
            functools.partial(real_space_kernel, devices, rows, planes),
            out_shape=(
                jax.ShapeDtypeStruct((devices, 2 * share, block_rows, span_z), f32),
                jax.ShapeDtypeStruct((2 * share, span_x, lanes), f32),
            ),
            grid=(share,),
            in_specs=[
                pl.BlockSpec(
                    (devices, None, block_rows, span_z), lambda j, c=c: (0, c * share + j, 0, 0)
                ),
                whole(pot.shape),
                whole(inv_x.shape),
                whole(fwd_x.shape),
                whole(proj.shape),
            ],
            out_specs=(
                pl.BlockSpec((devices, 2, block_rows, span_z), lambda j: (0, j, 0, 0)),
                pl.BlockSpec((2, span_x, lanes), lambda j: (j, 0, 0)),
            ),
            compiler_params=params,
            cost_estimate=cost(4 * 10**9, 8 * 10**6),
            name="real_space",
        )(arrived, pot, inv_x, fwd_x, proj)
        returned.append(lax.all_to_all(back, "ga", split_axis=0, concat_axis=0, tiled=True))
        fields.append(field)

    grams = pl.pallas_call(
        functools.partial(real_gram_kernel, bands),
        out_shape=jax.ShapeDtypeStruct((2, bands, bands, 128), f32),
        compiler_params=params,
        cost_estimate=cost(10**7, 2 * 10**6),
        name="real_gram",
    )(*fields, pot)
    grams = jnp.sum(grams, axis=-1)
    own = jnp.concatenate([proj, jnp.concatenate([grams[0], grams[1] + kin], axis=1)], axis=0)
    total = sum_over(own, devices)
    proj, s_real, h_real = total[:owners], total[owners:, :bands], total[owners:, bands:]
    weighted = strengths.reshape(-1)[:, None] * proj
    p_real, p_imag = proj[:, :bands], proj[:, bands:]
    w_real, w_imag = weighted[:, :bands], weighted[:, bands:]
    h_real = h_real + tdot("ja,jb->ab", p_real, w_real) + tdot("ja,jb->ab", p_imag, w_imag)
    h_imag = tdot("ja,jb->ab", p_real, w_imag) - tdot("ja,jb->ab", p_imag, w_real)
    m_real, m_imag = subspace_solve(s_real, h_real, h_imag)

    coefs = tdot("gsj,jc->gcs", owned, weighted)
    c_real, c_imag = coefs[:, :bands], coefs[:, bands:]
    from_beta = jnp.stack(
        [
            jnp.concatenate([c_real, -c_imag], axis=2),
            jnp.concatenate([c_imag, c_real], axis=2),
        ],
        axis=2,
    ).reshape(blocks, 2 * bands, 2 * slots)
    from_psi = jnp.stack(
        [
            jnp.stack([-m_real.T, m_imag.T], axis=-1),
            jnp.stack([-m_imag.T, -m_real.T], axis=-1),
        ],
        axis=1,
    ).reshape(1, 2 * bands, 2 * bands)
    coefs = jnp.concatenate(
        [jnp.broadcast_to(from_psi, (blocks, 2 * bands, 2 * bands)), from_beta], axis=2
    )
    base = pl.pallas_call(
        functools.partial(base_kernel, slots),
        out_shape=jax.ShapeDtypeStruct(orbitals.shape, f32),
        grid=(blocks,),
        in_specs=block_specs
        + [pl.BlockSpec((None, 2 * bands, 2 * bands + 2 * slots), lambda g: (g, 0, 0))],
        out_specs=block_specs[0],
        compiler_params=params,
        cost_estimate=cost(8 * 10**9, 12 * 10**6),
        name="base",
    )(orbitals, beta, kinetic, coefs)

    residual = base
    for c in range(parts):
        one_band = pl.BlockSpec(
            (1, 2, planes, span_y, span_z), lambda b, c=c: (2 * share * c + b, 0, 0, 0, 0)
        )
        residual = pl.pallas_call(
            functools.partial(to_planes_kernel, devices, rows, planes),
            out_shape=jax.ShapeDtypeStruct(orbitals.shape, f32),
            grid=(2 * share,),
            in_specs=[
                pl.BlockSpec((devices, None, block_rows, span_z), lambda b: (0, b, 0, 0)),
                one_band,
                whole(fwd_y.shape),
                whole(fwd_z.shape),
            ],
            out_specs=one_band,
            input_output_aliases={1: 0},
            compiler_params=params,
            cost_estimate=cost(8 * 10**9, 12 * 10**6),
            name="to_planes",
        )(returned[c], residual, fwd_y, fwd_z)
    return (residual, jnp.stack([m_real, m_imag]))


def solution(mesh):
    return jax.shard_map(
        functools.partial(on_device, mesh.shape["ga"]),
        mesh=mesh,
        in_specs=(
            P("rep", None, "ga", None, None),
            P("rep"),
            P("rep", "ga", None),
            P(("rep", "ga"), None, None, None),
            P(("rep", "ga"), None),
            P("rep", None),
        ),
        out_specs=(P("rep", None, "ga", None, None), P(None, "rep", None)),
        check_vma=False,
    )
```

```python
import functools
import math

import jax
import jax.numpy as jnp
import numpy as np
from jax import lax
from jax.experimental import pallas as pl
from jax.experimental.pallas import tpu as pltpu
from jax.sharding import PartitionSpec as P

highest = lax.Precision.HIGHEST
f32 = jnp.float32
bf16 = jnp.bfloat16
vmem_limit = 63 * 1024 * 1024


def signed_index(values, length):
    return jnp.where(values < length // 2, values, values - length)


def dft(length, orient):
    index = np.arange(length)
    angles = (index[:, None] * index[None, :] % length) * (2.0 * math.pi / length)
    factor = 1.0 / math.sqrt(length)
    return np.cos(angles) * factor, orient * np.sin(angles) * factor


def left_table(length, orient):
    cosine, sine = dft(length, orient)
    return np.block([[cosine, -sine], [sine, cosine]])


def right_table(length, orient):
    cosine, sine = dft(length, orient)
    return np.block([[cosine, sine], [-sine, cosine]])


def split(values):
    high = values.astype(bf16)
    low = (values - high.astype(f32)).astype(bf16)
    return high, low


def split_outside(values):
    high = lax.reduce_precision(values, exponent_bits=8, mantissa_bits=7)
    return high.astype(bf16), (values - high).astype(bf16)


def const_parts(table):
    table = np.asarray(table, np.float32)
    high = table.astype(jnp.bfloat16)
    low = (table - high.astype(np.float32)).astype(jnp.bfloat16)
    return high, low


def left_const(table):
    high, low = const_parts(table)
    return jnp.asarray(np.concatenate([high, high, low], axis=1))


def right_const(table):
    high, low = const_parts(table)
    return jnp.asarray(np.concatenate([high, high, low], axis=0))


def dot_left(table, values):
    high, low = split(values)
    return jnp.dot(
        table, jnp.concatenate([high, low, high], axis=0), preferred_element_type=f32
    )


def dot_right(values, table):
    high, low = split(values)
    return jnp.dot(
        jnp.concatenate([high, low, high], axis=1), table, preferred_element_type=f32
    )


def groups(count, width):
    size = max(1, 256 // width)
    return [list(range(i, min(i + size, count))) for i in range(0, count, size)]


def parts_in_lanes(values, span, width):
    items = values.shape[1] // width
    return jnp.concatenate(
        [
            jnp.concatenate(
                [values[:span, i * width : (i + 1) * width], values[span:, i * width : (i + 1) * width]],
                axis=1,
            )
            for i in range(items)
        ],
        axis=0,
    )


def to_rows_kernel(psi, y_table, out):
    _, _, planes, span_y, span_z = psi.shape
    devices, block_rows, _ = out.shape
    each = block_rows // planes
    for group in groups(planes, span_z):
        real = jnp.concatenate([psi[0, 0, p] - psi[1, 1, p] for p in group], axis=1)
        imag = jnp.concatenate([psi[0, 1, p] + psi[1, 0, p] for p in group], axis=1)
        along_y = dot_left(y_table[...], jnp.concatenate([real, imag], axis=0))
        for i, p in enumerate(group):
            out[:, p * each : (p + 1) * each, :] = along_y[
                :, i * span_z : (i + 1) * span_z
            ].reshape(devices, each, span_z)


def real_space_kernel(rows, planes, recv, pot, inverse, forward, inv_z, fwd_z, _, back, field):
    devices, size, span_z = recv.shape
    span_x = devices * planes
    arrived = recv.reshape(devices * size, span_z)
    leaving = back.reshape(devices * 2 * size, span_z)
    for group in groups(rows, span_z):
        columns = [
            jnp.concatenate(
                [
                    arrived[pl.ds((p * rows + r) * 2 + part, devices, stride=size), :]
                    for part in range(2)
                    for p in range(planes)
                ],
                axis=0,
            )
            for r in group
        ]
        along_x = dot_left(inverse[...], jnp.concatenate(columns, axis=1))
        spatial = dot_right(parts_in_lanes(along_x, span_x, span_z), inv_z[...])
        here = slice(group[0] * span_x, (group[-1] + 1) * span_x)
        for band in range(2):
            one = spatial[:, band * span_z : (band + 1) * span_z]
            field[band, here, :] = one
            product = one * pot[here, :]
            product = jnp.concatenate(
                [product[i * span_x : (i + 1) * span_x] for i in range(len(group))], axis=1
            )
            spectral = dot_left(forward[...], product)
            spectral = dot_right(parts_in_lanes(spectral, span_x, span_z), fwd_z[...])
            for i, r in enumerate(group):
                for p in range(planes):
                    first = i * span_x + p * devices
                    for part in range(2):
                        start = band * size + (p * rows + r) * 2 + part
                        leaving[pl.ds(start, devices, stride=2 * size), :] = spectral[
                            first : first + devices, part * span_z : (part + 1) * span_z
                        ]


def real_gram_kernel(bands, *refs):
    fields, (pot, out) = refs[:-2], refs[-2:]
    held = fields[0].shape[0]
    pairs = [(a, b) for a in range(bands) for b in range(a, bands)]
    for weighted in range(2):

        def step(i, sums):
            rows = pl.ds(pl.multiple_of(i * 8, 8), 8)
            values = [fields[a // held][a % held, rows, :] for a in range(bands)]
            other = [v * pot[rows, :] for v in values] if weighted else values
            result = []
            for (a, b), total in zip(pairs, sums):
                product = values[a] * other[b]
                lanes = product[:, :128]
                for c in range(128, product.shape[1], 128):
                    lanes = lanes + product[:, c : c + 128]
                result.append(total + lanes)
            return tuple(result)

        sums = lax.fori_loop(
            0, pot.shape[0] // 8, step, tuple(jnp.zeros((8, 128), f32) for _ in pairs)
        )
        for (a, b), total in zip(pairs, sums):
            line = jnp.sum(total, axis=0, keepdims=True)
            out[weighted, a, b : b + 1, :] = line
            out[weighted, b, a : a + 1, :] = line


def to_planes_kernel(recv, base, y_table, out):
    _, _, planes, span_y, span_z = base.shape
    each = recv.shape[1] // planes
    for group in groups(planes, span_z):
        columns = [
            recv[:, p * each : (p + 1) * each, :].reshape(2 * span_y, span_z) for p in group
        ]
        along_y = dot_left(y_table[...], jnp.concatenate(columns, axis=1))
        for i, p in enumerate(group):
            for part in range(2):
                out[0, part, p] = base[0, part, p] + (
                    along_y[part * span_y : (part + 1) * span_y, i * span_z : (i + 1) * span_z]
                )


def block_rows_of(psi, beta, slots):
    bands, _, span, span_z = psi.shape
    psi_flat = psi.reshape(bands * 2 * span, span_z)
    psi_rows = [psi_flat[pl.ds(y, 2 * bands, stride=span), :] for y in range(span)]
    beta_rows = [
        jnp.concatenate(
            [beta[pl.ds(2 * y + part, slots, stride=2 * span), :] for part in range(2)], axis=0
        )
        for y in range(span)
    ]
    return psi_rows, beta_rows


def project_kernel(slots, psi, beta, kinetic, out):
    bands, _, span, span_z = psi.shape
    psi_rows, beta_rows = block_rows_of(psi, beta, slots)
    kin_rows = [psi_rows[y] * kinetic[y : y + 1, :] for y in range(span)]
    right = jnp.concatenate(split(jnp.concatenate(psi_rows, axis=1)), axis=0)
    left = jnp.concatenate(
        split(jnp.concatenate(beta_rows, axis=1)) + split(jnp.concatenate(kin_rows, axis=1)), axis=0
    )
    full = lax.dot_general(left, right, (((1,), (1,)), ((), ())), preferred_element_type=f32)
    width, height = 2 * bands, 2 * slots
    full = full[:, :width] + full[:, width:]
    out[0:height] = full[0:height] + full[height : 2 * height]
    rest = full[2 * height :]
    out[height:] = rest[0:width] + rest[width:]


def base_kernel(slots, psi, beta, kinetic, coefs, out):
    bands, _, span, span_z = psi.shape
    psi_rows, beta_rows = block_rows_of(psi, beta, slots)
    values = jnp.concatenate(
        [jnp.concatenate(psi_rows, axis=1), jnp.concatenate(beta_rows, axis=1)], axis=0
    )
    high, low = split(coefs[...])
    summed = dot_left(jnp.concatenate([high, high, low], axis=1), values)
    flat = out.reshape(bands * 2 * span, span_z)
    for y in range(span):
        flat[pl.ds(y, 2 * bands, stride=span), :] = (
            psi_rows[y] * kinetic[y : y + 1, :] + summed[:, y * span_z : (y + 1) * span_z]
        )


def whole(shape):
    return pl.BlockSpec(shape, lambda *_: (0,) * len(shape))


def subspace_solve(s_real, h_real, h_imag):
    factor = jnp.linalg.cholesky(s_real)
    solved = jax.scipy.linalg.cho_solve((factor, True), jnp.concatenate([h_real, h_imag], axis=1))
    order_size = s_real.shape[0]
    return (solved[:, :order_size], solved[:, order_size:])


def tdot(pattern, left, right):
    return jnp.einsum(pattern, left, right, precision=highest, preferred_element_type=jnp.float32)


def partner(values, devices, k):
    return lax.ppermute(values, "ga", [(d, d ^ k) for d in range(devices)])


def sum_over(values, devices):
    if devices & (devices - 1) or devices < 4:
        return lax.psum(values, "ga")
    step = 1
    while step < devices // 4:
        values = values + partner(values, devices, step)
        step *= 2
    others = [partner(values, devices, k * step) for k in (1, 2, 3)]
    return (values + others[0]) + (others[1] + others[2])


def on_device(devices, orbitals, plane_order, potential, projectors, slot_owner, strengths):
    bands = orbitals.shape[0]
    planes = orbitals.shape[2]
    span_y = orbitals.shape[3]
    span_z = orbitals.shape[4]
    span_x = plane_order.shape[0]
    blocks, slots = slot_owner.shape
    owners = strengths.shape[0] * strengths.shape[1]
    rows = span_y // devices
    block_rows = 2 * planes * rows
    pairs = bands // 2
    block_span = projectors.shape[3] // span_z
    per_plane = span_y // block_span
    grid_x = jnp.arange(span_x, dtype=jnp.int32)
    grid_y = jnp.arange(span_y, dtype=jnp.int32)
    grid_z = jnp.arange(span_z, dtype=jnp.int32)
    params = pltpu.CompilerParams(vmem_limit_bytes=vmem_limit)

    def cost(flops, moved):
        return pl.CostEstimate(flops=flops, bytes_accessed=moved, transcendentals=0)

    order = np.arange(2 * span_y)
    order = (order % 2) * span_y + order // 2
    inv_y = left_const(left_table(span_y, 1.0)[order])
    fwd_y = left_const(left_table(span_y, -1.0)[:, order])
    inv_z = right_const(right_table(span_z, 1.0))
    fwd_z = right_const(right_table(span_z, -1.0))

    parts = 2 if pairs % 2 == 0 else 1
    share = pairs // parts
    arrived = []
    for c in range(parts):
        sent = pl.pallas_call(
            to_rows_kernel,
            out_shape=jax.ShapeDtypeStruct((devices, share, block_rows, span_z), f32),
            grid=(share,),
            in_specs=[
                pl.BlockSpec(
                    (2, 2, planes, span_y, span_z), lambda j, c=c: (c * share + j, 0, 0, 0, 0)
                ),
                whole(inv_y.shape),
            ],
            out_specs=pl.BlockSpec((devices, None, block_rows, span_z), lambda j: (0, j, 0, 0)),
            compiler_params=params,
            cost_estimate=cost(4 * 10**9, 3 * 10**6),
            name="to_rows",
        )(orbitals, inv_y)
        arrived.append(lax.all_to_all(sent, "ga", split_axis=0, concat_axis=0, tiled=True))

    stored = plane_order.reshape(devices, planes).T.reshape(-1)
    phases = (stored[:, None] * grid_x[None, :]) % span_x
    angles = phases.astype(f32) * (2.0 * math.pi / span_x)
    factor = 1.0 / math.sqrt(span_x)
    cosine, sine = jnp.cos(angles) * factor, jnp.sin(angles) * factor
    fwd_x = jnp.concatenate([cosine, -sine], axis=0)
    inv_x = jnp.concatenate([fwd_x, jnp.concatenate([sine, cosine], axis=0)], axis=1).T
    high, low = split_outside(fwd_x)
    fwd_x = jnp.concatenate([high, high, low], axis=1)
    high, low = split_outside(inv_x)
    inv_x = jnp.concatenate([high, high, low], axis=1)
    pot = potential.transpose(1, 0, 2).reshape(rows * span_x, span_z)

    local_order = lax.dynamic_slice_in_dim(plane_order, lax.axis_index("ga") * planes, planes)
    freq_x = signed_index(local_order, span_x).astype(f32) / span_x
    freq_y = signed_index(grid_y, span_y).astype(f32) / span_y
    freq_z = signed_index(grid_z, span_z).astype(f32) / span_z
    kinetic = 2.0 * (
        freq_x[:, None, None] ** 2 + freq_y[None, :, None] ** 2 + freq_z[None, None, :] ** 2
    )
    beta = projectors.reshape(blocks, slots, 2, block_span, span_z)
    beta = beta.transpose(0, 1, 3, 2, 4).reshape(blocks, slots * block_span * 2, span_z)
    block_specs = [
        pl.BlockSpec(
            (bands, 2, None, block_span, span_z),
            lambda g: (0, 0, g // per_plane, g % per_plane, 0),
        ),
        pl.BlockSpec((None, slots * block_span * 2, span_z), lambda g: (g, 0, 0)),
        pl.BlockSpec((None, block_span, span_z), lambda g: (g // per_plane, g % per_plane, 0)),
    ]
    products = pl.pallas_call(
        functools.partial(project_kernel, slots),
        out_shape=jax.ShapeDtypeStruct((blocks, 2 * slots + 2 * bands, 2 * bands), f32),
        grid=(blocks,),
        in_specs=block_specs,
        out_specs=pl.BlockSpec((None, 2 * slots + 2 * bands, 2 * bands), lambda g: (g, 0, 0)),
        compiler_params=params,
        cost_estimate=cost(8 * 10**9, 8 * 10**6),
        name="project",
    )(orbitals, beta, kinetic)
    with_real = products[:, :slots].reshape(blocks, slots, bands, 2)
    with_imag = products[:, slots : 2 * slots].reshape(blocks, slots, bands, 2)
    proj = jnp.concatenate(
        [
            with_real[..., 0] + with_imag[..., 1],
            with_real[..., 1] - with_imag[..., 0],
        ],
        axis=-1,
    )
    owned = (
        slot_owner[:, :, None] == jnp.arange(owners, dtype=jnp.int32)[None, None, :]
    ).astype(f32)
    proj = tdot("gsj,gsc->jc", owned, proj)
    kin = jnp.sum(products[:, 2 * slots :], axis=0).reshape(bands, 2, bands, 2)
    kin = kin[:, 0, :, 0] + kin[:, 1, :, 1]

    returned, fields = [], []
    for c in range(parts):
        back, field = pl.pallas_call(
            functools.partial(real_space_kernel, rows, planes),
            out_shape=(
                jax.ShapeDtypeStruct((devices, 2 * share, block_rows, span_z), f32),
                jax.ShapeDtypeStruct((2 * share, rows * span_x, span_z), f32),
            ),
            grid=(share,),
            in_specs=[
                pl.BlockSpec((devices, None, block_rows, span_z), lambda j: (0, j, 0, 0)),
                whole(pot.shape),
                whole(inv_x.shape),
                whole(fwd_x.shape),
                whole(inv_z.shape),
                whole(fwd_z.shape),
                whole(proj.shape),
            ],
            out_specs=(
                pl.BlockSpec((devices, 2, block_rows, span_z), lambda j: (0, j, 0, 0)),
                pl.BlockSpec((2, rows * span_x, span_z), lambda j: (j, 0, 0)),
            ),
            compiler_params=params,
            cost_estimate=cost(4 * 10**9, 8 * 10**6),
            name="real_space",
        )(arrived[c], pot, inv_x, fwd_x, inv_z, fwd_z, proj)
        returned.append(lax.all_to_all(back, "ga", split_axis=0, concat_axis=0, tiled=True))
        fields.append(field)

    grams = pl.pallas_call(
        functools.partial(real_gram_kernel, bands),
        out_shape=jax.ShapeDtypeStruct((2, bands, bands, 128), f32),
        compiler_params=params,
        cost_estimate=cost(10**7, 2 * 10**6),
        name="real_gram",
    )(*fields, pot)
    grams = jnp.sum(grams, axis=-1)
    own = jnp.concatenate([proj, jnp.concatenate([grams[0], grams[1] + kin], axis=1)], axis=0)
    total = sum_over(own, devices)
    proj, s_real, h_real = total[:owners], total[owners:, :bands], total[owners:, bands:]
    weighted = strengths.reshape(-1)[:, None] * proj
    p_real, p_imag = proj[:, :bands], proj[:, bands:]
    w_real, w_imag = weighted[:, :bands], weighted[:, bands:]
    h_real = h_real + tdot("ja,jb->ab", p_real, w_real) + tdot("ja,jb->ab", p_imag, w_imag)
    h_imag = tdot("ja,jb->ab", p_real, w_imag) - tdot("ja,jb->ab", p_imag, w_real)
    m_real, m_imag = subspace_solve(s_real, h_real, h_imag)

    coefs = tdot("gsj,jc->gcs", owned, weighted)
    c_real, c_imag = coefs[:, :bands], coefs[:, bands:]
    from_beta = jnp.stack(
        [
            jnp.concatenate([c_real, -c_imag], axis=2),
            jnp.concatenate([c_imag, c_real], axis=2),
        ],
        axis=2,
    ).reshape(blocks, 2 * bands, 2 * slots)
    from_psi = jnp.stack(
        [
            jnp.stack([-m_real.T, m_imag.T], axis=-1),
            jnp.stack([-m_imag.T, -m_real.T], axis=-1),
        ],
        axis=1,
    ).reshape(1, 2 * bands, 2 * bands)
    coefs = jnp.concatenate(
        [jnp.broadcast_to(from_psi, (blocks, 2 * bands, 2 * bands)), from_beta], axis=2
    )
    base = pl.pallas_call(
        functools.partial(base_kernel, slots),
        out_shape=jax.ShapeDtypeStruct(orbitals.shape, f32),
        grid=(blocks,),
        in_specs=block_specs
        + [pl.BlockSpec((None, 2 * bands, 2 * bands + 2 * slots), lambda g: (g, 0, 0))],
        out_specs=block_specs[0],
        compiler_params=params,
        cost_estimate=cost(8 * 10**9, 12 * 10**6),
        name="base",
    )(orbitals, beta, kinetic, coefs)

    residual = base
    for c in range(parts):
        one_band = pl.BlockSpec(
            (1, 2, planes, span_y, span_z), lambda b, c=c: (2 * share * c + b, 0, 0, 0, 0)
        )
        residual = pl.pallas_call(
            to_planes_kernel,
            out_shape=jax.ShapeDtypeStruct(orbitals.shape, f32),
            grid=(2 * share,),
            in_specs=[
                pl.BlockSpec((devices, None, block_rows, span_z), lambda b: (0, b, 0, 0)),
                one_band,
                whole(fwd_y.shape),
            ],
            out_specs=one_band,
            input_output_aliases={1: 0},
            compiler_params=params,
            cost_estimate=cost(8 * 10**9, 12 * 10**6),
            name="to_planes",
        )(returned[c], residual, fwd_y)
    return (residual, jnp.stack([m_real, m_imag]))


def solution(mesh):
    return jax.shard_map(
        functools.partial(on_device, mesh.shape["ga"]),
        mesh=mesh,
        in_specs=(
            P("rep", None, "ga", None, None),
            P("rep"),
            P("rep", "ga", None),
            P(("rep", "ga"), None, None, None),
            P(("rep", "ga"), None),
            P("rep", None),
        ),
        out_specs=(P("rep", None, "ga", None, None), P(None, "rep", None)),
        check_vma=False,
    )
```

```python
import functools
import math

import jax
import jax.numpy as jnp
import numpy as np
from jax import lax
from jax.experimental import pallas as pl
from jax.experimental.pallas import tpu as pltpu
from jax.sharding import PartitionSpec as P

highest = lax.Precision.HIGHEST
f32 = jnp.float32
bf16 = jnp.bfloat16
vmem_limit = 63 * 1024 * 1024


def signed_index(values, length):
    return jnp.where(values < length // 2, values, values - length)


def dft(length, orient):
    index = np.arange(length)
    angles = (index[:, None] * index[None, :] % length) * (2.0 * math.pi / length)
    factor = 1.0 / math.sqrt(length)
    return np.cos(angles) * factor, orient * np.sin(angles) * factor


def left_table(length, orient):
    cosine, sine = dft(length, orient)
    return np.block([[cosine, -sine], [sine, cosine]])


def right_table(length, orient):
    cosine, sine = dft(length, orient)
    return np.block([[cosine, sine], [-sine, cosine]])


def split(values):
    high = values.astype(bf16)
    low = (values - high.astype(f32)).astype(bf16)
    return high, low


def split_outside(values):
    high = lax.reduce_precision(values, exponent_bits=8, mantissa_bits=7)
    return high.astype(bf16), (values - high).astype(bf16)


def const_parts(table):
    table = np.asarray(table, np.float32)
    high = table.astype(jnp.bfloat16)
    low = (table - high.astype(np.float32)).astype(jnp.bfloat16)
    return high, low


def left_const(table):
    high, low = const_parts(table)
    return jnp.asarray(np.concatenate([high, high, low], axis=1))


def right_const(table):
    high, low = const_parts(table)
    return jnp.asarray(np.concatenate([high, high, low], axis=0))


def dot_left(table, values):
    high, low = split(values)
    return jnp.dot(
        table, jnp.concatenate([high, low, high], axis=0), preferred_element_type=f32
    )


def dot_right(values, table):
    high, low = split(values)
    return jnp.dot(
        jnp.concatenate([high, low, high], axis=1), table, preferred_element_type=f32
    )


def groups(count, width):
    size = max(1, 256 // width)
    return [list(range(i, min(i + size, count))) for i in range(0, count, size)]


def parts_in_lanes(values, span, width):
    items = values.shape[1] // width
    return jnp.concatenate(
        [
            jnp.concatenate(
                [values[:span, i * width : (i + 1) * width], values[span:, i * width : (i + 1) * width]],
                axis=1,
            )
            for i in range(items)
        ],
        axis=0,
    )


def to_rows_kernel(psi, y_table, out):
    _, _, planes, span_y, span_z = psi.shape
    devices, block_rows, _ = out.shape
    each = block_rows // planes
    for group in groups(planes, span_z):
        real = jnp.concatenate([psi[0, 0, p] - psi[1, 1, p] for p in group], axis=1)
        imag = jnp.concatenate([psi[0, 1, p] + psi[1, 0, p] for p in group], axis=1)
        along_y = dot_left(y_table[...], jnp.concatenate([real, imag], axis=0))
        for i, p in enumerate(group):
            out[:, p * each : (p + 1) * each, :] = along_y[
                :, i * span_z : (i + 1) * span_z
            ].reshape(devices, each, span_z)


def real_space_kernel(rows, planes, recv, pot, inverse, forward, inv_z, fwd_z, _, back, field):
    devices, size, span_z = recv.shape
    span_x = devices * planes
    arrived = recv.reshape(devices * size, span_z)
    leaving = back.reshape(devices * 2 * size, span_z)
    for group in groups(rows, span_z):
        columns = [
            jnp.concatenate(
                [
                    arrived[pl.ds((p * rows + r) * 2 + part, devices, stride=size), :]
                    for part in range(2)
                    for p in range(planes)
                ],
                axis=0,
            )
            for r in group
        ]
        along_x = dot_left(inverse[...], jnp.concatenate(columns, axis=1))
        spatial = dot_right(parts_in_lanes(along_x, span_x, span_z), inv_z[...])
        here = slice(group[0] * span_x, (group[-1] + 1) * span_x)
        for band in range(2):
            one = spatial[:, band * span_z : (band + 1) * span_z]
            field[band, here, :] = one
            product = one * pot[here, :]
            product = jnp.concatenate(
                [product[i * span_x : (i + 1) * span_x] for i in range(len(group))], axis=1
            )
            spectral = dot_left(forward[...], product)
            spectral = dot_right(parts_in_lanes(spectral, span_x, span_z), fwd_z[...])
            for i, r in enumerate(group):
                for p in range(planes):
                    first = i * span_x + p * devices
                    for part in range(2):
                        start = band * size + (p * rows + r) * 2 + part
                        leaving[pl.ds(start, devices, stride=2 * size), :] = spectral[
                            first : first + devices, part * span_z : (part + 1) * span_z
                        ]


def real_gram_kernel(bands, *refs):
    fields, (pot, out) = refs[:-2], refs[-2:]
    held = fields[0].shape[0]
    pairs = [(a, b) for a in range(bands) for b in range(a, bands)]
    for weighted in range(2):

        def step(i, sums):
            rows = pl.ds(pl.multiple_of(i * 8, 8), 8)
            values = [fields[a // held][a % held, rows, :] for a in range(bands)]
            other = [v * pot[rows, :] for v in values] if weighted else values
            result = []
            for (a, b), total in zip(pairs, sums):
                product = values[a] * other[b]
                lanes = product[:, :128]
                for c in range(128, product.shape[1], 128):
                    lanes = lanes + product[:, c : c + 128]
                result.append(total + lanes)
            return tuple(result)

        sums = lax.fori_loop(
            0, pot.shape[0] // 8, step, tuple(jnp.zeros((8, 128), f32) for _ in pairs)
        )
        for (a, b), total in zip(pairs, sums):
            line = jnp.sum(total, axis=0, keepdims=True)
            out[weighted, a, b : b + 1, :] = line
            out[weighted, b, a : a + 1, :] = line


def to_planes_kernel(recv, base, y_table, out):
    _, _, planes, span_y, span_z = base.shape
    each = recv.shape[1] // planes
    for group in groups(planes, span_z):
        columns = [
            recv[:, p * each : (p + 1) * each, :].reshape(2 * span_y, span_z) for p in group
        ]
        along_y = dot_left(y_table[...], jnp.concatenate(columns, axis=1))
        for i, p in enumerate(group):
            for part in range(2):
                out[0, part, p] = base[0, part, p] + (
                    along_y[part * span_y : (part + 1) * span_y, i * span_z : (i + 1) * span_z]
                )


def pass_on_kernel(values, _, out):
    out[...] = values[...]


def block_rows_of(psi, beta, slots):
    bands, _, span, span_z = psi.shape
    psi_flat = psi.reshape(bands * 2 * span, span_z)
    psi_rows = [psi_flat[pl.ds(y, 2 * bands, stride=span), :] for y in range(span)]
    beta_rows = [
        jnp.concatenate(
            [beta[pl.ds(2 * y + part, slots, stride=2 * span), :] for part in range(2)], axis=0
        )
        for y in range(span)
    ]
    return psi_rows, beta_rows


def project_kernel(slots, psi, beta, kinetic, out):
    bands, _, span, span_z = psi.shape
    psi_rows, beta_rows = block_rows_of(psi, beta, slots)
    kin_rows = [psi_rows[y] * kinetic[y : y + 1, :] for y in range(span)]
    right = jnp.concatenate(split(jnp.concatenate(psi_rows, axis=1)), axis=0)
    left = jnp.concatenate(
        split(jnp.concatenate(beta_rows, axis=1)) + split(jnp.concatenate(kin_rows, axis=1)), axis=0
    )
    full = lax.dot_general(left, right, (((1,), (1,)), ((), ())), preferred_element_type=f32)
    width, height = 2 * bands, 2 * slots
    full = full[:, :width] + full[:, width:]
    out[0:height] = full[0:height] + full[height : 2 * height]
    rest = full[2 * height :]
    out[height:] = rest[0:width] + rest[width:]


def base_kernel(slots, psi, beta, kinetic, coefs, out):
    bands, _, span, span_z = psi.shape
    psi_rows, beta_rows = block_rows_of(psi, beta, slots)
    values = jnp.concatenate(
        [jnp.concatenate(psi_rows, axis=1), jnp.concatenate(beta_rows, axis=1)], axis=0
    )
    high, low = split(coefs[...])
    summed = dot_left(jnp.concatenate([high, high, low], axis=1), values)
    flat = out.reshape(bands * 2 * span, span_z)
    for y in range(span):
        flat[pl.ds(y, 2 * bands, stride=span), :] = (
            psi_rows[y] * kinetic[y : y + 1, :] + summed[:, y * span_z : (y + 1) * span_z]
        )


def whole(shape):
    return pl.BlockSpec(shape, lambda *_: (0,) * len(shape))


def subspace_solve(s_real, h_real, h_imag):
    factor = jnp.linalg.cholesky(s_real)
    solved = jax.scipy.linalg.cho_solve((factor, True), jnp.concatenate([h_real, h_imag], axis=1))
    order_size = s_real.shape[0]
    return (solved[:, :order_size], solved[:, order_size:])


def tdot(pattern, left, right):
    return jnp.einsum(pattern, left, right, precision=highest, preferred_element_type=jnp.float32)


def partner(values, devices, k):
    return lax.ppermute(values, "ga", [(d, d ^ k) for d in range(devices)])


def sum_over(values, devices):
    if devices & (devices - 1) or devices < 4:
        return lax.psum(values, "ga")
    step = 1
    while step < devices // 4:
        values = values + partner(values, devices, step)
        step *= 2
    others = [partner(values, devices, k * step) for k in (1, 2, 3)]
    return (values + others[0]) + (others[1] + others[2])


def on_device(devices, orbitals, plane_order, potential, projectors, slot_owner, strengths):
    bands = orbitals.shape[0]
    planes = orbitals.shape[2]
    span_y = orbitals.shape[3]
    span_z = orbitals.shape[4]
    span_x = plane_order.shape[0]
    blocks, slots = slot_owner.shape
    owners = strengths.shape[0] * strengths.shape[1]
    rows = span_y // devices
    block_rows = 2 * planes * rows
    pairs = bands // 2
    block_span = projectors.shape[3] // span_z
    per_plane = span_y // block_span
    grid_x = jnp.arange(span_x, dtype=jnp.int32)
    grid_y = jnp.arange(span_y, dtype=jnp.int32)
    grid_z = jnp.arange(span_z, dtype=jnp.int32)
    params = pltpu.CompilerParams(vmem_limit_bytes=vmem_limit)

    def cost(flops, moved):
        return pl.CostEstimate(flops=flops, bytes_accessed=moved, transcendentals=0)

    order = np.arange(2 * span_y)
    order = (order % 2) * span_y + order // 2
    inv_y = left_const(left_table(span_y, 1.0)[order])
    fwd_y = left_const(left_table(span_y, -1.0)[:, order])
    inv_z = right_const(right_table(span_z, 1.0))
    fwd_z = right_const(right_table(span_z, -1.0))

    parts = 2 if pairs % 2 == 0 else 1
    share = pairs // parts
    some = math.gcd(planes, max(1, 256 // span_z))
    some_rows = block_rows // planes * some
    arrived = []
    for c in range(parts):
        sent = pl.pallas_call(
            to_rows_kernel,
            out_shape=jax.ShapeDtypeStruct((devices, share, block_rows, span_z), f32),
            grid=(share, planes // some),
            in_specs=[
                pl.BlockSpec(
                    (2, 2, some, span_y, span_z), lambda j, p, c=c: (c * share + j, 0, p, 0, 0)
                ),
                whole(inv_y.shape),
            ],
            out_specs=pl.BlockSpec(
                (devices, None, some_rows, span_z), lambda j, p: (0, j, p, 0)
            ),
            compiler_params=params,
            cost_estimate=cost(4 * 10**9, 3 * 10**6),
            name="to_rows",
        )(orbitals, inv_y)
        arrived.append(lax.all_to_all(sent, "ga", split_axis=0, concat_axis=0, tiled=True))

    stored = plane_order.reshape(devices, planes).T.reshape(-1)
    phases = (stored[:, None] * grid_x[None, :]) % span_x
    angles = phases.astype(f32) * (2.0 * math.pi / span_x)
    factor = 1.0 / math.sqrt(span_x)
    cosine, sine = jnp.cos(angles) * factor, jnp.sin(angles) * factor
    fwd_x = jnp.concatenate([cosine, -sine], axis=0)
    inv_x = jnp.concatenate([fwd_x, jnp.concatenate([sine, cosine], axis=0)], axis=1).T
    high, low = split_outside(fwd_x)
    fwd_x = jnp.concatenate([high, high, low], axis=1)
    high, low = split_outside(inv_x)
    inv_x = jnp.concatenate([high, high, low], axis=1)
    pot = potential.transpose(1, 0, 2).reshape(rows * span_x, span_z)

    local_order = lax.dynamic_slice_in_dim(plane_order, lax.axis_index("ga") * planes, planes)
    freq_x = signed_index(local_order, span_x).astype(f32) / span_x
    freq_y = signed_index(grid_y, span_y).astype(f32) / span_y
    freq_z = signed_index(grid_z, span_z).astype(f32) / span_z
    kinetic = 2.0 * (
        freq_x[:, None, None] ** 2 + freq_y[None, :, None] ** 2 + freq_z[None, None, :] ** 2
    )
    beta = projectors.reshape(blocks, slots, 2, block_span, span_z)
    beta = beta.transpose(0, 1, 3, 2, 4).reshape(blocks, slots * block_span * 2, span_z)
    block_specs = [
        pl.BlockSpec(
            (bands, 2, None, block_span, span_z),
            lambda g: (0, 0, g // per_plane, g % per_plane, 0),
        ),
        pl.BlockSpec((None, slots * block_span * 2, span_z), lambda g: (g, 0, 0)),
        pl.BlockSpec((None, block_span, span_z), lambda g: (g // per_plane, g % per_plane, 0)),
    ]
    products = pl.pallas_call(
        functools.partial(project_kernel, slots),
        out_shape=jax.ShapeDtypeStruct((blocks, 2 * slots + 2 * bands, 2 * bands), f32),
        grid=(blocks,),
        in_specs=block_specs,
        out_specs=pl.BlockSpec((None, 2 * slots + 2 * bands, 2 * bands), lambda g: (g, 0, 0)),
        compiler_params=params,
        cost_estimate=cost(8 * 10**9, 8 * 10**6),
        name="project",
    )(orbitals, beta, kinetic)
    with_real = products[:, :slots].reshape(blocks, slots, bands, 2)
    with_imag = products[:, slots : 2 * slots].reshape(blocks, slots, bands, 2)
    proj = jnp.concatenate(
        [
            with_real[..., 0] + with_imag[..., 1],
            with_real[..., 1] - with_imag[..., 0],
        ],
        axis=-1,
    )
    owned = (
        slot_owner[:, :, None] == jnp.arange(owners, dtype=jnp.int32)[None, None, :]
    ).astype(f32)
    proj = tdot("gsj,gsc->jc", owned, proj)
    kin = jnp.sum(products[:, 2 * slots :], axis=0).reshape(bands, 2, bands, 2)
    kin = kin[:, 0, :, 0] + kin[:, 1, :, 1]

    returned, fields = [], []
    for c in range(parts):
        back, field = pl.pallas_call(
            functools.partial(real_space_kernel, rows, planes),
            out_shape=(
                jax.ShapeDtypeStruct((devices, 2 * share, block_rows, span_z), f32),
                jax.ShapeDtypeStruct((2 * share, rows * span_x, span_z), f32),
            ),
            grid=(share,),
            in_specs=[
                pl.BlockSpec((devices, None, block_rows, span_z), lambda j: (0, j, 0, 0)),
                whole(pot.shape),
                whole(inv_x.shape),
                whole(fwd_x.shape),
                whole(inv_z.shape),
                whole(fwd_z.shape),
                whole(proj.shape),
            ],
            out_specs=(
                pl.BlockSpec((devices, 2, block_rows, span_z), lambda j: (0, j, 0, 0)),
                pl.BlockSpec((2, rows * span_x, span_z), lambda j: (j, 0, 0)),
            ),
            compiler_params=params,
            cost_estimate=cost(4 * 10**9, 8 * 10**6),
            name="real_space",
        )(arrived[c], pot, inv_x, fwd_x, inv_z, fwd_z, proj)
        returned.append(lax.all_to_all(back, "ga", split_axis=0, concat_axis=0, tiled=True))
        fields.append(field)

    grams = pl.pallas_call(
        functools.partial(real_gram_kernel, bands),
        out_shape=jax.ShapeDtypeStruct((2, bands, bands, 128), f32),
        compiler_params=params,
        cost_estimate=cost(10**7, 2 * 10**6),
        name="real_gram",
    )(*fields, pot)
    grams = jnp.sum(grams, axis=-1)
    own = jnp.concatenate([proj, jnp.concatenate([grams[0], grams[1] + kin], axis=1)], axis=0)
    total = sum_over(own, devices)
    total = pl.pallas_call(
        pass_on_kernel,
        out_shape=jax.ShapeDtypeStruct(total.shape, f32),
        in_specs=[pl.BlockSpec(memory_space=pltpu.VMEM), pl.BlockSpec(memory_space=pl.ANY)],
        out_specs=pl.BlockSpec(memory_space=pltpu.VMEM),
        name="pass_on",
    )(total, returned[0])
    proj, s_real, h_real = total[:owners], total[owners:, :bands], total[owners:, bands:]
    weighted = strengths.reshape(-1)[:, None] * proj
    p_real, p_imag = proj[:, :bands], proj[:, bands:]
    w_real, w_imag = weighted[:, :bands], weighted[:, bands:]
    h_real = h_real + tdot("ja,jb->ab", p_real, w_real) + tdot("ja,jb->ab", p_imag, w_imag)
    h_imag = tdot("ja,jb->ab", p_real, w_imag) - tdot("ja,jb->ab", p_imag, w_real)
    m_real, m_imag = subspace_solve(s_real, h_real, h_imag)

    coefs = tdot("gsj,jc->gcs", owned, weighted)
    c_real, c_imag = coefs[:, :bands], coefs[:, bands:]
    from_beta = jnp.stack(
        [
            jnp.concatenate([c_real, -c_imag], axis=2),
            jnp.concatenate([c_imag, c_real], axis=2),
        ],
        axis=2,
    ).reshape(blocks, 2 * bands, 2 * slots)
    from_psi = jnp.stack(
        [
            jnp.stack([-m_real.T, m_imag.T], axis=-1),
            jnp.stack([-m_imag.T, -m_real.T], axis=-1),
        ],
        axis=1,
    ).reshape(1, 2 * bands, 2 * bands)
    coefs = jnp.concatenate(
        [jnp.broadcast_to(from_psi, (blocks, 2 * bands, 2 * bands)), from_beta], axis=2
    )
    base = pl.pallas_call(
        functools.partial(base_kernel, slots),
        out_shape=jax.ShapeDtypeStruct(orbitals.shape, f32),
        grid=(blocks,),
        in_specs=block_specs
        + [pl.BlockSpec((None, 2 * bands, 2 * bands + 2 * slots), lambda g: (g, 0, 0))],
        out_specs=block_specs[0],
        compiler_params=params,
        cost_estimate=cost(8 * 10**9, 12 * 10**6),
        name="base",
    )(orbitals, beta, kinetic, coefs)

    residual = base
    for c in range(parts):
        one_band = pl.BlockSpec(
            (1, 2, some, span_y, span_z), lambda b, p, c=c: (2 * share * c + b, 0, p, 0, 0)
        )
        residual = pl.pallas_call(
            to_planes_kernel,
            out_shape=jax.ShapeDtypeStruct(orbitals.shape, f32),
            grid=(2 * share, planes // some),
            in_specs=[
                pl.BlockSpec((devices, None, some_rows, span_z), lambda b, p: (0, b, p, 0)),
                one_band,
                whole(fwd_y.shape),
            ],
            out_specs=one_band,
            input_output_aliases={1: 0},
            compiler_params=params,
            cost_estimate=cost(8 * 10**9, 12 * 10**6),
            name="to_planes",
        )(returned[c], residual, fwd_y)
    return (residual, jnp.stack([m_real, m_imag]))


def solution(mesh):
    return jax.shard_map(
        functools.partial(on_device, mesh.shape["ga"]),
        mesh=mesh,
        in_specs=(
            P("rep", None, "ga", None, None),
            P("rep"),
            P("rep", "ga", None),
            P(("rep", "ga"), None, None, None),
            P(("rep", "ga"), None),
            P("rep", None),
        ),
        out_specs=(P("rep", None, "ga", None, None), P(None, "rep", None)),
        check_vma=False,
    )
```

```python
import functools
import math

import jax
import jax.numpy as jnp
import numpy as np
from jax import lax
from jax.experimental import pallas as pl
from jax.experimental.pallas import tpu as pltpu
from jax.sharding import PartitionSpec as P

highest = lax.Precision.HIGHEST
f32 = jnp.float32
bf16 = jnp.bfloat16
vmem_limit = 63 * 1024 * 1024


def signed_index(values, length):
    return jnp.where(values < length // 2, values, values - length)


def dft(length, orient):
    index = np.arange(length)
    angles = (index[:, None] * index[None, :] % length) * (2.0 * math.pi / length)
    factor = 1.0 / math.sqrt(length)
    return np.cos(angles) * factor, orient * np.sin(angles) * factor


def left_table(length, orient):
    cosine, sine = dft(length, orient)
    return np.block([[cosine, -sine], [sine, cosine]])


def right_table(length, orient):
    cosine, sine = dft(length, orient)
    return np.block([[cosine, sine], [-sine, cosine]])


def split(values):
    high = values.astype(bf16)
    low = (values - high.astype(f32)).astype(bf16)
    return high, low


def split_outside(values):
    high = lax.reduce_precision(values, exponent_bits=8, mantissa_bits=7)
    return high.astype(bf16), (values - high).astype(bf16)


def const_parts(table):
    table = np.asarray(table, np.float32)
    high = table.astype(jnp.bfloat16)
    low = (table - high.astype(np.float32)).astype(jnp.bfloat16)
    return high, low


def left_const(table):
    high, low = const_parts(table)
    return jnp.asarray(np.concatenate([high, high, low], axis=1))


def right_const(table):
    high, low = const_parts(table)
    return jnp.asarray(np.concatenate([high, high, low], axis=0))


def dot_left(table, values):
    high, low = split(values)
    return jnp.dot(
        table, jnp.concatenate([high, low, high], axis=0), preferred_element_type=f32
    )


def dot_right(values, table):
    high, low = split(values)
    return jnp.dot(
        jnp.concatenate([high, low, high], axis=1), table, preferred_element_type=f32
    )


def groups(count, width):
    size = max(1, 256 // width)
    return [list(range(i, min(i + size, count))) for i in range(0, count, size)]


def parts_in_lanes(values, span, width):
    items = values.shape[1] // width
    return jnp.concatenate(
        [
            jnp.concatenate(
                [values[:span, i * width : (i + 1) * width], values[span:, i * width : (i + 1) * width]],
                axis=1,
            )
            for i in range(items)
        ],
        axis=0,
    )


def to_rows_kernel(psi, y_table, out):
    _, _, planes, span_y, span_z = psi.shape
    devices, block_rows, _ = out.shape
    each = block_rows // planes
    for group in groups(planes, span_z):
        real = jnp.concatenate([psi[0, 0, p] - psi[1, 1, p] for p in group], axis=1)
        imag = jnp.concatenate([psi[0, 1, p] + psi[1, 0, p] for p in group], axis=1)
        along_y = dot_left(y_table[...], jnp.concatenate([real, imag], axis=0))
        for i, p in enumerate(group):
            out[:, p * each : (p + 1) * each, :] = along_y[
                :, i * span_z : (i + 1) * span_z
            ].reshape(devices, each, span_z)


def to_rows_split_kernel(my_layer, psi, y_table, *rest):
    outs, staged = rest[:-1], rest[-1]
    to_rows_kernel(psi, y_table, staged)
    each = staged.shape[0] // len(outs)
    for k, out in enumerate(outs):
        out[...] = staged[pl.ds((my_layer[0] ^ k) * each, each)]


def regroup_kernel(layers, my_member, *refs):
    arrived, outs = refs[:layers], refs[layers + 1 :]
    for k, out in enumerate(outs):
        for layer in range(layers):
            out[layer] = arrived[layer][my_member[0] ^ k]


def real_space_parts_kernel(rows, planes, members, *refs):
    arrived, rest, staged = refs[:members], refs[members:-1], refs[-1]
    each = staged.shape[0] // members
    for k in range(members):
        staged[k * each : (k + 1) * each] = arrived[k][...]
    real_space_kernel(rows, planes, staged, *rest)


def real_space_kernel(rows, planes, recv, pot, inverse, forward, inv_z, fwd_z, _, back, field):
    devices, size, span_z = recv.shape
    span_x = devices * planes
    arrived = recv.reshape(devices * size, span_z)
    leaving = back.reshape(devices * 2 * size, span_z)
    for group in groups(rows, span_z):
        columns = [
            jnp.concatenate(
                [
                    arrived[pl.ds((p * rows + r) * 2 + part, devices, stride=size), :]
                    for part in range(2)
                    for p in range(planes)
                ],
                axis=0,
            )
            for r in group
        ]
        along_x = dot_left(inverse[...], jnp.concatenate(columns, axis=1))
        spatial = dot_right(parts_in_lanes(along_x, span_x, span_z), inv_z[...])
        here = slice(group[0] * span_x, (group[-1] + 1) * span_x)
        for band in range(2):
            one = spatial[:, band * span_z : (band + 1) * span_z]
            field[band, here, :] = one
            product = one * pot[here, :]
            product = jnp.concatenate(
                [product[i * span_x : (i + 1) * span_x] for i in range(len(group))], axis=1
            )
            spectral = dot_left(forward[...], product)
            spectral = dot_right(parts_in_lanes(spectral, span_x, span_z), fwd_z[...])
            for i, r in enumerate(group):
                for p in range(planes):
                    first = i * span_x + p * devices
                    for part in range(2):
                        start = band * size + (p * rows + r) * 2 + part
                        leaving[pl.ds(start, devices, stride=2 * size), :] = spectral[
                            first : first + devices, part * span_z : (part + 1) * span_z
                        ]


def real_gram_kernel(bands, *refs):
    fields, (pot, out) = refs[:-2], refs[-2:]
    held = fields[0].shape[0]
    pairs = [(a, b) for a in range(bands) for b in range(a, bands)]
    for weighted in range(2):

        def step(i, sums):
            rows = pl.ds(pl.multiple_of(i * 8, 8), 8)
            values = [fields[a // held][a % held, rows, :] for a in range(bands)]
            other = [v * pot[rows, :] for v in values] if weighted else values
            result = []
            for (a, b), total in zip(pairs, sums):
                product = values[a] * other[b]
                lanes = product[:, :128]
                for c in range(128, product.shape[1], 128):
                    lanes = lanes + product[:, c : c + 128]
                result.append(total + lanes)
            return tuple(result)

        sums = lax.fori_loop(
            0, pot.shape[0] // 8, step, tuple(jnp.zeros((8, 128), f32) for _ in pairs)
        )
        for (a, b), total in zip(pairs, sums):
            line = jnp.sum(total, axis=0, keepdims=True)
            out[weighted, a, b : b + 1, :] = line
            out[weighted, b, a : a + 1, :] = line


def to_planes_kernel(recv, base, y_table, out):
    _, _, planes, span_y, span_z = base.shape
    each = recv.shape[1] // planes
    for group in groups(planes, span_z):
        columns = [
            recv[:, p * each : (p + 1) * each, :].reshape(2 * span_y, span_z) for p in group
        ]
        along_y = dot_left(y_table[...], jnp.concatenate(columns, axis=1))
        for i, p in enumerate(group):
            for part in range(2):
                out[0, part, p] = base[0, part, p] + (
                    along_y[part * span_y : (part + 1) * span_y, i * span_z : (i + 1) * span_z]
                )


def pass_on_kernel(values, _, out):
    out[...] = values[...]


def block_rows_of(psi, beta, slots):
    bands, _, span, span_z = psi.shape
    psi_flat = psi.reshape(bands * 2 * span, span_z)
    psi_rows = [psi_flat[pl.ds(y, 2 * bands, stride=span), :] for y in range(span)]
    beta_rows = [
        jnp.concatenate(
            [beta[pl.ds(2 * y + part, slots, stride=2 * span), :] for part in range(2)], axis=0
        )
        for y in range(span)
    ]
    return psi_rows, beta_rows


def project_kernel(slots, psi, beta, kinetic, out):
    bands, _, span, span_z = psi.shape
    psi_rows, beta_rows = block_rows_of(psi, beta, slots)
    kin_rows = [psi_rows[y] * kinetic[y : y + 1, :] for y in range(span)]
    right = jnp.concatenate(split(jnp.concatenate(psi_rows, axis=1)), axis=0)
    left = jnp.concatenate(
        split(jnp.concatenate(beta_rows, axis=1)) + split(jnp.concatenate(kin_rows, axis=1)), axis=0
    )
    full = lax.dot_general(left, right, (((1,), (1,)), ((), ())), preferred_element_type=f32)
    width, height = 2 * bands, 2 * slots
    full = full[:, :width] + full[:, width:]
    out[0:height] = full[0:height] + full[height : 2 * height]
    rest = full[2 * height :]
    out[height:] = rest[0:width] + rest[width:]


def base_kernel(slots, psi, beta, kinetic, coefs, out):
    bands, _, span, span_z = psi.shape
    psi_rows, beta_rows = block_rows_of(psi, beta, slots)
    values = jnp.concatenate(
        [jnp.concatenate(psi_rows, axis=1), jnp.concatenate(beta_rows, axis=1)], axis=0
    )
    high, low = split(coefs[...])
    summed = dot_left(jnp.concatenate([high, high, low], axis=1), values)
    flat = out.reshape(bands * 2 * span, span_z)
    for y in range(span):
        flat[pl.ds(y, 2 * bands, stride=span), :] = (
            psi_rows[y] * kinetic[y : y + 1, :] + summed[:, y * span_z : (y + 1) * span_z]
        )


def whole(shape):
    return pl.BlockSpec(shape, lambda *_: (0,) * len(shape))


def subspace_solve(s_real, h_real, h_imag):
    factor = jnp.linalg.cholesky(s_real)
    solved = jax.scipy.linalg.cho_solve((factor, True), jnp.concatenate([h_real, h_imag], axis=1))
    order_size = s_real.shape[0]
    return (solved[:, :order_size], solved[:, order_size:])


def tdot(pattern, left, right):
    return jnp.einsum(pattern, left, right, precision=highest, preferred_element_type=jnp.float32)


def partner(values, devices, k):
    return lax.ppermute(values, "ga", [(d, d ^ k) for d in range(devices)])


def sum_over(values, devices):
    if devices & (devices - 1) or devices < 4:
        return lax.psum(values, "ga")
    step = 1
    while step < devices // 4:
        values = values + partner(values, devices, step)
        step *= 2
    others = [partner(values, devices, k * step) for k in (1, 2, 3)]
    return (values + others[0]) + (others[1] + others[2])


def on_device(devices, orbitals, plane_order, potential, projectors, slot_owner, strengths):
    bands = orbitals.shape[0]
    planes = orbitals.shape[2]
    span_y = orbitals.shape[3]
    span_z = orbitals.shape[4]
    span_x = plane_order.shape[0]
    blocks, slots = slot_owner.shape
    owners = strengths.shape[0] * strengths.shape[1]
    rows = span_y // devices
    block_rows = 2 * planes * rows
    pairs = bands // 2
    block_span = projectors.shape[3] // span_z
    per_plane = span_y // block_span
    grid_x = jnp.arange(span_x, dtype=jnp.int32)
    grid_y = jnp.arange(span_y, dtype=jnp.int32)
    grid_z = jnp.arange(span_z, dtype=jnp.int32)
    params = pltpu.CompilerParams(vmem_limit_bytes=vmem_limit)

    def cost(flops, moved):
        return pl.CostEstimate(flops=flops, bytes_accessed=moved, transcendentals=0)

    order = np.arange(2 * span_y)
    order = (order % 2) * span_y + order // 2
    inv_y = left_const(left_table(span_y, 1.0)[order])
    fwd_y = left_const(left_table(span_y, -1.0)[:, order])
    inv_z = right_const(right_table(span_z, 1.0))
    fwd_z = right_const(right_table(span_z, -1.0))

    parts = 2 if pairs % 2 == 0 else 1
    share = pairs // parts
    mine = lax.axis_index("ga").astype(jnp.int32)
    layers = 4 if parts == 2 and devices >= 8 and devices & (devices - 1) == 0 else 1
    members = devices // layers
    my_layer, my_member = (mine // members).reshape(1), (mine % members).reshape(1)
    scalar = pl.BlockSpec(memory_space=pltpu.SMEM)

    def to_rows(c, split):
        spec = pl.BlockSpec((devices, None, block_rows, span_z), lambda j: (0, j, 0, 0))
        shape = jax.ShapeDtypeStruct((devices, share, block_rows, span_z), f32)
        if split:
            spec = pl.BlockSpec((members, None, block_rows, span_z), lambda j: (0, j, 0, 0))
            shape = jax.ShapeDtypeStruct((members, share, block_rows, span_z), f32)
        return pl.pallas_call(
            to_rows_split_kernel if split else to_rows_kernel,
            out_shape=[shape] * layers if split else shape,
            grid=(share,),
            in_specs=([scalar] if split else [])
            + [
                pl.BlockSpec((2, 2, planes, span_y, span_z), lambda j: (c * share + j, 0, 0, 0, 0)),
                whole(inv_y.shape),
            ],
            out_specs=[spec] * layers if split else spec,
            scratch_shapes=[pltpu.VMEM((devices, block_rows, span_z), f32)] if split else [],
            compiler_params=params,
            cost_estimate=cost(4 * 10**9, 3 * 10**6),
            name="to_rows",
        )(*([my_layer] if split else []), orbitals, inv_y)

    arrived = []
    for c in range(parts):
        if c > 0 and layers > 1:
            sent = to_rows(c, True)
            arrived.append(
                [sent[0]] + [partner(sent[k], devices, k * members) for k in range(1, layers)]
            )
        else:
            arrived.append(
                lax.all_to_all(to_rows(c, False), "ga", split_axis=0, concat_axis=0, tiled=True)
            )

    def tables_x(owned):
        phases = (owned.T.reshape(-1)[:, None] * grid_x[None, :]) % span_x
        angles = phases.astype(f32) * (2.0 * math.pi / span_x)
        factor = 1.0 / math.sqrt(span_x)
        cosine, sine = jnp.cos(angles) * factor, jnp.sin(angles) * factor
        forward = jnp.concatenate([cosine, -sine], axis=0)
        inverse = jnp.concatenate([forward, jnp.concatenate([sine, cosine], axis=0)], axis=1).T
        tables = []
        for table in (forward, inverse):
            high, low = split_outside(table)
            tables.append(jnp.concatenate([high, high, low], axis=1))
        return tables

    owned = plane_order.reshape(devices, planes)
    fwd_x, inv_x = tables_x(owned)
    steps = np.arange(layers)[None, :] * members + np.arange(members)[:, None]
    _, inv_x_steps = tables_x(
        jnp.take(owned, mine ^ jnp.asarray(steps.reshape(-1), jnp.int32), axis=0)
    )
    pot = potential.transpose(1, 0, 2).reshape(rows * span_x, span_z)

    local_order = lax.dynamic_slice_in_dim(plane_order, lax.axis_index("ga") * planes, planes)
    freq_x = signed_index(local_order, span_x).astype(f32) / span_x
    freq_y = signed_index(grid_y, span_y).astype(f32) / span_y
    freq_z = signed_index(grid_z, span_z).astype(f32) / span_z
    kinetic = 2.0 * (
        freq_x[:, None, None] ** 2 + freq_y[None, :, None] ** 2 + freq_z[None, None, :] ** 2
    )
    beta = projectors.reshape(blocks, slots, 2, block_span, span_z)
    beta = beta.transpose(0, 1, 3, 2, 4).reshape(blocks, slots * block_span * 2, span_z)
    block_specs = [
        pl.BlockSpec(
            (bands, 2, None, block_span, span_z),
            lambda g: (0, 0, g // per_plane, g % per_plane, 0),
        ),
        pl.BlockSpec((None, slots * block_span * 2, span_z), lambda g: (g, 0, 0)),
        pl.BlockSpec((None, block_span, span_z), lambda g: (g // per_plane, g % per_plane, 0)),
    ]
    products = pl.pallas_call(
        functools.partial(project_kernel, slots),
        out_shape=jax.ShapeDtypeStruct((blocks, 2 * slots + 2 * bands, 2 * bands), f32),
        grid=(blocks,),
        in_specs=block_specs,
        out_specs=pl.BlockSpec((None, 2 * slots + 2 * bands, 2 * bands), lambda g: (g, 0, 0)),
        compiler_params=params,
        cost_estimate=cost(8 * 10**9, 8 * 10**6),
        name="project",
    )(orbitals, beta, kinetic)
    with_real = products[:, :slots].reshape(blocks, slots, bands, 2)
    with_imag = products[:, slots : 2 * slots].reshape(blocks, slots, bands, 2)
    proj = jnp.concatenate(
        [
            with_real[..., 0] + with_imag[..., 1],
            with_real[..., 1] - with_imag[..., 0],
        ],
        axis=-1,
    )
    chosen = (
        slot_owner[:, :, None] == jnp.arange(owners, dtype=jnp.int32)[None, None, :]
    ).astype(f32)
    proj = tdot("gsj,gsc->jc", chosen, proj)
    kin = jnp.sum(products[:, 2 * slots :], axis=0).reshape(bands, 2, bands, 2)
    kin = kin[:, 0, :, 0] + kin[:, 1, :, 1]

    returned, fields, backs = [], [], []
    for c in range(parts):
        steps = c > 0 and layers > 1
        if steps:
            regrouped = pl.pallas_call(
                functools.partial(regroup_kernel, layers),
                out_shape=[jax.ShapeDtypeStruct((layers, share, block_rows, span_z), f32)] * members,
                in_specs=[scalar]
                + [pl.BlockSpec(memory_space=pltpu.VMEM)] * layers
                + [pl.BlockSpec(memory_space=pl.ANY)],
                out_specs=[pl.BlockSpec(memory_space=pltpu.VMEM)] * members,
                compiler_params=params,
                cost_estimate=cost(0, 2 * 10**6),
                name="regroup",
            )(my_member, *arrived[c], backs[0])
            operands = [regrouped[0]] + [
                partner(regrouped[k], devices, k) for k in range(1, members)
            ]
            kernel = functools.partial(real_space_parts_kernel, rows, planes, members)
            spec = pl.BlockSpec((layers, None, block_rows, span_z), lambda j: (0, j, 0, 0))
        else:
            operands = [arrived[c]]
            kernel = functools.partial(real_space_kernel, rows, planes)
            spec = pl.BlockSpec((devices, None, block_rows, span_z), lambda j: (0, j, 0, 0))
        back, field = pl.pallas_call(
            kernel,
            out_shape=(
                jax.ShapeDtypeStruct((devices, 2 * share, block_rows, span_z), f32),
                jax.ShapeDtypeStruct((2 * share, rows * span_x, span_z), f32),
            ),
            grid=(share,),
            in_specs=[spec] * len(operands)
            + [
                whole(pot.shape),
                whole(inv_x.shape),
                whole(fwd_x.shape),
                whole(inv_z.shape),
                whole(fwd_z.shape),
                whole(proj.shape),
            ],
            out_specs=(
                pl.BlockSpec((devices, 2, block_rows, span_z), lambda j: (0, j, 0, 0)),
                pl.BlockSpec((2, rows * span_x, span_z), lambda j: (j, 0, 0)),
            ),
            scratch_shapes=[pltpu.VMEM((devices, block_rows, span_z), f32)] if steps else [],
            compiler_params=params,
            cost_estimate=cost(4 * 10**9, 8 * 10**6),
            name="real_space",
        )(*operands, pot, inv_x_steps if steps else inv_x, fwd_x, inv_z, fwd_z, proj)
        returned.append(lax.all_to_all(back, "ga", split_axis=0, concat_axis=0, tiled=True))
        fields.append(field)
        backs.append(back)

    grams = pl.pallas_call(
        functools.partial(real_gram_kernel, bands),
        out_shape=jax.ShapeDtypeStruct((2, bands, bands, 128), f32),
        compiler_params=params,
        cost_estimate=cost(10**7, 2 * 10**6),
        name="real_gram",
    )(*fields, pot)
    grams = jnp.sum(grams, axis=-1)
    own = jnp.concatenate([proj, jnp.concatenate([grams[0], grams[1] + kin], axis=1)], axis=0)
    total = sum_over(own, devices)
    total = pl.pallas_call(
        pass_on_kernel,
        out_shape=jax.ShapeDtypeStruct(total.shape, f32),
        in_specs=[pl.BlockSpec(memory_space=pltpu.VMEM), pl.BlockSpec(memory_space=pl.ANY)],
        out_specs=pl.BlockSpec(memory_space=pltpu.VMEM),
        name="pass_on",
    )(total, returned[0])
    proj, s_real, h_real = total[:owners], total[owners:, :bands], total[owners:, bands:]
    weighted = strengths.reshape(-1)[:, None] * proj
    p_real, p_imag = proj[:, :bands], proj[:, bands:]
    w_real, w_imag = weighted[:, :bands], weighted[:, bands:]
    h_real = h_real + tdot("ja,jb->ab", p_real, w_real) + tdot("ja,jb->ab", p_imag, w_imag)
    h_imag = tdot("ja,jb->ab", p_real, w_imag) - tdot("ja,jb->ab", p_imag, w_real)
    m_real, m_imag = subspace_solve(s_real, h_real, h_imag)

    coefs = tdot("gsj,jc->gcs", chosen, weighted)
    c_real, c_imag = coefs[:, :bands], coefs[:, bands:]
    from_beta = jnp.stack(
        [
            jnp.concatenate([c_real, -c_imag], axis=2),
            jnp.concatenate([c_imag, c_real], axis=2),
        ],
        axis=2,
    ).reshape(blocks, 2 * bands, 2 * slots)
    from_psi = jnp.stack(
        [
            jnp.stack([-m_real.T, m_imag.T], axis=-1),
            jnp.stack([-m_imag.T, -m_real.T], axis=-1),
        ],
        axis=1,
    ).reshape(1, 2 * bands, 2 * bands)
    coefs = jnp.concatenate(
        [jnp.broadcast_to(from_psi, (blocks, 2 * bands, 2 * bands)), from_beta], axis=2
    )
    base = pl.pallas_call(
        functools.partial(base_kernel, slots),
        out_shape=jax.ShapeDtypeStruct(orbitals.shape, f32),
        grid=(blocks,),
        in_specs=block_specs
        + [pl.BlockSpec((None, 2 * bands, 2 * bands + 2 * slots), lambda g: (g, 0, 0))],
        out_specs=block_specs[0],
        compiler_params=params,
        cost_estimate=cost(8 * 10**9, 12 * 10**6),
        name="base",
    )(orbitals, beta, kinetic, coefs)

    residual = base
    for c in range(parts):
        one_band = pl.BlockSpec(
            (1, 2, planes, span_y, span_z), lambda b, c=c: (2 * share * c + b, 0, 0, 0, 0)
        )
        residual = pl.pallas_call(
            to_planes_kernel,
            out_shape=jax.ShapeDtypeStruct(orbitals.shape, f32),
            grid=(2 * share,),
            in_specs=[
                pl.BlockSpec((devices, None, block_rows, span_z), lambda b: (0, b, 0, 0)),
                one_band,
                whole(fwd_y.shape),
            ],
            out_specs=one_band,
            input_output_aliases={1: 0},
            compiler_params=params,
            cost_estimate=cost(8 * 10**9, 12 * 10**6),
            name="to_planes",
        )(returned[c], residual, fwd_y)
    return (residual, jnp.stack([m_real, m_imag]))


def solution(mesh):
    return jax.shard_map(
        functools.partial(on_device, mesh.shape["ga"]),
        mesh=mesh,
        in_specs=(
            P("rep", None, "ga", None, None),
            P("rep"),
            P("rep", "ga", None),
            P(("rep", "ga"), None, None, None),
            P(("rep", "ga"), None),
            P("rep", None),
        ),
        out_specs=(P("rep", None, "ga", None, None), P(None, "rep", None)),
        check_vma=False,
    )
```

```python
import functools
import math

import jax
import jax.numpy as jnp
import numpy as np
from jax import lax
from jax.experimental import pallas as pl
from jax.experimental.pallas import tpu as pltpu
from jax.sharding import PartitionSpec as P

highest = lax.Precision.HIGHEST
f32 = jnp.float32
bf16 = jnp.bfloat16
vmem_limit = 63 * 1024 * 1024


def signed_index(values, length):
    return jnp.where(values < length // 2, values, values - length)


def dft(length, orient):
    index = np.arange(length)
    angles = (index[:, None] * index[None, :] % length) * (2.0 * math.pi / length)
    factor = 1.0 / math.sqrt(length)
    return np.cos(angles) * factor, orient * np.sin(angles) * factor


def left_table(length, orient):
    cosine, sine = dft(length, orient)
    return np.block([[cosine, -sine], [sine, cosine]])


def right_table(length, orient):
    cosine, sine = dft(length, orient)
    return np.block([[cosine, sine], [-sine, cosine]])


def split(values):
    high = values.astype(bf16)
    low = (values - high.astype(f32)).astype(bf16)
    return high, low


def split_outside(values):
    high = lax.reduce_precision(values, exponent_bits=8, mantissa_bits=7)
    return high.astype(bf16), (values - high).astype(bf16)


def const_parts(table):
    table = np.asarray(table, np.float32)
    high = table.astype(jnp.bfloat16)
    low = (table - high.astype(np.float32)).astype(jnp.bfloat16)
    return high, low


def left_const(table):
    high, low = const_parts(table)
    return jnp.asarray(np.concatenate([high, high, low], axis=1))


def right_const(table):
    high, low = const_parts(table)
    return jnp.asarray(np.concatenate([high, high, low], axis=0))


def dot_left(table, values):
    high, low = split(values)
    return jnp.dot(
        table, jnp.concatenate([high, low, high], axis=0), preferred_element_type=f32
    )


def dot_right(values, table):
    high, low = split(values)
    return jnp.dot(
        jnp.concatenate([high, low, high], axis=1), table, preferred_element_type=f32
    )


def groups(count, width):
    size = max(1, 256 // width)
    return [list(range(i, min(i + size, count))) for i in range(0, count, size)]


def parts_in_lanes(values, span, width):
    items = values.shape[1] // width
    return jnp.concatenate(
        [
            jnp.concatenate(
                [values[:span, i * width : (i + 1) * width], values[span:, i * width : (i + 1) * width]],
                axis=1,
            )
            for i in range(items)
        ],
        axis=0,
    )


def to_rows_kernel(psi, y_table, out):
    _, _, planes, span_y, span_z = psi.shape
    devices, block_rows, _ = out.shape
    each = block_rows // planes
    for group in groups(planes, span_z):
        real = jnp.concatenate([psi[0, 0, p] - psi[1, 1, p] for p in group], axis=1)
        imag = jnp.concatenate([psi[0, 1, p] + psi[1, 0, p] for p in group], axis=1)
        along_y = dot_left(y_table[...], jnp.concatenate([real, imag], axis=0))
        for i, p in enumerate(group):
            out[:, p * each : (p + 1) * each, :] = along_y[
                :, i * span_z : (i + 1) * span_z
            ].reshape(devices, each, span_z)


def real_space_kernel(rows, planes, recv, pot, inverse, forward, inv_z, fwd_z, _, back, field):
    devices, size, span_z = recv.shape
    span_x = devices * planes
    arrived = recv.reshape(devices * size, span_z)
    leaving = back.reshape(devices * 2 * size, span_z)
    for group in groups(rows, span_z):
        columns = [
            jnp.concatenate(
                [
                    arrived[pl.ds((p * rows + r) * 2 + part, devices, stride=size), :]
                    for part in range(2)
                    for p in range(planes)
                ],
                axis=0,
            )
            for r in group
        ]
        along_x = dot_left(inverse[...], jnp.concatenate(columns, axis=1))
        spatial = dot_right(parts_in_lanes(along_x, span_x, span_z), inv_z[...])
        here = slice(group[0] * span_x, (group[-1] + 1) * span_x)
        for band in range(2):
            one = spatial[:, band * span_z : (band + 1) * span_z]
            field[band, here, :] = one
            product = one * pot[here, :]
            product = jnp.concatenate(
                [product[i * span_x : (i + 1) * span_x] for i in range(len(group))], axis=1
            )
            spectral = dot_left(forward[...], product)
            spectral = dot_right(parts_in_lanes(spectral, span_x, span_z), fwd_z[...])
            for i, r in enumerate(group):
                for p in range(planes):
                    first = i * span_x + p * devices
                    for part in range(2):
                        start = band * size + (p * rows + r) * 2 + part
                        leaving[pl.ds(start, devices, stride=2 * size), :] = spectral[
                            first : first + devices, part * span_z : (part + 1) * span_z
                        ]


def real_gram_kernel(bands, *refs):
    fields, (pot, out) = refs[:-2], refs[-2:]
    held = fields[0].shape[0]
    pairs = [(a, b) for a in range(bands) for b in range(a, bands)]
    for weighted in range(2):

        def step(i, sums):
            rows = pl.ds(pl.multiple_of(i * 8, 8), 8)
            values = [fields[a // held][a % held, rows, :] for a in range(bands)]
            other = [v * pot[rows, :] for v in values] if weighted else values
            result = []
            for (a, b), total in zip(pairs, sums):
                product = values[a] * other[b]
                lanes = product[:, :128]
                for c in range(128, product.shape[1], 128):
                    lanes = lanes + product[:, c : c + 128]
                result.append(total + lanes)
            return tuple(result)

        sums = lax.fori_loop(
            0, pot.shape[0] // 8, step, tuple(jnp.zeros((8, 128), f32) for _ in pairs)
        )
        for (a, b), total in zip(pairs, sums):
            line = jnp.sum(total, axis=0, keepdims=True)
            out[weighted, a, b : b + 1, :] = line
            out[weighted, b, a : a + 1, :] = line


def to_planes_kernel(recv, base, y_table, out):
    bands, _, planes, span_y, span_z = base.shape
    each = recv.shape[2] // planes
    for band in range(bands):
        for group in groups(planes, span_z):
            columns = [
                recv[:, band, p * each : (p + 1) * each, :].reshape(2 * span_y, span_z)
                for p in group
            ]
            along_y = dot_left(y_table[...], jnp.concatenate(columns, axis=1))
            for i, p in enumerate(group):
                for part in range(2):
                    out[band, part, p] = base[band, part, p] + (
                        along_y[part * span_y : (part + 1) * span_y, i * span_z : (i + 1) * span_z]
                    )


def last_sum_kernel(*refs):
    first, second, third, fourth, _, out = refs
    out[...] = (first[...] + second[...]) + (third[...] + fourth[...])


def block_rows_of(psi, beta, slots):
    bands, _, span, span_z = psi.shape
    psi_flat = psi.reshape(bands * 2 * span, span_z)
    psi_rows = [psi_flat[pl.ds(y, 2 * bands, stride=span), :] for y in range(span)]
    beta_rows = [
        jnp.concatenate(
            [beta[pl.ds(2 * y + part, slots, stride=2 * span), :] for part in range(2)], axis=0
        )
        for y in range(span)
    ]
    return psi_rows, beta_rows


def project_kernel(slots, psi, beta, kinetic, out):
    bands, _, span, span_z = psi.shape
    psi_rows, beta_rows = block_rows_of(psi, beta, slots)
    kin_rows = [psi_rows[y] * kinetic[y : y + 1, :] for y in range(span)]
    right = jnp.concatenate(split(jnp.concatenate(psi_rows, axis=1)), axis=0)
    left = jnp.concatenate(
        split(jnp.concatenate(beta_rows, axis=1)) + split(jnp.concatenate(kin_rows, axis=1)), axis=0
    )
    full = lax.dot_general(left, right, (((1,), (1,)), ((), ())), preferred_element_type=f32)
    width, height = 2 * bands, 2 * slots
    full = full[:, :width] + full[:, width:]
    out[0:height] = full[0:height] + full[height : 2 * height]
    rest = full[2 * height :]
    out[height:] = rest[0:width] + rest[width:]


def base_kernel(slots, psi, beta, kinetic, coefs, out):
    bands, _, span, span_z = psi.shape
    psi_rows, beta_rows = block_rows_of(psi, beta, slots)
    values = jnp.concatenate(
        [jnp.concatenate(psi_rows, axis=1), jnp.concatenate(beta_rows, axis=1)], axis=0
    )
    high, low = split(coefs[...])
    summed = dot_left(jnp.concatenate([high, high, low], axis=1), values)
    flat = out.reshape(bands * 2 * span, span_z)
    for y in range(span):
        flat[pl.ds(y, 2 * bands, stride=span), :] = (
            psi_rows[y] * kinetic[y : y + 1, :] + summed[:, y * span_z : (y + 1) * span_z]
        )


def whole(shape):
    return pl.BlockSpec(shape, lambda *_: (0,) * len(shape))


def subspace_solve(s_real, h_real, h_imag):
    factor = jnp.linalg.cholesky(s_real)
    solved = jax.scipy.linalg.cho_solve((factor, True), jnp.concatenate([h_real, h_imag], axis=1))
    order_size = s_real.shape[0]
    return (solved[:, :order_size], solved[:, order_size:])


def tdot(pattern, left, right):
    return jnp.einsum(pattern, left, right, precision=highest, preferred_element_type=jnp.float32)


def partner(values, devices, k):
    return lax.ppermute(values, "ga", [(d, d ^ k) for d in range(devices)])


def sum_over(values, devices, after):
    if devices & (devices - 1) or devices < 4:
        return lax.psum(values, "ga")
    step = 1
    while step < devices // 4:
        values = values + partner(values, devices, step)
        step *= 2
    others = [partner(values, devices, k * step) for k in (1, 2, 3)]
    held = pl.BlockSpec(memory_space=pltpu.VMEM)
    return pl.pallas_call(
        last_sum_kernel,
        out_shape=jax.ShapeDtypeStruct(values.shape, f32),
        in_specs=[held] * 4 + [pl.BlockSpec(memory_space=pl.ANY)],
        out_specs=held,
        name="last_sum",
    )(values, *others, after)


def on_device(devices, orbitals, plane_order, potential, projectors, slot_owner, strengths):
    bands = orbitals.shape[0]
    planes = orbitals.shape[2]
    span_y = orbitals.shape[3]
    span_z = orbitals.shape[4]
    span_x = plane_order.shape[0]
    blocks, slots = slot_owner.shape
    owners = strengths.shape[0] * strengths.shape[1]
    rows = span_y // devices
    block_rows = 2 * planes * rows
    pairs = bands // 2
    block_span = projectors.shape[3] // span_z
    per_plane = span_y // block_span
    grid_x = jnp.arange(span_x, dtype=jnp.int32)
    grid_y = jnp.arange(span_y, dtype=jnp.int32)
    grid_z = jnp.arange(span_z, dtype=jnp.int32)
    params = pltpu.CompilerParams(vmem_limit_bytes=vmem_limit)

    def cost(flops, moved):
        return pl.CostEstimate(flops=flops, bytes_accessed=moved, transcendentals=0)

    order = np.arange(2 * span_y)
    order = (order % 2) * span_y + order // 2
    inv_y = left_const(left_table(span_y, 1.0)[order])
    fwd_y = left_const(left_table(span_y, -1.0)[:, order])
    inv_z = right_const(right_table(span_z, 1.0))
    fwd_z = right_const(right_table(span_z, -1.0))

    parts = 2 if pairs % 2 == 0 else 1
    share = pairs // parts
    arrived = []
    for c in range(parts):
        sent = pl.pallas_call(
            to_rows_kernel,
            out_shape=jax.ShapeDtypeStruct((devices, share, block_rows, span_z), f32),
            grid=(share,),
            in_specs=[
                pl.BlockSpec(
                    (2, 2, planes, span_y, span_z), lambda j, c=c: (c * share + j, 0, 0, 0, 0)
                ),
                whole(inv_y.shape),
            ],
            out_specs=pl.BlockSpec((devices, None, block_rows, span_z), lambda j: (0, j, 0, 0)),
            compiler_params=params,
            cost_estimate=cost(4 * 10**9, 3 * 10**6),
            name="to_rows",
        )(orbitals, inv_y)
        arrived.append(lax.all_to_all(sent, "ga", split_axis=0, concat_axis=0, tiled=True))

    stored = plane_order.reshape(devices, planes).T.reshape(-1)
    phases = (stored[:, None] * grid_x[None, :]) % span_x
    angles = phases.astype(f32) * (2.0 * math.pi / span_x)
    factor = 1.0 / math.sqrt(span_x)
    cosine, sine = jnp.cos(angles) * factor, jnp.sin(angles) * factor
    fwd_x = jnp.concatenate([cosine, -sine], axis=0)
    inv_x = jnp.concatenate([fwd_x, jnp.concatenate([sine, cosine], axis=0)], axis=1).T
    high, low = split_outside(fwd_x)
    fwd_x = jnp.concatenate([high, high, low], axis=1)
    high, low = split_outside(inv_x)
    inv_x = jnp.concatenate([high, high, low], axis=1)
    pot = potential.transpose(1, 0, 2).reshape(rows * span_x, span_z)

    local_order = lax.dynamic_slice_in_dim(plane_order, lax.axis_index("ga") * planes, planes)
    freq_x = signed_index(local_order, span_x).astype(f32) / span_x
    freq_y = signed_index(grid_y, span_y).astype(f32) / span_y
    freq_z = signed_index(grid_z, span_z).astype(f32) / span_z
    kinetic = 2.0 * (
        freq_x[:, None, None] ** 2 + freq_y[None, :, None] ** 2 + freq_z[None, None, :] ** 2
    )
    beta = projectors.reshape(blocks, slots, 2, block_span, span_z)
    beta = beta.transpose(0, 1, 3, 2, 4).reshape(blocks, slots * block_span * 2, span_z)
    block_specs = [
        pl.BlockSpec(
            (bands, 2, None, block_span, span_z),
            lambda g: (0, 0, g // per_plane, g % per_plane, 0),
        ),
        pl.BlockSpec((None, slots * block_span * 2, span_z), lambda g: (g, 0, 0)),
        pl.BlockSpec((None, block_span, span_z), lambda g: (g // per_plane, g % per_plane, 0)),
    ]
    products = pl.pallas_call(
        functools.partial(project_kernel, slots),
        out_shape=jax.ShapeDtypeStruct((blocks, 2 * slots + 2 * bands, 2 * bands), f32),
        grid=(blocks,),
        in_specs=block_specs,
        out_specs=pl.BlockSpec((None, 2 * slots + 2 * bands, 2 * bands), lambda g: (g, 0, 0)),
        compiler_params=params,
        cost_estimate=cost(8 * 10**9, 8 * 10**6),
        name="project",
    )(orbitals, beta, kinetic)
    with_real = products[:, :slots].reshape(blocks, slots, bands, 2)
    with_imag = products[:, slots : 2 * slots].reshape(blocks, slots, bands, 2)
    proj = jnp.concatenate(
        [
            with_real[..., 0] + with_imag[..., 1],
            with_real[..., 1] - with_imag[..., 0],
        ],
        axis=-1,
    )
    owned = (
        slot_owner[:, :, None] == jnp.arange(owners, dtype=jnp.int32)[None, None, :]
    ).astype(f32)
    proj = tdot("gsj,gsc->jc", owned, proj)
    kin = jnp.sum(products[:, 2 * slots :], axis=0).reshape(bands, 2, bands, 2)
    kin = kin[:, 0, :, 0] + kin[:, 1, :, 1]

    returned, fields = [], []
    for c in range(parts):
        back, field = pl.pallas_call(
            functools.partial(real_space_kernel, rows, planes),
            out_shape=(
                jax.ShapeDtypeStruct((devices, 2 * share, block_rows, span_z), f32),
                jax.ShapeDtypeStruct((2 * share, rows * span_x, span_z), f32),
            ),
            grid=(share,),
            in_specs=[
                pl.BlockSpec((devices, None, block_rows, span_z), lambda j: (0, j, 0, 0)),
                whole(pot.shape),
                whole(inv_x.shape),
                whole(fwd_x.shape),
                whole(inv_z.shape),
                whole(fwd_z.shape),
                whole(proj.shape),
            ],
            out_specs=(
                pl.BlockSpec((devices, 2, block_rows, span_z), lambda j: (0, j, 0, 0)),
                pl.BlockSpec((2, rows * span_x, span_z), lambda j: (j, 0, 0)),
            ),
            compiler_params=params,
            cost_estimate=cost(4 * 10**9, 8 * 10**6),
            name="real_space",
        )(arrived[c], pot, inv_x, fwd_x, inv_z, fwd_z, proj)
        returned.append(lax.all_to_all(back, "ga", split_axis=0, concat_axis=0, tiled=True))
        fields.append(field)

    grams = pl.pallas_call(
        functools.partial(real_gram_kernel, bands),
        out_shape=jax.ShapeDtypeStruct((2, bands, bands, 128), f32),
        compiler_params=params,
        cost_estimate=cost(10**7, 2 * 10**6),
        name="real_gram",
    )(*fields, pot)
    grams = jnp.sum(grams, axis=-1)
    own = jnp.concatenate([proj, jnp.concatenate([grams[0], grams[1] + kin], axis=1)], axis=0)
    total = sum_over(own, devices, returned[0])
    proj, s_real, h_real = total[:owners], total[owners:, :bands], total[owners:, bands:]
    weighted = strengths.reshape(-1)[:, None] * proj
    p_real, p_imag = proj[:, :bands], proj[:, bands:]
    w_real, w_imag = weighted[:, :bands], weighted[:, bands:]
    h_real = h_real + tdot("ja,jb->ab", p_real, w_real) + tdot("ja,jb->ab", p_imag, w_imag)
    h_imag = tdot("ja,jb->ab", p_real, w_imag) - tdot("ja,jb->ab", p_imag, w_real)
    m_real, m_imag = subspace_solve(s_real, h_real, h_imag)

    coefs = tdot("gsj,jc->gcs", owned, weighted)
    c_real, c_imag = coefs[:, :bands], coefs[:, bands:]
    from_beta = jnp.stack(
        [
            jnp.concatenate([c_real, -c_imag], axis=2),
            jnp.concatenate([c_imag, c_real], axis=2),
        ],
        axis=2,
    ).reshape(blocks, 2 * bands, 2 * slots)
    from_psi = jnp.stack(
        [
            jnp.stack([-m_real.T, m_imag.T], axis=-1),
            jnp.stack([-m_imag.T, -m_real.T], axis=-1),
        ],
        axis=1,
    ).reshape(1, 2 * bands, 2 * bands)
    coefs = jnp.concatenate(
        [jnp.broadcast_to(from_psi, (blocks, 2 * bands, 2 * bands)), from_beta], axis=2
    )
    base = pl.pallas_call(
        functools.partial(base_kernel, slots),
        out_shape=jax.ShapeDtypeStruct(orbitals.shape, f32),
        grid=(blocks,),
        in_specs=block_specs
        + [pl.BlockSpec((None, 2 * bands, 2 * bands + 2 * slots), lambda g: (g, 0, 0))],
        out_specs=block_specs[0],
        compiler_params=params,
        cost_estimate=cost(8 * 10**9, 12 * 10**6),
        name="base",
    )(orbitals, beta, kinetic, coefs)

    residual = base
    for c in range(parts):
        two_bands = pl.BlockSpec(
            (2, 2, planes, span_y, span_z), lambda j, c=c: (share * c + j, 0, 0, 0, 0)
        )
        residual = pl.pallas_call(
            to_planes_kernel,
            out_shape=jax.ShapeDtypeStruct(orbitals.shape, f32),
            grid=(share,),
            in_specs=[
                pl.BlockSpec((devices, 2, block_rows, span_z), lambda j: (0, j, 0, 0)),
                two_bands,
                whole(fwd_y.shape),
            ],
            out_specs=two_bands,
            input_output_aliases={1: 0},
            compiler_params=params,
            cost_estimate=cost(8 * 10**9, 12 * 10**6),
            name="to_planes",
        )(returned[c], residual, fwd_y)
    return (residual, jnp.stack([m_real, m_imag]))


def solution(mesh):
    return jax.shard_map(
        functools.partial(on_device, mesh.shape["ga"]),
        mesh=mesh,
        in_specs=(
            P("rep", None, "ga", None, None),
            P("rep"),
            P("rep", "ga", None),
            P(("rep", "ga"), None, None, None),
            P(("rep", "ga"), None),
            P("rep", None),
        ),
        out_specs=(P("rep", None, "ga", None, None), P(None, "rep", None)),
        check_vma=False,
    )
```

```python
import functools
import math

import jax
import jax.numpy as jnp
import numpy as np
from jax import lax
from jax.experimental import pallas as pl
from jax.experimental.pallas import tpu as pltpu
from jax.sharding import PartitionSpec as P

highest = lax.Precision.HIGHEST
f32 = jnp.float32
bf16 = jnp.bfloat16
vmem_limit = 63 * 1024 * 1024


def signed_index(values, length):
    return jnp.where(values < length // 2, values, values - length)


def dft(length, orient):
    index = np.arange(length)
    angles = (index[:, None] * index[None, :] % length) * (2.0 * math.pi / length)
    factor = 1.0 / math.sqrt(length)
    return np.cos(angles) * factor, orient * np.sin(angles) * factor


def left_table(length, orient):
    cosine, sine = dft(length, orient)
    return np.block([[cosine, -sine], [sine, cosine]])


def right_table(length, orient):
    cosine, sine = dft(length, orient)
    return np.block([[cosine, sine], [-sine, cosine]])


def split(values):
    high = values.astype(bf16)
    low = (values - high.astype(f32)).astype(bf16)
    return high, low


def split_outside(values):
    high = lax.reduce_precision(values, exponent_bits=8, mantissa_bits=7)
    return high.astype(bf16), (values - high).astype(bf16)


def const_parts(table):
    table = np.asarray(table, np.float32)
    high = table.astype(jnp.bfloat16)
    low = (table - high.astype(np.float32)).astype(jnp.bfloat16)
    return high, low


def left_const(table):
    high, low = const_parts(table)
    return jnp.asarray(np.concatenate([high, high, low], axis=1))


def right_const(table):
    high, low = const_parts(table)
    return jnp.asarray(np.concatenate([high, high, low], axis=0))


def dot_left(table, values):
    high, low = split(values)
    return jnp.dot(
        table, jnp.concatenate([high, low, high], axis=0), preferred_element_type=f32
    )


def dot_right(values, table):
    high, low = split(values)
    return jnp.dot(
        jnp.concatenate([high, low, high], axis=1), table, preferred_element_type=f32
    )


def groups(count, width):
    size = max(1, 256 // width)
    return [list(range(i, min(i + size, count))) for i in range(0, count, size)]


def parts_in_lanes(values, span, width):
    items = values.shape[1] // width
    return jnp.concatenate(
        [
            jnp.concatenate(
                [values[:span, i * width : (i + 1) * width], values[span:, i * width : (i + 1) * width]],
                axis=1,
            )
            for i in range(items)
        ],
        axis=0,
    )


def to_rows_kernel(psi, y_table, out):
    _, _, planes, span_y, span_z = psi.shape
    devices, block_rows, _ = out.shape
    each = block_rows // planes
    for group in groups(planes, span_z):
        real = jnp.concatenate([psi[0, 0, p] - psi[1, 1, p] for p in group], axis=1)
        imag = jnp.concatenate([psi[0, 1, p] + psi[1, 0, p] for p in group], axis=1)
        along_y = dot_left(y_table[...], jnp.concatenate([real, imag], axis=0))
        for i, p in enumerate(group):
            out[:, p * each : (p + 1) * each, :] = along_y[
                :, i * span_z : (i + 1) * span_z
            ].reshape(devices, each, span_z)


def real_space_kernel(rows, planes, recv, pot, inverse, forward, inv_z, fwd_z, _, *refs):
    devices, size, span_z = recv.shape
    span_x = devices * planes
    arrived = recv.reshape(devices * size, span_z)
    field, back, staged = refs[-devices - 2], refs[-devices - 1 : -1], refs[-1]
    for group in groups(rows, span_z):
        columns = [
            jnp.concatenate(
                [
                    arrived[pl.ds((p * rows + r) * 2 + part, devices, stride=size), :]
                    for part in range(2)
                    for p in range(planes)
                ],
                axis=0,
            )
            for r in group
        ]
        along_x = dot_left(inverse[...], jnp.concatenate(columns, axis=1))
        spatial = dot_right(parts_in_lanes(along_x, span_x, span_z), inv_z[...])
        here = slice(group[0] * span_x, (group[-1] + 1) * span_x)
        for band in range(2):
            one = spatial[:, band * span_z : (band + 1) * span_z]
            field[band, here, :] = one
            product = one * pot[here, :]
            product = jnp.concatenate(
                [product[i * span_x : (i + 1) * span_x] for i in range(len(group))], axis=1
            )
            spectral = dot_left(forward[...], product)
            spectral = dot_right(parts_in_lanes(spectral, span_x, span_z), fwd_z[...])
            for i, r in enumerate(group):
                for p in range(planes):
                    first = i * span_x + p * devices
                    for part in range(2):
                        start = (p * rows + r) * 2 + part
                        staged[band, pl.ds(start, devices, stride=size), :] = spectral[
                            first : first + devices, part * span_z : (part + 1) * span_z
                        ]
    for k in range(devices):
        for band in range(2):
            back[k][band] = staged[band, k * size : (k + 1) * size, :]


def real_gram_kernel(bands, *refs):
    fields, (pot, _, out) = refs[:-3], refs[-3:]
    held = fields[0].shape[0]
    pairs = [(a, b) for a in range(bands) for b in range(a, bands)]
    for weighted in range(2):

        def step(i, sums):
            rows = pl.ds(pl.multiple_of(i * 8, 8), 8)
            values = [fields[a // held][a % held, rows, :] for a in range(bands)]
            other = [v * pot[rows, :] for v in values] if weighted else values
            result = []
            for (a, b), total in zip(pairs, sums):
                product = values[a] * other[b]
                lanes = product[:, :128]
                for c in range(128, product.shape[1], 128):
                    lanes = lanes + product[:, c : c + 128]
                result.append(total + lanes)
            return tuple(result)

        sums = lax.fori_loop(
            0, pot.shape[0] // 8, step, tuple(jnp.zeros((8, 128), f32) for _ in pairs)
        )
        for (a, b), total in zip(pairs, sums):
            line = jnp.sum(total, axis=0, keepdims=True)
            out[weighted, a, b : b + 1, :] = line
            out[weighted, b, a : a + 1, :] = line


def to_planes_kernel(*refs):
    recv, (base, y_table, out) = refs[:-3], refs[-3:]
    bands, _, planes, span_y, span_z = base.shape
    each = recv[0].shape[1] // planes
    for band in range(bands):
        for group in groups(planes, span_z):
            columns = [
                jnp.concatenate([one[band, p * each : (p + 1) * each, :] for one in recv], axis=0)
                for p in group
            ]
            along_y = dot_left(y_table[...], jnp.concatenate(columns, axis=1))
            for i, p in enumerate(group):
                for part in range(2):
                    out[band, part, p] = base[band, part, p] + (
                        along_y[part * span_y : (part + 1) * span_y, i * span_z : (i + 1) * span_z]
                    )


def block_rows_of(psi, beta, slots):
    bands, _, span, span_z = psi.shape
    psi_flat = psi.reshape(bands * 2 * span, span_z)
    psi_rows = [psi_flat[pl.ds(y, 2 * bands, stride=span), :] for y in range(span)]
    beta_rows = [
        jnp.concatenate(
            [beta[pl.ds(2 * y + part, slots, stride=2 * span), :] for part in range(2)], axis=0
        )
        for y in range(span)
    ]
    return psi_rows, beta_rows


def project_kernel(slots, psi, beta, kinetic, out):
    bands, _, span, span_z = psi.shape
    psi_rows, beta_rows = block_rows_of(psi, beta, slots)
    kin_rows = [psi_rows[y] * kinetic[y : y + 1, :] for y in range(span)]
    right = jnp.concatenate(split(jnp.concatenate(psi_rows, axis=1)), axis=0)
    left = jnp.concatenate(
        split(jnp.concatenate(beta_rows, axis=1)) + split(jnp.concatenate(kin_rows, axis=1)), axis=0
    )
    full = lax.dot_general(left, right, (((1,), (1,)), ((), ())), preferred_element_type=f32)
    width, height = 2 * bands, 2 * slots
    full = full[:, :width] + full[:, width:]
    out[0:height] = full[0:height] + full[height : 2 * height]
    rest = full[2 * height :]
    out[height:] = rest[0:width] + rest[width:]


def base_kernel(slots, psi, beta, kinetic, coefs, out):
    bands, _, span, span_z = psi.shape
    psi_rows, beta_rows = block_rows_of(psi, beta, slots)
    values = jnp.concatenate(
        [jnp.concatenate(psi_rows, axis=1), jnp.concatenate(beta_rows, axis=1)], axis=0
    )
    high, low = split(coefs[...])
    summed = dot_left(jnp.concatenate([high, high, low], axis=1), values)
    flat = out.reshape(bands * 2 * span, span_z)
    for y in range(span):
        flat[pl.ds(y, 2 * bands, stride=span), :] = (
            psi_rows[y] * kinetic[y : y + 1, :] + summed[:, y * span_z : (y + 1) * span_z]
        )


def whole(shape):
    return pl.BlockSpec(shape, lambda *_: (0,) * len(shape))


def subspace_solve(s_real, h_real, h_imag):
    factor = jnp.linalg.cholesky(s_real)
    solved = jax.scipy.linalg.cho_solve((factor, True), jnp.concatenate([h_real, h_imag], axis=1))
    order_size = s_real.shape[0]
    return (solved[:, :order_size], solved[:, order_size:])


def tdot(pattern, left, right):
    return jnp.einsum(pattern, left, right, precision=highest, preferred_element_type=jnp.float32)


def partner(values, devices, k):
    return lax.ppermute(values, "ga", [(d, d ^ k) for d in range(devices)])


def sum_over(values, devices):
    if devices & (devices - 1) or devices < 4:
        return lax.psum(values, "ga")
    step = 1
    while step < devices // 4:
        values = values + partner(values, devices, step)
        step *= 2
    others = [partner(values, devices, k * step) for k in (1, 2, 3)]
    return (values + others[0]) + (others[1] + others[2])


def on_device(devices, orbitals, plane_order, potential, projectors, slot_owner, strengths):
    bands = orbitals.shape[0]
    planes = orbitals.shape[2]
    span_y = orbitals.shape[3]
    span_z = orbitals.shape[4]
    span_x = plane_order.shape[0]
    blocks, slots = slot_owner.shape
    owners = strengths.shape[0] * strengths.shape[1]
    rows = span_y // devices
    block_rows = 2 * planes * rows
    pairs = bands // 2
    block_span = projectors.shape[3] // span_z
    per_plane = span_y // block_span
    grid_x = jnp.arange(span_x, dtype=jnp.int32)
    grid_y = jnp.arange(span_y, dtype=jnp.int32)
    grid_z = jnp.arange(span_z, dtype=jnp.int32)
    params = pltpu.CompilerParams(vmem_limit_bytes=vmem_limit)

    def cost(flops, moved):
        return pl.CostEstimate(flops=flops, bytes_accessed=moved, transcendentals=0)

    order = np.arange(2 * span_y)
    order = (order % 2) * span_y + order // 2
    inv_y = left_const(left_table(span_y, 1.0)[order])
    mine = lax.axis_index("ga").astype(jnp.int32)
    fwd_y = jnp.asarray(np.concatenate(const_parts(left_table(span_y, -1.0)[:, order]), axis=0))
    swap = jnp.arange(2 * span_y, dtype=jnp.int32)
    swap = (swap[:, None] == (swap[None, :] ^ (mine * 2 * rows))).astype(bf16)
    fwd_y = jnp.dot(fwd_y, swap, preferred_element_type=f32).astype(bf16)
    high, low = fwd_y[: 2 * span_y], fwd_y[2 * span_y :]
    fwd_y = jnp.concatenate([high, high, low], axis=1)
    inv_z = right_const(right_table(span_z, 1.0))
    fwd_z = right_const(right_table(span_z, -1.0))

    parts = 2 if pairs % 2 == 0 else 1
    share = pairs // parts
    arrived = []
    for c in range(parts):
        sent = pl.pallas_call(
            to_rows_kernel,
            out_shape=jax.ShapeDtypeStruct((devices, share, block_rows, span_z), f32),
            grid=(share,),
            in_specs=[
                pl.BlockSpec(
                    (2, 2, planes, span_y, span_z), lambda j, c=c: (c * share + j, 0, 0, 0, 0)
                ),
                whole(inv_y.shape),
            ],
            out_specs=pl.BlockSpec((devices, None, block_rows, span_z), lambda j: (0, j, 0, 0)),
            compiler_params=params,
            cost_estimate=cost(4 * 10**9, 3 * 10**6),
            name="to_rows",
        )(orbitals, inv_y)
        arrived.append(lax.all_to_all(sent, "ga", split_axis=0, concat_axis=0, tiled=True))

    def along_x(owned):
        phases = (owned.T.reshape(-1)[:, None] * grid_x[None, :]) % span_x
        angles = phases.astype(f32) * (2.0 * math.pi / span_x)
        factor = 1.0 / math.sqrt(span_x)
        return jnp.cos(angles) * factor, jnp.sin(angles) * factor

    owned = plane_order.reshape(devices, planes)
    cosine, sine = along_x(owned)
    high, low = split_outside(
        jnp.concatenate(
            [jnp.concatenate([cosine, -sine], axis=0), jnp.concatenate([sine, cosine], axis=0)],
            axis=1,
        ).T
    )
    inv_x = jnp.concatenate([high, high, low], axis=1)
    cosine, sine = along_x(jnp.take(owned, mine ^ jnp.arange(devices, dtype=jnp.int32), axis=0))
    high, low = split_outside(jnp.concatenate([cosine, -sine], axis=0))
    fwd_x = jnp.concatenate([high, high, low], axis=1)
    pot = potential.transpose(1, 0, 2).reshape(rows * span_x, span_z)

    local_order = lax.dynamic_slice_in_dim(plane_order, lax.axis_index("ga") * planes, planes)
    freq_x = signed_index(local_order, span_x).astype(f32) / span_x
    freq_y = signed_index(grid_y, span_y).astype(f32) / span_y
    freq_z = signed_index(grid_z, span_z).astype(f32) / span_z
    kinetic = 2.0 * (
        freq_x[:, None, None] ** 2 + freq_y[None, :, None] ** 2 + freq_z[None, None, :] ** 2
    )
    beta = projectors.reshape(blocks, slots, 2, block_span, span_z)
    beta = beta.transpose(0, 1, 3, 2, 4).reshape(blocks, slots * block_span * 2, span_z)
    block_specs = [
        pl.BlockSpec(
            (bands, 2, None, block_span, span_z),
            lambda g: (0, 0, g // per_plane, g % per_plane, 0),
        ),
        pl.BlockSpec((None, slots * block_span * 2, span_z), lambda g: (g, 0, 0)),
        pl.BlockSpec((None, block_span, span_z), lambda g: (g // per_plane, g % per_plane, 0)),
    ]
    products = pl.pallas_call(
        functools.partial(project_kernel, slots),
        out_shape=jax.ShapeDtypeStruct((blocks, 2 * slots + 2 * bands, 2 * bands), f32),
        grid=(blocks,),
        in_specs=block_specs,
        out_specs=pl.BlockSpec((None, 2 * slots + 2 * bands, 2 * bands), lambda g: (g, 0, 0)),
        compiler_params=params,
        cost_estimate=cost(8 * 10**9, 8 * 10**6),
        name="project",
    )(orbitals, beta, kinetic)
    with_real = products[:, :slots].reshape(blocks, slots, bands, 2)
    with_imag = products[:, slots : 2 * slots].reshape(blocks, slots, bands, 2)
    proj = jnp.concatenate(
        [
            with_real[..., 0] + with_imag[..., 1],
            with_real[..., 1] - with_imag[..., 0],
        ],
        axis=-1,
    )
    owned = (
        slot_owner[:, :, None] == jnp.arange(owners, dtype=jnp.int32)[None, None, :]
    ).astype(f32)
    proj = tdot("gsj,gsc->jc", owned, proj)
    kin = jnp.sum(products[:, 2 * slots :], axis=0).reshape(bands, 2, bands, 2)
    kin = kin[:, 0, :, 0] + kin[:, 1, :, 1]

    fields, back = [], []
    for c in range(parts):
        held = len(back)
        field, *back = pl.pallas_call(
            functools.partial(real_space_kernel, rows, planes),
            out_shape=[jax.ShapeDtypeStruct((2 * share, rows * span_x, span_z), f32)]
            + [jax.ShapeDtypeStruct((bands, block_rows, span_z), f32)] * devices,
            grid=(share,),
            in_specs=[
                pl.BlockSpec((devices, None, block_rows, span_z), lambda j: (0, j, 0, 0)),
                whole(pot.shape),
                whole(inv_x.shape),
                whole(fwd_x.shape),
                whole(inv_z.shape),
                whole(fwd_z.shape),
                whole(proj.shape),
            ]
            + [pl.BlockSpec(memory_space=pl.ANY)] * held,
            out_specs=[pl.BlockSpec((2, rows * span_x, span_z), lambda j: (j, 0, 0))]
            + [
                pl.BlockSpec((2, block_rows, span_z), lambda j, c=c: (c * share + j, 0, 0))
            ] * devices,
            scratch_shapes=[pltpu.VMEM((2, devices * block_rows, span_z), f32)],
            input_output_aliases={7 + k: 1 + k for k in range(held)},
            compiler_params=params,
            cost_estimate=cost(4 * 10**9, 8 * 10**6),
            name="real_space",
        )(arrived[c], pot, inv_x, fwd_x, inv_z, fwd_z, proj, *back)
        fields.append(field)
    layers = min(4, devices)
    rest = devices // layers
    sequence = [
        j * rest + (2 * ((j + i) % max(1, rest // 2)) + c) % rest
        for c in range(min(2, rest))
        for i in range(max(1, rest // 2))
        for j in range(layers)
    ]
    sequence = [k for k in sequence if k > 0]
    returned = {k: partner(back[k], devices, k) for k in sequence}
    early = returned[sequence[min(4, len(sequence) - 1)]]
    returned = [back[0]] + [returned[k] for k in range(1, devices)]

    grams = pl.pallas_call(
        functools.partial(real_gram_kernel, bands),
        out_shape=jax.ShapeDtypeStruct((2, bands, bands, 128), f32),
        in_specs=[pl.BlockSpec(memory_space=pltpu.VMEM)] * (parts + 1)
        + [pl.BlockSpec(memory_space=pl.ANY)],
        compiler_params=params,
        cost_estimate=cost(10**7, 2 * 10**6),
        name="real_gram",
    )(*fields, pot, early)
    grams = jnp.sum(grams, axis=-1)
    own = jnp.concatenate([proj, jnp.concatenate([grams[0], grams[1] + kin], axis=1)], axis=0)
    total = sum_over(own, devices)
    proj, s_real, h_real = total[:owners], total[owners:, :bands], total[owners:, bands:]
    weighted = strengths.reshape(-1)[:, None] * proj
    p_real, p_imag = proj[:, :bands], proj[:, bands:]
    w_real, w_imag = weighted[:, :bands], weighted[:, bands:]
    h_real = h_real + tdot("ja,jb->ab", p_real, w_real) + tdot("ja,jb->ab", p_imag, w_imag)
    h_imag = tdot("ja,jb->ab", p_real, w_imag) - tdot("ja,jb->ab", p_imag, w_real)
    m_real, m_imag = subspace_solve(s_real, h_real, h_imag)

    coefs = tdot("gsj,jc->gcs", owned, weighted)
    c_real, c_imag = coefs[:, :bands], coefs[:, bands:]
    from_beta = jnp.stack(
        [
            jnp.concatenate([c_real, -c_imag], axis=2),
            jnp.concatenate([c_imag, c_real], axis=2),
        ],
        axis=2,
    ).reshape(blocks, 2 * bands, 2 * slots)
    from_psi = jnp.stack(
        [
            jnp.stack([-m_real.T, m_imag.T], axis=-1),
            jnp.stack([-m_imag.T, -m_real.T], axis=-1),
        ],
        axis=1,
    ).reshape(1, 2 * bands, 2 * bands)
    coefs = jnp.concatenate(
        [jnp.broadcast_to(from_psi, (blocks, 2 * bands, 2 * bands)), from_beta], axis=2
    )
    base = pl.pallas_call(
        functools.partial(base_kernel, slots),
        out_shape=jax.ShapeDtypeStruct(orbitals.shape, f32),
        grid=(blocks,),
        in_specs=block_specs
        + [pl.BlockSpec((None, 2 * bands, 2 * bands + 2 * slots), lambda g: (g, 0, 0))],
        out_specs=block_specs[0],
        compiler_params=params,
        cost_estimate=cost(8 * 10**9, 12 * 10**6),
        name="base",
    )(orbitals, beta, kinetic, coefs)

    two_bands = pl.BlockSpec((2, 2, planes, span_y, span_z), lambda j: (j, 0, 0, 0, 0))
    residual = pl.pallas_call(
        to_planes_kernel,
        out_shape=jax.ShapeDtypeStruct(orbitals.shape, f32),
        grid=(pairs,),
        in_specs=[pl.BlockSpec((2, block_rows, span_z), lambda j: (j, 0, 0))] * devices
        + [two_bands, whole(fwd_y.shape)],
        out_specs=two_bands,
        compiler_params=params,
        cost_estimate=cost(8 * 10**9, 12 * 10**6),
        name="to_planes",
    )(*returned, base, fwd_y)
    return (residual, jnp.stack([m_real, m_imag]))


def solution(mesh):
    return jax.shard_map(
        functools.partial(on_device, mesh.shape["ga"]),
        mesh=mesh,
        in_specs=(
            P("rep", None, "ga", None, None),
            P("rep"),
            P("rep", "ga", None),
            P(("rep", "ga"), None, None, None),
            P(("rep", "ga"), None),
            P("rep", None),
        ),
        out_specs=(P("rep", None, "ga", None, None), P(None, "rep", None)),
        check_vma=False,
    )
```

```python
import functools
import math

import jax
import jax.numpy as jnp
import numpy as np
from jax import lax
from jax.experimental import pallas as pl
from jax.experimental.pallas import tpu as pltpu
from jax.sharding import PartitionSpec as P

highest = lax.Precision.HIGHEST
f32 = jnp.float32
bf16 = jnp.bfloat16
vmem_limit = 63 * 1024 * 1024


def signed_index(values, length):
    return jnp.where(values < length // 2, values, values - length)


def dft(length, orient):
    index = np.arange(length)
    angles = (index[:, None] * index[None, :] % length) * (2.0 * math.pi / length)
    factor = 1.0 / math.sqrt(length)
    return np.cos(angles) * factor, orient * np.sin(angles) * factor


def left_table(length, orient):
    cosine, sine = dft(length, orient)
    return np.block([[cosine, -sine], [sine, cosine]])


def right_table(length, orient):
    cosine, sine = dft(length, orient)
    return np.block([[cosine, sine], [-sine, cosine]])


def split(values):
    high = values.astype(bf16)
    low = (values - high.astype(f32)).astype(bf16)
    return high, low


def split_outside(values):
    high = lax.reduce_precision(values, exponent_bits=8, mantissa_bits=7)
    return high.astype(bf16), (values - high).astype(bf16)


def const_parts(table):
    table = np.asarray(table, np.float32)
    high = table.astype(jnp.bfloat16)
    low = (table - high.astype(np.float32)).astype(jnp.bfloat16)
    return high, low


def left_const(table):
    high, low = const_parts(table)
    return jnp.asarray(np.concatenate([high, high, low], axis=1))


def right_const(table):
    high, low = const_parts(table)
    return jnp.asarray(np.concatenate([high, high, low], axis=0))


def dot_left(table, values):
    high, low = split(values)
    return jnp.dot(
        table, jnp.concatenate([high, low, high], axis=0), preferred_element_type=f32
    )


def dot_right(values, table):
    high, low = split(values)
    return jnp.dot(
        jnp.concatenate([high, low, high], axis=1), table, preferred_element_type=f32
    )


def groups(count, width):
    size = max(1, 256 // width)
    return [list(range(i, min(i + size, count))) for i in range(0, count, size)]


def parts_in_lanes(values, span, width):
    items = values.shape[1] // width
    return jnp.concatenate(
        [
            jnp.concatenate(
                [values[:span, i * width : (i + 1) * width], values[span:, i * width : (i + 1) * width]],
                axis=1,
            )
            for i in range(items)
        ],
        axis=0,
    )


def to_rows_kernel(psi, y_table, out):
    _, _, planes, span_y, span_z = psi.shape
    devices, block_rows, _ = out.shape
    each = block_rows // planes
    for group in groups(planes, span_z):
        real = jnp.concatenate([psi[0, 0, p] - psi[1, 1, p] for p in group], axis=1)
        imag = jnp.concatenate([psi[0, 1, p] + psi[1, 0, p] for p in group], axis=1)
        along_y = dot_left(y_table[...], jnp.concatenate([real, imag], axis=0))
        for i, p in enumerate(group):
            out[:, p * each : (p + 1) * each, :] = along_y[
                :, i * span_z : (i + 1) * span_z
            ].reshape(devices, each, span_z)


def real_space_kernel(rows, planes, recv, pot, inverse, forward, inv_z, fwd_z, _, back, field):
    devices, size, span_z = recv.shape
    span_x = devices * planes
    arrived = recv.reshape(devices * size, span_z)
    leaving = back.reshape(devices * 2 * size, span_z)
    columns = [
        jnp.concatenate(
            [
                arrived[pl.ds((p * rows + r) * 2 + part, devices, stride=size), :]
                for part in range(2)
                for p in range(planes)
            ],
            axis=0,
        )
        for r in range(rows)
    ]
    along_x = dot_left(inverse[...], jnp.concatenate(columns, axis=1))
    spatial = dot_right(parts_in_lanes(along_x, span_x, span_z), inv_z[...])
    spectral = []
    for band in range(2):
        one = spatial[:, band * span_z : (band + 1) * span_z]
        field[band] = one
        product = one * pot[...]
        product = jnp.concatenate(
            [product[r * span_x : (r + 1) * span_x] for r in range(rows)], axis=1
        )
        spectral.append(parts_in_lanes(dot_left(forward[...], product), span_x, span_z))
    spectral = dot_right(jnp.concatenate(spectral, axis=0), fwd_z[...])
    for band in range(2):
        for r in range(rows):
            for p in range(planes):
                first = ((band * rows + r) * planes + p) * devices
                for part in range(2):
                    start = band * size + (p * rows + r) * 2 + part
                    leaving[pl.ds(start, devices, stride=2 * size), :] = spectral[
                        first : first + devices, part * span_z : (part + 1) * span_z
                    ]


def real_gram_kernel(bands, *refs):
    fields, (pot, out) = refs[:-2], refs[-2:]
    lines = [(one, i) for one in fields for i in range(one.shape[0])]
    pairs = [(a, b) for a in range(bands) for b in range(a, bands)]
    for weighted in range(2):

        def step(i, sums):
            rows = pl.ds(pl.multiple_of(i * 8, 8), 8)
            values = [one[i, rows, :] for one, i in lines]
            other = [v * pot[rows, :] for v in values] if weighted else values
            result = []
            for (a, b), total in zip(pairs, sums):
                product = values[a] * other[b]
                lanes = product[:, :128]
                for c in range(128, product.shape[1], 128):
                    lanes = lanes + product[:, c : c + 128]
                result.append(total + lanes)
            return tuple(result)

        sums = lax.fori_loop(
            0, pot.shape[0] // 8, step, tuple(jnp.zeros((8, 128), f32) for _ in pairs)
        )
        for (a, b), total in zip(pairs, sums):
            line = jnp.sum(total, axis=0, keepdims=True)
            out[weighted, a, b : b + 1, :] = line
            out[weighted, b, a : a + 1, :] = line


def to_planes_kernel(recv, base, y_table, out):
    bands, _, planes, span_y, span_z = base.shape
    each = recv.shape[2] // planes
    for band in range(bands):
        for group in groups(planes, span_z):
            columns = [
                recv[:, band, p * each : (p + 1) * each, :].reshape(2 * span_y, span_z)
                for p in group
            ]
            along_y = dot_left(y_table[...], jnp.concatenate(columns, axis=1))
            for i, p in enumerate(group):
                for part in range(2):
                    out[band, part, p] = base[band, part, p] + (
                        along_y[part * span_y : (part + 1) * span_y, i * span_z : (i + 1) * span_z]
                    )


def pass_on_kernel(values, _, out):
    out[...] = values[...]


def block_rows_of(psi, beta, slots):
    bands, _, span, span_z = psi.shape
    psi_flat = psi.reshape(bands * 2 * span, span_z)
    psi_rows = [psi_flat[pl.ds(y, 2 * bands, stride=span), :] for y in range(span)]
    beta_rows = [
        jnp.concatenate(
            [beta[pl.ds(2 * y + part, slots, stride=2 * span), :] for part in range(2)], axis=0
        )
        for y in range(span)
    ]
    return psi_rows, beta_rows


def project_kernel(slots, psi, beta, kinetic, out):
    bands, _, span, span_z = psi.shape
    psi_rows, beta_rows = block_rows_of(psi, beta, slots)
    kin_rows = [psi_rows[y] * kinetic[y : y + 1, :] for y in range(span)]
    right = jnp.concatenate(split(jnp.concatenate(psi_rows, axis=1)), axis=0)
    left = jnp.concatenate(
        split(jnp.concatenate(beta_rows, axis=1)) + split(jnp.concatenate(kin_rows, axis=1)), axis=0
    )
    full = lax.dot_general(left, right, (((1,), (1,)), ((), ())), preferred_element_type=f32)
    width, height = 2 * bands, 2 * slots
    full = full[:, :width] + full[:, width:]
    out[0:height] = full[0:height] + full[height : 2 * height]
    rest = full[2 * height :]
    out[height:] = rest[0:width] + rest[width:]


def base_kernel(slots, psi, beta, kinetic, coefs, out):
    bands, _, span, span_z = psi.shape
    psi_rows, beta_rows = block_rows_of(psi, beta, slots)
    values = jnp.concatenate(
        [jnp.concatenate(psi_rows, axis=1), jnp.concatenate(beta_rows, axis=1)], axis=0
    )
    high, low = split(coefs[...])
    summed = dot_left(jnp.concatenate([high, high, low], axis=1), values)
    flat = out.reshape(bands * 2 * span, span_z)
    for y in range(span):
        flat[pl.ds(y, 2 * bands, stride=span), :] = (
            psi_rows[y] * kinetic[y : y + 1, :] + summed[:, y * span_z : (y + 1) * span_z]
        )


def whole(shape):
    return pl.BlockSpec(shape, lambda *_: (0,) * len(shape))


def subspace_solve(s_real, h_real, h_imag):
    factor = jnp.linalg.cholesky(s_real)
    solved = jax.scipy.linalg.cho_solve((factor, True), jnp.concatenate([h_real, h_imag], axis=1))
    order_size = s_real.shape[0]
    return (solved[:, :order_size], solved[:, order_size:])


def tdot(pattern, left, right):
    return jnp.einsum(pattern, left, right, precision=highest, preferred_element_type=jnp.float32)


def partner(values, devices, k):
    return lax.ppermute(values, "ga", [(d, d ^ k) for d in range(devices)])


def sum_over(values, devices, after):
    if devices & (devices - 1) or devices < 4:
        return lax.psum(values, "ga")
    step = devices // 4
    others = [partner(values, devices, k * step) for k in (1, 2, 3)]
    values = (values + others[0]) + (others[1] + others[2])
    held = pl.BlockSpec(memory_space=pltpu.VMEM)
    values = pl.pallas_call(
        pass_on_kernel,
        out_shape=jax.ShapeDtypeStruct(values.shape, f32),
        in_specs=[held, pl.BlockSpec(memory_space=pl.ANY)],
        out_specs=held,
        name="pass_on",
    )(values, after)
    while step > 1:
        step //= 2
        values = values + partner(values, devices, step)
    return values


def on_device(devices, orbitals, plane_order, potential, projectors, slot_owner, strengths):
    bands = orbitals.shape[0]
    planes = orbitals.shape[2]
    span_y = orbitals.shape[3]
    span_z = orbitals.shape[4]
    span_x = plane_order.shape[0]
    blocks, slots = slot_owner.shape
    owners = strengths.shape[0] * strengths.shape[1]
    rows = span_y // devices
    block_rows = 2 * planes * rows
    pairs = bands // 2
    block_span = projectors.shape[3] // span_z
    per_plane = span_y // block_span
    grid_x = jnp.arange(span_x, dtype=jnp.int32)
    grid_y = jnp.arange(span_y, dtype=jnp.int32)
    grid_z = jnp.arange(span_z, dtype=jnp.int32)
    params = pltpu.CompilerParams(vmem_limit_bytes=vmem_limit)

    def cost(flops, moved):
        return pl.CostEstimate(flops=flops, bytes_accessed=moved, transcendentals=0)

    order = np.arange(2 * span_y)
    order = (order % 2) * span_y + order // 2
    inv_y = left_const(left_table(span_y, 1.0)[order])
    fwd_y = left_const(left_table(span_y, -1.0)[:, order])
    inv_z = right_const(right_table(span_z, 1.0))
    fwd_z = right_const(right_table(span_z, -1.0))

    sent = pl.pallas_call(
        to_rows_kernel,
        out_shape=jax.ShapeDtypeStruct((devices, pairs, block_rows, span_z), f32),
        grid=(pairs,),
        in_specs=[
            pl.BlockSpec((2, 2, planes, span_y, span_z), lambda j: (j, 0, 0, 0, 0)),
            whole(inv_y.shape),
        ],
        out_specs=pl.BlockSpec((devices, None, block_rows, span_z), lambda j: (0, j, 0, 0)),
        compiler_params=params,
        cost_estimate=cost(4 * 10**9, 6 * 10**6),
        name="to_rows",
    )(orbitals, inv_y)
    arrived = lax.all_to_all(sent, "ga", split_axis=0, concat_axis=0, tiled=True)

    stored = plane_order.reshape(devices, planes).T.reshape(-1)
    phases = (stored[:, None] * grid_x[None, :]) % span_x
    angles = phases.astype(f32) * (2.0 * math.pi / span_x)
    factor = 1.0 / math.sqrt(span_x)
    cosine, sine = jnp.cos(angles) * factor, jnp.sin(angles) * factor
    fwd_x = jnp.concatenate([cosine, -sine], axis=0)
    inv_x = jnp.concatenate([fwd_x, jnp.concatenate([sine, cosine], axis=0)], axis=1).T
    high, low = split_outside(fwd_x)
    fwd_x = jnp.concatenate([high, high, low], axis=1)
    high, low = split_outside(inv_x)
    inv_x = jnp.concatenate([high, high, low], axis=1)
    pot = potential.transpose(1, 0, 2).reshape(rows * span_x, span_z)

    local_order = lax.dynamic_slice_in_dim(plane_order, lax.axis_index("ga") * planes, planes)
    freq_x = signed_index(local_order, span_x).astype(f32) / span_x
    freq_y = signed_index(grid_y, span_y).astype(f32) / span_y
    freq_z = signed_index(grid_z, span_z).astype(f32) / span_z
    kinetic = 2.0 * (
        freq_x[:, None, None] ** 2 + freq_y[None, :, None] ** 2 + freq_z[None, None, :] ** 2
    )
    beta = projectors.reshape(blocks, slots, 2, block_span, span_z)
    beta = beta.transpose(0, 1, 3, 2, 4).reshape(blocks, slots * block_span * 2, span_z)
    block_specs = [
        pl.BlockSpec(
            (bands, 2, None, block_span, span_z),
            lambda g: (0, 0, g // per_plane, g % per_plane, 0),
        ),
        pl.BlockSpec((None, slots * block_span * 2, span_z), lambda g: (g, 0, 0)),
        pl.BlockSpec((None, block_span, span_z), lambda g: (g // per_plane, g % per_plane, 0)),
    ]
    products = pl.pallas_call(
        functools.partial(project_kernel, slots),
        out_shape=jax.ShapeDtypeStruct((blocks, 2 * slots + 2 * bands, 2 * bands), f32),
        grid=(blocks,),
        in_specs=block_specs,
        out_specs=pl.BlockSpec((None, 2 * slots + 2 * bands, 2 * bands), lambda g: (g, 0, 0)),
        compiler_params=params,
        cost_estimate=cost(8 * 10**9, 8 * 10**6),
        name="project",
    )(orbitals, beta, kinetic)
    with_real = products[:, :slots].reshape(blocks, slots, bands, 2)
    with_imag = products[:, slots : 2 * slots].reshape(blocks, slots, bands, 2)
    proj = jnp.concatenate(
        [
            with_real[..., 0] + with_imag[..., 1],
            with_real[..., 1] - with_imag[..., 0],
        ],
        axis=-1,
    )
    owned = (
        slot_owner[:, :, None] == jnp.arange(owners, dtype=jnp.int32)[None, None, :]
    ).astype(f32)
    proj = tdot("gsj,gsc->jc", owned, proj)
    kin = jnp.sum(products[:, 2 * slots :], axis=0).reshape(bands, 2, bands, 2)
    kin = kin[:, 0, :, 0] + kin[:, 1, :, 1]

    parts = [(0, 1), (1, pairs)] if pairs > 1 else [(0, pairs)]
    returned, fields = [], []
    for first, end in parts:
        share = end - first
        back, field = pl.pallas_call(
            functools.partial(real_space_kernel, rows, planes),
            out_shape=(
                jax.ShapeDtypeStruct((devices, 2 * share, block_rows, span_z), f32),
                jax.ShapeDtypeStruct((2 * share, rows * span_x, span_z), f32),
            ),
            grid=(share,),
            in_specs=[
                pl.BlockSpec(
                    (devices, None, block_rows, span_z), lambda j, first=first: (0, first + j, 0, 0)
                ),
                whole(pot.shape),
                whole(inv_x.shape),
                whole(fwd_x.shape),
                whole(inv_z.shape),
                whole(fwd_z.shape),
                whole(proj.shape),
            ],
            out_specs=(
                pl.BlockSpec((devices, 2, block_rows, span_z), lambda j: (0, j, 0, 0)),
                pl.BlockSpec((2, rows * span_x, span_z), lambda j: (j, 0, 0)),
            ),
            compiler_params=params,
            cost_estimate=cost(4 * 10**9, 8 * 10**6),
            name="real_space",
        )(arrived, pot, inv_x, fwd_x, inv_z, fwd_z, proj)
        returned.append(lax.all_to_all(back, "ga", split_axis=0, concat_axis=0, tiled=True))
        fields.append(field)

    grams = pl.pallas_call(
        functools.partial(real_gram_kernel, bands),
        out_shape=jax.ShapeDtypeStruct((2, bands, bands, 128), f32),
        compiler_params=params,
        cost_estimate=cost(10**7, 2 * 10**6),
        name="real_gram",
    )(*fields, pot)
    grams = jnp.sum(grams, axis=-1)
    own = jnp.concatenate([proj, jnp.concatenate([grams[0], grams[1] + kin], axis=1)], axis=0)
    total = sum_over(own, devices, returned[0])
    proj, s_real, h_real = total[:owners], total[owners:, :bands], total[owners:, bands:]
    weighted = strengths.reshape(-1)[:, None] * proj
    p_real, p_imag = proj[:, :bands], proj[:, bands:]
    w_real, w_imag = weighted[:, :bands], weighted[:, bands:]
    h_real = h_real + tdot("ja,jb->ab", p_real, w_real) + tdot("ja,jb->ab", p_imag, w_imag)
    h_imag = tdot("ja,jb->ab", p_real, w_imag) - tdot("ja,jb->ab", p_imag, w_real)
    m_real, m_imag = subspace_solve(s_real, h_real, h_imag)

    coefs = tdot("gsj,jc->gcs", owned, weighted)
    c_real, c_imag = coefs[:, :bands], coefs[:, bands:]
    from_beta = jnp.stack(
        [
            jnp.concatenate([c_real, -c_imag], axis=2),
            jnp.concatenate([c_imag, c_real], axis=2),
        ],
        axis=2,
    ).reshape(blocks, 2 * bands, 2 * slots)
    from_psi = jnp.stack(
        [
            jnp.stack([-m_real.T, m_imag.T], axis=-1),
            jnp.stack([-m_imag.T, -m_real.T], axis=-1),
        ],
        axis=1,
    ).reshape(1, 2 * bands, 2 * bands)
    coefs = jnp.concatenate(
        [jnp.broadcast_to(from_psi, (blocks, 2 * bands, 2 * bands)), from_beta], axis=2
    )
    base = pl.pallas_call(
        functools.partial(base_kernel, slots),
        out_shape=jax.ShapeDtypeStruct(orbitals.shape, f32),
        grid=(blocks,),
        in_specs=block_specs
        + [pl.BlockSpec((None, 2 * bands, 2 * bands + 2 * slots), lambda g: (g, 0, 0))],
        out_specs=block_specs[0],
        compiler_params=params,
        cost_estimate=cost(8 * 10**9, 12 * 10**6),
        name="base",
    )(orbitals, beta, kinetic, coefs)

    residual = base
    for (first, end), one_return in zip(parts, returned):
        two_bands = pl.BlockSpec(
            (2, 2, planes, span_y, span_z), lambda j, first=first: (first + j, 0, 0, 0, 0)
        )
        residual = pl.pallas_call(
            to_planes_kernel,
            out_shape=jax.ShapeDtypeStruct(orbitals.shape, f32),
            grid=(end - first,),
            in_specs=[
                pl.BlockSpec((devices, 2, block_rows, span_z), lambda j: (0, j, 0, 0)),
                two_bands,
                whole(fwd_y.shape),
            ],
            out_specs=two_bands,
            input_output_aliases={1: 0},
            compiler_params=params,
            cost_estimate=cost(8 * 10**9, 12 * 10**6),
            name="to_planes",
        )(one_return, residual, fwd_y)
    return (residual, jnp.stack([m_real, m_imag]))


def solution(mesh):
    return jax.shard_map(
        functools.partial(on_device, mesh.shape["ga"]),
        mesh=mesh,
        in_specs=(
            P("rep", None, "ga", None, None),
            P("rep"),
            P("rep", "ga", None),
            P(("rep", "ga"), None, None, None),
            P(("rep", "ga"), None),
            P("rep", None),
        ),
        out_specs=(P("rep", None, "ga", None, None), P(None, "rep", None)),
        check_vma=False,
    )
```

```python
import functools
import math

import jax
import jax.numpy as jnp
import numpy as np
from jax import lax
from jax.experimental import pallas as pl
from jax.experimental.pallas import tpu as pltpu
from jax.sharding import PartitionSpec as P

highest = lax.Precision.HIGHEST
f32 = jnp.float32
bf16 = jnp.bfloat16
vmem_limit = 63 * 1024 * 1024


def signed_index(values, length):
    return jnp.where(values < length // 2, values, values - length)


def dft(length, orient):
    index = np.arange(length)
    angles = (index[:, None] * index[None, :] % length) * (2.0 * math.pi / length)
    factor = 1.0 / math.sqrt(length)
    return np.cos(angles) * factor, orient * np.sin(angles) * factor


def left_table(length, orient):
    cosine, sine = dft(length, orient)
    return np.block([[cosine, -sine], [sine, cosine]])


def right_table(length, orient):
    cosine, sine = dft(length, orient)
    return np.block([[cosine, sine], [-sine, cosine]])


def split(values):
    high = values.astype(bf16)
    low = (values - high.astype(f32)).astype(bf16)
    return high, low


def split_outside(values):
    high = lax.reduce_precision(values, exponent_bits=8, mantissa_bits=7)
    return high.astype(bf16), (values - high).astype(bf16)


def const_parts(table):
    table = np.asarray(table, np.float32)
    high = table.astype(jnp.bfloat16)
    low = (table - high.astype(np.float32)).astype(jnp.bfloat16)
    return high, low


def left_const(table):
    high, low = const_parts(table)
    return jnp.asarray(np.concatenate([high, high, low], axis=1))


def right_const(table):
    high, low = const_parts(table)
    return jnp.asarray(np.concatenate([high, high, low], axis=0))


def dot_left(table, values):
    high, low = split(values)
    return jnp.dot(
        table, jnp.concatenate([high, low, high], axis=0), preferred_element_type=f32
    )


def dot_right(values, table):
    high, low = split(values)
    return jnp.dot(
        jnp.concatenate([high, low, high], axis=1), table, preferred_element_type=f32
    )


def groups(count, width):
    size = max(1, 256 // width)
    return [list(range(i, min(i + size, count))) for i in range(0, count, size)]


def parts_in_lanes(values, span, width):
    items = values.shape[1] // width
    return jnp.concatenate(
        [
            jnp.concatenate(
                [values[:span, i * width : (i + 1) * width], values[span:, i * width : (i + 1) * width]],
                axis=1,
            )
            for i in range(items)
        ],
        axis=0,
    )


def to_rows_kernel(psi, y_table, out):
    _, _, planes, span_y, span_z = psi.shape
    devices, block_rows, _ = out.shape
    each = block_rows // planes
    for group in groups(planes, span_z):
        real = jnp.concatenate([psi[0, 0, p] - psi[1, 1, p] for p in group], axis=1)
        imag = jnp.concatenate([psi[0, 1, p] + psi[1, 0, p] for p in group], axis=1)
        along_y = dot_left(y_table[...], jnp.concatenate([real, imag], axis=0))
        for i, p in enumerate(group):
            out[:, p * each : (p + 1) * each, :] = along_y[
                :, i * span_z : (i + 1) * span_z
            ].reshape(devices, each, span_z)


def to_rows_split_kernel(my_layer, psi, y_table, *rest):
    outs, staged = rest[:-1], rest[-1]
    to_rows_kernel(psi, y_table, staged)
    each = staged.shape[0] // len(outs)
    for k, out in enumerate(outs):
        out[...] = staged[pl.ds((my_layer[0] ^ k) * each, each)]


def regroup_kernel(layers, my_member, *refs):
    arrived, outs = refs[:layers], refs[layers + 1 : -1]
    for k, out in enumerate(outs):
        for layer in range(layers):
            out[layer] = arrived[layer][my_member[0] ^ k]


def real_space_parts_kernel(rows, planes, members, *refs):
    arrived, rest, staged = refs[:members], refs[members:-1], refs[-1]
    each = staged.shape[0] // members
    for k in range(members):
        staged[k * each : (k + 1) * each] = arrived[k][...]
    real_space_kernel(rows, planes, staged, *rest)


def real_space_kernel(rows, planes, recv, pot, inverse, forward, inv_z, fwd_z, _, back, field):
    devices, size, span_z = recv.shape
    span_x = devices * planes
    arrived = recv.reshape(devices * size, span_z)
    leaving = back.reshape(devices * 2 * size, span_z)
    columns = [
        jnp.concatenate(
            [
                arrived[pl.ds((p * rows + r) * 2 + part, devices, stride=size), :]
                for part in range(2)
                for p in range(planes)
            ],
            axis=0,
        )
        for r in range(rows)
    ]
    along_x = dot_left(inverse[...], jnp.concatenate(columns, axis=1))
    spatial = dot_right(parts_in_lanes(along_x, span_x, span_z), inv_z[...])
    spectral = []
    for band in range(2):
        one = spatial[:, band * span_z : (band + 1) * span_z]
        field[band] = one
        product = one * pot[...]
        product = jnp.concatenate(
            [product[r * span_x : (r + 1) * span_x] for r in range(rows)], axis=1
        )
        spectral.append(parts_in_lanes(dot_left(forward[...], product), span_x, span_z))
    spectral = dot_right(jnp.concatenate(spectral, axis=0), fwd_z[...])
    for band in range(2):
        for r in range(rows):
            for p in range(planes):
                first = ((band * rows + r) * planes + p) * devices
                for part in range(2):
                    start = band * size + (p * rows + r) * 2 + part
                    leaving[pl.ds(start, devices, stride=2 * size), :] = spectral[
                        first : first + devices, part * span_z : (part + 1) * span_z
                    ]


def real_gram_kernel(bands, *refs):
    fields, (pot, out) = refs[:-2], refs[-2:]
    held = fields[0].shape[0]
    pairs = [(a, b) for a in range(bands) for b in range(a, bands)]
    for weighted in range(2):

        def step(i, sums):
            rows = pl.ds(pl.multiple_of(i * 8, 8), 8)
            values = [fields[a // held][a % held, rows, :] for a in range(bands)]
            other = [v * pot[rows, :] for v in values] if weighted else values
            result = []
            for (a, b), total in zip(pairs, sums):
                product = values[a] * other[b]
                lanes = product[:, :128]
                for c in range(128, product.shape[1], 128):
                    lanes = lanes + product[:, c : c + 128]
                result.append(total + lanes)
            return tuple(result)

        sums = lax.fori_loop(
            0, pot.shape[0] // 8, step, tuple(jnp.zeros((8, 128), f32) for _ in pairs)
        )
        for (a, b), total in zip(pairs, sums):
            line = jnp.sum(total, axis=0, keepdims=True)
            out[weighted, a, b : b + 1, :] = line
            out[weighted, b, a : a + 1, :] = line


def to_planes_kernel(recv, base, y_table, out):
    bands, _, planes, span_y, span_z = base.shape
    each = recv.shape[2] // planes
    for band in range(bands):
        for group in groups(planes, span_z):
            columns = [
                recv[:, band, p * each : (p + 1) * each, :].reshape(2 * span_y, span_z)
                for p in group
            ]
            along_y = dot_left(y_table[...], jnp.concatenate(columns, axis=1))
            for i, p in enumerate(group):
                for part in range(2):
                    out[band, part, p] = base[band, part, p] + (
                        along_y[part * span_y : (part + 1) * span_y, i * span_z : (i + 1) * span_z]
                    )


def last_sum_kernel(*refs):
    first, second, third, fourth, _, out = refs
    out[...] = (first[...] + second[...]) + (third[...] + fourth[...])


def block_rows_of(psi, beta, slots):
    bands, _, span, span_z = psi.shape
    psi_flat = psi.reshape(bands * 2 * span, span_z)
    psi_rows = [psi_flat[pl.ds(y, 2 * bands, stride=span), :] for y in range(span)]
    beta_rows = [
        jnp.concatenate(
            [beta[pl.ds(2 * y + part, slots, stride=2 * span), :] for part in range(2)], axis=0
        )
        for y in range(span)
    ]
    return psi_rows, beta_rows


def project_kernel(slots, psi, beta, kinetic, out):
    bands, _, span, span_z = psi.shape
    psi_rows, beta_rows = block_rows_of(psi, beta, slots)
    kin_rows = [psi_rows[y] * kinetic[y : y + 1, :] for y in range(span)]
    right = jnp.concatenate(split(jnp.concatenate(psi_rows, axis=1)), axis=0)
    left = jnp.concatenate(
        split(jnp.concatenate(beta_rows, axis=1)) + split(jnp.concatenate(kin_rows, axis=1)), axis=0
    )
    full = lax.dot_general(left, right, (((1,), (1,)), ((), ())), preferred_element_type=f32)
    width, height = 2 * bands, 2 * slots
    full = full[:, :width] + full[:, width:]
    out[0:height] = full[0:height] + full[height : 2 * height]
    rest = full[2 * height :]
    out[height:] = rest[0:width] + rest[width:]


def base_kernel(slots, psi, beta, kinetic, coefs, out):
    bands, _, span, span_z = psi.shape
    psi_rows, beta_rows = block_rows_of(psi, beta, slots)
    values = jnp.concatenate(
        [jnp.concatenate(psi_rows, axis=1), jnp.concatenate(beta_rows, axis=1)], axis=0
    )
    high, low = split(coefs[...])
    summed = dot_left(jnp.concatenate([high, high, low], axis=1), values)
    flat = out.reshape(bands * 2 * span, span_z)
    for y in range(span):
        flat[pl.ds(y, 2 * bands, stride=span), :] = (
            psi_rows[y] * kinetic[y : y + 1, :] + summed[:, y * span_z : (y + 1) * span_z]
        )


def whole(shape):
    return pl.BlockSpec(shape, lambda *_: (0,) * len(shape))


def subspace_solve(s_real, h_real, h_imag):
    factor = jnp.linalg.cholesky(s_real)
    solved = jax.scipy.linalg.cho_solve((factor, True), jnp.concatenate([h_real, h_imag], axis=1))
    order_size = s_real.shape[0]
    return (solved[:, :order_size], solved[:, order_size:])


def tdot(pattern, left, right):
    return jnp.einsum(pattern, left, right, precision=highest, preferred_element_type=jnp.float32)


def partner(values, devices, k):
    return lax.ppermute(values, "ga", [(d, d ^ k) for d in range(devices)])


def sum_over(values, devices, after):
    if devices & (devices - 1) or devices < 4:
        return lax.psum(values, "ga")
    step = 1
    while step < devices // 4:
        values = values + partner(values, devices, step)
        step *= 2
    others = [partner(values, devices, k * step) for k in (1, 2, 3)]
    held = pl.BlockSpec(memory_space=pltpu.VMEM)
    return pl.pallas_call(
        last_sum_kernel,
        out_shape=jax.ShapeDtypeStruct(values.shape, f32),
        in_specs=[held] * 4 + [pl.BlockSpec(memory_space=pl.ANY)],
        out_specs=held,
        name="last_sum",
    )(values, *others, after)


def on_device(devices, orbitals, plane_order, potential, projectors, slot_owner, strengths):
    bands = orbitals.shape[0]
    planes = orbitals.shape[2]
    span_y = orbitals.shape[3]
    span_z = orbitals.shape[4]
    span_x = plane_order.shape[0]
    blocks, slots = slot_owner.shape
    owners = strengths.shape[0] * strengths.shape[1]
    rows = span_y // devices
    block_rows = 2 * planes * rows
    pairs = bands // 2
    block_span = projectors.shape[3] // span_z
    per_plane = span_y // block_span
    grid_x = jnp.arange(span_x, dtype=jnp.int32)
    grid_y = jnp.arange(span_y, dtype=jnp.int32)
    grid_z = jnp.arange(span_z, dtype=jnp.int32)
    params = pltpu.CompilerParams(vmem_limit_bytes=vmem_limit)

    def cost(flops, moved):
        return pl.CostEstimate(flops=flops, bytes_accessed=moved, transcendentals=0)

    order = np.arange(2 * span_y)
    order = (order % 2) * span_y + order // 2
    inv_y = left_const(left_table(span_y, 1.0)[order])
    fwd_y = left_const(left_table(span_y, -1.0)[:, order])
    inv_z = right_const(right_table(span_z, 1.0))
    fwd_z = right_const(right_table(span_z, -1.0))

    parts = 2 if pairs % 2 == 0 else 1
    share = pairs // parts
    mine = lax.axis_index("ga").astype(jnp.int32)
    layers = 4 if parts == 2 and devices >= 8 and devices & (devices - 1) == 0 else 1
    members = devices // layers
    my_layer, my_member = (mine // members).reshape(1), (mine % members).reshape(1)
    scalar = pl.BlockSpec(memory_space=pltpu.SMEM)

    def to_rows(c, split):
        spec = pl.BlockSpec((devices, None, block_rows, span_z), lambda j: (0, j, 0, 0))
        shape = jax.ShapeDtypeStruct((devices, share, block_rows, span_z), f32)
        if split:
            spec = pl.BlockSpec((members, None, block_rows, span_z), lambda j: (0, j, 0, 0))
            shape = jax.ShapeDtypeStruct((members, share, block_rows, span_z), f32)
        return pl.pallas_call(
            to_rows_split_kernel if split else to_rows_kernel,
            out_shape=[shape] * layers if split else shape,
            grid=(share,),
            in_specs=([scalar] if split else [])
            + [
                pl.BlockSpec((2, 2, planes, span_y, span_z), lambda j: (c * share + j, 0, 0, 0, 0)),
                whole(inv_y.shape),
            ],
            out_specs=[spec] * layers if split else spec,
            scratch_shapes=[pltpu.VMEM((devices, block_rows, span_z), f32)] if split else [],
            compiler_params=params,
            cost_estimate=cost(4 * 10**9, 3 * 10**6),
            name="to_rows",
        )(*([my_layer] if split else []), orbitals, inv_y)

    sent = [to_rows(c, c == 0 and layers > 1) for c in range(parts)]
    arrived = []
    if layers > 1:
        crossed = [sent[0][0]] + [
            partner(sent[0][k], devices, k * members) for k in range(1, layers)
        ]
        *regrouped, sent[1] = pl.pallas_call(
            functools.partial(regroup_kernel, layers),
            out_shape=[jax.ShapeDtypeStruct((layers, share, block_rows, span_z), f32)] * members
            + [jax.ShapeDtypeStruct(sent[1].shape, f32)],
            in_specs=[scalar]
            + [pl.BlockSpec(memory_space=pltpu.VMEM)] * layers
            + [pl.BlockSpec(memory_space=pl.ANY)],
            out_specs=[pl.BlockSpec(memory_space=pltpu.VMEM)] * members
            + [pl.BlockSpec(memory_space=pl.ANY)],
            input_output_aliases={1 + layers: members},
            compiler_params=params,
            cost_estimate=cost(0, 2 * 10**6),
            name="regroup",
        )(my_member, *crossed, sent[1])
        arrived.append(
            [regrouped[0]] + [partner(regrouped[k], devices, k) for k in range(1, members)]
        )
        sent = sent[1:]
    for one in sent:
        arrived.append([lax.all_to_all(one, "ga", split_axis=0, concat_axis=0, tiled=True)])

    def tables_x(owned):
        phases = (owned.T.reshape(-1)[:, None] * grid_x[None, :]) % span_x
        angles = phases.astype(f32) * (2.0 * math.pi / span_x)
        factor = 1.0 / math.sqrt(span_x)
        cosine, sine = jnp.cos(angles) * factor, jnp.sin(angles) * factor
        forward = jnp.concatenate([cosine, -sine], axis=0)
        inverse = jnp.concatenate([forward, jnp.concatenate([sine, cosine], axis=0)], axis=1).T
        tables = []
        for table in (forward, inverse):
            high, low = split_outside(table)
            tables.append(jnp.concatenate([high, high, low], axis=1))
        return tables

    owned = plane_order.reshape(devices, planes)
    fwd_x, inv_x = tables_x(owned)
    steps = np.arange(layers)[None, :] * members + np.arange(members)[:, None]
    _, inv_x_steps = tables_x(
        jnp.take(owned, mine ^ jnp.asarray(steps.reshape(-1), jnp.int32), axis=0)
    )
    pot = potential.transpose(1, 0, 2).reshape(rows * span_x, span_z)

    local_order = lax.dynamic_slice_in_dim(plane_order, lax.axis_index("ga") * planes, planes)
    freq_x = signed_index(local_order, span_x).astype(f32) / span_x
    freq_y = signed_index(grid_y, span_y).astype(f32) / span_y
    freq_z = signed_index(grid_z, span_z).astype(f32) / span_z
    kinetic = 2.0 * (
        freq_x[:, None, None] ** 2 + freq_y[None, :, None] ** 2 + freq_z[None, None, :] ** 2
    )
    beta = projectors.reshape(blocks, slots, 2, block_span, span_z)
    beta = beta.transpose(0, 1, 3, 2, 4).reshape(blocks, slots * block_span * 2, span_z)
    block_specs = [
        pl.BlockSpec(
            (bands, 2, None, block_span, span_z),
            lambda g: (0, 0, g // per_plane, g % per_plane, 0),
        ),
        pl.BlockSpec((None, slots * block_span * 2, span_z), lambda g: (g, 0, 0)),
        pl.BlockSpec((None, block_span, span_z), lambda g: (g // per_plane, g % per_plane, 0)),
    ]
    products = pl.pallas_call(
        functools.partial(project_kernel, slots),
        out_shape=jax.ShapeDtypeStruct((blocks, 2 * slots + 2 * bands, 2 * bands), f32),
        grid=(blocks,),
        in_specs=block_specs,
        out_specs=pl.BlockSpec((None, 2 * slots + 2 * bands, 2 * bands), lambda g: (g, 0, 0)),
        compiler_params=params,
        cost_estimate=cost(8 * 10**9, 8 * 10**6),
        name="project",
    )(orbitals, beta, kinetic)
    with_real = products[:, :slots].reshape(blocks, slots, bands, 2)
    with_imag = products[:, slots : 2 * slots].reshape(blocks, slots, bands, 2)
    proj = jnp.concatenate(
        [
            with_real[..., 0] + with_imag[..., 1],
            with_real[..., 1] - with_imag[..., 0],
        ],
        axis=-1,
    )
    chosen = (
        slot_owner[:, :, None] == jnp.arange(owners, dtype=jnp.int32)[None, None, :]
    ).astype(f32)
    proj = tdot("gsj,gsc->jc", chosen, proj)
    kin = jnp.sum(products[:, 2 * slots :], axis=0).reshape(bands, 2, bands, 2)
    kin = kin[:, 0, :, 0] + kin[:, 1, :, 1]

    returned, fields = [], []
    before = proj
    for operands in arrived:
        steps = len(operands) > 1
        held = devices // len(operands)
        kernel = functools.partial(real_space_kernel, rows, planes)
        if steps:
            kernel = functools.partial(real_space_parts_kernel, rows, planes, members)
        back, field = pl.pallas_call(
            kernel,
            out_shape=(
                jax.ShapeDtypeStruct((devices, 2 * share, block_rows, span_z), f32),
                jax.ShapeDtypeStruct((2 * share, rows * span_x, span_z), f32),
            ),
            grid=(share,),
            in_specs=[pl.BlockSpec((held, None, block_rows, span_z), lambda j: (0, j, 0, 0))]
            * len(operands)
            + [
                whole(pot.shape),
                whole(inv_x.shape),
                whole(fwd_x.shape),
                whole(inv_z.shape),
                whole(fwd_z.shape),
                pl.BlockSpec(memory_space=pl.ANY),
            ],
            out_specs=(
                pl.BlockSpec((devices, 2, block_rows, span_z), lambda j: (0, j, 0, 0)),
                pl.BlockSpec((2, rows * span_x, span_z), lambda j: (j, 0, 0)),
            ),
            scratch_shapes=[pltpu.VMEM((devices, block_rows, span_z), f32)] if steps else [],
            compiler_params=params,
            cost_estimate=cost(4 * 10**9, 8 * 10**6),
            name="real_space",
        )(*operands, pot, inv_x_steps if steps else inv_x, fwd_x, inv_z, fwd_z, before)
        before = back
        returned.append(lax.all_to_all(back, "ga", split_axis=0, concat_axis=0, tiled=True))
        fields.append(field)

    grams = pl.pallas_call(
        functools.partial(real_gram_kernel, bands),
        out_shape=jax.ShapeDtypeStruct((2, bands, bands, 128), f32),
        compiler_params=params,
        cost_estimate=cost(10**7, 2 * 10**6),
        name="real_gram",
    )(*fields, pot)
    grams = jnp.sum(grams, axis=-1)
    own = jnp.concatenate([proj, jnp.concatenate([grams[0], grams[1] + kin], axis=1)], axis=0)
    total = sum_over(own, devices, returned[0])
    proj, s_real, h_real = total[:owners], total[owners:, :bands], total[owners:, bands:]
    weighted = strengths.reshape(-1)[:, None] * proj
    p_real, p_imag = proj[:, :bands], proj[:, bands:]
    w_real, w_imag = weighted[:, :bands], weighted[:, bands:]
    h_real = h_real + tdot("ja,jb->ab", p_real, w_real) + tdot("ja,jb->ab", p_imag, w_imag)
    h_imag = tdot("ja,jb->ab", p_real, w_imag) - tdot("ja,jb->ab", p_imag, w_real)
    m_real, m_imag = subspace_solve(s_real, h_real, h_imag)

    coefs = tdot("gsj,jc->gcs", chosen, weighted)
    c_real, c_imag = coefs[:, :bands], coefs[:, bands:]
    from_beta = jnp.stack(
        [
            jnp.concatenate([c_real, -c_imag], axis=2),
            jnp.concatenate([c_imag, c_real], axis=2),
        ],
        axis=2,
    ).reshape(blocks, 2 * bands, 2 * slots)
    from_psi = jnp.stack(
        [
            jnp.stack([-m_real.T, m_imag.T], axis=-1),
            jnp.stack([-m_imag.T, -m_real.T], axis=-1),
        ],
        axis=1,
    ).reshape(1, 2 * bands, 2 * bands)
    coefs = jnp.concatenate(
        [jnp.broadcast_to(from_psi, (blocks, 2 * bands, 2 * bands)), from_beta], axis=2
    )
    base = pl.pallas_call(
        functools.partial(base_kernel, slots),
        out_shape=jax.ShapeDtypeStruct(orbitals.shape, f32),
        grid=(blocks,),
        in_specs=block_specs
        + [pl.BlockSpec((None, 2 * bands, 2 * bands + 2 * slots), lambda g: (g, 0, 0))],
        out_specs=block_specs[0],
        compiler_params=params,
        cost_estimate=cost(8 * 10**9, 12 * 10**6),
        name="base",
    )(orbitals, beta, kinetic, coefs)

    residual = base
    for c in range(parts):
        two_bands = pl.BlockSpec(
            (2, 2, planes, span_y, span_z), lambda j, c=c: (share * c + j, 0, 0, 0, 0)
        )
        residual = pl.pallas_call(
            to_planes_kernel,
            out_shape=jax.ShapeDtypeStruct(orbitals.shape, f32),
            grid=(share,),
            in_specs=[
                pl.BlockSpec((devices, 2, block_rows, span_z), lambda j: (0, j, 0, 0)),
                two_bands,
                whole(fwd_y.shape),
            ],
            out_specs=two_bands,
            input_output_aliases={1: 0},
            compiler_params=params,
            cost_estimate=cost(8 * 10**9, 12 * 10**6),
            name="to_planes",
        )(returned[c], residual, fwd_y)
    return (residual, jnp.stack([m_real, m_imag]))


def solution(mesh):
    return jax.shard_map(
        functools.partial(on_device, mesh.shape["ga"]),
        mesh=mesh,
        in_specs=(
            P("rep", None, "ga", None, None),
            P("rep"),
            P("rep", "ga", None),
            P(("rep", "ga"), None, None, None),
            P(("rep", "ga"), None),
            P("rep", None),
        ),
        out_specs=(P("rep", None, "ga", None, None), P(None, "rep", None)),
        check_vma=False,
    )
```

```python
import functools
import math

import jax
import jax.numpy as jnp
import numpy as np
from jax import lax
from jax.experimental import pallas as pl
from jax.experimental.pallas import tpu as pltpu
from jax.sharding import PartitionSpec as P

highest = lax.Precision.HIGHEST
f32 = jnp.float32
bf16 = jnp.bfloat16
vmem_limit = 63 * 1024 * 1024


def signed_index(values, length):
    return jnp.where(values < length // 2, values, values - length)


def dft(length, orient):
    index = np.arange(length)
    angles = (index[:, None] * index[None, :] % length) * (2.0 * math.pi / length)
    factor = 1.0 / math.sqrt(length)
    return np.cos(angles) * factor, orient * np.sin(angles) * factor


def left_table(length, orient):
    cosine, sine = dft(length, orient)
    return np.block([[cosine, -sine], [sine, cosine]])


def right_table(length, orient):
    cosine, sine = dft(length, orient)
    return np.block([[cosine, sine], [-sine, cosine]])


def split(values):
    high = values.astype(bf16)
    low = (values - high.astype(f32)).astype(bf16)
    return high, low


def split_outside(values):
    high = lax.reduce_precision(values, exponent_bits=8, mantissa_bits=7)
    return high.astype(bf16), (values - high).astype(bf16)


def const_parts(table):
    table = np.asarray(table, np.float32)
    high = table.astype(jnp.bfloat16)
    low = (table - high.astype(np.float32)).astype(jnp.bfloat16)
    return high, low


def left_const(table):
    high, low = const_parts(table)
    return jnp.asarray(np.concatenate([high, high, low], axis=1))


def right_const(table):
    high, low = const_parts(table)
    return jnp.asarray(np.concatenate([high, high, low], axis=0))


def dot_left(table, values):
    high, low = split(values)
    return jnp.dot(
        table, jnp.concatenate([high, low, high], axis=0), preferred_element_type=f32
    )


def dot_right(values, table):
    high, low = split(values)
    return jnp.dot(
        jnp.concatenate([high, low, high], axis=1), table, preferred_element_type=f32
    )


def groups(count, width):
    size = max(1, 256 // width)
    return [list(range(i, min(i + size, count))) for i in range(0, count, size)]


def parts_in_lanes(values, span, width):
    items = values.shape[1] // width
    return jnp.concatenate(
        [
            jnp.concatenate(
                [values[:span, i * width : (i + 1) * width], values[span:, i * width : (i + 1) * width]],
                axis=1,
            )
            for i in range(items)
        ],
        axis=0,
    )


def to_rows_kernel(psi, y_table, out):
    _, _, planes, span_y, span_z = psi.shape
    devices, block_rows, _ = out.shape
    each = block_rows // planes
    for group in groups(planes, span_z):
        real = jnp.concatenate([psi[0, 0, p] - psi[1, 1, p] for p in group], axis=1)
        imag = jnp.concatenate([psi[0, 1, p] + psi[1, 0, p] for p in group], axis=1)
        along_y = dot_left(y_table[...], jnp.concatenate([real, imag], axis=0))
        for i, p in enumerate(group):
            out[:, p * each : (p + 1) * each, :] = along_y[
                :, i * span_z : (i + 1) * span_z
            ].reshape(devices, each, span_z)


def to_rows_split_kernel(my_layer, psi, y_table, *rest):
    outs, staged = rest[:-1], rest[-1]
    to_rows_kernel(psi, y_table, staged)
    each = staged.shape[0] // len(outs)
    for k, out in enumerate(outs):
        out[...] = staged[pl.ds((my_layer[0] ^ k) * each, each)]


def regroup_kernel(layers, members, my_member, *refs):
    passed = (len(refs) - layers - members) // 2
    arrived, outs = refs[:layers], refs[layers + passed : layers + passed + members]
    for k, out in enumerate(outs):
        for layer in range(layers):
            out[layer] = arrived[layer][my_member[0] ^ k]


def real_space_parts_kernel(rows, planes, members, *refs):
    arrived, rest, staged = refs[:members], refs[members:-1], refs[-1]
    each = staged.shape[0] // members
    for k in range(members):
        staged[k * each : (k + 1) * each] = arrived[k][...]
    real_space_kernel(rows, planes, staged, *rest)


def real_space_kernel(rows, planes, recv, pot, inverse, forward, inv_z, fwd_z, *refs):
    back, field = refs[-2:]
    devices, size, span_z = recv.shape
    span_x = devices * planes
    arrived = recv.reshape(devices * size, span_z)
    leaving = back.reshape(devices * 2 * size, span_z)
    columns = [
        jnp.concatenate(
            [
                arrived[pl.ds((p * rows + r) * 2 + part, devices, stride=size), :]
                for part in range(2)
                for p in range(planes)
            ],
            axis=0,
        )
        for r in range(rows)
    ]
    along_x = dot_left(inverse[...], jnp.concatenate(columns, axis=1))
    spatial = dot_right(parts_in_lanes(along_x, span_x, span_z), inv_z[...])
    spectral = []
    for band in range(2):
        one = spatial[:, band * span_z : (band + 1) * span_z]
        field[band] = one
        product = one * pot[...]
        product = jnp.concatenate(
            [product[r * span_x : (r + 1) * span_x] for r in range(rows)], axis=1
        )
        spectral.append(parts_in_lanes(dot_left(forward[...], product), span_x, span_z))
    spectral = dot_right(jnp.concatenate(spectral, axis=0), fwd_z[...])
    for band in range(2):
        for r in range(rows):
            for p in range(planes):
                first = ((band * rows + r) * planes + p) * devices
                for part in range(2):
                    start = band * size + (p * rows + r) * 2 + part
                    leaving[pl.ds(start, devices, stride=2 * size), :] = spectral[
                        first : first + devices, part * span_z : (part + 1) * span_z
                    ]


def real_gram_kernel(bands, *refs):
    fields, (pot, out) = refs[:-2], refs[-2:]
    held = fields[0].shape[0]
    pairs = [(a, b) for a in range(bands) for b in range(a, bands)]
    for weighted in range(2):

        def step(i, sums):
            rows = pl.ds(pl.multiple_of(i * 8, 8), 8)
            values = [fields[a // held][a % held, rows, :] for a in range(bands)]
            other = [v * pot[rows, :] for v in values] if weighted else values
            result = []
            for (a, b), total in zip(pairs, sums):
                product = values[a] * other[b]
                lanes = product[:, :128]
                for c in range(128, product.shape[1], 128):
                    lanes = lanes + product[:, c : c + 128]
                result.append(total + lanes)
            return tuple(result)

        sums = lax.fori_loop(
            0, pot.shape[0] // 8, step, tuple(jnp.zeros((8, 128), f32) for _ in pairs)
        )
        for (a, b), total in zip(pairs, sums):
            line = jnp.sum(total, axis=0, keepdims=True)
            out[weighted, a, b : b + 1, :] = line
            out[weighted, b, a : a + 1, :] = line


def to_planes_kernel(recv, base, y_table, out):
    bands, _, planes, span_y, span_z = base.shape
    each = recv.shape[2] // planes
    for band in range(bands):
        for group in groups(planes, span_z):
            columns = [
                recv[:, band, p * each : (p + 1) * each, :].reshape(2 * span_y, span_z)
                for p in group
            ]
            along_y = dot_left(y_table[...], jnp.concatenate(columns, axis=1))
            for i, p in enumerate(group):
                for part in range(2):
                    out[band, part, p] = base[band, part, p] + (
                        along_y[part * span_y : (part + 1) * span_y, i * span_z : (i + 1) * span_z]
                    )


def last_sum_kernel(*refs):
    first, second, third, fourth, _, out = refs
    out[...] = (first[...] + second[...]) + (third[...] + fourth[...])


def block_rows_of(psi, beta, slots):
    bands, _, span, span_z = psi.shape
    psi_flat = psi.reshape(bands * 2 * span, span_z)
    psi_rows = [psi_flat[pl.ds(y, 2 * bands, stride=span), :] for y in range(span)]
    beta_rows = [
        jnp.concatenate(
            [beta[pl.ds(2 * y + part, slots, stride=2 * span), :] for part in range(2)], axis=0
        )
        for y in range(span)
    ]
    return psi_rows, beta_rows


def project_kernel(slots, psi, beta, kinetic, out):
    bands, _, span, span_z = psi.shape
    psi_rows, beta_rows = block_rows_of(psi, beta, slots)
    kin_rows = [psi_rows[y] * kinetic[y : y + 1, :] for y in range(span)]
    right = jnp.concatenate(split(jnp.concatenate(psi_rows, axis=1)), axis=0)
    left = jnp.concatenate(
        split(jnp.concatenate(beta_rows, axis=1)) + split(jnp.concatenate(kin_rows, axis=1)), axis=0
    )
    full = lax.dot_general(left, right, (((1,), (1,)), ((), ())), preferred_element_type=f32)
    width, height = 2 * bands, 2 * slots
    full = full[:, :width] + full[:, width:]
    out[0:height] = full[0:height] + full[height : 2 * height]
    rest = full[2 * height :]
    out[height:] = rest[0:width] + rest[width:]


def base_kernel(slots, psi, beta, kinetic, coefs, out):
    bands, _, span, span_z = psi.shape
    psi_rows, beta_rows = block_rows_of(psi, beta, slots)
    values = jnp.concatenate(
        [jnp.concatenate(psi_rows, axis=1), jnp.concatenate(beta_rows, axis=1)], axis=0
    )
    high, low = split(coefs[...])
    summed = dot_left(jnp.concatenate([high, high, low], axis=1), values)
    flat = out.reshape(bands * 2 * span, span_z)
    for y in range(span):
        flat[pl.ds(y, 2 * bands, stride=span), :] = (
            psi_rows[y] * kinetic[y : y + 1, :] + summed[:, y * span_z : (y + 1) * span_z]
        )


def whole(shape):
    return pl.BlockSpec(shape, lambda *_: (0,) * len(shape))


def subspace_solve(s_real, h_real, h_imag):
    factor = jnp.linalg.cholesky(s_real)
    solved = jax.scipy.linalg.cho_solve((factor, True), jnp.concatenate([h_real, h_imag], axis=1))
    order_size = s_real.shape[0]
    return (solved[:, :order_size], solved[:, order_size:])


def tdot(pattern, left, right):
    return jnp.einsum(pattern, left, right, precision=highest, preferred_element_type=jnp.float32)


def partner(values, devices, k):
    return lax.ppermute(values, "ga", [(d, d ^ k) for d in range(devices)])


def sum_over(values, devices, after):
    if devices & (devices - 1) or devices < 4:
        return lax.psum(values, "ga")
    step = 1
    while step < devices // 4:
        values = values + partner(values, devices, step)
        step *= 2
    others = [partner(values, devices, k * step) for k in (1, 2, 3)]
    held = pl.BlockSpec(memory_space=pltpu.VMEM)
    return pl.pallas_call(
        last_sum_kernel,
        out_shape=jax.ShapeDtypeStruct(values.shape, f32),
        in_specs=[held] * 4 + [pl.BlockSpec(memory_space=pl.ANY)],
        out_specs=held,
        name="last_sum",
    )(values, *others, after)


def on_device(devices, orbitals, plane_order, potential, projectors, slot_owner, strengths):
    bands = orbitals.shape[0]
    planes = orbitals.shape[2]
    span_y = orbitals.shape[3]
    span_z = orbitals.shape[4]
    span_x = plane_order.shape[0]
    blocks, slots = slot_owner.shape
    owners = strengths.shape[0] * strengths.shape[1]
    rows = span_y // devices
    block_rows = 2 * planes * rows
    pairs = bands // 2
    block_span = projectors.shape[3] // span_z
    per_plane = span_y // block_span
    grid_x = jnp.arange(span_x, dtype=jnp.int32)
    grid_y = jnp.arange(span_y, dtype=jnp.int32)
    grid_z = jnp.arange(span_z, dtype=jnp.int32)
    params = pltpu.CompilerParams(vmem_limit_bytes=vmem_limit)

    def cost(flops, moved):
        return pl.CostEstimate(flops=flops, bytes_accessed=moved, transcendentals=0)

    order = np.arange(2 * span_y)
    order = (order % 2) * span_y + order // 2
    inv_y = left_const(left_table(span_y, 1.0)[order])
    fwd_y = left_const(left_table(span_y, -1.0)[:, order])
    inv_z = right_const(right_table(span_z, 1.0))
    fwd_z = right_const(right_table(span_z, -1.0))

    parts = 2 if pairs % 2 == 0 else 1
    share = pairs // parts
    mine = lax.axis_index("ga").astype(jnp.int32)
    layers = 4 if parts == 2 and devices >= 8 and devices & (devices - 1) == 0 else 1
    members = devices // layers
    my_layer, my_member = (mine // members).reshape(1), (mine % members).reshape(1)
    scalar = pl.BlockSpec(memory_space=pltpu.SMEM)

    def to_rows(c, split):
        spec = pl.BlockSpec((devices, None, block_rows, span_z), lambda j: (0, j, 0, 0))
        shape = jax.ShapeDtypeStruct((devices, share, block_rows, span_z), f32)
        if split:
            spec = pl.BlockSpec((members, None, block_rows, span_z), lambda j: (0, j, 0, 0))
            shape = jax.ShapeDtypeStruct((members, share, block_rows, span_z), f32)
        return pl.pallas_call(
            to_rows_split_kernel if split else to_rows_kernel,
            out_shape=[shape] * layers if split else shape,
            grid=(share,),
            in_specs=([scalar] if split else [])
            + [
                pl.BlockSpec((2, 2, planes, span_y, span_z), lambda j: (c * share + j, 0, 0, 0, 0)),
                whole(inv_y.shape),
            ],
            out_specs=[spec] * layers if split else spec,
            scratch_shapes=[pltpu.VMEM((devices, block_rows, span_z), f32)] if split else [],
            compiler_params=params,
            cost_estimate=cost(4 * 10**9, 3 * 10**6),
            name="to_rows",
        )(*([my_layer] if split else []), orbitals, inv_y)

    sent = [to_rows(c, layers > 1) for c in range(parts)]

    def cross(one):
        return [one[0]] + [partner(one[k], devices, k * members) for k in range(1, layers)]

    def regroup(crossed, through):
        anywhere = pl.BlockSpec(memory_space=pl.ANY)
        held = pl.BlockSpec(memory_space=pltpu.VMEM)
        shape = jax.ShapeDtypeStruct((layers, share, block_rows, span_z), f32)
        outs = pl.pallas_call(
            functools.partial(regroup_kernel, layers, members),
            out_shape=[shape] * members
            + [jax.ShapeDtypeStruct(one.shape, f32) for one in through],
            in_specs=[scalar] + [held] * layers + [anywhere] * len(through),
            out_specs=[held] * members + [anywhere] * len(through),
            input_output_aliases={1 + layers + i: members + i for i in range(len(through))},
            compiler_params=params,
            cost_estimate=cost(0, 2 * 10**6),
            name="regroup",
        )(my_member, *crossed, *through)
        return outs[:members], outs[members:]

    def spread(one):
        return [one[0]] + [partner(one[k], devices, k) for k in range(1, members)]

    if layers > 1:
        one, sent[1] = regroup(cross(sent[0]), sent[1])
        crossed = cross(sent[1])
        arrived = [spread(one), crossed]
    else:
        arrived = [
            [lax.all_to_all(one, "ga", split_axis=0, concat_axis=0, tiled=True)] for one in sent
        ]

    def tables_x(owned):
        phases = (owned.T.reshape(-1)[:, None] * grid_x[None, :]) % span_x
        angles = phases.astype(f32) * (2.0 * math.pi / span_x)
        factor = 1.0 / math.sqrt(span_x)
        cosine, sine = jnp.cos(angles) * factor, jnp.sin(angles) * factor
        forward = jnp.concatenate([cosine, -sine], axis=0)
        inverse = jnp.concatenate([forward, jnp.concatenate([sine, cosine], axis=0)], axis=1).T
        tables = []
        for table in (forward, inverse):
            high, low = split_outside(table)
            tables.append(jnp.concatenate([high, high, low], axis=1))
        return tables

    owned = plane_order.reshape(devices, planes)
    fwd_x, inv_x = tables_x(owned)
    steps = np.arange(layers)[None, :] * members + np.arange(members)[:, None]
    _, inv_x_steps = tables_x(
        jnp.take(owned, mine ^ jnp.asarray(steps.reshape(-1), jnp.int32), axis=0)
    )
    pot = potential.transpose(1, 0, 2).reshape(rows * span_x, span_z)

    local_order = lax.dynamic_slice_in_dim(plane_order, lax.axis_index("ga") * planes, planes)
    freq_x = signed_index(local_order, span_x).astype(f32) / span_x
    freq_y = signed_index(grid_y, span_y).astype(f32) / span_y
    freq_z = signed_index(grid_z, span_z).astype(f32) / span_z
    kinetic = 2.0 * (
        freq_x[:, None, None] ** 2 + freq_y[None, :, None] ** 2 + freq_z[None, None, :] ** 2
    )
    beta = projectors.reshape(blocks, slots, 2, block_span, span_z)
    beta = beta.transpose(0, 1, 3, 2, 4).reshape(blocks, slots * block_span * 2, span_z)
    block_specs = [
        pl.BlockSpec(
            (bands, 2, None, block_span, span_z),
            lambda g: (0, 0, g // per_plane, g % per_plane, 0),
        ),
        pl.BlockSpec((None, slots * block_span * 2, span_z), lambda g: (g, 0, 0)),
        pl.BlockSpec((None, block_span, span_z), lambda g: (g // per_plane, g % per_plane, 0)),
    ]
    products = pl.pallas_call(
        functools.partial(project_kernel, slots),
        out_shape=jax.ShapeDtypeStruct((blocks, 2 * slots + 2 * bands, 2 * bands), f32),
        grid=(blocks,),
        in_specs=block_specs,
        out_specs=pl.BlockSpec((None, 2 * slots + 2 * bands, 2 * bands), lambda g: (g, 0, 0)),
        compiler_params=params,
        cost_estimate=cost(8 * 10**9, 8 * 10**6),
        name="project",
    )(orbitals, beta, kinetic)
    with_real = products[:, :slots].reshape(blocks, slots, bands, 2)
    with_imag = products[:, slots : 2 * slots].reshape(blocks, slots, bands, 2)
    proj = jnp.concatenate(
        [
            with_real[..., 0] + with_imag[..., 1],
            with_real[..., 1] - with_imag[..., 0],
        ],
        axis=-1,
    )
    chosen = (
        slot_owner[:, :, None] == jnp.arange(owners, dtype=jnp.int32)[None, None, :]
    ).astype(f32)
    proj = tdot("gsj,gsc->jc", chosen, proj)
    kin = jnp.sum(products[:, 2 * slots :], axis=0).reshape(bands, 2, bands, 2)
    kin = kin[:, 0, :, 0] + kin[:, 1, :, 1]

    returned, fields = [], []
    before = proj
    for c, operands in enumerate(arrived):
        steps = layers > 1
        if steps and c > 0:
            operands = spread(operands)
        held = devices // len(operands)
        kernel = functools.partial(real_space_kernel, rows, planes)
        if steps:
            kernel = functools.partial(real_space_parts_kernel, rows, planes, members)
        back, field = pl.pallas_call(
            kernel,
            out_shape=(
                jax.ShapeDtypeStruct((devices, 2 * share, block_rows, span_z), f32),
                jax.ShapeDtypeStruct((2 * share, rows * span_x, span_z), f32),
            ),
            grid=(share,),
            in_specs=[pl.BlockSpec((held, None, block_rows, span_z), lambda j: (0, j, 0, 0))]
            * len(operands)
            + [
                whole(pot.shape),
                whole(inv_x.shape),
                whole(fwd_x.shape),
                whole(inv_z.shape),
                whole(fwd_z.shape),
            ]
            + [pl.BlockSpec(memory_space=pl.ANY)],
            out_specs=(
                pl.BlockSpec((devices, 2, block_rows, span_z), lambda j: (0, j, 0, 0)),
                pl.BlockSpec((2, rows * span_x, span_z), lambda j: (j, 0, 0)),
            ),
            scratch_shapes=[pltpu.VMEM((devices, block_rows, span_z), f32)] if steps else [],
            compiler_params=params,
            cost_estimate=cost(10**6, 10**4),
            name="real_space",
        )(*operands, pot, inv_x_steps if steps else inv_x, fwd_x, inv_z, fwd_z, before)
        if steps and c == 0:
            arrived[1], (back,) = regroup(arrived[1], [back])
        before = back
        returned.append(lax.all_to_all(back, "ga", split_axis=0, concat_axis=0, tiled=True))
        fields.append(field)

    grams = pl.pallas_call(
        functools.partial(real_gram_kernel, bands),
        out_shape=jax.ShapeDtypeStruct((2, bands, bands, 128), f32),
        compiler_params=params,
        cost_estimate=cost(10**7, 2 * 10**6),
        name="real_gram",
    )(*fields, pot)
    grams = jnp.sum(grams, axis=-1)
    own = jnp.concatenate([proj, jnp.concatenate([grams[0], grams[1] + kin], axis=1)], axis=0)
    total = sum_over(own, devices, returned[0])
    proj, s_real, h_real = total[:owners], total[owners:, :bands], total[owners:, bands:]
    weighted = strengths.reshape(-1)[:, None] * proj
    p_real, p_imag = proj[:, :bands], proj[:, bands:]
    w_real, w_imag = weighted[:, :bands], weighted[:, bands:]
    h_real = h_real + tdot("ja,jb->ab", p_real, w_real) + tdot("ja,jb->ab", p_imag, w_imag)
    h_imag = tdot("ja,jb->ab", p_real, w_imag) - tdot("ja,jb->ab", p_imag, w_real)
    m_real, m_imag = subspace_solve(s_real, h_real, h_imag)

    coefs = tdot("gsj,jc->gcs", chosen, weighted)
    c_real, c_imag = coefs[:, :bands], coefs[:, bands:]
    from_beta = jnp.stack(
        [
            jnp.concatenate([c_real, -c_imag], axis=2),
            jnp.concatenate([c_imag, c_real], axis=2),
        ],
        axis=2,
    ).reshape(blocks, 2 * bands, 2 * slots)
    from_psi = jnp.stack(
        [
            jnp.stack([-m_real.T, m_imag.T], axis=-1),
            jnp.stack([-m_imag.T, -m_real.T], axis=-1),
        ],
        axis=1,
    ).reshape(1, 2 * bands, 2 * bands)
    coefs = jnp.concatenate(
        [jnp.broadcast_to(from_psi, (blocks, 2 * bands, 2 * bands)), from_beta], axis=2
    )
    base = pl.pallas_call(
        functools.partial(base_kernel, slots),
        out_shape=jax.ShapeDtypeStruct(orbitals.shape, f32),
        grid=(blocks,),
        in_specs=block_specs
        + [pl.BlockSpec((None, 2 * bands, 2 * bands + 2 * slots), lambda g: (g, 0, 0))],
        out_specs=block_specs[0],
        compiler_params=params,
        cost_estimate=cost(8 * 10**9, 12 * 10**6),
        name="base",
    )(orbitals, beta, kinetic, coefs)

    residual = base
    for c in range(parts):
        two_bands = pl.BlockSpec(
            (2, 2, planes, span_y, span_z), lambda j, c=c: (share * c + j, 0, 0, 0, 0)
        )
        residual = pl.pallas_call(
            to_planes_kernel,
            out_shape=jax.ShapeDtypeStruct(orbitals.shape, f32),
            grid=(share,),
            in_specs=[
                pl.BlockSpec((devices, 2, block_rows, span_z), lambda j: (0, j, 0, 0)),
                two_bands,
                whole(fwd_y.shape),
            ],
            out_specs=two_bands,
            input_output_aliases={1: 0},
            compiler_params=params,
            cost_estimate=cost(8 * 10**9, 12 * 10**6),
            name="to_planes",
        )(returned[c], residual, fwd_y)
    return (residual, jnp.stack([m_real, m_imag]))


def solution(mesh):
    return jax.shard_map(
        functools.partial(on_device, mesh.shape["ga"]),
        mesh=mesh,
        in_specs=(
            P("rep", None, "ga", None, None),
            P("rep"),
            P("rep", "ga", None),
            P(("rep", "ga"), None, None, None),
            P(("rep", "ga"), None),
            P("rep", None),
        ),
        out_specs=(P("rep", None, "ga", None, None), P(None, "rep", None)),
        check_vma=False,
    )
```

```python
import functools
import math

import jax
import jax.numpy as jnp
import numpy as np
from jax import lax
from jax.experimental import pallas as pl
from jax.experimental.pallas import tpu as pltpu
from jax.sharding import PartitionSpec as P

highest = lax.Precision.HIGHEST
f32 = jnp.float32
bf16 = jnp.bfloat16
vmem_limit = 63 * 1024 * 1024


def signed_index(values, length):
    return jnp.where(values < length // 2, values, values - length)


def dft(length, orient):
    index = np.arange(length)
    angles = (index[:, None] * index[None, :] % length) * (2.0 * math.pi / length)
    factor = 1.0 / math.sqrt(length)
    return np.cos(angles) * factor, orient * np.sin(angles) * factor


def left_table(length, orient):
    cosine, sine = dft(length, orient)
    return np.block([[cosine, -sine], [sine, cosine]])


def right_table(length, orient):
    cosine, sine = dft(length, orient)
    return np.block([[cosine, sine], [-sine, cosine]])


def split(values):
    high = values.astype(bf16)
    low = (values - high.astype(f32)).astype(bf16)
    return high, low


def split_outside(values):
    high = lax.reduce_precision(values, exponent_bits=8, mantissa_bits=7)
    return high.astype(bf16), (values - high).astype(bf16)


def const_parts(table):
    table = np.asarray(table, np.float32)
    high = table.astype(jnp.bfloat16)
    low = (table - high.astype(np.float32)).astype(jnp.bfloat16)
    return high, low


def left_const(table):
    high, low = const_parts(table)
    return jnp.asarray(np.concatenate([high, high, low], axis=1))


def right_const(table):
    high, low = const_parts(table)
    return jnp.asarray(np.concatenate([high, high, low], axis=0))


def dot_left(table, values):
    high, low = split(values)
    return jnp.dot(
        table, jnp.concatenate([high, low, high], axis=0), preferred_element_type=f32
    )


def dot_right(values, table):
    high, low = split(values)
    return jnp.dot(
        jnp.concatenate([high, low, high], axis=1), table, preferred_element_type=f32
    )


def groups(count, width):
    size = max(1, 256 // width)
    return [list(range(i, min(i + size, count))) for i in range(0, count, size)]


def parts_in_lanes(values, span, width):
    items = values.shape[1] // width
    return jnp.concatenate(
        [
            jnp.concatenate(
                [values[:span, i * width : (i + 1) * width], values[span:, i * width : (i + 1) * width]],
                axis=1,
            )
            for i in range(items)
        ],
        axis=0,
    )


def to_rows_kernel(psi, y_table, out):
    _, _, planes, span_y, span_z = psi.shape
    devices, block_rows, _ = out.shape
    each = block_rows // planes
    for group in groups(planes, span_z):
        real = jnp.concatenate([psi[0, 0, p] - psi[1, 1, p] for p in group], axis=1)
        imag = jnp.concatenate([psi[0, 1, p] + psi[1, 0, p] for p in group], axis=1)
        along_y = dot_left(y_table[...], jnp.concatenate([real, imag], axis=0))
        for i, p in enumerate(group):
            out[:, p * each : (p + 1) * each, :] = along_y[
                :, i * span_z : (i + 1) * span_z
            ].reshape(devices, each, span_z)


def real_space_kernel(rows, planes, recv, pot, inverse, forward, inv_z, fwd_z, _, back, field):
    devices, size, span_z = recv.shape
    span_x = devices * planes
    arrived = recv.reshape(devices * size, span_z)
    leaving = back.reshape(devices * 2 * size, span_z)
    columns = [
        jnp.concatenate(
            [
                arrived[pl.ds((p * rows + r) * 2 + part, devices, stride=size), :]
                for part in range(2)
                for p in range(planes)
            ],
            axis=0,
        )
        for r in range(rows)
    ]
    along_x = dot_left(inverse[...], jnp.concatenate(columns, axis=1))
    spatial = dot_right(parts_in_lanes(along_x, span_x, span_z), inv_z[...])
    spectral = []
    for band in range(2):
        one = spatial[:, band * span_z : (band + 1) * span_z]
        field[band] = one
        product = one * pot[...]
        product = jnp.concatenate(
            [product[r * span_x : (r + 1) * span_x] for r in range(rows)], axis=1
        )
        spectral.append(parts_in_lanes(dot_left(forward[...], product), span_x, span_z))
    spectral = dot_right(jnp.concatenate(spectral, axis=0), fwd_z[...])
    for band in range(2):
        for r in range(rows):
            for p in range(planes):
                first = ((band * rows + r) * planes + p) * devices
                for part in range(2):
                    start = band * size + (p * rows + r) * 2 + part
                    leaving[pl.ds(start, devices, stride=2 * size), :] = spectral[
                        first : first + devices, part * span_z : (part + 1) * span_z
                    ]


def real_gram_kernel(bands, *refs):
    fields, (pot, out) = refs[:-2], refs[-2:]
    held = fields[0].shape[0]
    pairs = [(a, b) for a in range(bands) for b in range(a, bands)]
    for weighted in range(2):

        def step(i, sums):
            rows = pl.ds(pl.multiple_of(i * 8, 8), 8)
            values = [fields[a // held][a % held, rows, :] for a in range(bands)]
            other = [v * pot[rows, :] for v in values] if weighted else values
            result = []
            for (a, b), total in zip(pairs, sums):
                product = values[a] * other[b]
                lanes = product[:, :128]
                for c in range(128, product.shape[1], 128):
                    lanes = lanes + product[:, c : c + 128]
                result.append(total + lanes)
            return tuple(result)

        sums = lax.fori_loop(
            0, pot.shape[0] // 8, step, tuple(jnp.zeros((8, 128), f32) for _ in pairs)
        )
        for (a, b), total in zip(pairs, sums):
            line = jnp.sum(total, axis=0, keepdims=True)
            out[weighted, a, b : b + 1, :] = line
            out[weighted, b, a : a + 1, :] = line


def to_planes_kernel(recv, base, y_table, *refs):
    out = refs[-1]
    bands, _, planes, span_y, span_z = base.shape
    each = recv.shape[2] // planes
    for band in range(bands):
        for group in groups(planes, span_z):
            columns = [
                recv[:, band, p * each : (p + 1) * each, :].reshape(2 * span_y, span_z)
                for p in group
            ]
            along_y = dot_left(y_table[...], jnp.concatenate(columns, axis=1))
            for i, p in enumerate(group):
                for part in range(2):
                    out[band, part, p] = base[band, part, p] + (
                        along_y[part * span_y : (part + 1) * span_y, i * span_z : (i + 1) * span_z]
                    )


def last_sum_kernel(first, second, _, out):
    out[...] = first[...] + second[...]


def block_rows_of(psi, beta, slots):
    bands, _, span, span_z = psi.shape
    psi_flat = psi.reshape(bands * 2 * span, span_z)
    psi_rows = [psi_flat[pl.ds(y, 2 * bands, stride=span), :] for y in range(span)]
    beta_rows = [
        jnp.concatenate(
            [beta[pl.ds(2 * y + part, slots, stride=2 * span), :] for part in range(2)], axis=0
        )
        for y in range(span)
    ]
    return psi_rows, beta_rows


def project_kernel(slots, psi, beta, kinetic, out):
    bands, _, span, span_z = psi.shape
    psi_rows, beta_rows = block_rows_of(psi, beta, slots)
    kin_rows = [psi_rows[y] * kinetic[y : y + 1, :] for y in range(span)]
    right = jnp.concatenate(split(jnp.concatenate(psi_rows, axis=1)), axis=0)
    left = jnp.concatenate(
        split(jnp.concatenate(beta_rows, axis=1)) + split(jnp.concatenate(kin_rows, axis=1)), axis=0
    )
    full = lax.dot_general(left, right, (((1,), (1,)), ((), ())), preferred_element_type=f32)
    width, height = 2 * bands, 2 * slots
    full = full[:, :width] + full[:, width:]
    out[0:height] = full[0:height] + full[height : 2 * height]
    rest = full[2 * height :]
    out[height:] = rest[0:width] + rest[width:]


def base_kernel(slots, psi, beta, kinetic, coefs, out):
    bands, _, span, span_z = psi.shape
    psi_rows, beta_rows = block_rows_of(psi, beta, slots)
    values = jnp.concatenate(
        [jnp.concatenate(psi_rows, axis=1), jnp.concatenate(beta_rows, axis=1)], axis=0
    )
    high, low = split(coefs[...])
    summed = dot_left(jnp.concatenate([high, high, low], axis=1), values)
    flat = out.reshape(bands * 2 * span, span_z)
    for y in range(span):
        flat[pl.ds(y, 2 * bands, stride=span), :] = (
            psi_rows[y] * kinetic[y : y + 1, :] + summed[:, y * span_z : (y + 1) * span_z]
        )


def whole(shape):
    return pl.BlockSpec(shape, lambda *_: (0,) * len(shape))


def subspace_solve(s_real, h_real, h_imag):
    factor = jnp.linalg.cholesky(s_real)
    solved = jax.scipy.linalg.cho_solve((factor, True), jnp.concatenate([h_real, h_imag], axis=1))
    order_size = s_real.shape[0]
    return (solved[:, :order_size], solved[:, order_size:])


def tdot(pattern, left, right):
    return jnp.einsum(pattern, left, right, precision=highest, preferred_element_type=jnp.float32)


def partner(values, devices, k):
    return lax.ppermute(values, "ga", [(d, d ^ k) for d in range(devices)])


def sum_over(values, devices, after):
    if devices & (devices - 1) or devices < 2:
        return lax.psum(values, "ga")
    step = 1
    while step < devices // 2:
        values = values + partner(values, devices, step)
        step *= 2
    held = pl.BlockSpec(memory_space=pltpu.VMEM)
    return pl.pallas_call(
        last_sum_kernel,
        out_shape=jax.ShapeDtypeStruct(values.shape, f32),
        in_specs=[held] * 2 + [pl.BlockSpec(memory_space=pl.ANY)],
        out_specs=held,
        name="last_sum",
    )(values, partner(values, devices, step), after)


def on_device(devices, orbitals, plane_order, potential, projectors, slot_owner, strengths):
    bands = orbitals.shape[0]
    planes = orbitals.shape[2]
    span_y = orbitals.shape[3]
    span_z = orbitals.shape[4]
    span_x = plane_order.shape[0]
    blocks, slots = slot_owner.shape
    owners = strengths.shape[0] * strengths.shape[1]
    rows = span_y // devices
    block_rows = 2 * planes * rows
    pairs = bands // 2
    block_span = projectors.shape[3] // span_z
    per_plane = span_y // block_span
    grid_x = jnp.arange(span_x, dtype=jnp.int32)
    grid_y = jnp.arange(span_y, dtype=jnp.int32)
    grid_z = jnp.arange(span_z, dtype=jnp.int32)
    params = pltpu.CompilerParams(vmem_limit_bytes=vmem_limit)
    tail_params = pltpu.CompilerParams(vmem_limit_bytes=vmem_limit // 2)

    def cost(flops, moved):
        return pl.CostEstimate(flops=flops, bytes_accessed=moved, transcendentals=0)

    order = np.arange(2 * span_y)
    order = (order % 2) * span_y + order // 2
    inv_y = left_const(left_table(span_y, 1.0)[order])
    fwd_y = left_const(left_table(span_y, -1.0)[:, order])
    inv_z = right_const(right_table(span_z, 1.0))
    fwd_z = right_const(right_table(span_z, -1.0))

    parts = 2 if pairs % 2 == 0 else 1
    share = pairs // parts
    arrived = []
    for c in range(parts):
        sent = pl.pallas_call(
            to_rows_kernel,
            out_shape=jax.ShapeDtypeStruct((devices, share, block_rows, span_z), f32),
            grid=(share,),
            in_specs=[
                pl.BlockSpec(
                    (2, 2, planes, span_y, span_z), lambda j, c=c: (c * share + j, 0, 0, 0, 0)
                ),
                whole(inv_y.shape),
            ],
            out_specs=pl.BlockSpec((devices, None, block_rows, span_z), lambda j: (0, j, 0, 0)),
            compiler_params=params,
            cost_estimate=cost(4 * 10**9, 3 * 10**6),
            name="to_rows",
        )(orbitals, inv_y)
        arrived.append(lax.all_to_all(sent, "ga", split_axis=0, concat_axis=0, tiled=True))

    stored = plane_order.reshape(devices, planes).T.reshape(-1)
    phases = (stored[:, None] * grid_x[None, :]) % span_x
    angles = phases.astype(f32) * (2.0 * math.pi / span_x)
    factor = 1.0 / math.sqrt(span_x)
    cosine, sine = jnp.cos(angles) * factor, jnp.sin(angles) * factor
    fwd_x = jnp.concatenate([cosine, -sine], axis=0)
    inv_x = jnp.concatenate([fwd_x, jnp.concatenate([sine, cosine], axis=0)], axis=1).T
    high, low = split_outside(fwd_x)
    fwd_x = jnp.concatenate([high, high, low], axis=1)
    high, low = split_outside(inv_x)
    inv_x = jnp.concatenate([high, high, low], axis=1)
    pot = potential.transpose(1, 0, 2).reshape(rows * span_x, span_z)

    local_order = lax.dynamic_slice_in_dim(plane_order, lax.axis_index("ga") * planes, planes)
    freq_x = signed_index(local_order, span_x).astype(f32) / span_x
    freq_y = signed_index(grid_y, span_y).astype(f32) / span_y
    freq_z = signed_index(grid_z, span_z).astype(f32) / span_z
    kinetic = 2.0 * (
        freq_x[:, None, None] ** 2 + freq_y[None, :, None] ** 2 + freq_z[None, None, :] ** 2
    )
    beta = projectors.reshape(blocks, slots, 2, block_span, span_z)
    beta = beta.transpose(0, 1, 3, 2, 4).reshape(blocks, slots * block_span * 2, span_z)
    block_specs = [
        pl.BlockSpec(
            (bands, 2, None, block_span, span_z),
            lambda g: (0, 0, g // per_plane, g % per_plane, 0),
        ),
        pl.BlockSpec((None, slots * block_span * 2, span_z), lambda g: (g, 0, 0)),
        pl.BlockSpec((None, block_span, span_z), lambda g: (g // per_plane, g % per_plane, 0)),
    ]
    products = pl.pallas_call(
        functools.partial(project_kernel, slots),
        out_shape=jax.ShapeDtypeStruct((blocks, 2 * slots + 2 * bands, 2 * bands), f32),
        grid=(blocks,),
        in_specs=block_specs,
        out_specs=pl.BlockSpec((None, 2 * slots + 2 * bands, 2 * bands), lambda g: (g, 0, 0)),
        compiler_params=params,
        cost_estimate=cost(8 * 10**9, 8 * 10**6),
        name="project",
    )(orbitals, beta, kinetic)
    with_real = products[:, :slots].reshape(blocks, slots, bands, 2)
    with_imag = products[:, slots : 2 * slots].reshape(blocks, slots, bands, 2)
    proj = jnp.concatenate(
        [
            with_real[..., 0] + with_imag[..., 1],
            with_real[..., 1] - with_imag[..., 0],
        ],
        axis=-1,
    )
    owned = (
        slot_owner[:, :, None] == jnp.arange(owners, dtype=jnp.int32)[None, None, :]
    ).astype(f32)
    proj = tdot("gsj,gsc->jc", owned, proj)
    kin = jnp.sum(products[:, 2 * slots :], axis=0).reshape(bands, 2, bands, 2)
    kin = kin[:, 0, :, 0] + kin[:, 1, :, 1]

    returned, fields = [], []
    for c in range(parts):
        back, field = pl.pallas_call(
            functools.partial(real_space_kernel, rows, planes),
            out_shape=(
                jax.ShapeDtypeStruct((devices, 2 * share, block_rows, span_z), f32),
                jax.ShapeDtypeStruct((2 * share, rows * span_x, span_z), f32),
            ),
            grid=(share,),
            in_specs=[
                pl.BlockSpec((devices, None, block_rows, span_z), lambda j: (0, j, 0, 0)),
                whole(pot.shape),
                whole(inv_x.shape),
                whole(fwd_x.shape),
                whole(inv_z.shape),
                whole(fwd_z.shape),
                whole(proj.shape),
            ],
            out_specs=(
                pl.BlockSpec((devices, 2, block_rows, span_z), lambda j: (0, j, 0, 0)),
                pl.BlockSpec((2, rows * span_x, span_z), lambda j: (j, 0, 0)),
            ),
            compiler_params=params,
            cost_estimate=cost(4 * 10**9, 8 * 10**6),
            name="real_space",
        )(arrived[c], pot, inv_x, fwd_x, inv_z, fwd_z, proj)
        returned.append(lax.all_to_all(back, "ga", split_axis=0, concat_axis=0, tiled=True))
        fields.append(field)

    grams = pl.pallas_call(
        functools.partial(real_gram_kernel, bands),
        out_shape=jax.ShapeDtypeStruct((2, bands, bands, 128), f32),
        compiler_params=params,
        cost_estimate=cost(10**7, 2 * 10**6),
        name="real_gram",
    )(*fields, pot)
    grams = jnp.sum(grams, axis=-1)
    own = jnp.concatenate([proj, jnp.concatenate([grams[0], grams[1] + kin], axis=1)], axis=0)
    total = sum_over(own, devices, returned[0])
    proj, s_real, h_real = total[:owners], total[owners:, :bands], total[owners:, bands:]
    weighted = strengths.reshape(-1)[:, None] * proj
    p_real, p_imag = proj[:, :bands], proj[:, bands:]
    w_real, w_imag = weighted[:, :bands], weighted[:, bands:]
    h_real = h_real + tdot("ja,jb->ab", p_real, w_real) + tdot("ja,jb->ab", p_imag, w_imag)
    h_imag = tdot("ja,jb->ab", p_real, w_imag) - tdot("ja,jb->ab", p_imag, w_real)
    m_real, m_imag = subspace_solve(s_real, h_real, h_imag)

    coefs = tdot("gsj,jc->gcs", owned, weighted)
    c_real, c_imag = coefs[:, :bands], coefs[:, bands:]
    from_beta = jnp.stack(
        [
            jnp.concatenate([c_real, -c_imag], axis=2),
            jnp.concatenate([c_imag, c_real], axis=2),
        ],
        axis=2,
    ).reshape(blocks, 2 * bands, 2 * slots)
    from_psi = jnp.stack(
        [
            jnp.stack([-m_real.T, m_imag.T], axis=-1),
            jnp.stack([-m_imag.T, -m_real.T], axis=-1),
        ],
        axis=1,
    ).reshape(1, 2 * bands, 2 * bands)
    coefs = jnp.concatenate(
        [jnp.broadcast_to(from_psi, (blocks, 2 * bands, 2 * bands)), from_beta], axis=2
    )
    base = pl.pallas_call(
        functools.partial(base_kernel, slots),
        out_shape=jax.ShapeDtypeStruct(orbitals.shape, f32),
        grid=(blocks,),
        in_specs=block_specs
        + [pl.BlockSpec((None, 2 * bands, 2 * bands + 2 * slots), lambda g: (g, 0, 0))],
        out_specs=block_specs[0],
        compiler_params=tail_params,
        cost_estimate=cost(8 * 10**9, 12 * 10**6),
        name="base",
    )(orbitals, beta, kinetic, coefs)

    earlier = []
    for c in range(parts):
        two_bands = pl.BlockSpec(
            (2, 2, planes, span_y, span_z), lambda j, c=c: (share * c + j, 0, 0, 0, 0)
        )
        residual = pl.pallas_call(
            to_planes_kernel,
            out_shape=jax.ShapeDtypeStruct(orbitals.shape, f32),
            grid=(share,),
            in_specs=[
                pl.BlockSpec((devices, 2, block_rows, span_z), lambda j: (0, j, 0, 0)),
                two_bands,
                whole(fwd_y.shape),
            ]
            + [pl.BlockSpec(memory_space=pl.ANY)] * len(earlier),
            out_specs=two_bands,
            input_output_aliases={3: 0} if earlier else {},
            compiler_params=tail_params,
            cost_estimate=cost(8 * 10**9, 12 * 10**6),
            name="to_planes",
        )(returned[c], base, fwd_y, *earlier)
        earlier = [residual]
    return (residual, jnp.stack([m_real, m_imag]))


def solution(mesh):
    return jax.shard_map(
        functools.partial(on_device, mesh.shape["ga"]),
        mesh=mesh,
        in_specs=(
            P("rep", None, "ga", None, None),
            P("rep"),
            P("rep", "ga", None),
            P(("rep", "ga"), None, None, None),
            P(("rep", "ga"), None),
            P("rep", None),
        ),
        out_specs=(P("rep", None, "ga", None, None), P(None, "rep", None)),
        check_vma=False,
    )
```

```python
import functools
import math

import jax
import jax.numpy as jnp
import numpy as np
from jax import lax
from jax.experimental import pallas as pl
from jax.experimental.pallas import tpu as pltpu
from jax.sharding import PartitionSpec as P

highest = lax.Precision.HIGHEST
f32 = jnp.float32
bf16 = jnp.bfloat16
vmem_limit = 63 * 1024 * 1024


def signed_index(values, length):
    return jnp.where(values < length // 2, values, values - length)


def dft(length, orient):
    index = np.arange(length)
    angles = (index[:, None] * index[None, :] % length) * (2.0 * math.pi / length)
    factor = 1.0 / math.sqrt(length)
    return np.cos(angles) * factor, orient * np.sin(angles) * factor


def left_table(length, orient):
    cosine, sine = dft(length, orient)
    return np.block([[cosine, -sine], [sine, cosine]])


def right_table(length, orient):
    cosine, sine = dft(length, orient)
    return np.block([[cosine, sine], [-sine, cosine]])


def split(values):
    high = values.astype(bf16)
    low = (values - high.astype(f32)).astype(bf16)
    return high, low


def split_outside(values):
    high = lax.reduce_precision(values, exponent_bits=8, mantissa_bits=7)
    return high.astype(bf16), (values - high).astype(bf16)


def const_parts(table):
    table = np.asarray(table, np.float32)
    high = table.astype(jnp.bfloat16)
    low = (table - high.astype(np.float32)).astype(jnp.bfloat16)
    return high, low


def left_const(table):
    high, low = const_parts(table)
    return jnp.asarray(np.concatenate([high, high, low], axis=1))


def right_const(table):
    high, low = const_parts(table)
    return jnp.asarray(np.concatenate([high, high, low], axis=0))


def dot_left(table, values):
    high, low = split(values)
    return jnp.dot(
        table, jnp.concatenate([high, low, high], axis=0), preferred_element_type=f32
    )


def dot_right(values, table):
    high, low = split(values)
    return jnp.dot(
        jnp.concatenate([high, low, high], axis=1), table, preferred_element_type=f32
    )


def groups(count, width):
    size = max(1, 256 // width)
    return [list(range(i, min(i + size, count))) for i in range(0, count, size)]


def parts_in_lanes(values, span, width):
    items = values.shape[1] // width
    return jnp.concatenate(
        [
            jnp.concatenate(
                [values[:span, i * width : (i + 1) * width], values[span:, i * width : (i + 1) * width]],
                axis=1,
            )
            for i in range(items)
        ],
        axis=0,
    )


def to_rows_kernel(psi, y_table, out):
    _, _, planes, span_y, span_z = psi.shape
    devices, block_rows, _ = out.shape
    each = block_rows // planes
    for group in groups(planes, span_z):
        real = jnp.concatenate([psi[0, 0, p] - psi[1, 1, p] for p in group], axis=1)
        imag = jnp.concatenate([psi[0, 1, p] + psi[1, 0, p] for p in group], axis=1)
        along_y = dot_left(y_table[...], jnp.concatenate([real, imag], axis=0))
        for i, p in enumerate(group):
            out[:, p * each : (p + 1) * each, :] = along_y[
                :, i * span_z : (i + 1) * span_z
            ].reshape(devices, each, span_z)


def real_space_kernel(rows, planes, recv, pot, inverse, forward, inv_z, fwd_z, _, back, field):
    devices, size, span_z = recv.shape
    span_x = devices * planes
    arrived = recv.reshape(devices * size, span_z)
    leaving = back.reshape(devices * 2 * size, span_z)
    columns = [
        jnp.concatenate(
            [
                arrived[pl.ds((p * rows + r) * 2 + part, devices, stride=size), :]
                for part in range(2)
                for p in range(planes)
            ],
            axis=0,
        )
        for r in range(rows)
    ]
    along_x = dot_left(inverse[...], jnp.concatenate(columns, axis=1))
    spatial = dot_right(parts_in_lanes(along_x, span_x, span_z), inv_z[...])
    spectral = []
    for band in range(2):
        one = spatial[:, band * span_z : (band + 1) * span_z]
        field[band] = one
        product = one * pot[...]
        product = jnp.concatenate(
            [product[r * span_x : (r + 1) * span_x] for r in range(rows)], axis=1
        )
        spectral.append(parts_in_lanes(dot_left(forward[...], product), span_x, span_z))
    spectral = dot_right(jnp.concatenate(spectral, axis=0), fwd_z[...])
    for band in range(2):
        for r in range(rows):
            for p in range(planes):
                first = ((band * rows + r) * planes + p) * devices
                for part in range(2):
                    start = band * size + (p * rows + r) * 2 + part
                    leaving[pl.ds(start, devices, stride=2 * size), :] = spectral[
                        first : first + devices, part * span_z : (part + 1) * span_z
                    ]


def real_gram_kernel(bands, *refs):
    fields, (pot, out) = refs[:-2], refs[-2:]
    held = fields[0].shape[0]
    pairs = [(a, b) for a in range(bands) for b in range(a, bands)]
    for weighted in range(2):

        def step(i, sums):
            rows = pl.ds(pl.multiple_of(i * 8, 8), 8)
            values = [fields[a // held][a % held, rows, :] for a in range(bands)]
            other = [v * pot[rows, :] for v in values] if weighted else values
            result = []
            for (a, b), total in zip(pairs, sums):
                product = values[a] * other[b]
                lanes = product[:, :128]
                for c in range(128, product.shape[1], 128):
                    lanes = lanes + product[:, c : c + 128]
                result.append(total + lanes)
            return tuple(result)

        sums = lax.fori_loop(
            0, pot.shape[0] // 8, step, tuple(jnp.zeros((8, 128), f32) for _ in pairs)
        )
        for (a, b), total in zip(pairs, sums):
            line = jnp.sum(total, axis=0, keepdims=True)
            out[weighted, a, b : b + 1, :] = line
            out[weighted, b, a : a + 1, :] = line


def to_planes_kernel(recv, base, y_table, out):
    bands, _, planes, span_y, span_z = base.shape
    each = recv.shape[2] // planes
    for band in range(bands):
        for group in groups(planes, span_z):
            columns = [
                recv[:, band, p * each : (p + 1) * each, :].reshape(2 * span_y, span_z)
                for p in group
            ]
            along_y = dot_left(y_table[...], jnp.concatenate(columns, axis=1))
            for i, p in enumerate(group):
                for part in range(2):
                    out[band, part, p] = base[band, part, p] + (
                        along_y[part * span_y : (part + 1) * span_y, i * span_z : (i + 1) * span_z]
                    )


def last_sum_kernel(first, second, _, out):
    out[...] = first[...] + second[...]


def block_rows_of(psi, beta, slots):
    bands, _, span, span_z = psi.shape
    psi_flat = psi.reshape(bands * 2 * span, span_z)
    psi_rows = [psi_flat[pl.ds(y, 2 * bands, stride=span), :] for y in range(span)]
    beta_rows = [
        jnp.concatenate(
            [beta[pl.ds(2 * y + part, slots, stride=2 * span), :] for part in range(2)], axis=0
        )
        for y in range(span)
    ]
    return psi_rows, beta_rows


def project_kernel(slots, psi, beta, kinetic, out):
    bands, _, span, span_z = psi.shape
    psi_rows, beta_rows = block_rows_of(psi, beta, slots)
    kin_rows = [psi_rows[y] * kinetic[y : y + 1, :] for y in range(span)]
    right = jnp.concatenate(split(jnp.concatenate(psi_rows, axis=1)), axis=0)
    left = jnp.concatenate(
        split(jnp.concatenate(beta_rows, axis=1)) + split(jnp.concatenate(kin_rows, axis=1)), axis=0
    )
    full = lax.dot_general(left, right, (((1,), (1,)), ((), ())), preferred_element_type=f32)
    width, height = 2 * bands, 2 * slots
    full = full[:, :width] + full[:, width:]
    out[0:height] = full[0:height] + full[height : 2 * height]
    rest = full[2 * height :]
    out[height:] = rest[0:width] + rest[width:]


def base_kernel(slots, psi, beta, kinetic, coefs, out):
    bands, _, span, span_z = psi.shape
    psi_rows, beta_rows = block_rows_of(psi, beta, slots)
    values = jnp.concatenate(
        [jnp.concatenate(psi_rows, axis=1), jnp.concatenate(beta_rows, axis=1)], axis=0
    )
    high, low = split(coefs[...])
    summed = dot_left(jnp.concatenate([high, high, low], axis=1), values)
    flat = out.reshape(bands * 2 * span, span_z)
    for y in range(span):
        flat[pl.ds(y, 2 * bands, stride=span), :] = (
            psi_rows[y] * kinetic[y : y + 1, :] + summed[:, y * span_z : (y + 1) * span_z]
        )


def whole(shape):
    return pl.BlockSpec(shape, lambda *_: (0,) * len(shape))


def subspace_solve(s_real, h_real, h_imag):
    factor = jnp.linalg.cholesky(s_real)
    solved = jax.scipy.linalg.cho_solve((factor, True), jnp.concatenate([h_real, h_imag], axis=1))
    order_size = s_real.shape[0]
    return (solved[:, :order_size], solved[:, order_size:])


def tdot(pattern, left, right):
    return jnp.einsum(pattern, left, right, precision=highest, preferred_element_type=jnp.float32)


def partner(values, devices, k):
    return lax.ppermute(values, "ga", [(d, d ^ k) for d in range(devices)])


def sum_over(values, devices, after):
    if devices & (devices - 1) or devices < 2:
        return lax.psum(values, "ga")
    step = 1
    while step < devices // 2:
        values = values + partner(values, devices, step)
        step *= 2
    held = pl.BlockSpec(memory_space=pltpu.VMEM)
    return pl.pallas_call(
        last_sum_kernel,
        out_shape=jax.ShapeDtypeStruct(values.shape, f32),
        in_specs=[held] * 2 + [pl.BlockSpec(memory_space=pl.ANY)],
        out_specs=held,
        name="last_sum",
    )(values, partner(values, devices, step), after)


def on_device(devices, orbitals, plane_order, potential, projectors, slot_owner, strengths):
    bands = orbitals.shape[0]
    planes = orbitals.shape[2]
    span_y = orbitals.shape[3]
    span_z = orbitals.shape[4]
    span_x = plane_order.shape[0]
    blocks, slots = slot_owner.shape
    owners = strengths.shape[0] * strengths.shape[1]
    rows = span_y // devices
    block_rows = 2 * planes * rows
    pairs = bands // 2
    block_span = projectors.shape[3] // span_z
    per_plane = span_y // block_span
    grid_x = jnp.arange(span_x, dtype=jnp.int32)
    grid_y = jnp.arange(span_y, dtype=jnp.int32)
    grid_z = jnp.arange(span_z, dtype=jnp.int32)
    params = pltpu.CompilerParams(vmem_limit_bytes=vmem_limit)
    tail_params = pltpu.CompilerParams(vmem_limit_bytes=vmem_limit // 2)

    def cost(flops, moved):
        return pl.CostEstimate(flops=flops, bytes_accessed=moved, transcendentals=0)

    order = np.arange(2 * span_y)
    order = (order % 2) * span_y + order // 2
    inv_y = left_const(left_table(span_y, 1.0)[order])
    fwd_y = left_const(left_table(span_y, -1.0)[:, order])
    inv_z = right_const(right_table(span_z, 1.0))
    fwd_z = right_const(right_table(span_z, -1.0))

    parts = 2 if pairs % 2 == 0 else 1
    share = pairs // parts
    arrived = []
    for c in range(parts):
        sent = pl.pallas_call(
            to_rows_kernel,
            out_shape=jax.ShapeDtypeStruct((devices, share, block_rows, span_z), f32),
            grid=(share,),
            in_specs=[
                pl.BlockSpec(
                    (2, 2, planes, span_y, span_z), lambda j, c=c: (c * share + j, 0, 0, 0, 0)
                ),
                whole(inv_y.shape),
            ],
            out_specs=pl.BlockSpec((devices, None, block_rows, span_z), lambda j: (0, j, 0, 0)),
            compiler_params=params,
            cost_estimate=cost(4 * 10**9, 3 * 10**6),
            name="to_rows",
        )(orbitals, inv_y)
        arrived.append(lax.all_to_all(sent, "ga", split_axis=0, concat_axis=0, tiled=True))

    stored = plane_order.reshape(devices, planes).T.reshape(-1)
    phases = (stored[:, None] * grid_x[None, :]) % span_x
    angles = phases.astype(f32) * (2.0 * math.pi / span_x)
    factor = 1.0 / math.sqrt(span_x)
    cosine, sine = jnp.cos(angles) * factor, jnp.sin(angles) * factor
    fwd_x = jnp.concatenate([cosine, -sine], axis=0)
    inv_x = jnp.concatenate([fwd_x, jnp.concatenate([sine, cosine], axis=0)], axis=1).T
    high, low = split_outside(fwd_x)
    fwd_x = jnp.concatenate([high, high, low], axis=1)
    high, low = split_outside(inv_x)
    inv_x = jnp.concatenate([high, high, low], axis=1)
    pot = potential.transpose(1, 0, 2).reshape(rows * span_x, span_z)

    local_order = lax.dynamic_slice_in_dim(plane_order, lax.axis_index("ga") * planes, planes)
    freq_x = signed_index(local_order, span_x).astype(f32) / span_x
    freq_y = signed_index(grid_y, span_y).astype(f32) / span_y
    freq_z = signed_index(grid_z, span_z).astype(f32) / span_z
    kinetic = 2.0 * (
        freq_x[:, None, None] ** 2 + freq_y[None, :, None] ** 2 + freq_z[None, None, :] ** 2
    )
    beta = projectors.reshape(blocks, slots, 2, block_span, span_z)
    beta = beta.transpose(0, 1, 3, 2, 4).reshape(blocks, slots * block_span * 2, span_z)
    block_specs = [
        pl.BlockSpec(
            (bands, 2, None, block_span, span_z),
            lambda g: (0, 0, g // per_plane, g % per_plane, 0),
        ),
        pl.BlockSpec((None, slots * block_span * 2, span_z), lambda g: (g, 0, 0)),
        pl.BlockSpec((None, block_span, span_z), lambda g: (g // per_plane, g % per_plane, 0)),
    ]
    products = pl.pallas_call(
        functools.partial(project_kernel, slots),
        out_shape=jax.ShapeDtypeStruct((blocks, 2 * slots + 2 * bands, 2 * bands), f32),
        grid=(blocks,),
        in_specs=block_specs,
        out_specs=pl.BlockSpec((None, 2 * slots + 2 * bands, 2 * bands), lambda g: (g, 0, 0)),
        compiler_params=params,
        cost_estimate=cost(8 * 10**9, 8 * 10**6),
        name="project",
    )(orbitals, beta, kinetic)
    with_real = products[:, :slots].reshape(blocks, slots, bands, 2)
    with_imag = products[:, slots : 2 * slots].reshape(blocks, slots, bands, 2)
    proj = jnp.concatenate(
        [
            with_real[..., 0] + with_imag[..., 1],
            with_real[..., 1] - with_imag[..., 0],
        ],
        axis=-1,
    )
    owned = (
        slot_owner[:, :, None] == jnp.arange(owners, dtype=jnp.int32)[None, None, :]
    ).astype(f32)
    proj = tdot("gsj,gsc->jc", owned, proj)
    kin = jnp.sum(products[:, 2 * slots :], axis=0).reshape(bands, 2, bands, 2)
    kin = kin[:, 0, :, 0] + kin[:, 1, :, 1]

    returned, fields = [], []
    for c in range(parts):
        back, field = pl.pallas_call(
            functools.partial(real_space_kernel, rows, planes),
            out_shape=(
                jax.ShapeDtypeStruct((devices, 2 * share, block_rows, span_z), f32),
                jax.ShapeDtypeStruct((2 * share, rows * span_x, span_z), f32),
            ),
            grid=(share,),
            in_specs=[
                pl.BlockSpec((devices, None, block_rows, span_z), lambda j: (0, j, 0, 0)),
                whole(pot.shape),
                whole(inv_x.shape),
                whole(fwd_x.shape),
                whole(inv_z.shape),
                whole(fwd_z.shape),
                whole(proj.shape),
            ],
            out_specs=(
                pl.BlockSpec((devices, 2, block_rows, span_z), lambda j: (0, j, 0, 0)),
                pl.BlockSpec((2, rows * span_x, span_z), lambda j: (j, 0, 0)),
            ),
            compiler_params=params,
            cost_estimate=cost(4 * 10**9, 8 * 10**6),
            name="real_space",
        )(arrived[c], pot, inv_x, fwd_x, inv_z, fwd_z, proj)
        returned.append(lax.all_to_all(back, "ga", split_axis=0, concat_axis=0, tiled=True))
        fields.append(field)

    grams = pl.pallas_call(
        functools.partial(real_gram_kernel, bands),
        out_shape=jax.ShapeDtypeStruct((2, bands, bands, 128), f32),
        compiler_params=params,
        cost_estimate=cost(10**7, 2 * 10**6),
        name="real_gram",
    )(*fields, pot)
    grams = jnp.sum(grams, axis=-1)
    own = jnp.concatenate([proj, jnp.concatenate([grams[0], grams[1] + kin], axis=1)], axis=0)
    total = sum_over(own, devices, returned[0])
    proj, s_real, h_real = total[:owners], total[owners:, :bands], total[owners:, bands:]
    weighted = strengths.reshape(-1)[:, None] * proj
    p_real, p_imag = proj[:, :bands], proj[:, bands:]
    w_real, w_imag = weighted[:, :bands], weighted[:, bands:]
    h_real = h_real + tdot("ja,jb->ab", p_real, w_real) + tdot("ja,jb->ab", p_imag, w_imag)
    h_imag = tdot("ja,jb->ab", p_real, w_imag) - tdot("ja,jb->ab", p_imag, w_real)
    m_real, m_imag = subspace_solve(s_real, h_real, h_imag)

    coefs = tdot("gsj,jc->gcs", owned, weighted)
    c_real, c_imag = coefs[:, :bands], coefs[:, bands:]
    from_beta = jnp.stack(
        [
            jnp.concatenate([c_real, -c_imag], axis=2),
            jnp.concatenate([c_imag, c_real], axis=2),
        ],
        axis=2,
    ).reshape(blocks, 2 * bands, 2 * slots)
    from_psi = jnp.stack(
        [
            jnp.stack([-m_real.T, m_imag.T], axis=-1),
            jnp.stack([-m_imag.T, -m_real.T], axis=-1),
        ],
        axis=1,
    ).reshape(1, 2 * bands, 2 * bands)
    coefs = jnp.concatenate(
        [jnp.broadcast_to(from_psi, (blocks, 2 * bands, 2 * bands)), from_beta], axis=2
    )
    base = pl.pallas_call(
        functools.partial(base_kernel, slots),
        out_shape=jax.ShapeDtypeStruct(orbitals.shape, f32),
        grid=(blocks,),
        in_specs=block_specs
        + [pl.BlockSpec((None, 2 * bands, 2 * bands + 2 * slots), lambda g: (g, 0, 0))],
        out_specs=block_specs[0],
        compiler_params=tail_params,
        cost_estimate=cost(8 * 10**9, 12 * 10**6),
        name="base",
    )(orbitals, beta, kinetic, coefs)

    residual = base
    for c in range(parts):
        two_bands = pl.BlockSpec(
            (2, 2, planes, span_y, span_z), lambda j, c=c: (share * c + j, 0, 0, 0, 0)
        )
        residual = pl.pallas_call(
            to_planes_kernel,
            out_shape=jax.ShapeDtypeStruct(orbitals.shape, f32),
            grid=(share,),
            in_specs=[
                pl.BlockSpec((devices, 2, block_rows, span_z), lambda j: (0, j, 0, 0)),
                two_bands,
                whole(fwd_y.shape),
            ],
            out_specs=two_bands,
            input_output_aliases={1: 0},
            compiler_params=tail_params,
            cost_estimate=cost(8 * 10**9, 12 * 10**6),
            name="to_planes",
        )(returned[c], residual, fwd_y)
    return (residual, jnp.stack([m_real, m_imag]))


def solution(mesh):
    return jax.shard_map(
        functools.partial(on_device, mesh.shape["ga"]),
        mesh=mesh,
        in_specs=(
            P("rep", None, "ga", None, None),
            P("rep"),
            P("rep", "ga", None),
            P(("rep", "ga"), None, None, None),
            P(("rep", "ga"), None),
            P("rep", None),
        ),
        out_specs=(P("rep", None, "ga", None, None), P(None, "rep", None)),
        check_vma=False,
    )
```

```python
import functools
import math

import jax
import jax.numpy as jnp
import numpy as np
from jax import lax
from jax.experimental import pallas as pl
from jax.experimental.pallas import tpu as pltpu
from jax.sharding import PartitionSpec as P

highest = lax.Precision.HIGHEST
f32 = jnp.float32
bf16 = jnp.bfloat16
vmem_limit = 63 * 1024 * 1024


def signed_index(values, length):
    return jnp.where(values < length // 2, values, values - length)


def dft(length, orient):
    index = np.arange(length)
    angles = (index[:, None] * index[None, :] % length) * (2.0 * math.pi / length)
    factor = 1.0 / math.sqrt(length)
    return np.cos(angles) * factor, orient * np.sin(angles) * factor


def left_table(length, orient):
    cosine, sine = dft(length, orient)
    return np.block([[cosine, -sine], [sine, cosine]])


def right_table(length, orient):
    cosine, sine = dft(length, orient)
    return np.block([[cosine, sine], [-sine, cosine]])


def split(values):
    high = values.astype(bf16)
    low = (values - high.astype(f32)).astype(bf16)
    return high, low


def split_outside(values):
    high = lax.reduce_precision(values, exponent_bits=8, mantissa_bits=7)
    return high.astype(bf16), (values - high).astype(bf16)


def const_parts(table):
    table = np.asarray(table, np.float32)
    high = table.astype(jnp.bfloat16)
    low = (table - high.astype(np.float32)).astype(jnp.bfloat16)
    return high, low


def left_const(table):
    high, low = const_parts(table)
    return jnp.asarray(np.concatenate([high, high, low], axis=1))


def right_const(table):
    high, low = const_parts(table)
    return jnp.asarray(np.concatenate([high, high, low], axis=0))


def dot_left(table, values):
    high, low = split(values)
    return jnp.dot(
        table, jnp.concatenate([high, low, high], axis=0), preferred_element_type=f32
    )


def dot_right(values, table):
    high, low = split(values)
    return jnp.dot(
        jnp.concatenate([high, low, high], axis=1), table, preferred_element_type=f32
    )


def groups(count, width):
    size = max(1, 256 // width)
    return [list(range(i, min(i + size, count))) for i in range(0, count, size)]


def parts_in_lanes(values, span, width):
    items = values.shape[1] // width
    return jnp.concatenate(
        [
            jnp.concatenate(
                [values[:span, i * width : (i + 1) * width], values[span:, i * width : (i + 1) * width]],
                axis=1,
            )
            for i in range(items)
        ],
        axis=0,
    )


def to_rows_kernel(psi, y_table, out):
    _, _, planes, span_y, span_z = psi.shape
    devices, block_rows, _ = out.shape
    each = block_rows // planes
    for group in groups(planes, span_z):
        real = jnp.concatenate([psi[0, 0, p] - psi[1, 1, p] for p in group], axis=1)
        imag = jnp.concatenate([psi[0, 1, p] + psi[1, 0, p] for p in group], axis=1)
        along_y = dot_left(y_table[...], jnp.concatenate([real, imag], axis=0))
        for i, p in enumerate(group):
            out[:, p * each : (p + 1) * each, :] = along_y[
                :, i * span_z : (i + 1) * span_z
            ].reshape(devices, each, span_z)


def real_space_kernel(rows, planes, recv, pot, inverse, forward, inv_z, fwd_z, _, back, field):
    devices, size, span_z = recv.shape
    span_x = devices * planes
    arrived = recv.reshape(devices * size, span_z)
    leaving = back.reshape(devices * 2 * size, span_z)
    columns = [
        jnp.concatenate(
            [
                arrived[pl.ds((p * rows + r) * 2 + part, devices, stride=size), :]
                for part in range(2)
                for p in range(planes)
            ],
            axis=0,
        )
        for r in range(rows)
    ]
    along_x = dot_left(inverse[...], jnp.concatenate(columns, axis=1))
    spatial = dot_right(parts_in_lanes(along_x, span_x, span_z), inv_z[...])
    spectral = []
    for band in range(2):
        one = spatial[:, band * span_z : (band + 1) * span_z]
        field[band] = one
        product = one * pot[...]
        product = jnp.concatenate(
            [product[r * span_x : (r + 1) * span_x] for r in range(rows)], axis=1
        )
        spectral.append(parts_in_lanes(dot_left(forward[...], product), span_x, span_z))
    spectral = dot_right(jnp.concatenate(spectral, axis=0), fwd_z[...])
    for band in range(2):
        for r in range(rows):
            for p in range(planes):
                first = ((band * rows + r) * planes + p) * devices
                for part in range(2):
                    start = band * size + (p * rows + r) * 2 + part
                    leaving[pl.ds(start, devices, stride=2 * size), :] = spectral[
                        first : first + devices, part * span_z : (part + 1) * span_z
                    ]


def real_gram_kernel(bands, *refs):
    fields, (pot, out) = refs[:-2], refs[-2:]
    held = fields[0].shape[0]
    pairs = [(a, b) for a in range(bands) for b in range(a, bands)]
    for weighted in range(2):

        def step(i, sums):
            rows = pl.ds(pl.multiple_of(i * 8, 8), 8)
            values = [fields[a // held][a % held, rows, :] for a in range(bands)]
            other = [v * pot[rows, :] for v in values] if weighted else values
            result = []
            for (a, b), total in zip(pairs, sums):
                product = values[a] * other[b]
                lanes = product[:, :128]
                for c in range(128, product.shape[1], 128):
                    lanes = lanes + product[:, c : c + 128]
                result.append(total + lanes)
            return tuple(result)

        sums = lax.fori_loop(
            0, pot.shape[0] // 8, step, tuple(jnp.zeros((8, 128), f32) for _ in pairs)
        )
        for (a, b), total in zip(pairs, sums):
            line = jnp.sum(total, axis=0, keepdims=True)
            out[weighted, a, b : b + 1, :] = line
            out[weighted, b, a : a + 1, :] = line


def to_planes_kernel(recv, base, y_table, *refs):
    out = refs[-1]
    bands, _, planes, span_y, span_z = base.shape
    each = recv.shape[2] // planes
    for band in range(bands):
        for group in groups(planes, span_z):
            columns = [
                recv[:, band, p * each : (p + 1) * each, :].reshape(2 * span_y, span_z)
                for p in group
            ]
            along_y = dot_left(y_table[...], jnp.concatenate(columns, axis=1))
            for i, p in enumerate(group):
                for part in range(2):
                    out[band, part, p] = base[band, part, p] + (
                        along_y[part * span_y : (part + 1) * span_y, i * span_z : (i + 1) * span_z]
                    )


def last_sum_kernel(first, second, _, out):
    out[...] = first[...] + second[...]


def block_rows_of(psi, beta, slots):
    bands, _, span, span_z = psi.shape
    psi_flat = psi.reshape(bands * 2 * span, span_z)
    psi_rows = [psi_flat[pl.ds(y, 2 * bands, stride=span), :] for y in range(span)]
    beta_rows = [
        jnp.concatenate(
            [beta[pl.ds(2 * y + part, slots, stride=2 * span), :] for part in range(2)], axis=0
        )
        for y in range(span)
    ]
    return psi_rows, beta_rows


def project_kernel(slots, psi, beta, kinetic, out):
    bands, _, span, span_z = psi.shape
    psi_rows, beta_rows = block_rows_of(psi, beta, slots)
    kin_rows = [psi_rows[y] * kinetic[y : y + 1, :] for y in range(span)]
    right = jnp.concatenate(split(jnp.concatenate(psi_rows, axis=1)), axis=0)
    left = jnp.concatenate(
        split(jnp.concatenate(beta_rows, axis=1)) + split(jnp.concatenate(kin_rows, axis=1)), axis=0
    )
    full = lax.dot_general(left, right, (((1,), (1,)), ((), ())), preferred_element_type=f32)
    width, height = 2 * bands, 2 * slots
    full = full[:, :width] + full[:, width:]
    out[0:height] = full[0:height] + full[height : 2 * height]
    rest = full[2 * height :]
    out[height:] = rest[0:width] + rest[width:]


def base_kernel(slots, psi, beta, kinetic, coefs, *outs):
    bands, _, span, span_z = psi.shape
    psi_rows, beta_rows = block_rows_of(psi, beta, slots)
    values = jnp.concatenate(
        [jnp.concatenate(psi_rows, axis=1), jnp.concatenate(beta_rows, axis=1)], axis=0
    )
    high, low = split(coefs[...])
    summed = dot_left(jnp.concatenate([high, high, low], axis=1), values)
    height = 2 * bands // len(outs)
    flat = [out.reshape(height * span, span_z) for out in outs]
    for y in range(span):
        values = psi_rows[y] * kinetic[y : y + 1, :] + summed[:, y * span_z : (y + 1) * span_z]
        for i, out in enumerate(flat):
            out[pl.ds(y, height, stride=span), :] = values[i * height : (i + 1) * height]


def whole(shape):
    return pl.BlockSpec(shape, lambda *_: (0,) * len(shape))


def subspace_solve(s_real, h_real, h_imag):
    factor = jnp.linalg.cholesky(s_real)
    solved = jax.scipy.linalg.cho_solve((factor, True), jnp.concatenate([h_real, h_imag], axis=1))
    order_size = s_real.shape[0]
    return (solved[:, :order_size], solved[:, order_size:])


def tdot(pattern, left, right):
    return jnp.einsum(pattern, left, right, precision=highest, preferred_element_type=jnp.float32)


def partner(values, devices, k):
    return lax.ppermute(values, "ga", [(d, d ^ k) for d in range(devices)])


def sum_over(values, devices, after):
    if devices & (devices - 1) or devices < 2:
        return lax.psum(values, "ga")
    step = 1
    while step < devices // 2:
        values = values + partner(values, devices, step)
        step *= 2
    held = pl.BlockSpec(memory_space=pltpu.VMEM)
    return pl.pallas_call(
        last_sum_kernel,
        out_shape=jax.ShapeDtypeStruct(values.shape, f32),
        in_specs=[held] * 2 + [pl.BlockSpec(memory_space=pl.ANY)],
        out_specs=held,
        name="last_sum",
    )(values, partner(values, devices, step), after)


def on_device(devices, orbitals, plane_order, potential, projectors, slot_owner, strengths):
    bands = orbitals.shape[0]
    planes = orbitals.shape[2]
    span_y = orbitals.shape[3]
    span_z = orbitals.shape[4]
    span_x = plane_order.shape[0]
    blocks, slots = slot_owner.shape
    owners = strengths.shape[0] * strengths.shape[1]
    rows = span_y // devices
    block_rows = 2 * planes * rows
    pairs = bands // 2
    block_span = projectors.shape[3] // span_z
    per_plane = span_y // block_span
    grid_x = jnp.arange(span_x, dtype=jnp.int32)
    grid_y = jnp.arange(span_y, dtype=jnp.int32)
    grid_z = jnp.arange(span_z, dtype=jnp.int32)
    params = pltpu.CompilerParams(vmem_limit_bytes=vmem_limit)
    tail_params = pltpu.CompilerParams(vmem_limit_bytes=vmem_limit // 2)

    def cost(flops, moved):
        return pl.CostEstimate(flops=flops, bytes_accessed=moved, transcendentals=0)

    order = np.arange(2 * span_y)
    order = (order % 2) * span_y + order // 2
    inv_y = left_const(left_table(span_y, 1.0)[order])
    fwd_y = left_const(left_table(span_y, -1.0)[:, order])
    inv_z = right_const(right_table(span_z, 1.0))
    fwd_z = right_const(right_table(span_z, -1.0))

    parts = 2 if pairs % 2 == 0 else 1
    share = pairs // parts
    arrived = []
    for c in range(parts):
        sent = pl.pallas_call(
            to_rows_kernel,
            out_shape=jax.ShapeDtypeStruct((devices, share, block_rows, span_z), f32),
            grid=(share,),
            in_specs=[
                pl.BlockSpec(
                    (2, 2, planes, span_y, span_z), lambda j, c=c: (c * share + j, 0, 0, 0, 0)
                ),
                whole(inv_y.shape),
            ],
            out_specs=pl.BlockSpec((devices, None, block_rows, span_z), lambda j: (0, j, 0, 0)),
            compiler_params=params,
            cost_estimate=cost(4 * 10**9, 3 * 10**6),
            name="to_rows",
        )(orbitals, inv_y)
        arrived.append(lax.all_to_all(sent, "ga", split_axis=0, concat_axis=0, tiled=True))

    stored = plane_order.reshape(devices, planes).T.reshape(-1)
    phases = (stored[:, None] * grid_x[None, :]) % span_x
    angles = phases.astype(f32) * (2.0 * math.pi / span_x)
    factor = 1.0 / math.sqrt(span_x)
    cosine, sine = jnp.cos(angles) * factor, jnp.sin(angles) * factor
    fwd_x = jnp.concatenate([cosine, -sine], axis=0)
    inv_x = jnp.concatenate([fwd_x, jnp.concatenate([sine, cosine], axis=0)], axis=1).T
    high, low = split_outside(fwd_x)
    fwd_x = jnp.concatenate([high, high, low], axis=1)
    high, low = split_outside(inv_x)
    inv_x = jnp.concatenate([high, high, low], axis=1)
    pot = potential.transpose(1, 0, 2).reshape(rows * span_x, span_z)

    local_order = lax.dynamic_slice_in_dim(plane_order, lax.axis_index("ga") * planes, planes)
    freq_x = signed_index(local_order, span_x).astype(f32) / span_x
    freq_y = signed_index(grid_y, span_y).astype(f32) / span_y
    freq_z = signed_index(grid_z, span_z).astype(f32) / span_z
    kinetic = 2.0 * (
        freq_x[:, None, None] ** 2 + freq_y[None, :, None] ** 2 + freq_z[None, None, :] ** 2
    )
    beta = projectors.reshape(blocks, slots, 2, block_span, span_z)
    beta = beta.transpose(0, 1, 3, 2, 4).reshape(blocks, slots * block_span * 2, span_z)
    block_specs = [
        pl.BlockSpec(
            (bands, 2, None, block_span, span_z),
            lambda g: (0, 0, g // per_plane, g % per_plane, 0),
        ),
        pl.BlockSpec((None, slots * block_span * 2, span_z), lambda g: (g, 0, 0)),
        pl.BlockSpec((None, block_span, span_z), lambda g: (g // per_plane, g % per_plane, 0)),
    ]
    products = pl.pallas_call(
        functools.partial(project_kernel, slots),
        out_shape=jax.ShapeDtypeStruct((blocks, 2 * slots + 2 * bands, 2 * bands), f32),
        grid=(blocks,),
        in_specs=block_specs,
        out_specs=pl.BlockSpec((None, 2 * slots + 2 * bands, 2 * bands), lambda g: (g, 0, 0)),
        compiler_params=params,
        cost_estimate=cost(8 * 10**9, 8 * 10**6),
        name="project",
    )(orbitals, beta, kinetic)
    with_real = products[:, :slots].reshape(blocks, slots, bands, 2)
    with_imag = products[:, slots : 2 * slots].reshape(blocks, slots, bands, 2)
    proj = jnp.concatenate(
        [
            with_real[..., 0] + with_imag[..., 1],
            with_real[..., 1] - with_imag[..., 0],
        ],
        axis=-1,
    )
    owned = (
        slot_owner[:, :, None] == jnp.arange(owners, dtype=jnp.int32)[None, None, :]
    ).astype(f32)
    proj = tdot("gsj,gsc->jc", owned, proj)
    kin = jnp.sum(products[:, 2 * slots :], axis=0).reshape(bands, 2, bands, 2)
    kin = kin[:, 0, :, 0] + kin[:, 1, :, 1]

    returned, fields = [], []
    for c in range(parts):
        back, field = pl.pallas_call(
            functools.partial(real_space_kernel, rows, planes),
            out_shape=(
                jax.ShapeDtypeStruct((devices, 2 * share, block_rows, span_z), f32),
                jax.ShapeDtypeStruct((2 * share, rows * span_x, span_z), f32),
            ),
            grid=(share,),
            in_specs=[
                pl.BlockSpec((devices, None, block_rows, span_z), lambda j: (0, j, 0, 0)),
                whole(pot.shape),
                whole(inv_x.shape),
                whole(fwd_x.shape),
                whole(inv_z.shape),
                whole(fwd_z.shape),
                whole(proj.shape),
            ],
            out_specs=(
                pl.BlockSpec((devices, 2, block_rows, span_z), lambda j: (0, j, 0, 0)),
                pl.BlockSpec((2, rows * span_x, span_z), lambda j: (j, 0, 0)),
            ),
            compiler_params=params,
            cost_estimate=cost(4 * 10**9, 8 * 10**6),
            name="real_space",
        )(arrived[c], pot, inv_x, fwd_x, inv_z, fwd_z, proj)
        returned.append(lax.all_to_all(back, "ga", split_axis=0, concat_axis=0, tiled=True))
        fields.append(field)

    grams = pl.pallas_call(
        functools.partial(real_gram_kernel, bands),
        out_shape=jax.ShapeDtypeStruct((2, bands, bands, 128), f32),
        compiler_params=params,
        cost_estimate=cost(10**7, 2 * 10**6),
        name="real_gram",
    )(*fields, pot)
    grams = jnp.sum(grams, axis=-1)
    own = jnp.concatenate([proj, jnp.concatenate([grams[0], grams[1] + kin], axis=1)], axis=0)
    total = sum_over(own, devices, returned[0])
    proj, s_real, h_real = total[:owners], total[owners:, :bands], total[owners:, bands:]
    weighted = strengths.reshape(-1)[:, None] * proj
    p_real, p_imag = proj[:, :bands], proj[:, bands:]
    w_real, w_imag = weighted[:, :bands], weighted[:, bands:]
    h_real = h_real + tdot("ja,jb->ab", p_real, w_real) + tdot("ja,jb->ab", p_imag, w_imag)
    h_imag = tdot("ja,jb->ab", p_real, w_imag) - tdot("ja,jb->ab", p_imag, w_real)
    m_real, m_imag = subspace_solve(s_real, h_real, h_imag)

    coefs = tdot("gsj,jc->gcs", owned, weighted)
    c_real, c_imag = coefs[:, :bands], coefs[:, bands:]
    from_beta = jnp.stack(
        [
            jnp.concatenate([c_real, -c_imag], axis=2),
            jnp.concatenate([c_imag, c_real], axis=2),
        ],
        axis=2,
    ).reshape(blocks, 2 * bands, 2 * slots)
    from_psi = jnp.stack(
        [
            jnp.stack([-m_real.T, m_imag.T], axis=-1),
            jnp.stack([-m_imag.T, -m_real.T], axis=-1),
        ],
        axis=1,
    ).reshape(1, 2 * bands, 2 * bands)
    coefs = jnp.concatenate(
        [jnp.broadcast_to(from_psi, (blocks, 2 * bands, 2 * bands)), from_beta], axis=2
    )
    held = bands // parts
    base = pl.pallas_call(
        functools.partial(base_kernel, slots),
        out_shape=[jax.ShapeDtypeStruct((held,) + orbitals.shape[1:], f32)] * parts,
        grid=(blocks,),
        in_specs=block_specs
        + [pl.BlockSpec((None, 2 * bands, 2 * bands + 2 * slots), lambda g: (g, 0, 0))],
        out_specs=[
            pl.BlockSpec(
                (held, 2, None, block_span, span_z),
                lambda g: (0, 0, g // per_plane, g % per_plane, 0),
            )
        ]
        * parts,
        compiler_params=tail_params,
        cost_estimate=cost(8 * 10**9, 12 * 10**6),
        name="base",
    )(orbitals, beta, kinetic, coefs)

    earlier = []
    for c in range(parts):

        def two_bands(first):
            return pl.BlockSpec(
                (2, 2, planes, span_y, span_z), lambda j: (first + j, 0, 0, 0, 0)
            )

        residual = pl.pallas_call(
            to_planes_kernel,
            out_shape=jax.ShapeDtypeStruct(orbitals.shape, f32),
            grid=(share,),
            in_specs=[
                pl.BlockSpec((devices, 2, block_rows, span_z), lambda j: (0, j, 0, 0)),
                two_bands(0),
                whole(fwd_y.shape),
            ]
            + [pl.BlockSpec(memory_space=pl.ANY)] * len(earlier),
            out_specs=two_bands(share * c),
            input_output_aliases={3: 0} if earlier else {},
            compiler_params=tail_params,
            cost_estimate=cost(8 * 10**9, 12 * 10**6),
            name="to_planes",
        )(returned[c], base[c], fwd_y, *earlier)
        earlier = [residual]
    return (residual, jnp.stack([m_real, m_imag]))


def solution(mesh):
    return jax.shard_map(
        functools.partial(on_device, mesh.shape["ga"]),
        mesh=mesh,
        in_specs=(
            P("rep", None, "ga", None, None),
            P("rep"),
            P("rep", "ga", None),
            P(("rep", "ga"), None, None, None),
            P(("rep", "ga"), None),
            P("rep", None),
        ),
        out_specs=(P("rep", None, "ga", None, None), P(None, "rep", None)),
        check_vma=False,
    )
```

```python
import functools
import math

import jax
import jax.numpy as jnp
import numpy as np
from jax import lax
from jax.experimental import pallas as pl
from jax.experimental.pallas import tpu as pltpu
from jax.sharding import PartitionSpec as P

highest = lax.Precision.HIGHEST
f32 = jnp.float32
bf16 = jnp.bfloat16
vmem_limit = 63 * 1024 * 1024


def signed_index(values, length):
    return jnp.where(values < length // 2, values, values - length)


def dft(length, orient):
    index = np.arange(length)
    angles = (index[:, None] * index[None, :] % length) * (2.0 * math.pi / length)
    factor = 1.0 / math.sqrt(length)
    return np.cos(angles) * factor, orient * np.sin(angles) * factor


def left_table(length, orient):
    cosine, sine = dft(length, orient)
    return np.block([[cosine, -sine], [sine, cosine]])


def right_table(length, orient):
    cosine, sine = dft(length, orient)
    return np.block([[cosine, sine], [-sine, cosine]])


def split(values):
    high = values.astype(bf16)
    low = (values - high.astype(f32)).astype(bf16)
    return high, low


def split_outside(values):
    high = lax.reduce_precision(values, exponent_bits=8, mantissa_bits=7)
    return high.astype(bf16), (values - high).astype(bf16)


def const_parts(table):
    table = np.asarray(table, np.float32)
    high = table.astype(jnp.bfloat16)
    low = (table - high.astype(np.float32)).astype(jnp.bfloat16)
    return high, low


def left_const(table):
    high, low = const_parts(table)
    return jnp.asarray(np.concatenate([high, high, low], axis=1))


def right_const(table):
    high, low = const_parts(table)
    return jnp.asarray(np.concatenate([high, high, low], axis=0))


def dot_left(table, values):
    high, low = split(values)
    return jnp.dot(
        table, jnp.concatenate([high, low, high], axis=0), preferred_element_type=f32
    )


def dot_right(values, table):
    high, low = split(values)
    return jnp.dot(
        jnp.concatenate([high, low, high], axis=1), table, preferred_element_type=f32
    )


def groups(count, width):
    size = max(1, 256 // width)
    return [list(range(i, min(i + size, count))) for i in range(0, count, size)]


def parts_in_lanes(values, span, width):
    items = values.shape[1] // width
    return jnp.concatenate(
        [
            jnp.concatenate(
                [values[:span, i * width : (i + 1) * width], values[span:, i * width : (i + 1) * width]],
                axis=1,
            )
            for i in range(items)
        ],
        axis=0,
    )


def to_rows_kernel(psi, y_table, out):
    _, _, planes, span_y, span_z = psi.shape
    devices, block_rows, _ = out.shape
    each = block_rows // planes
    for group in groups(planes, span_z):
        real = jnp.concatenate([psi[0, 0, p] - psi[1, 1, p] for p in group], axis=1)
        imag = jnp.concatenate([psi[0, 1, p] + psi[1, 0, p] for p in group], axis=1)
        along_y = dot_left(y_table[...], jnp.concatenate([real, imag], axis=0))
        for i, p in enumerate(group):
            out[:, p * each : (p + 1) * each, :] = along_y[
                :, i * span_z : (i + 1) * span_z
            ].reshape(devices, each, span_z)


def real_space_kernel(rows, planes, recv, pot, inverse, forward, inv_z, fwd_z, _, back, field):
    devices, size, span_z = recv.shape
    span_x = devices * planes
    arrived = recv.reshape(devices * size, span_z)
    leaving = back.reshape(devices * 2 * size, span_z)
    columns = [
        jnp.concatenate(
            [
                arrived[pl.ds((p * rows + r) * 2 + part, devices, stride=size), :]
                for part in range(2)
                for p in range(planes)
            ],
            axis=0,
        )
        for r in range(rows)
    ]
    along_x = dot_left(inverse[...], jnp.concatenate(columns, axis=1))
    spatial = dot_right(parts_in_lanes(along_x, span_x, span_z), inv_z[...])
    spectral = []
    for band in range(2):
        one = spatial[:, band * span_z : (band + 1) * span_z]
        field[band] = one
        product = one * pot[...]
        product = jnp.concatenate(
            [product[r * span_x : (r + 1) * span_x] for r in range(rows)], axis=1
        )
        spectral.append(parts_in_lanes(dot_left(forward[...], product), span_x, span_z))
    spectral = dot_right(jnp.concatenate(spectral, axis=0), fwd_z[...])
    for band in range(2):
        for r in range(rows):
            for p in range(planes):
                first = ((band * rows + r) * planes + p) * devices
                for part in range(2):
                    start = band * size + (p * rows + r) * 2 + part
                    leaving[pl.ds(start, devices, stride=2 * size), :] = spectral[
                        first : first + devices, part * span_z : (part + 1) * span_z
                    ]


def real_gram_kernel(bands, *refs):
    fields, (pot, out) = refs[:-2], refs[-2:]
    held = fields[0].shape[0]
    pairs = [(a, b) for a in range(bands) for b in range(a, bands)]
    for weighted in range(2):

        def step(i, sums):
            rows = pl.ds(pl.multiple_of(i * 8, 8), 8)
            values = [fields[a // held][a % held, rows, :] for a in range(bands)]
            other = [v * pot[rows, :] for v in values] if weighted else values
            result = []
            for (a, b), total in zip(pairs, sums):
                product = values[a] * other[b]
                lanes = product[:, :128]
                for c in range(128, product.shape[1], 128):
                    lanes = lanes + product[:, c : c + 128]
                result.append(total + lanes)
            return tuple(result)

        sums = lax.fori_loop(
            0, pot.shape[0] // 8, step, tuple(jnp.zeros((8, 128), f32) for _ in pairs)
        )
        for (a, b), total in zip(pairs, sums):
            line = jnp.sum(total, axis=0, keepdims=True)
            out[weighted, a, b : b + 1, :] = line
            out[weighted, b, a : a + 1, :] = line


def to_planes_kernel(recv, base, y_table, out):
    bands, _, planes, span_y, span_z = base.shape
    each = recv.shape[2] // planes
    for band in range(bands):
        for group in groups(planes, span_z):
            columns = [
                recv[:, band, p * each : (p + 1) * each, :].reshape(2 * span_y, span_z)
                for p in group
            ]
            along_y = dot_left(y_table[...], jnp.concatenate(columns, axis=1))
            for i, p in enumerate(group):
                for part in range(2):
                    out[band, part, p] = base[band, part, p] + (
                        along_y[part * span_y : (part + 1) * span_y, i * span_z : (i + 1) * span_z]
                    )


def last_sum_kernel(first, second, _, out):
    out[...] = first[...] + second[...]


def block_rows_of(psi, beta, slots):
    bands, _, span, span_z = psi.shape
    psi_flat = psi.reshape(bands * 2 * span, span_z)
    psi_rows = [psi_flat[pl.ds(y, 2 * bands, stride=span), :] for y in range(span)]
    beta_rows = [
        jnp.concatenate(
            [beta[pl.ds(2 * y + part, slots, stride=2 * span), :] for part in range(2)], axis=0
        )
        for y in range(span)
    ]
    return psi_rows, beta_rows


def project_kernel(slots, psi, beta, kinetic, out):
    bands, _, span, span_z = psi.shape
    psi_rows, beta_rows = block_rows_of(psi, beta, slots)
    kin_rows = [psi_rows[y] * kinetic[y : y + 1, :] for y in range(span)]
    right = jnp.concatenate(split(jnp.concatenate(psi_rows, axis=1)), axis=0)
    left = jnp.concatenate(
        split(jnp.concatenate(beta_rows, axis=1)) + split(jnp.concatenate(kin_rows, axis=1)), axis=0
    )
    full = lax.dot_general(left, right, (((1,), (1,)), ((), ())), preferred_element_type=f32)
    width, height = 2 * bands, 2 * slots
    full = full[:, :width] + full[:, width:]
    out[0:height] = full[0:height] + full[height : 2 * height]
    rest = full[2 * height :]
    out[height:] = rest[0:width] + rest[width:]


def base_kernel(slots, psi, beta, kinetic, coefs, out):
    bands, _, span, span_z = psi.shape
    psi_rows, beta_rows = block_rows_of(psi, beta, slots)
    values = jnp.concatenate(
        [jnp.concatenate(psi_rows, axis=1), jnp.concatenate(beta_rows, axis=1)], axis=0
    )
    high, low = split(coefs[...])
    summed = dot_left(jnp.concatenate([high, high, low], axis=1), values)
    flat = out.reshape(bands * 2 * span, span_z)
    for y in range(span):
        flat[pl.ds(y, 2 * bands, stride=span), :] = (
            psi_rows[y] * kinetic[y : y + 1, :] + summed[:, y * span_z : (y + 1) * span_z]
        )


def whole(shape):
    return pl.BlockSpec(shape, lambda *_: (0,) * len(shape))


def subspace_solve(s_real, h_real, h_imag):
    factor = jnp.linalg.cholesky(s_real)
    solved = jax.scipy.linalg.cho_solve((factor, True), jnp.concatenate([h_real, h_imag], axis=1))
    order_size = s_real.shape[0]
    return (solved[:, :order_size], solved[:, order_size:])


def tdot(pattern, left, right):
    return jnp.einsum(pattern, left, right, precision=highest, preferred_element_type=jnp.float32)


def partner(values, devices, k):
    return lax.ppermute(values, "ga", [(d, d ^ k) for d in range(devices)])


def sum_over(values, devices, after):
    if devices & (devices - 1) or devices < 2:
        return lax.psum(values, "ga")
    step = 1
    while step < devices // 2:
        values = values + partner(values, devices, step)
        step *= 2
    held = pl.BlockSpec(memory_space=pltpu.VMEM)
    return pl.pallas_call(
        last_sum_kernel,
        out_shape=jax.ShapeDtypeStruct(values.shape, f32),
        in_specs=[held] * 2 + [pl.BlockSpec(memory_space=pl.ANY)],
        out_specs=held,
        name="last_sum",
    )(values, partner(values, devices, step), after)


def on_device(devices, orbitals, plane_order, potential, projectors, slot_owner, strengths):
    bands = orbitals.shape[0]
    planes = orbitals.shape[2]
    span_y = orbitals.shape[3]
    span_z = orbitals.shape[4]
    span_x = plane_order.shape[0]
    blocks, slots = slot_owner.shape
    owners = strengths.shape[0] * strengths.shape[1]
    rows = span_y // devices
    block_rows = 2 * planes * rows
    pairs = bands // 2
    block_span = projectors.shape[3] // span_z
    per_plane = span_y // block_span
    grid_x = jnp.arange(span_x, dtype=jnp.int32)
    grid_y = jnp.arange(span_y, dtype=jnp.int32)
    grid_z = jnp.arange(span_z, dtype=jnp.int32)
    params = pltpu.CompilerParams(vmem_limit_bytes=vmem_limit)
    tail_params = pltpu.CompilerParams(vmem_limit_bytes=vmem_limit // 2)

    def cost(flops, moved):
        return pl.CostEstimate(flops=flops, bytes_accessed=moved, transcendentals=0)

    layers = 4 if devices % 4 == 0 else 1
    ranks = np.arange(devices).reshape(layers, -1).T.reshape(-1)
    order = np.arange(2 * span_y)
    order = (order % 2) * span_y + (ranks[:, None] * rows + np.arange(rows)).reshape(-1)[order // 2]

    def exchange(values):
        return lax.all_to_all(
            values,
            "ga",
            split_axis=0,
            concat_axis=0,
            axis_index_groups=[[int(rank) for rank in ranks]],
            tiled=True,
        )

    inv_y = left_const(left_table(span_y, 1.0)[order])
    fwd_y = left_const(left_table(span_y, -1.0)[:, order])
    inv_z = right_const(right_table(span_z, 1.0))
    fwd_z = right_const(right_table(span_z, -1.0))

    parts = 2 if pairs % 2 == 0 else 1
    share = pairs // parts
    arrived = []
    for c in range(parts):
        sent = pl.pallas_call(
            to_rows_kernel,
            out_shape=jax.ShapeDtypeStruct((devices, share, block_rows, span_z), f32),
            grid=(share,),
            in_specs=[
                pl.BlockSpec(
                    (2, 2, planes, span_y, span_z), lambda j, c=c: (c * share + j, 0, 0, 0, 0)
                ),
                whole(inv_y.shape),
            ],
            out_specs=pl.BlockSpec((devices, None, block_rows, span_z), lambda j: (0, j, 0, 0)),
            compiler_params=params,
            cost_estimate=cost(4 * 10**9, 3 * 10**6),
            name="to_rows",
        )(orbitals, inv_y)
        arrived.append(exchange(sent))

    stored = plane_order.reshape(devices, planes)[ranks].T.reshape(-1)
    phases = (stored[:, None] * grid_x[None, :]) % span_x
    angles = phases.astype(f32) * (2.0 * math.pi / span_x)
    factor = 1.0 / math.sqrt(span_x)
    cosine, sine = jnp.cos(angles) * factor, jnp.sin(angles) * factor
    fwd_x = jnp.concatenate([cosine, -sine], axis=0)
    inv_x = jnp.concatenate([fwd_x, jnp.concatenate([sine, cosine], axis=0)], axis=1).T
    high, low = split_outside(fwd_x)
    fwd_x = jnp.concatenate([high, high, low], axis=1)
    high, low = split_outside(inv_x)
    inv_x = jnp.concatenate([high, high, low], axis=1)
    pot = potential.transpose(1, 0, 2).reshape(rows * span_x, span_z)

    local_order = lax.dynamic_slice_in_dim(plane_order, lax.axis_index("ga") * planes, planes)
    freq_x = signed_index(local_order, span_x).astype(f32) / span_x
    freq_y = signed_index(grid_y, span_y).astype(f32) / span_y
    freq_z = signed_index(grid_z, span_z).astype(f32) / span_z
    kinetic = 2.0 * (
        freq_x[:, None, None] ** 2 + freq_y[None, :, None] ** 2 + freq_z[None, None, :] ** 2
    )
    beta = projectors.reshape(blocks, slots, 2, block_span, span_z)
    beta = beta.transpose(0, 1, 3, 2, 4).reshape(blocks, slots * block_span * 2, span_z)
    block_specs = [
        pl.BlockSpec(
            (bands, 2, None, block_span, span_z),
            lambda g: (0, 0, g // per_plane, g % per_plane, 0),
        ),
        pl.BlockSpec((None, slots * block_span * 2, span_z), lambda g: (g, 0, 0)),
        pl.BlockSpec((None, block_span, span_z), lambda g: (g // per_plane, g % per_plane, 0)),
    ]
    products = pl.pallas_call(
        functools.partial(project_kernel, slots),
        out_shape=jax.ShapeDtypeStruct((blocks, 2 * slots + 2 * bands, 2 * bands), f32),
        grid=(blocks,),
        in_specs=block_specs,
        out_specs=pl.BlockSpec((None, 2 * slots + 2 * bands, 2 * bands), lambda g: (g, 0, 0)),
        compiler_params=params,
        cost_estimate=cost(8 * 10**9, 8 * 10**6),
        name="project",
    )(orbitals, beta, kinetic)
    with_real = products[:, :slots].reshape(blocks, slots, bands, 2)
    with_imag = products[:, slots : 2 * slots].reshape(blocks, slots, bands, 2)
    proj = jnp.concatenate(
        [
            with_real[..., 0] + with_imag[..., 1],
            with_real[..., 1] - with_imag[..., 0],
        ],
        axis=-1,
    )
    owned = (
        slot_owner[:, :, None] == jnp.arange(owners, dtype=jnp.int32)[None, None, :]
    ).astype(f32)
    proj = tdot("gsj,gsc->jc", owned, proj)
    kin = jnp.sum(products[:, 2 * slots :], axis=0).reshape(bands, 2, bands, 2)
    kin = kin[:, 0, :, 0] + kin[:, 1, :, 1]

    returned, fields = [], []
    for c in range(parts):
        back, field = pl.pallas_call(
            functools.partial(real_space_kernel, rows, planes),
            out_shape=(
                jax.ShapeDtypeStruct((devices, 2 * share, block_rows, span_z), f32),
                jax.ShapeDtypeStruct((2 * share, rows * span_x, span_z), f32),
            ),
            grid=(share,),
            in_specs=[
                pl.BlockSpec((devices, None, block_rows, span_z), lambda j: (0, j, 0, 0)),
                whole(pot.shape),
                whole(inv_x.shape),
                whole(fwd_x.shape),
                whole(inv_z.shape),
                whole(fwd_z.shape),
                whole(proj.shape),
            ],
            out_specs=(
                pl.BlockSpec((devices, 2, block_rows, span_z), lambda j: (0, j, 0, 0)),
                pl.BlockSpec((2, rows * span_x, span_z), lambda j: (j, 0, 0)),
            ),
            compiler_params=params,
            cost_estimate=cost(4 * 10**9, 8 * 10**6),
            name="real_space",
        )(arrived[c], pot, inv_x, fwd_x, inv_z, fwd_z, proj)
        returned.append(exchange(back))
        fields.append(field)

    grams = pl.pallas_call(
        functools.partial(real_gram_kernel, bands),
        out_shape=jax.ShapeDtypeStruct((2, bands, bands, 128), f32),
        compiler_params=params,
        cost_estimate=cost(10**7, 2 * 10**6),
        name="real_gram",
    )(*fields, pot)
    grams = jnp.sum(grams, axis=-1)
    own = jnp.concatenate([proj, jnp.concatenate([grams[0], grams[1] + kin], axis=1)], axis=0)
    total = sum_over(own, devices, returned[0])
    proj, s_real, h_real = total[:owners], total[owners:, :bands], total[owners:, bands:]
    weighted = strengths.reshape(-1)[:, None] * proj
    p_real, p_imag = proj[:, :bands], proj[:, bands:]
    w_real, w_imag = weighted[:, :bands], weighted[:, bands:]
    h_real = h_real + tdot("ja,jb->ab", p_real, w_real) + tdot("ja,jb->ab", p_imag, w_imag)
    h_imag = tdot("ja,jb->ab", p_real, w_imag) - tdot("ja,jb->ab", p_imag, w_real)
    m_real, m_imag = subspace_solve(s_real, h_real, h_imag)

    coefs = tdot("gsj,jc->gcs", owned, weighted)
    c_real, c_imag = coefs[:, :bands], coefs[:, bands:]
    from_beta = jnp.stack(
        [
            jnp.concatenate([c_real, -c_imag], axis=2),
            jnp.concatenate([c_imag, c_real], axis=2),
        ],
        axis=2,
    ).reshape(blocks, 2 * bands, 2 * slots)
    from_psi = jnp.stack(
        [
            jnp.stack([-m_real.T, m_imag.T], axis=-1),
            jnp.stack([-m_imag.T, -m_real.T], axis=-1),
        ],
        axis=1,
    ).reshape(1, 2 * bands, 2 * bands)
    coefs = jnp.concatenate(
        [jnp.broadcast_to(from_psi, (blocks, 2 * bands, 2 * bands)), from_beta], axis=2
    )
    base = pl.pallas_call(
        functools.partial(base_kernel, slots),
        out_shape=jax.ShapeDtypeStruct(orbitals.shape, f32),
        grid=(blocks,),
        in_specs=block_specs
        + [pl.BlockSpec((None, 2 * bands, 2 * bands + 2 * slots), lambda g: (g, 0, 0))],
        out_specs=block_specs[0],
        compiler_params=tail_params,
        cost_estimate=cost(8 * 10**9, 12 * 10**6),
        name="base",
    )(orbitals, beta, kinetic, coefs)

    residual = base
    for c in range(parts):
        two_bands = pl.BlockSpec(
            (2, 2, planes, span_y, span_z), lambda j, c=c: (share * c + j, 0, 0, 0, 0)
        )
        residual = pl.pallas_call(
            to_planes_kernel,
            out_shape=jax.ShapeDtypeStruct(orbitals.shape, f32),
            grid=(share,),
            in_specs=[
                pl.BlockSpec((devices, 2, block_rows, span_z), lambda j: (0, j, 0, 0)),
                two_bands,
                whole(fwd_y.shape),
            ],
            out_specs=two_bands,
            input_output_aliases={1: 0},
            compiler_params=tail_params,
            cost_estimate=cost(8 * 10**9, 12 * 10**6),
            name="to_planes",
        )(returned[c], residual, fwd_y)
    return (residual, jnp.stack([m_real, m_imag]))


def solution(mesh):
    return jax.shard_map(
        functools.partial(on_device, mesh.shape["ga"]),
        mesh=mesh,
        in_specs=(
            P("rep", None, "ga", None, None),
            P("rep"),
            P("rep", "ga", None),
            P(("rep", "ga"), None, None, None),
            P(("rep", "ga"), None),
            P("rep", None),
        ),
        out_specs=(P("rep", None, "ga", None, None), P(None, "rep", None)),
        check_vma=False,
    )
```

```python
import functools
import math

import jax
import jax.numpy as jnp
import numpy as np
from jax import lax
from jax.experimental import pallas as pl
from jax.experimental.pallas import tpu as pltpu
from jax.sharding import PartitionSpec as P

highest = lax.Precision.HIGHEST
f32 = jnp.float32
bf16 = jnp.bfloat16
vmem_limit = 63 * 1024 * 1024


def signed_index(values, length):
    return jnp.where(values < length // 2, values, values - length)


def dft(length, orient):
    index = np.arange(length)
    angles = (index[:, None] * index[None, :] % length) * (2.0 * math.pi / length)
    factor = 1.0 / math.sqrt(length)
    return np.cos(angles) * factor, orient * np.sin(angles) * factor


def left_table(length, orient):
    cosine, sine = dft(length, orient)
    return np.block([[cosine, -sine], [sine, cosine]])


def right_table(length, orient):
    cosine, sine = dft(length, orient)
    return np.block([[cosine, sine], [-sine, cosine]])


def split(values):
    high = values.astype(bf16)
    low = (values - high.astype(f32)).astype(bf16)
    return high, low


def split_outside(values):
    high = lax.reduce_precision(values, exponent_bits=8, mantissa_bits=7)
    return high.astype(bf16), (values - high).astype(bf16)


def const_parts(table):
    table = np.asarray(table, np.float32)
    high = table.astype(jnp.bfloat16)
    low = (table - high.astype(np.float32)).astype(jnp.bfloat16)
    return high, low


def left_const(table):
    high, low = const_parts(table)
    return jnp.asarray(np.concatenate([high, high, low], axis=1))


def right_const(table):
    high, low = const_parts(table)
    return jnp.asarray(np.concatenate([high, high, low], axis=0))


def dot_left(table, values):
    high, low = split(values)
    return jnp.dot(
        table, jnp.concatenate([high, low, high], axis=0), preferred_element_type=f32
    )


def dot_right(values, table):
    high, low = split(values)
    return jnp.dot(
        jnp.concatenate([high, low, high], axis=1), table, preferred_element_type=f32
    )


def groups(count, width):
    size = max(1, 256 // width)
    return [list(range(i, min(i + size, count))) for i in range(0, count, size)]


def parts_in_lanes(values, span, width):
    items = values.shape[1] // width
    return jnp.concatenate(
        [
            jnp.concatenate(
                [values[:span, i * width : (i + 1) * width], values[span:, i * width : (i + 1) * width]],
                axis=1,
            )
            for i in range(items)
        ],
        axis=0,
    )


def to_rows_kernel(psi, y_table, out):
    _, _, planes, span_y, span_z = psi.shape
    devices, block_rows, _ = out.shape
    each = block_rows // planes
    for group in groups(planes, span_z):
        real = jnp.concatenate([psi[0, 0, p] - psi[1, 1, p] for p in group], axis=1)
        imag = jnp.concatenate([psi[0, 1, p] + psi[1, 0, p] for p in group], axis=1)
        along_y = dot_left(y_table[...], jnp.concatenate([real, imag], axis=0))
        for i, p in enumerate(group):
            out[:, p * each : (p + 1) * each, :] = along_y[
                :, i * span_z : (i + 1) * span_z
            ].reshape(devices, each, span_z)


def real_space_kernel(rows, planes, recv, pot, inverse, forward, inv_z, fwd_z, _, back, field):
    devices, size, span_z = recv.shape
    span_x = devices * planes
    arrived = recv.reshape(devices * size, span_z)
    leaving = back.reshape(devices * 2 * size, span_z)
    columns = [
        jnp.concatenate(
            [
                arrived[pl.ds((p * rows + r) * 2 + part, devices, stride=size), :]
                for part in range(2)
                for p in range(planes)
            ],
            axis=0,
        )
        for r in range(rows)
    ]
    along_x = dot_left(inverse[...], jnp.concatenate(columns, axis=1))
    spatial = dot_right(parts_in_lanes(along_x, span_x, span_z), inv_z[...])
    spectral = []
    for band in range(2):
        one = spatial[:, band * span_z : (band + 1) * span_z]
        field[band] = one
        product = one * pot[...]
        product = jnp.concatenate(
            [product[r * span_x : (r + 1) * span_x] for r in range(rows)], axis=1
        )
        spectral.append(parts_in_lanes(dot_left(forward[...], product), span_x, span_z))
    spectral = dot_right(jnp.concatenate(spectral, axis=0), fwd_z[...])
    for band in range(2):
        for r in range(rows):
            for p in range(planes):
                first = ((band * rows + r) * planes + p) * devices
                for part in range(2):
                    start = band * size + (p * rows + r) * 2 + part
                    leaving[pl.ds(start, devices, stride=2 * size), :] = spectral[
                        first : first + devices, part * span_z : (part + 1) * span_z
                    ]


def real_gram_kernel(bands, *refs):
    fields, (pot, out) = refs[:-2], refs[-2:]
    held = fields[0].shape[0]
    pairs = [(a, b) for a in range(bands) for b in range(a, bands)]
    for weighted in range(2):

        def step(i, sums):
            rows = pl.ds(pl.multiple_of(i * 8, 8), 8)
            values = [fields[a // held][a % held, rows, :] for a in range(bands)]
            other = [v * pot[rows, :] for v in values] if weighted else values
            result = []
            for (a, b), total in zip(pairs, sums):
                product = values[a] * other[b]
                lanes = product[:, :128]
                for c in range(128, product.shape[1], 128):
                    lanes = lanes + product[:, c : c + 128]
                result.append(total + lanes)
            return tuple(result)

        sums = lax.fori_loop(
            0, pot.shape[0] // 8, step, tuple(jnp.zeros((8, 128), f32) for _ in pairs)
        )
        for (a, b), total in zip(pairs, sums):
            line = jnp.sum(total, axis=0, keepdims=True)
            out[weighted, a, b : b + 1, :] = line
            out[weighted, b, a : a + 1, :] = line


def to_planes_kernel(recv, base, y_table, out):
    bands, _, planes, span_y, span_z = base.shape
    each = recv.shape[2] // planes
    for band in range(bands):
        for group in groups(planes, span_z):
            columns = [
                recv[:, band, p * each : (p + 1) * each, :].reshape(2 * span_y, span_z)
                for p in group
            ]
            along_y = dot_left(y_table[...], jnp.concatenate(columns, axis=1))
            for i, p in enumerate(group):
                for part in range(2):
                    out[band, part, p] = base[band, part, p] + (
                        along_y[part * span_y : (part + 1) * span_y, i * span_z : (i + 1) * span_z]
                    )


def last_sum_kernel(first, second, _, out):
    out[...] = first[...] + second[...]


def block_rows_of(psi, beta, slots):
    bands, _, span, span_z = psi.shape
    psi_flat = psi.reshape(bands * 2 * span, span_z)
    psi_rows = [psi_flat[pl.ds(y, 2 * bands, stride=span), :] for y in range(span)]
    beta_rows = [
        jnp.concatenate(
            [beta[pl.ds(2 * y + part, slots, stride=2 * span), :] for part in range(2)], axis=0
        )
        for y in range(span)
    ]
    return psi_rows, beta_rows


def project_kernel(slots, psi, beta, kinetic, out):
    bands, _, span, span_z = psi.shape
    psi_rows, beta_rows = block_rows_of(psi, beta, slots)
    kin_rows = [psi_rows[y] * kinetic[y : y + 1, :] for y in range(span)]
    right = jnp.concatenate(split(jnp.concatenate(psi_rows, axis=1)), axis=0)
    left = jnp.concatenate(
        split(jnp.concatenate(beta_rows, axis=1)) + split(jnp.concatenate(kin_rows, axis=1)), axis=0
    )
    full = lax.dot_general(left, right, (((1,), (1,)), ((), ())), preferred_element_type=f32)
    width, height = 2 * bands, 2 * slots
    full = full[:, :width] + full[:, width:]
    out[0:height] = full[0:height] + full[height : 2 * height]
    rest = full[2 * height :]
    out[height:] = rest[0:width] + rest[width:]


def base_kernel(slots, psi, beta, kinetic, coefs, out):
    bands, _, span, span_z = psi.shape
    psi_rows, beta_rows = block_rows_of(psi, beta, slots)
    values = jnp.concatenate(
        [jnp.concatenate(psi_rows, axis=1), jnp.concatenate(beta_rows, axis=1)], axis=0
    )
    high, low = split(coefs[...])
    summed = dot_left(jnp.concatenate([high, high, low], axis=1), values)
    flat = out.reshape(bands * 2 * span, span_z)
    for y in range(span):
        flat[pl.ds(y, 2 * bands, stride=span), :] = (
            psi_rows[y] * kinetic[y : y + 1, :] + summed[:, y * span_z : (y + 1) * span_z]
        )


def whole(shape):
    return pl.BlockSpec(shape, lambda *_: (0,) * len(shape))


def subspace_solve(s_real, h_real, h_imag):
    factor = jnp.linalg.cholesky(s_real)
    solved = jax.scipy.linalg.cho_solve((factor, True), jnp.concatenate([h_real, h_imag], axis=1))
    order_size = s_real.shape[0]
    return (solved[:, :order_size], solved[:, order_size:])


def tdot(pattern, left, right):
    return jnp.einsum(pattern, left, right, precision=highest, preferred_element_type=jnp.float32)


def partner(values, devices, k):
    return lax.ppermute(values, "ga", [(d, d ^ k) for d in range(devices)])


def sum_over(values, devices, after):
    if devices & (devices - 1) or devices < 2:
        return lax.psum(values, "ga")
    step = 1
    while step < devices // 2:
        values = values + partner(values, devices, step)
        step *= 2
    held = pl.BlockSpec(memory_space=pltpu.VMEM)
    return pl.pallas_call(
        last_sum_kernel,
        out_shape=jax.ShapeDtypeStruct(values.shape, f32),
        in_specs=[held] * 2 + [pl.BlockSpec(memory_space=pl.ANY)],
        out_specs=held,
        name="last_sum",
    )(values, partner(values, devices, step), after)


def on_device(devices, orbitals, plane_order, potential, projectors, slot_owner, strengths):
    bands = orbitals.shape[0]
    planes = orbitals.shape[2]
    span_y = orbitals.shape[3]
    span_z = orbitals.shape[4]
    span_x = plane_order.shape[0]
    blocks, slots = slot_owner.shape
    owners = strengths.shape[0] * strengths.shape[1]
    rows = span_y // devices
    block_rows = 2 * planes * rows
    pairs = bands // 2
    block_span = projectors.shape[3] // span_z
    per_plane = span_y // block_span
    grid_x = jnp.arange(span_x, dtype=jnp.int32)
    grid_y = jnp.arange(span_y, dtype=jnp.int32)
    grid_z = jnp.arange(span_z, dtype=jnp.int32)
    params = pltpu.CompilerParams(vmem_limit_bytes=vmem_limit)
    tail_params = pltpu.CompilerParams(vmem_limit_bytes=vmem_limit // 2)

    def cost(flops, moved):
        return pl.CostEstimate(flops=flops, bytes_accessed=moved, transcendentals=0)

    layers = 4 if devices % 4 == 0 else 1
    ranks = np.arange(devices).reshape(layers, -1)[[0, 2, 1, 3] if layers == 4 else [0]].T.reshape(-1)
    order = np.arange(2 * span_y)
    order = (order % 2) * span_y + (ranks[:, None] * rows + np.arange(rows)).reshape(-1)[order // 2]

    def exchange(values):
        return lax.all_to_all(
            values,
            "ga",
            split_axis=0,
            concat_axis=0,
            axis_index_groups=[[int(rank) for rank in ranks]],
            tiled=True,
        )

    inv_y = left_const(left_table(span_y, 1.0)[order])
    fwd_y = left_const(left_table(span_y, -1.0)[:, order])
    inv_z = right_const(right_table(span_z, 1.0))
    fwd_z = right_const(right_table(span_z, -1.0))

    parts = 2 if pairs % 2 == 0 else 1
    share = pairs // parts
    arrived = []
    for c in range(parts):
        sent = pl.pallas_call(
            to_rows_kernel,
            out_shape=jax.ShapeDtypeStruct((devices, share, block_rows, span_z), f32),
            grid=(share,),
            in_specs=[
                pl.BlockSpec(
                    (2, 2, planes, span_y, span_z), lambda j, c=c: (c * share + j, 0, 0, 0, 0)
                ),
                whole(inv_y.shape),
            ],
            out_specs=pl.BlockSpec((devices, None, block_rows, span_z), lambda j: (0, j, 0, 0)),
            compiler_params=params,
            cost_estimate=cost(4 * 10**9, 3 * 10**6),
            name="to_rows",
        )(orbitals, inv_y)
        arrived.append(exchange(sent))

    stored = plane_order.reshape(devices, planes)[ranks].T.reshape(-1)
    phases = (stored[:, None] * grid_x[None, :]) % span_x
    angles = phases.astype(f32) * (2.0 * math.pi / span_x)
    factor = 1.0 / math.sqrt(span_x)
    cosine, sine = jnp.cos(angles) * factor, jnp.sin(angles) * factor
    fwd_x = jnp.concatenate([cosine, -sine], axis=0)
    inv_x = jnp.concatenate([fwd_x, jnp.concatenate([sine, cosine], axis=0)], axis=1).T
    high, low = split_outside(fwd_x)
    fwd_x = jnp.concatenate([high, high, low], axis=1)
    high, low = split_outside(inv_x)
    inv_x = jnp.concatenate([high, high, low], axis=1)
    pot = potential.transpose(1, 0, 2).reshape(rows * span_x, span_z)

    local_order = lax.dynamic_slice_in_dim(plane_order, lax.axis_index("ga") * planes, planes)
    freq_x = signed_index(local_order, span_x).astype(f32) / span_x
    freq_y = signed_index(grid_y, span_y).astype(f32) / span_y
    freq_z = signed_index(grid_z, span_z).astype(f32) / span_z
    kinetic = 2.0 * (
        freq_x[:, None, None] ** 2 + freq_y[None, :, None] ** 2 + freq_z[None, None, :] ** 2
    )
    beta = projectors.reshape(blocks, slots, 2, block_span, span_z)
    beta = beta.transpose(0, 1, 3, 2, 4).reshape(blocks, slots * block_span * 2, span_z)
    block_specs = [
        pl.BlockSpec(
            (bands, 2, None, block_span, span_z),
            lambda g: (0, 0, g // per_plane, g % per_plane, 0),
        ),
        pl.BlockSpec((None, slots * block_span * 2, span_z), lambda g: (g, 0, 0)),
        pl.BlockSpec((None, block_span, span_z), lambda g: (g // per_plane, g % per_plane, 0)),
    ]
    products = pl.pallas_call(
        functools.partial(project_kernel, slots),
        out_shape=jax.ShapeDtypeStruct((blocks, 2 * slots + 2 * bands, 2 * bands), f32),
        grid=(blocks,),
        in_specs=block_specs,
        out_specs=pl.BlockSpec((None, 2 * slots + 2 * bands, 2 * bands), lambda g: (g, 0, 0)),
        compiler_params=params,
        cost_estimate=cost(8 * 10**9, 8 * 10**6),
        name="project",
    )(orbitals, beta, kinetic)
    with_real = products[:, :slots].reshape(blocks, slots, bands, 2)
    with_imag = products[:, slots : 2 * slots].reshape(blocks, slots, bands, 2)
    proj = jnp.concatenate(
        [
            with_real[..., 0] + with_imag[..., 1],
            with_real[..., 1] - with_imag[..., 0],
        ],
        axis=-1,
    )
    owned = (
        slot_owner[:, :, None] == jnp.arange(owners, dtype=jnp.int32)[None, None, :]
    ).astype(f32)
    proj = tdot("gsj,gsc->jc", owned, proj)
    kin = jnp.sum(products[:, 2 * slots :], axis=0).reshape(bands, 2, bands, 2)
    kin = kin[:, 0, :, 0] + kin[:, 1, :, 1]

    returned, fields = [], []
    for c in range(parts):
        back, field = pl.pallas_call(
            functools.partial(real_space_kernel, rows, planes),
            out_shape=(
                jax.ShapeDtypeStruct((devices, 2 * share, block_rows, span_z), f32),
                jax.ShapeDtypeStruct((2 * share, rows * span_x, span_z), f32),
            ),
            grid=(share,),
            in_specs=[
                pl.BlockSpec((devices, None, block_rows, span_z), lambda j: (0, j, 0, 0)),
                whole(pot.shape),
                whole(inv_x.shape),
                whole(fwd_x.shape),
                whole(inv_z.shape),
                whole(fwd_z.shape),
                whole(proj.shape),
            ],
            out_specs=(
                pl.BlockSpec((devices, 2, block_rows, span_z), lambda j: (0, j, 0, 0)),
                pl.BlockSpec((2, rows * span_x, span_z), lambda j: (j, 0, 0)),
            ),
            compiler_params=params,
            cost_estimate=cost(4 * 10**9, 8 * 10**6),
            name="real_space",
        )(arrived[c], pot, inv_x, fwd_x, inv_z, fwd_z, proj)
        returned.append(exchange(back))
        fields.append(field)

    grams = pl.pallas_call(
        functools.partial(real_gram_kernel, bands),
        out_shape=jax.ShapeDtypeStruct((2, bands, bands, 128), f32),
        compiler_params=params,
        cost_estimate=cost(10**7, 2 * 10**6),
        name="real_gram",
    )(*fields, pot)
    grams = jnp.sum(grams, axis=-1)
    own = jnp.concatenate([proj, jnp.concatenate([grams[0], grams[1] + kin], axis=1)], axis=0)
    total = sum_over(own, devices, returned[0])
    proj, s_real, h_real = total[:owners], total[owners:, :bands], total[owners:, bands:]
    weighted = strengths.reshape(-1)[:, None] * proj
    p_real, p_imag = proj[:, :bands], proj[:, bands:]
    w_real, w_imag = weighted[:, :bands], weighted[:, bands:]
    h_real = h_real + tdot("ja,jb->ab", p_real, w_real) + tdot("ja,jb->ab", p_imag, w_imag)
    h_imag = tdot("ja,jb->ab", p_real, w_imag) - tdot("ja,jb->ab", p_imag, w_real)
    m_real, m_imag = subspace_solve(s_real, h_real, h_imag)

    coefs = tdot("gsj,jc->gcs", owned, weighted)
    c_real, c_imag = coefs[:, :bands], coefs[:, bands:]
    from_beta = jnp.stack(
        [
            jnp.concatenate([c_real, -c_imag], axis=2),
            jnp.concatenate([c_imag, c_real], axis=2),
        ],
        axis=2,
    ).reshape(blocks, 2 * bands, 2 * slots)
    from_psi = jnp.stack(
        [
            jnp.stack([-m_real.T, m_imag.T], axis=-1),
            jnp.stack([-m_imag.T, -m_real.T], axis=-1),
        ],
        axis=1,
    ).reshape(1, 2 * bands, 2 * bands)
    coefs = jnp.concatenate(
        [jnp.broadcast_to(from_psi, (blocks, 2 * bands, 2 * bands)), from_beta], axis=2
    )
    base = pl.pallas_call(
        functools.partial(base_kernel, slots),
        out_shape=jax.ShapeDtypeStruct(orbitals.shape, f32),
        grid=(blocks,),
        in_specs=block_specs
        + [pl.BlockSpec((None, 2 * bands, 2 * bands + 2 * slots), lambda g: (g, 0, 0))],
        out_specs=block_specs[0],
        compiler_params=tail_params,
        cost_estimate=cost(8 * 10**9, 12 * 10**6),
        name="base",
    )(orbitals, beta, kinetic, coefs)

    residual = base
    for c in range(parts):
        two_bands = pl.BlockSpec(
            (2, 2, planes, span_y, span_z), lambda j, c=c: (share * c + j, 0, 0, 0, 0)
        )
        residual = pl.pallas_call(
            to_planes_kernel,
            out_shape=jax.ShapeDtypeStruct(orbitals.shape, f32),
            grid=(share,),
            in_specs=[
                pl.BlockSpec((devices, 2, block_rows, span_z), lambda j: (0, j, 0, 0)),
                two_bands,
                whole(fwd_y.shape),
            ],
            out_specs=two_bands,
            input_output_aliases={1: 0},
            compiler_params=tail_params,
            cost_estimate=cost(8 * 10**9, 12 * 10**6),
            name="to_planes",
        )(returned[c], residual, fwd_y)
    return (residual, jnp.stack([m_real, m_imag]))


def solution(mesh):
    return jax.shard_map(
        functools.partial(on_device, mesh.shape["ga"]),
        mesh=mesh,
        in_specs=(
            P("rep", None, "ga", None, None),
            P("rep"),
            P("rep", "ga", None),
            P(("rep", "ga"), None, None, None),
            P(("rep", "ga"), None),
            P("rep", None),
        ),
        out_specs=(P("rep", None, "ga", None, None), P(None, "rep", None)),
        check_vma=False,
    )
```

```python
import functools
import math

import jax
import jax.numpy as jnp
import numpy as np
from jax import lax
from jax.experimental import pallas as pl
from jax.experimental.pallas import tpu as pltpu
from jax.sharding import PartitionSpec as P

highest = lax.Precision.HIGHEST
f32 = jnp.float32
bf16 = jnp.bfloat16
vmem_limit = 63 * 1024 * 1024


def signed_index(values, length):
    return jnp.where(values < length // 2, values, values - length)


def dft(length, orient):
    index = np.arange(length)
    angles = (index[:, None] * index[None, :] % length) * (2.0 * math.pi / length)
    factor = 1.0 / math.sqrt(length)
    return np.cos(angles) * factor, orient * np.sin(angles) * factor


def left_table(length, orient):
    cosine, sine = dft(length, orient)
    return np.block([[cosine, -sine], [sine, cosine]])


def right_table(length, orient):
    cosine, sine = dft(length, orient)
    return np.block([[cosine, sine], [-sine, cosine]])


def split(values):
    high = values.astype(bf16)
    low = (values - high.astype(f32)).astype(bf16)
    return high, low


def split_outside(values):
    high = lax.reduce_precision(values, exponent_bits=8, mantissa_bits=7)
    return high.astype(bf16), (values - high).astype(bf16)


def const_parts(table):
    table = np.asarray(table, np.float32)
    high = table.astype(jnp.bfloat16)
    low = (table - high.astype(np.float32)).astype(jnp.bfloat16)
    return high, low


def left_const(table):
    high, low = const_parts(table)
    return jnp.asarray(np.concatenate([high, high, low], axis=1))


def right_const(table):
    high, low = const_parts(table)
    return jnp.asarray(np.concatenate([high, high, low], axis=0))


def dot_left(table, values):
    high, low = split(values)
    return jnp.dot(
        table, jnp.concatenate([high, low, high], axis=0), preferred_element_type=f32
    )


def dot_right(values, table):
    high, low = split(values)
    return jnp.dot(
        jnp.concatenate([high, low, high], axis=1), table, preferred_element_type=f32
    )


def groups(count, width):
    size = max(1, 256 // width)
    return [list(range(i, min(i + size, count))) for i in range(0, count, size)]


def parts_in_lanes(values, span, width):
    items = values.shape[1] // width
    return jnp.concatenate(
        [
            jnp.concatenate(
                [values[:span, i * width : (i + 1) * width], values[span:, i * width : (i + 1) * width]],
                axis=1,
            )
            for i in range(items)
        ],
        axis=0,
    )


def to_rows_kernel(psi, y_table, out):
    _, _, planes, span_y, span_z = psi.shape
    devices, block_rows, _ = out.shape
    each = block_rows // planes
    for group in groups(planes, span_z):
        real = jnp.concatenate([psi[0, 0, p] - psi[1, 1, p] for p in group], axis=1)
        imag = jnp.concatenate([psi[0, 1, p] + psi[1, 0, p] for p in group], axis=1)
        along_y = dot_left(y_table[...], jnp.concatenate([real, imag], axis=0))
        for i, p in enumerate(group):
            out[:, p * each : (p + 1) * each, :] = along_y[
                :, i * span_z : (i + 1) * span_z
            ].reshape(devices, each, span_z)


def real_space_kernel(rows, planes, recv, pot, inverse, forward, inv_z, fwd_z, _, back, field):
    devices, size, span_z = recv.shape
    span_x = devices * planes
    arrived = recv.reshape(devices * size, span_z)
    leaving = back.reshape(devices * 2 * size, span_z)
    columns = [
        jnp.concatenate(
            [
                arrived[pl.ds((p * rows + r) * 2 + part, devices, stride=size), :]
                for part in range(2)
                for p in range(planes)
            ],
            axis=0,
        )
        for r in range(rows)
    ]
    along_x = dot_left(inverse[...], jnp.concatenate(columns, axis=1))
    spatial = dot_right(parts_in_lanes(along_x, span_x, span_z), inv_z[...])
    spectral = []
    for band in range(2):
        one = spatial[:, band * span_z : (band + 1) * span_z]
        field[band] = one
        product = one * pot[...]
        product = jnp.concatenate(
            [product[r * span_x : (r + 1) * span_x] for r in range(rows)], axis=1
        )
        spectral.append(parts_in_lanes(dot_left(forward[...], product), span_x, span_z))
    spectral = dot_right(jnp.concatenate(spectral, axis=0), fwd_z[...])
    for band in range(2):
        for r in range(rows):
            for p in range(planes):
                first = ((band * rows + r) * planes + p) * devices
                for part in range(2):
                    start = band * size + (p * rows + r) * 2 + part
                    leaving[pl.ds(start, devices, stride=2 * size), :] = spectral[
                        first : first + devices, part * span_z : (part + 1) * span_z
                    ]


def real_gram_kernel(bands, *refs):
    fields, (pot, out) = refs[:-2], refs[-2:]
    held = fields[0].shape[0]
    pairs = [(a, b) for a in range(bands) for b in range(a, bands)]
    for weighted in range(2):

        def step(i, sums):
            rows = pl.ds(pl.multiple_of(i * 8, 8), 8)
            values = [fields[a // held][a % held, rows, :] for a in range(bands)]
            other = [v * pot[rows, :] for v in values] if weighted else values
            result = []
            for (a, b), total in zip(pairs, sums):
                product = values[a] * other[b]
                lanes = product[:, :128]
                for c in range(128, product.shape[1], 128):
                    lanes = lanes + product[:, c : c + 128]
                result.append(total + lanes)
            return tuple(result)

        sums = lax.fori_loop(
            0, pot.shape[0] // 8, step, tuple(jnp.zeros((8, 128), f32) for _ in pairs)
        )
        for (a, b), total in zip(pairs, sums):
            line = jnp.sum(total, axis=0, keepdims=True)
            out[weighted, a, b : b + 1, :] = line
            out[weighted, b, a : a + 1, :] = line


def to_planes_kernel(recv, base, y_table, out):
    bands, _, planes, span_y, span_z = base.shape
    each = recv.shape[2] // planes
    for band in range(bands):
        for group in groups(planes, span_z):
            columns = [
                recv[:, band, p * each : (p + 1) * each, :].reshape(2 * span_y, span_z)
                for p in group
            ]
            along_y = dot_left(y_table[...], jnp.concatenate(columns, axis=1))
            for i, p in enumerate(group):
                for part in range(2):
                    out[band, part, p] = base[band, part, p] + (
                        along_y[part * span_y : (part + 1) * span_y, i * span_z : (i + 1) * span_z]
                    )


def last_sum_kernel(first, second, _, out):
    out[...] = first[...] + second[...]


def block_rows_of(psi, beta, slots):
    bands, _, span, span_z = psi.shape
    psi_flat = psi.reshape(bands * 2 * span, span_z)
    psi_rows = [psi_flat[pl.ds(y, 2 * bands, stride=span), :] for y in range(span)]
    beta_rows = [
        jnp.concatenate(
            [beta[pl.ds(2 * y + part, slots, stride=2 * span), :] for part in range(2)], axis=0
        )
        for y in range(span)
    ]
    return psi_rows, beta_rows


def project_kernel(slots, psi, beta, kinetic, out):
    bands, _, span, span_z = psi.shape
    psi_rows, beta_rows = block_rows_of(psi, beta, slots)
    kin_rows = [psi_rows[y] * kinetic[y : y + 1, :] for y in range(span)]
    right = jnp.concatenate(split(jnp.concatenate(psi_rows, axis=1)), axis=0)
    left = jnp.concatenate(
        split(jnp.concatenate(beta_rows, axis=1)) + split(jnp.concatenate(kin_rows, axis=1)), axis=0
    )
    full = lax.dot_general(left, right, (((1,), (1,)), ((), ())), preferred_element_type=f32)
    width, height = 2 * bands, 2 * slots
    full = full[:, :width] + full[:, width:]
    out[0:height] = full[0:height] + full[height : 2 * height]
    rest = full[2 * height :]
    out[height:] = rest[0:width] + rest[width:]


def base_kernel(slots, psi, beta, kinetic, coefs, out):
    bands, _, span, span_z = psi.shape
    psi_rows, beta_rows = block_rows_of(psi, beta, slots)
    values = jnp.concatenate(
        [jnp.concatenate(psi_rows, axis=1), jnp.concatenate(beta_rows, axis=1)], axis=0
    )
    high, low = split(coefs[...])
    summed = dot_left(jnp.concatenate([high, high, low], axis=1), values)
    flat = out.reshape(bands * 2 * span, span_z)
    for y in range(span):
        flat[pl.ds(y, 2 * bands, stride=span), :] = (
            psi_rows[y] * kinetic[y : y + 1, :] + summed[:, y * span_z : (y + 1) * span_z]
        )


def whole(shape):
    return pl.BlockSpec(shape, lambda *_: (0,) * len(shape))


def subspace_solve(s_real, h_real, h_imag):
    factor = jnp.linalg.cholesky(s_real)
    solved = jax.scipy.linalg.cho_solve((factor, True), jnp.concatenate([h_real, h_imag], axis=1))
    order_size = s_real.shape[0]
    return (solved[:, :order_size], solved[:, order_size:])


def tdot(pattern, left, right):
    return jnp.einsum(pattern, left, right, precision=highest, preferred_element_type=jnp.float32)


def partner(values, devices, k):
    return lax.ppermute(values, "ga", [(d, d ^ k) for d in range(devices)])


def sum_over(values, devices, after):
    if devices & (devices - 1) or devices < 2:
        return lax.psum(values, "ga")
    step = 1
    while step < devices // 2:
        values = values + partner(values, devices, step)
        step *= 2
    held = pl.BlockSpec(memory_space=pltpu.VMEM)
    return pl.pallas_call(
        last_sum_kernel,
        out_shape=jax.ShapeDtypeStruct(values.shape, f32),
        in_specs=[held] * 2 + [pl.BlockSpec(memory_space=pl.ANY)],
        out_specs=held,
        name="last_sum",
    )(values, partner(values, devices, step), after)


def on_device(devices, orbitals, plane_order, potential, projectors, slot_owner, strengths):
    bands = orbitals.shape[0]
    planes = orbitals.shape[2]
    span_y = orbitals.shape[3]
    span_z = orbitals.shape[4]
    span_x = plane_order.shape[0]
    blocks, slots = slot_owner.shape
    owners = strengths.shape[0] * strengths.shape[1]
    rows = span_y // devices
    block_rows = 2 * planes * rows
    pairs = bands // 2
    block_span = projectors.shape[3] // span_z
    per_plane = span_y // block_span
    grid_x = jnp.arange(span_x, dtype=jnp.int32)
    grid_y = jnp.arange(span_y, dtype=jnp.int32)
    grid_z = jnp.arange(span_z, dtype=jnp.int32)
    params = pltpu.CompilerParams(vmem_limit_bytes=vmem_limit)
    tail_params = pltpu.CompilerParams(vmem_limit_bytes=vmem_limit // 2)

    def cost(flops, moved):
        return pl.CostEstimate(flops=flops, bytes_accessed=moved, transcendentals=0)

    layers = 4 if devices % 4 == 0 else 1
    ranks = np.arange(devices).reshape(layers, -1)[[0, 1, 3, 2] if layers == 4 else [0]].T.reshape(-1)
    order = np.arange(2 * span_y)
    order = (order % 2) * span_y + (ranks[:, None] * rows + np.arange(rows)).reshape(-1)[order // 2]

    def exchange(values):
        return lax.all_to_all(
            values,
            "ga",
            split_axis=0,
            concat_axis=0,
            axis_index_groups=[[int(rank) for rank in ranks]],
            tiled=True,
        )

    inv_y = left_const(left_table(span_y, 1.0)[order])
    fwd_y = left_const(left_table(span_y, -1.0)[:, order])
    inv_z = right_const(right_table(span_z, 1.0))
    fwd_z = right_const(right_table(span_z, -1.0))

    parts = 2 if pairs % 2 == 0 else 1
    share = pairs // parts
    arrived = []
    for c in range(parts):
        sent = pl.pallas_call(
            to_rows_kernel,
            out_shape=jax.ShapeDtypeStruct((devices, share, block_rows, span_z), f32),
            grid=(share,),
            in_specs=[
                pl.BlockSpec(
                    (2, 2, planes, span_y, span_z), lambda j, c=c: (c * share + j, 0, 0, 0, 0)
                ),
                whole(inv_y.shape),
            ],
            out_specs=pl.BlockSpec((devices, None, block_rows, span_z), lambda j: (0, j, 0, 0)),
            compiler_params=params,
            cost_estimate=cost(4 * 10**9, 3 * 10**6),
            name="to_rows",
        )(orbitals, inv_y)
        arrived.append(exchange(sent))

    stored = plane_order.reshape(devices, planes)[ranks].T.reshape(-1)
    phases = (stored[:, None] * grid_x[None, :]) % span_x
    angles = phases.astype(f32) * (2.0 * math.pi / span_x)
    factor = 1.0 / math.sqrt(span_x)
    cosine, sine = jnp.cos(angles) * factor, jnp.sin(angles) * factor
    fwd_x = jnp.concatenate([cosine, -sine], axis=0)
    inv_x = jnp.concatenate([fwd_x, jnp.concatenate([sine, cosine], axis=0)], axis=1).T
    high, low = split_outside(fwd_x)
    fwd_x = jnp.concatenate([high, high, low], axis=1)
    high, low = split_outside(inv_x)
    inv_x = jnp.concatenate([high, high, low], axis=1)
    pot = potential.transpose(1, 0, 2).reshape(rows * span_x, span_z)

    local_order = lax.dynamic_slice_in_dim(plane_order, lax.axis_index("ga") * planes, planes)
    freq_x = signed_index(local_order, span_x).astype(f32) / span_x
    freq_y = signed_index(grid_y, span_y).astype(f32) / span_y
    freq_z = signed_index(grid_z, span_z).astype(f32) / span_z
    kinetic = 2.0 * (
        freq_x[:, None, None] ** 2 + freq_y[None, :, None] ** 2 + freq_z[None, None, :] ** 2
    )
    beta = projectors.reshape(blocks, slots, 2, block_span, span_z)
    beta = beta.transpose(0, 1, 3, 2, 4).reshape(blocks, slots * block_span * 2, span_z)
    block_specs = [
        pl.BlockSpec(
            (bands, 2, None, block_span, span_z),
            lambda g: (0, 0, g // per_plane, g % per_plane, 0),
        ),
        pl.BlockSpec((None, slots * block_span * 2, span_z), lambda g: (g, 0, 0)),
        pl.BlockSpec((None, block_span, span_z), lambda g: (g // per_plane, g % per_plane, 0)),
    ]
    products = pl.pallas_call(
        functools.partial(project_kernel, slots),
        out_shape=jax.ShapeDtypeStruct((blocks, 2 * slots + 2 * bands, 2 * bands), f32),
        grid=(blocks,),
        in_specs=block_specs,
        out_specs=pl.BlockSpec((None, 2 * slots + 2 * bands, 2 * bands), lambda g: (g, 0, 0)),
        compiler_params=params,
        cost_estimate=cost(8 * 10**9, 8 * 10**6),
        name="project",
    )(orbitals, beta, kinetic)
    with_real = products[:, :slots].reshape(blocks, slots, bands, 2)
    with_imag = products[:, slots : 2 * slots].reshape(blocks, slots, bands, 2)
    proj = jnp.concatenate(
        [
            with_real[..., 0] + with_imag[..., 1],
            with_real[..., 1] - with_imag[..., 0],
        ],
        axis=-1,
    )
    owned = (
        slot_owner[:, :, None] == jnp.arange(owners, dtype=jnp.int32)[None, None, :]
    ).astype(f32)
    proj = tdot("gsj,gsc->jc", owned, proj)
    kin = jnp.sum(products[:, 2 * slots :], axis=0).reshape(bands, 2, bands, 2)
    kin = kin[:, 0, :, 0] + kin[:, 1, :, 1]

    returned, fields = [], []
    for c in range(parts):
        back, field = pl.pallas_call(
            functools.partial(real_space_kernel, rows, planes),
            out_shape=(
                jax.ShapeDtypeStruct((devices, 2 * share, block_rows, span_z), f32),
                jax.ShapeDtypeStruct((2 * share, rows * span_x, span_z), f32),
            ),
            grid=(share,),
            in_specs=[
                pl.BlockSpec((devices, None, block_rows, span_z), lambda j: (0, j, 0, 0)),
                whole(pot.shape),
                whole(inv_x.shape),
                whole(fwd_x.shape),
                whole(inv_z.shape),
                whole(fwd_z.shape),
                whole(proj.shape),
            ],
            out_specs=(
                pl.BlockSpec((devices, 2, block_rows, span_z), lambda j: (0, j, 0, 0)),
                pl.BlockSpec((2, rows * span_x, span_z), lambda j: (j, 0, 0)),
            ),
            compiler_params=params,
            cost_estimate=cost(4 * 10**9, 8 * 10**6),
            name="real_space",
        )(arrived[c], pot, inv_x, fwd_x, inv_z, fwd_z, proj)
        returned.append(exchange(back))
        fields.append(field)

    grams = pl.pallas_call(
        functools.partial(real_gram_kernel, bands),
        out_shape=jax.ShapeDtypeStruct((2, bands, bands, 128), f32),
        compiler_params=params,
        cost_estimate=cost(10**7, 2 * 10**6),
        name="real_gram",
    )(*fields, pot)
    grams = jnp.sum(grams, axis=-1)
    own = jnp.concatenate([proj, jnp.concatenate([grams[0], grams[1] + kin], axis=1)], axis=0)
    total = sum_over(own, devices, returned[0])
    proj, s_real, h_real = total[:owners], total[owners:, :bands], total[owners:, bands:]
    weighted = strengths.reshape(-1)[:, None] * proj
    p_real, p_imag = proj[:, :bands], proj[:, bands:]
    w_real, w_imag = weighted[:, :bands], weighted[:, bands:]
    h_real = h_real + tdot("ja,jb->ab", p_real, w_real) + tdot("ja,jb->ab", p_imag, w_imag)
    h_imag = tdot("ja,jb->ab", p_real, w_imag) - tdot("ja,jb->ab", p_imag, w_real)
    m_real, m_imag = subspace_solve(s_real, h_real, h_imag)

    coefs = tdot("gsj,jc->gcs", owned, weighted)
    c_real, c_imag = coefs[:, :bands], coefs[:, bands:]
    from_beta = jnp.stack(
        [
            jnp.concatenate([c_real, -c_imag], axis=2),
            jnp.concatenate([c_imag, c_real], axis=2),
        ],
        axis=2,
    ).reshape(blocks, 2 * bands, 2 * slots)
    from_psi = jnp.stack(
        [
            jnp.stack([-m_real.T, m_imag.T], axis=-1),
            jnp.stack([-m_imag.T, -m_real.T], axis=-1),
        ],
        axis=1,
    ).reshape(1, 2 * bands, 2 * bands)
    coefs = jnp.concatenate(
        [jnp.broadcast_to(from_psi, (blocks, 2 * bands, 2 * bands)), from_beta], axis=2
    )
    base = pl.pallas_call(
        functools.partial(base_kernel, slots),
        out_shape=jax.ShapeDtypeStruct(orbitals.shape, f32),
        grid=(blocks,),
        in_specs=block_specs
        + [pl.BlockSpec((None, 2 * bands, 2 * bands + 2 * slots), lambda g: (g, 0, 0))],
        out_specs=block_specs[0],
        compiler_params=tail_params,
        cost_estimate=cost(8 * 10**9, 12 * 10**6),
        name="base",
    )(orbitals, beta, kinetic, coefs)

    residual = base
    for c in range(parts):
        two_bands = pl.BlockSpec(
            (2, 2, planes, span_y, span_z), lambda j, c=c: (share * c + j, 0, 0, 0, 0)
        )
        residual = pl.pallas_call(
            to_planes_kernel,
            out_shape=jax.ShapeDtypeStruct(orbitals.shape, f32),
            grid=(share,),
            in_specs=[
                pl.BlockSpec((devices, 2, block_rows, span_z), lambda j: (0, j, 0, 0)),
                two_bands,
                whole(fwd_y.shape),
            ],
            out_specs=two_bands,
            input_output_aliases={1: 0},
            compiler_params=tail_params,
            cost_estimate=cost(8 * 10**9, 12 * 10**6),
            name="to_planes",
        )(returned[c], residual, fwd_y)
    return (residual, jnp.stack([m_real, m_imag]))


def solution(mesh):
    return jax.shard_map(
        functools.partial(on_device, mesh.shape["ga"]),
        mesh=mesh,
        in_specs=(
            P("rep", None, "ga", None, None),
            P("rep"),
            P("rep", "ga", None),
            P(("rep", "ga"), None, None, None),
            P(("rep", "ga"), None),
            P("rep", None),
        ),
        out_specs=(P("rep", None, "ga", None, None), P(None, "rep", None)),
        check_vma=False,
    )
```

```python
import functools
import math

import jax
import jax.numpy as jnp
import numpy as np
from jax import lax
from jax.experimental import pallas as pl
from jax.experimental.pallas import tpu as pltpu
from jax.sharding import PartitionSpec as P

highest = lax.Precision.HIGHEST
f32 = jnp.float32
bf16 = jnp.bfloat16
vmem_limit = 63 * 1024 * 1024


def signed_index(values, length):
    return jnp.where(values < length // 2, values, values - length)


def dft(length, orient):
    index = np.arange(length)
    angles = (index[:, None] * index[None, :] % length) * (2.0 * math.pi / length)
    factor = 1.0 / math.sqrt(length)
    return np.cos(angles) * factor, orient * np.sin(angles) * factor


def left_table(length, orient):
    cosine, sine = dft(length, orient)
    return np.block([[cosine, -sine], [sine, cosine]])


def right_table(length, orient):
    cosine, sine = dft(length, orient)
    return np.block([[cosine, sine], [-sine, cosine]])


def split(values):
    high = values.astype(bf16)
    low = (values - high.astype(f32)).astype(bf16)
    return high, low


def split_outside(values):
    high = lax.reduce_precision(values, exponent_bits=8, mantissa_bits=7)
    return high.astype(bf16), (values - high).astype(bf16)


def const_parts(table):
    table = np.asarray(table, np.float32)
    high = table.astype(jnp.bfloat16)
    low = (table - high.astype(np.float32)).astype(jnp.bfloat16)
    return high, low


def left_const(table):
    high, low = const_parts(table)
    return jnp.asarray(np.concatenate([high, high, low], axis=1))


def right_const(table):
    high, low = const_parts(table)
    return jnp.asarray(np.concatenate([high, high, low], axis=0))


def dot_left(table, values):
    high, low = split(values)
    return jnp.dot(
        table, jnp.concatenate([high, low, high], axis=0), preferred_element_type=f32
    )


def dot_right(values, table):
    high, low = split(values)
    return jnp.dot(
        jnp.concatenate([high, low, high], axis=1), table, preferred_element_type=f32
    )


def groups(count, width):
    size = max(1, 256 // width)
    return [list(range(i, min(i + size, count))) for i in range(0, count, size)]


def parts_in_lanes(values, span, width):
    items = values.shape[1] // width
    return jnp.concatenate(
        [
            jnp.concatenate(
                [values[:span, i * width : (i + 1) * width], values[span:, i * width : (i + 1) * width]],
                axis=1,
            )
            for i in range(items)
        ],
        axis=0,
    )


def to_rows_kernel(psi, y_table, out):
    _, _, planes, span_y, span_z = psi.shape
    devices, block_rows, _ = out.shape
    each = block_rows // planes
    for group in groups(planes, span_z):
        real = jnp.concatenate([psi[0, 0, p] - psi[1, 1, p] for p in group], axis=1)
        imag = jnp.concatenate([psi[0, 1, p] + psi[1, 0, p] for p in group], axis=1)
        along_y = dot_left(y_table[...], jnp.concatenate([real, imag], axis=0))
        for i, p in enumerate(group):
            out[:, p * each : (p + 1) * each, :] = along_y[
                :, i * span_z : (i + 1) * span_z
            ].reshape(devices, each, span_z)


def real_space_kernel(rows, planes, recv, pot, inverse, forward, inv_z, fwd_z, _, back, field):
    devices, size, span_z = recv.shape
    span_x = devices * planes
    arrived = recv.reshape(devices * size, span_z)
    leaving = back.reshape(devices * 2 * size, span_z)
    columns = [
        jnp.concatenate(
            [
                arrived[pl.ds((p * rows + r) * 2 + part, devices, stride=size), :]
                for part in range(2)
                for p in range(planes)
            ],
            axis=0,
        )
        for r in range(rows)
    ]
    along_x = dot_left(inverse[...], jnp.concatenate(columns, axis=1))
    spatial = dot_right(parts_in_lanes(along_x, span_x, span_z), inv_z[...])
    spectral = []
    for band in range(2):
        one = spatial[:, band * span_z : (band + 1) * span_z]
        field[band] = one
        product = one * pot[...]
        product = jnp.concatenate(
            [product[r * span_x : (r + 1) * span_x] for r in range(rows)], axis=1
        )
        spectral.append(parts_in_lanes(dot_left(forward[...], product), span_x, span_z))
    spectral = dot_right(jnp.concatenate(spectral, axis=0), fwd_z[...])
    for band in range(2):
        for r in range(rows):
            for p in range(planes):
                first = ((band * rows + r) * planes + p) * devices
                for part in range(2):
                    start = band * size + (p * rows + r) * 2 + part
                    leaving[pl.ds(start, devices, stride=2 * size), :] = spectral[
                        first : first + devices, part * span_z : (part + 1) * span_z
                    ]


def real_gram_kernel(bands, *refs):
    fields, (pot, out) = refs[:-2], refs[-2:]
    held = fields[0].shape[0]
    pairs = [(a, b) for a in range(bands) for b in range(a, bands)]
    for weighted in range(2):

        def step(i, sums):
            rows = pl.ds(pl.multiple_of(i * 8, 8), 8)
            values = [fields[a // held][a % held, rows, :] for a in range(bands)]
            other = [v * pot[rows, :] for v in values] if weighted else values
            result = []
            for (a, b), total in zip(pairs, sums):
                product = values[a] * other[b]
                lanes = product[:, :128]
                for c in range(128, product.shape[1], 128):
                    lanes = lanes + product[:, c : c + 128]
                result.append(total + lanes)
            return tuple(result)

        sums = lax.fori_loop(
            0, pot.shape[0] // 8, step, tuple(jnp.zeros((8, 128), f32) for _ in pairs)
        )
        for (a, b), total in zip(pairs, sums):
            line = jnp.sum(total, axis=0, keepdims=True)
            out[weighted, a, b : b + 1, :] = line
            out[weighted, b, a : a + 1, :] = line


def to_planes_kernel(recv, base, y_table, out):
    bands, _, planes, span_y, span_z = base.shape
    each = recv.shape[2] // planes
    for band in range(bands):
        for group in groups(planes, span_z):
            columns = [
                recv[:, band, p * each : (p + 1) * each, :].reshape(2 * span_y, span_z)
                for p in group
            ]
            along_y = dot_left(y_table[...], jnp.concatenate(columns, axis=1))
            for i, p in enumerate(group):
                for part in range(2):
                    out[band, part, p] = base[band, part, p] + (
                        along_y[part * span_y : (part + 1) * span_y, i * span_z : (i + 1) * span_z]
                    )


def last_sum_kernel(first, second, _, out):
    out[...] = first[...] + second[...]


def block_rows_of(psi, beta, slots):
    bands, _, span, span_z = psi.shape
    psi_flat = psi.reshape(bands * 2 * span, span_z)
    psi_rows = [psi_flat[pl.ds(y, 2 * bands, stride=span), :] for y in range(span)]
    beta_rows = [
        jnp.concatenate(
            [beta[pl.ds(2 * y + part, slots, stride=2 * span), :] for part in range(2)], axis=0
        )
        for y in range(span)
    ]
    return psi_rows, beta_rows


def project_kernel(slots, psi, beta, kinetic, out):
    bands, _, span, span_z = psi.shape
    psi_rows, beta_rows = block_rows_of(psi, beta, slots)
    kin_rows = [psi_rows[y] * kinetic[y : y + 1, :] for y in range(span)]
    right = jnp.concatenate(split(jnp.concatenate(psi_rows, axis=1)), axis=0)
    left = jnp.concatenate(
        split(jnp.concatenate(beta_rows, axis=1)) + split(jnp.concatenate(kin_rows, axis=1)), axis=0
    )
    full = lax.dot_general(left, right, (((1,), (1,)), ((), ())), preferred_element_type=f32)
    width, height = 2 * bands, 2 * slots
    full = full[:, :width] + full[:, width:]
    out[0:height] = full[0:height] + full[height : 2 * height]
    rest = full[2 * height :]
    out[height:] = rest[0:width] + rest[width:]


def base_kernel(slots, psi, beta, kinetic, coefs, out):
    bands, _, span, span_z = psi.shape
    psi_rows, beta_rows = block_rows_of(psi, beta, slots)
    values = jnp.concatenate(
        [jnp.concatenate(psi_rows, axis=1), jnp.concatenate(beta_rows, axis=1)], axis=0
    )
    high, low = split(coefs[...])
    summed = dot_left(jnp.concatenate([high, high, low], axis=1), values)
    flat = out.reshape(bands * 2 * span, span_z)
    for y in range(span):
        flat[pl.ds(y, 2 * bands, stride=span), :] = (
            psi_rows[y] * kinetic[y : y + 1, :] + summed[:, y * span_z : (y + 1) * span_z]
        )


def whole(shape):
    return pl.BlockSpec(shape, lambda *_: (0,) * len(shape))


def subspace_solve(s_real, h_real, h_imag):
    factor = jnp.linalg.cholesky(s_real)
    solved = jax.scipy.linalg.cho_solve((factor, True), jnp.concatenate([h_real, h_imag], axis=1))
    order_size = s_real.shape[0]
    return (solved[:, :order_size], solved[:, order_size:])


def tdot(pattern, left, right):
    return jnp.einsum(pattern, left, right, precision=highest, preferred_element_type=jnp.float32)


def partner(values, devices, k):
    return lax.ppermute(values, "ga", [(d, d ^ k) for d in range(devices)])


def sum_over(values, devices, after):
    if devices & (devices - 1) or devices < 2:
        return lax.psum(values, "ga")
    step = 1
    while step < devices // 2:
        values = values + partner(values, devices, step)
        step *= 2
    held = pl.BlockSpec(memory_space=pltpu.VMEM)
    return pl.pallas_call(
        last_sum_kernel,
        out_shape=jax.ShapeDtypeStruct(values.shape, f32),
        in_specs=[held] * 2 + [pl.BlockSpec(memory_space=pl.ANY)],
        out_specs=held,
        name="last_sum",
    )(values, partner(values, devices, step), after)


def on_device(devices, orbitals, plane_order, potential, projectors, slot_owner, strengths):
    bands = orbitals.shape[0]
    planes = orbitals.shape[2]
    span_y = orbitals.shape[3]
    span_z = orbitals.shape[4]
    span_x = plane_order.shape[0]
    blocks, slots = slot_owner.shape
    owners = strengths.shape[0] * strengths.shape[1]
    rows = span_y // devices
    block_rows = 2 * planes * rows
    pairs = bands // 2
    block_span = projectors.shape[3] // span_z
    per_plane = span_y // block_span
    grid_x = jnp.arange(span_x, dtype=jnp.int32)
    grid_y = jnp.arange(span_y, dtype=jnp.int32)
    grid_z = jnp.arange(span_z, dtype=jnp.int32)
    params = pltpu.CompilerParams(vmem_limit_bytes=vmem_limit)
    tail_params = pltpu.CompilerParams(vmem_limit_bytes=vmem_limit // 2)

    def cost(flops, moved):
        return pl.CostEstimate(flops=flops, bytes_accessed=moved, transcendentals=0)

    layers = 4 if devices % 4 == 0 else 1
    cores = 2 if devices % 8 == 0 else 1
    ranks = np.arange(devices).reshape(layers, -1, cores).T.reshape(-1)
    order = np.arange(2 * span_y)
    order = (order % 2) * span_y + (ranks[:, None] * rows + np.arange(rows)).reshape(-1)[order // 2]

    def exchange(values):
        return lax.all_to_all(
            values,
            "ga",
            split_axis=0,
            concat_axis=0,
            axis_index_groups=[[int(rank) for rank in ranks]],
            tiled=True,
        )

    inv_y = left_const(left_table(span_y, 1.0)[order])
    fwd_y = left_const(left_table(span_y, -1.0)[:, order])
    inv_z = right_const(right_table(span_z, 1.0))
    fwd_z = right_const(right_table(span_z, -1.0))

    parts = 2 if pairs % 2 == 0 else 1
    share = pairs // parts
    arrived = []
    for c in range(parts):
        sent = pl.pallas_call(
            to_rows_kernel,
            out_shape=jax.ShapeDtypeStruct((devices, share, block_rows, span_z), f32),
            grid=(share,),
            in_specs=[
                pl.BlockSpec(
                    (2, 2, planes, span_y, span_z), lambda j, c=c: (c * share + j, 0, 0, 0, 0)
                ),
                whole(inv_y.shape),
            ],
            out_specs=pl.BlockSpec((devices, None, block_rows, span_z), lambda j: (0, j, 0, 0)),
            compiler_params=params,
            cost_estimate=cost(4 * 10**9, 3 * 10**6),
            name="to_rows",
        )(orbitals, inv_y)
        arrived.append(exchange(sent))

    stored = plane_order.reshape(devices, planes)[ranks].T.reshape(-1)
    phases = (stored[:, None] * grid_x[None, :]) % span_x
    angles = phases.astype(f32) * (2.0 * math.pi / span_x)
    factor = 1.0 / math.sqrt(span_x)
    cosine, sine = jnp.cos(angles) * factor, jnp.sin(angles) * factor
    fwd_x = jnp.concatenate([cosine, -sine], axis=0)
    inv_x = jnp.concatenate([fwd_x, jnp.concatenate([sine, cosine], axis=0)], axis=1).T
    high, low = split_outside(fwd_x)
    fwd_x = jnp.concatenate([high, high, low], axis=1)
    high, low = split_outside(inv_x)
    inv_x = jnp.concatenate([high, high, low], axis=1)
    pot = potential.transpose(1, 0, 2).reshape(rows * span_x, span_z)

    local_order = lax.dynamic_slice_in_dim(plane_order, lax.axis_index("ga") * planes, planes)
    freq_x = signed_index(local_order, span_x).astype(f32) / span_x
    freq_y = signed_index(grid_y, span_y).astype(f32) / span_y
    freq_z = signed_index(grid_z, span_z).astype(f32) / span_z
    kinetic = 2.0 * (
        freq_x[:, None, None] ** 2 + freq_y[None, :, None] ** 2 + freq_z[None, None, :] ** 2
    )
    beta = projectors.reshape(blocks, slots, 2, block_span, span_z)
    beta = beta.transpose(0, 1, 3, 2, 4).reshape(blocks, slots * block_span * 2, span_z)
    block_specs = [
        pl.BlockSpec(
            (bands, 2, None, block_span, span_z),
            lambda g: (0, 0, g // per_plane, g % per_plane, 0),
        ),
        pl.BlockSpec((None, slots * block_span * 2, span_z), lambda g: (g, 0, 0)),
        pl.BlockSpec((None, block_span, span_z), lambda g: (g // per_plane, g % per_plane, 0)),
    ]
    products = pl.pallas_call(
        functools.partial(project_kernel, slots),
        out_shape=jax.ShapeDtypeStruct((blocks, 2 * slots + 2 * bands, 2 * bands), f32),
        grid=(blocks,),
        in_specs=block_specs,
        out_specs=pl.BlockSpec((None, 2 * slots + 2 * bands, 2 * bands), lambda g: (g, 0, 0)),
        compiler_params=params,
        cost_estimate=cost(8 * 10**9, 8 * 10**6),
        name="project",
    )(orbitals, beta, kinetic)
    with_real = products[:, :slots].reshape(blocks, slots, bands, 2)
    with_imag = products[:, slots : 2 * slots].reshape(blocks, slots, bands, 2)
    proj = jnp.concatenate(
        [
            with_real[..., 0] + with_imag[..., 1],
            with_real[..., 1] - with_imag[..., 0],
        ],
        axis=-1,
    )
    owned = (
        slot_owner[:, :, None] == jnp.arange(owners, dtype=jnp.int32)[None, None, :]
    ).astype(f32)
    proj = tdot("gsj,gsc->jc", owned, proj)
    kin = jnp.sum(products[:, 2 * slots :], axis=0).reshape(bands, 2, bands, 2)
    kin = kin[:, 0, :, 0] + kin[:, 1, :, 1]

    returned, fields = [], []
    for c in range(parts):
        back, field = pl.pallas_call(
            functools.partial(real_space_kernel, rows, planes),
            out_shape=(
                jax.ShapeDtypeStruct((devices, 2 * share, block_rows, span_z), f32),
                jax.ShapeDtypeStruct((2 * share, rows * span_x, span_z), f32),
            ),
            grid=(share,),
            in_specs=[
                pl.BlockSpec((devices, None, block_rows, span_z), lambda j: (0, j, 0, 0)),
                whole(pot.shape),
                whole(inv_x.shape),
                whole(fwd_x.shape),
                whole(inv_z.shape),
                whole(fwd_z.shape),
                whole(proj.shape),
            ],
            out_specs=(
                pl.BlockSpec((devices, 2, block_rows, span_z), lambda j: (0, j, 0, 0)),
                pl.BlockSpec((2, rows * span_x, span_z), lambda j: (j, 0, 0)),
            ),
            compiler_params=params,
            cost_estimate=cost(4 * 10**9, 8 * 10**6),
            name="real_space",
        )(arrived[c], pot, inv_x, fwd_x, inv_z, fwd_z, proj)
        returned.append(exchange(back))
        fields.append(field)

    grams = pl.pallas_call(
        functools.partial(real_gram_kernel, bands),
        out_shape=jax.ShapeDtypeStruct((2, bands, bands, 128), f32),
        compiler_params=params,
        cost_estimate=cost(10**7, 2 * 10**6),
        name="real_gram",
    )(*fields, pot)
    grams = jnp.sum(grams, axis=-1)
    own = jnp.concatenate([proj, jnp.concatenate([grams[0], grams[1] + kin], axis=1)], axis=0)
    total = sum_over(own, devices, returned[0])
    proj, s_real, h_real = total[:owners], total[owners:, :bands], total[owners:, bands:]
    weighted = strengths.reshape(-1)[:, None] * proj
    p_real, p_imag = proj[:, :bands], proj[:, bands:]
    w_real, w_imag = weighted[:, :bands], weighted[:, bands:]
    h_real = h_real + tdot("ja,jb->ab", p_real, w_real) + tdot("ja,jb->ab", p_imag, w_imag)
    h_imag = tdot("ja,jb->ab", p_real, w_imag) - tdot("ja,jb->ab", p_imag, w_real)
    m_real, m_imag = subspace_solve(s_real, h_real, h_imag)

    coefs = tdot("gsj,jc->gcs", owned, weighted)
    c_real, c_imag = coefs[:, :bands], coefs[:, bands:]
    from_beta = jnp.stack(
        [
            jnp.concatenate([c_real, -c_imag], axis=2),
            jnp.concatenate([c_imag, c_real], axis=2),
        ],
        axis=2,
    ).reshape(blocks, 2 * bands, 2 * slots)
    from_psi = jnp.stack(
        [
            jnp.stack([-m_real.T, m_imag.T], axis=-1),
            jnp.stack([-m_imag.T, -m_real.T], axis=-1),
        ],
        axis=1,
    ).reshape(1, 2 * bands, 2 * bands)
    coefs = jnp.concatenate(
        [jnp.broadcast_to(from_psi, (blocks, 2 * bands, 2 * bands)), from_beta], axis=2
    )
    base = pl.pallas_call(
        functools.partial(base_kernel, slots),
        out_shape=jax.ShapeDtypeStruct(orbitals.shape, f32),
        grid=(blocks,),
        in_specs=block_specs
        + [pl.BlockSpec((None, 2 * bands, 2 * bands + 2 * slots), lambda g: (g, 0, 0))],
        out_specs=block_specs[0],
        compiler_params=tail_params,
        cost_estimate=cost(8 * 10**9, 12 * 10**6),
        name="base",
    )(orbitals, beta, kinetic, coefs)

    residual = base
    for c in range(parts):
        two_bands = pl.BlockSpec(
            (2, 2, planes, span_y, span_z), lambda j, c=c: (share * c + j, 0, 0, 0, 0)
        )
        residual = pl.pallas_call(
            to_planes_kernel,
            out_shape=jax.ShapeDtypeStruct(orbitals.shape, f32),
            grid=(share,),
            in_specs=[
                pl.BlockSpec((devices, 2, block_rows, span_z), lambda j: (0, j, 0, 0)),
                two_bands,
                whole(fwd_y.shape),
            ],
            out_specs=two_bands,
            input_output_aliases={1: 0},
            compiler_params=tail_params,
            cost_estimate=cost(8 * 10**9, 12 * 10**6),
            name="to_planes",
        )(returned[c], residual, fwd_y)
    return (residual, jnp.stack([m_real, m_imag]))


def solution(mesh):
    return jax.shard_map(
        functools.partial(on_device, mesh.shape["ga"]),
        mesh=mesh,
        in_specs=(
            P("rep", None, "ga", None, None),
            P("rep"),
            P("rep", "ga", None),
            P(("rep", "ga"), None, None, None),
            P(("rep", "ga"), None),
            P("rep", None),
        ),
        out_specs=(P("rep", None, "ga", None, None), P(None, "rep", None)),
        check_vma=False,
    )
```

```python
import functools
import math

import jax
import jax.numpy as jnp
import numpy as np
from jax import lax
from jax.experimental import pallas as pl
from jax.experimental.pallas import tpu as pltpu
from jax.sharding import PartitionSpec as P

highest = lax.Precision.HIGHEST
f32 = jnp.float32
bf16 = jnp.bfloat16
vmem_limit = 63 * 1024 * 1024


def signed_index(values, length):
    return jnp.where(values < length // 2, values, values - length)


def dft(length, orient):
    index = np.arange(length)
    angles = (index[:, None] * index[None, :] % length) * (2.0 * math.pi / length)
    factor = 1.0 / math.sqrt(length)
    return np.cos(angles) * factor, orient * np.sin(angles) * factor


def left_table(length, orient):
    cosine, sine = dft(length, orient)
    return np.block([[cosine, -sine], [sine, cosine]])


def right_table(length, orient):
    cosine, sine = dft(length, orient)
    return np.block([[cosine, sine], [-sine, cosine]])


def split(values):
    high = values.astype(bf16)
    low = (values - high.astype(f32)).astype(bf16)
    return high, low


def split_outside(values):
    high = lax.reduce_precision(values, exponent_bits=8, mantissa_bits=7)
    return high.astype(bf16), (values - high).astype(bf16)


def const_parts(table):
    table = np.asarray(table, np.float32)
    high = table.astype(jnp.bfloat16)
    low = (table - high.astype(np.float32)).astype(jnp.bfloat16)
    return high, low


def left_const(table):
    high, low = const_parts(table)
    return jnp.asarray(np.concatenate([high, high, low], axis=1))


def right_const(table):
    high, low = const_parts(table)
    return jnp.asarray(np.concatenate([high, high, low], axis=0))


def dot_left(table, values):
    high, low = split(values)
    return jnp.dot(
        table, jnp.concatenate([high, low, high], axis=0), preferred_element_type=f32
    )


def dot_right(values, table):
    high, low = split(values)
    return jnp.dot(
        jnp.concatenate([high, low, high], axis=1), table, preferred_element_type=f32
    )


def groups(count, width):
    size = max(1, 256 // width)
    return [list(range(i, min(i + size, count))) for i in range(0, count, size)]


def parts_in_lanes(values, span, width):
    items = values.shape[1] // width
    return jnp.concatenate(
        [
            jnp.concatenate(
                [values[:span, i * width : (i + 1) * width], values[span:, i * width : (i + 1) * width]],
                axis=1,
            )
            for i in range(items)
        ],
        axis=0,
    )


def to_rows_kernel(psi, y_table, out):
    _, _, planes, span_y, span_z = psi.shape
    devices, block_rows, _ = out.shape
    each = block_rows // planes
    for group in groups(planes, span_z):
        real = jnp.concatenate([psi[0, 0, p] - psi[1, 1, p] for p in group], axis=1)
        imag = jnp.concatenate([psi[0, 1, p] + psi[1, 0, p] for p in group], axis=1)
        along_y = dot_left(y_table[...], jnp.concatenate([real, imag], axis=0))
        for i, p in enumerate(group):
            out[:, p * each : (p + 1) * each, :] = along_y[
                :, i * span_z : (i + 1) * span_z
            ].reshape(devices, each, span_z)


def real_space_kernel(rows, planes, recv, pot, inverse, forward, inv_z, fwd_z, _, back, field):
    devices, size, span_z = recv.shape
    span_x = devices * planes
    arrived = recv.reshape(devices * size, span_z)
    leaving = back.reshape(devices * 2 * size, span_z)
    columns = [
        jnp.concatenate(
            [
                arrived[pl.ds((p * rows + r) * 2 + part, devices, stride=size), :]
                for part in range(2)
                for p in range(planes)
            ],
            axis=0,
        )
        for r in range(rows)
    ]
    along_x = dot_left(inverse[...], jnp.concatenate(columns, axis=1))
    spatial = dot_right(parts_in_lanes(along_x, span_x, span_z), inv_z[...])
    spectral = []
    for band in range(2):
        one = spatial[:, band * span_z : (band + 1) * span_z]
        field[band] = one
        product = one * pot[...]
        product = jnp.concatenate(
            [product[r * span_x : (r + 1) * span_x] for r in range(rows)], axis=1
        )
        spectral.append(parts_in_lanes(dot_left(forward[...], product), span_x, span_z))
    spectral = dot_right(jnp.concatenate(spectral, axis=0), fwd_z[...])
    for band in range(2):
        for r in range(rows):
            for p in range(planes):
                first = ((band * rows + r) * planes + p) * devices
                for part in range(2):
                    start = band * size + (p * rows + r) * 2 + part
                    leaving[pl.ds(start, devices, stride=2 * size), :] = spectral[
                        first : first + devices, part * span_z : (part + 1) * span_z
                    ]


def real_gram_kernel(bands, *refs):
    fields, (pot, out) = refs[:-2], refs[-2:]
    held = fields[0].shape[0]
    pairs = [(a, b) for a in range(bands) for b in range(a, bands)]
    for weighted in range(2):

        def step(i, sums):
            rows = pl.ds(pl.multiple_of(i * 8, 8), 8)
            values = [fields[a // held][a % held, rows, :] for a in range(bands)]
            other = [v * pot[rows, :] for v in values] if weighted else values
            result = []
            for (a, b), total in zip(pairs, sums):
                product = values[a] * other[b]
                lanes = product[:, :128]
                for c in range(128, product.shape[1], 128):
                    lanes = lanes + product[:, c : c + 128]
                result.append(total + lanes)
            return tuple(result)

        sums = lax.fori_loop(
            0, pot.shape[0] // 8, step, tuple(jnp.zeros((8, 128), f32) for _ in pairs)
        )
        for (a, b), total in zip(pairs, sums):
            line = jnp.sum(total, axis=0, keepdims=True)
            out[weighted, a, b : b + 1, :] = line
            out[weighted, b, a : a + 1, :] = line


def to_planes_kernel(recv, base, y_table, out):
    bands, _, planes, span_y, span_z = base.shape
    each = recv.shape[2] // planes
    for band in range(bands):
        for group in groups(planes, span_z):
            columns = [
                recv[:, band, p * each : (p + 1) * each, :].reshape(2 * span_y, span_z)
                for p in group
            ]
            along_y = dot_left(y_table[...], jnp.concatenate(columns, axis=1))
            for i, p in enumerate(group):
                for part in range(2):
                    out[band, part, p] = base[band, part, p] + (
                        along_y[part * span_y : (part + 1) * span_y, i * span_z : (i + 1) * span_z]
                    )


def last_sum_kernel(first, second, _, out):
    out[...] = first[...] + second[...]


def block_rows_of(psi, beta, slots):
    bands, _, span, span_z = psi.shape
    psi_flat = psi.reshape(bands * 2 * span, span_z)
    psi_rows = [psi_flat[pl.ds(y, 2 * bands, stride=span), :] for y in range(span)]
    beta_rows = [
        jnp.concatenate(
            [beta[pl.ds(2 * y + part, slots, stride=2 * span), :] for part in range(2)], axis=0
        )
        for y in range(span)
    ]
    return psi_rows, beta_rows


def project_kernel(slots, psi, beta, kinetic, out):
    bands, _, span, span_z = psi.shape
    psi_rows, beta_rows = block_rows_of(psi, beta, slots)
    kin_rows = [psi_rows[y] * kinetic[y : y + 1, :] for y in range(span)]
    right = jnp.concatenate(split(jnp.concatenate(psi_rows, axis=1)), axis=0)
    left = jnp.concatenate(
        split(jnp.concatenate(beta_rows, axis=1)) + split(jnp.concatenate(kin_rows, axis=1)), axis=0
    )
    full = lax.dot_general(left, right, (((1,), (1,)), ((), ())), preferred_element_type=f32)
    width, height = 2 * bands, 2 * slots
    full = full[:, :width] + full[:, width:]
    out[0:height] = full[0:height] + full[height : 2 * height]
    rest = full[2 * height :]
    out[height:] = rest[0:width] + rest[width:]


def base_kernel(slots, psi, beta, kinetic, coefs, out):
    bands, _, span, span_z = psi.shape
    psi_rows, beta_rows = block_rows_of(psi, beta, slots)
    values = jnp.concatenate(
        [jnp.concatenate(psi_rows, axis=1), jnp.concatenate(beta_rows, axis=1)], axis=0
    )
    high, low = split(coefs[...])
    summed = dot_left(jnp.concatenate([high, high, low], axis=1), values)
    flat = out.reshape(bands * 2 * span, span_z)
    for y in range(span):
        flat[pl.ds(y, 2 * bands, stride=span), :] = (
            psi_rows[y] * kinetic[y : y + 1, :] + summed[:, y * span_z : (y + 1) * span_z]
        )


def whole(shape):
    return pl.BlockSpec(shape, lambda *_: (0,) * len(shape))


def subspace_solve(s_real, h_real, h_imag):
    factor = jnp.linalg.cholesky(s_real)
    solved = jax.scipy.linalg.cho_solve((factor, True), jnp.concatenate([h_real, h_imag], axis=1))
    order_size = s_real.shape[0]
    return (solved[:, :order_size], solved[:, order_size:])


def tdot(pattern, left, right):
    return jnp.einsum(pattern, left, right, precision=highest, preferred_element_type=jnp.float32)


def partner(values, devices, k):
    return lax.ppermute(values, "ga", [(d, d ^ k) for d in range(devices)])


def sum_over(values, devices, after):
    if devices & (devices - 1) or devices < 2:
        return lax.psum(values, "ga")
    step = 1
    while step < devices // 2:
        values = values + partner(values, devices, step)
        step *= 2
    held = pl.BlockSpec(memory_space=pltpu.VMEM)
    return pl.pallas_call(
        last_sum_kernel,
        out_shape=jax.ShapeDtypeStruct(values.shape, f32),
        in_specs=[held] * 2 + [pl.BlockSpec(memory_space=pl.ANY)],
        out_specs=held,
        name="last_sum",
    )(values, partner(values, devices, step), after)


def on_device(devices, orbitals, plane_order, potential, projectors, slot_owner, strengths):
    bands = orbitals.shape[0]
    planes = orbitals.shape[2]
    span_y = orbitals.shape[3]
    span_z = orbitals.shape[4]
    span_x = plane_order.shape[0]
    blocks, slots = slot_owner.shape
    owners = strengths.shape[0] * strengths.shape[1]
    rows = span_y // devices
    block_rows = 2 * planes * rows
    pairs = bands // 2
    block_span = projectors.shape[3] // span_z
    per_plane = span_y // block_span
    grid_x = jnp.arange(span_x, dtype=jnp.int32)
    grid_y = jnp.arange(span_y, dtype=jnp.int32)
    grid_z = jnp.arange(span_z, dtype=jnp.int32)
    params = pltpu.CompilerParams(vmem_limit_bytes=vmem_limit)
    tail_params = pltpu.CompilerParams(vmem_limit_bytes=vmem_limit // 2)

    def cost(flops, moved):
        return pl.CostEstimate(flops=flops, bytes_accessed=moved, transcendentals=0)

    layers = 4 if devices % 4 == 0 else 1
    cores = 2 if devices % 8 == 0 else 1
    ranks = np.arange(devices).reshape(layers, -1, cores).transpose(1, 0, 2).reshape(-1)
    order = np.arange(2 * span_y)
    order = (order % 2) * span_y + (ranks[:, None] * rows + np.arange(rows)).reshape(-1)[order // 2]

    def exchange(values):
        return lax.all_to_all(
            values,
            "ga",
            split_axis=0,
            concat_axis=0,
            axis_index_groups=[[int(rank) for rank in ranks]],
            tiled=True,
        )

    inv_y = left_const(left_table(span_y, 1.0)[order])
    fwd_y = left_const(left_table(span_y, -1.0)[:, order])
    inv_z = right_const(right_table(span_z, 1.0))
    fwd_z = right_const(right_table(span_z, -1.0))

    parts = 2 if pairs % 2 == 0 else 1
    share = pairs // parts
    arrived = []
    for c in range(parts):
        sent = pl.pallas_call(
            to_rows_kernel,
            out_shape=jax.ShapeDtypeStruct((devices, share, block_rows, span_z), f32),
            grid=(share,),
            in_specs=[
                pl.BlockSpec(
                    (2, 2, planes, span_y, span_z), lambda j, c=c: (c * share + j, 0, 0, 0, 0)
                ),
                whole(inv_y.shape),
            ],
            out_specs=pl.BlockSpec((devices, None, block_rows, span_z), lambda j: (0, j, 0, 0)),
            compiler_params=params,
            cost_estimate=cost(4 * 10**9, 3 * 10**6),
            name="to_rows",
        )(orbitals, inv_y)
        arrived.append(exchange(sent))

    stored = plane_order.reshape(devices, planes)[ranks].T.reshape(-1)
    phases = (stored[:, None] * grid_x[None, :]) % span_x
    angles = phases.astype(f32) * (2.0 * math.pi / span_x)
    factor = 1.0 / math.sqrt(span_x)
    cosine, sine = jnp.cos(angles) * factor, jnp.sin(angles) * factor
    fwd_x = jnp.concatenate([cosine, -sine], axis=0)
    inv_x = jnp.concatenate([fwd_x, jnp.concatenate([sine, cosine], axis=0)], axis=1).T
    high, low = split_outside(fwd_x)
    fwd_x = jnp.concatenate([high, high, low], axis=1)
    high, low = split_outside(inv_x)
    inv_x = jnp.concatenate([high, high, low], axis=1)
    pot = potential.transpose(1, 0, 2).reshape(rows * span_x, span_z)

    local_order = lax.dynamic_slice_in_dim(plane_order, lax.axis_index("ga") * planes, planes)
    freq_x = signed_index(local_order, span_x).astype(f32) / span_x
    freq_y = signed_index(grid_y, span_y).astype(f32) / span_y
    freq_z = signed_index(grid_z, span_z).astype(f32) / span_z
    kinetic = 2.0 * (
        freq_x[:, None, None] ** 2 + freq_y[None, :, None] ** 2 + freq_z[None, None, :] ** 2
    )
    beta = projectors.reshape(blocks, slots, 2, block_span, span_z)
    beta = beta.transpose(0, 1, 3, 2, 4).reshape(blocks, slots * block_span * 2, span_z)
    block_specs = [
        pl.BlockSpec(
            (bands, 2, None, block_span, span_z),
            lambda g: (0, 0, g // per_plane, g % per_plane, 0),
        ),
        pl.BlockSpec((None, slots * block_span * 2, span_z), lambda g: (g, 0, 0)),
        pl.BlockSpec((None, block_span, span_z), lambda g: (g // per_plane, g % per_plane, 0)),
    ]
    products = pl.pallas_call(
        functools.partial(project_kernel, slots),
        out_shape=jax.ShapeDtypeStruct((blocks, 2 * slots + 2 * bands, 2 * bands), f32),
        grid=(blocks,),
        in_specs=block_specs,
        out_specs=pl.BlockSpec((None, 2 * slots + 2 * bands, 2 * bands), lambda g: (g, 0, 0)),
        compiler_params=params,
        cost_estimate=cost(8 * 10**9, 8 * 10**6),
        name="project",
    )(orbitals, beta, kinetic)
    with_real = products[:, :slots].reshape(blocks, slots, bands, 2)
    with_imag = products[:, slots : 2 * slots].reshape(blocks, slots, bands, 2)
    proj = jnp.concatenate(
        [
            with_real[..., 0] + with_imag[..., 1],
            with_real[..., 1] - with_imag[..., 0],
        ],
        axis=-1,
    )
    owned = (
        slot_owner[:, :, None] == jnp.arange(owners, dtype=jnp.int32)[None, None, :]
    ).astype(f32)
    proj = tdot("gsj,gsc->jc", owned, proj)
    kin = jnp.sum(products[:, 2 * slots :], axis=0).reshape(bands, 2, bands, 2)
    kin = kin[:, 0, :, 0] + kin[:, 1, :, 1]

    returned, fields = [], []
    for c in range(parts):
        back, field = pl.pallas_call(
            functools.partial(real_space_kernel, rows, planes),
            out_shape=(
                jax.ShapeDtypeStruct((devices, 2 * share, block_rows, span_z), f32),
                jax.ShapeDtypeStruct((2 * share, rows * span_x, span_z), f32),
            ),
            grid=(share,),
            in_specs=[
                pl.BlockSpec((devices, None, block_rows, span_z), lambda j: (0, j, 0, 0)),
                whole(pot.shape),
                whole(inv_x.shape),
                whole(fwd_x.shape),
                whole(inv_z.shape),
                whole(fwd_z.shape),
                whole(proj.shape),
            ],
            out_specs=(
                pl.BlockSpec((devices, 2, block_rows, span_z), lambda j: (0, j, 0, 0)),
                pl.BlockSpec((2, rows * span_x, span_z), lambda j: (j, 0, 0)),
            ),
            compiler_params=params,
            cost_estimate=cost(4 * 10**9, 8 * 10**6),
            name="real_space",
        )(arrived[c], pot, inv_x, fwd_x, inv_z, fwd_z, proj)
        returned.append(exchange(back))
        fields.append(field)

    grams = pl.pallas_call(
        functools.partial(real_gram_kernel, bands),
        out_shape=jax.ShapeDtypeStruct((2, bands, bands, 128), f32),
        compiler_params=params,
        cost_estimate=cost(10**7, 2 * 10**6),
        name="real_gram",
    )(*fields, pot)
    grams = jnp.sum(grams, axis=-1)
    own = jnp.concatenate([proj, jnp.concatenate([grams[0], grams[1] + kin], axis=1)], axis=0)
    total = sum_over(own, devices, returned[0])
    proj, s_real, h_real = total[:owners], total[owners:, :bands], total[owners:, bands:]
    weighted = strengths.reshape(-1)[:, None] * proj
    p_real, p_imag = proj[:, :bands], proj[:, bands:]
    w_real, w_imag = weighted[:, :bands], weighted[:, bands:]
    h_real = h_real + tdot("ja,jb->ab", p_real, w_real) + tdot("ja,jb->ab", p_imag, w_imag)
    h_imag = tdot("ja,jb->ab", p_real, w_imag) - tdot("ja,jb->ab", p_imag, w_real)
    m_real, m_imag = subspace_solve(s_real, h_real, h_imag)

    coefs = tdot("gsj,jc->gcs", owned, weighted)
    c_real, c_imag = coefs[:, :bands], coefs[:, bands:]
    from_beta = jnp.stack(
        [
            jnp.concatenate([c_real, -c_imag], axis=2),
            jnp.concatenate([c_imag, c_real], axis=2),
        ],
        axis=2,
    ).reshape(blocks, 2 * bands, 2 * slots)
    from_psi = jnp.stack(
        [
            jnp.stack([-m_real.T, m_imag.T], axis=-1),
            jnp.stack([-m_imag.T, -m_real.T], axis=-1),
        ],
        axis=1,
    ).reshape(1, 2 * bands, 2 * bands)
    coefs = jnp.concatenate(
        [jnp.broadcast_to(from_psi, (blocks, 2 * bands, 2 * bands)), from_beta], axis=2
    )
    base = pl.pallas_call(
        functools.partial(base_kernel, slots),
        out_shape=jax.ShapeDtypeStruct(orbitals.shape, f32),
        grid=(blocks,),
        in_specs=block_specs
        + [pl.BlockSpec((None, 2 * bands, 2 * bands + 2 * slots), lambda g: (g, 0, 0))],
        out_specs=block_specs[0],
        compiler_params=tail_params,
        cost_estimate=cost(8 * 10**9, 12 * 10**6),
        name="base",
    )(orbitals, beta, kinetic, coefs)

    residual = base
    for c in range(parts):
        two_bands = pl.BlockSpec(
            (2, 2, planes, span_y, span_z), lambda j, c=c: (share * c + j, 0, 0, 0, 0)
        )
        residual = pl.pallas_call(
            to_planes_kernel,
            out_shape=jax.ShapeDtypeStruct(orbitals.shape, f32),
            grid=(share,),
            in_specs=[
                pl.BlockSpec((devices, 2, block_rows, span_z), lambda j: (0, j, 0, 0)),
                two_bands,
                whole(fwd_y.shape),
            ],
            out_specs=two_bands,
            input_output_aliases={1: 0},
            compiler_params=tail_params,
            cost_estimate=cost(8 * 10**9, 12 * 10**6),
            name="to_planes",
        )(returned[c], residual, fwd_y)
    return (residual, jnp.stack([m_real, m_imag]))


def solution(mesh):
    return jax.shard_map(
        functools.partial(on_device, mesh.shape["ga"]),
        mesh=mesh,
        in_specs=(
            P("rep", None, "ga", None, None),
            P("rep"),
            P("rep", "ga", None),
            P(("rep", "ga"), None, None, None),
            P(("rep", "ga"), None),
            P("rep", None),
        ),
        out_specs=(P("rep", None, "ga", None, None), P(None, "rep", None)),
        check_vma=False,
    )
```

```python
import functools
import math

import jax
import jax.numpy as jnp
import numpy as np
from jax import lax
from jax.experimental import pallas as pl
from jax.experimental.pallas import tpu as pltpu
from jax.sharding import PartitionSpec as P

highest = lax.Precision.HIGHEST
f32 = jnp.float32
bf16 = jnp.bfloat16
vmem_limit = 63 * 1024 * 1024


def signed_index(values, length):
    return jnp.where(values < length // 2, values, values - length)


def dft(length, orient):
    index = np.arange(length)
    angles = (index[:, None] * index[None, :] % length) * (2.0 * math.pi / length)
    factor = 1.0 / math.sqrt(length)
    return np.cos(angles) * factor, orient * np.sin(angles) * factor


def left_table(length, orient):
    cosine, sine = dft(length, orient)
    return np.block([[cosine, -sine], [sine, cosine]])


def right_table(length, orient):
    cosine, sine = dft(length, orient)
    return np.block([[cosine, sine], [-sine, cosine]])


def split(values):
    high = values.astype(bf16)
    low = (values - high.astype(f32)).astype(bf16)
    return high, low


def split_outside(values):
    high = lax.reduce_precision(values, exponent_bits=8, mantissa_bits=7)
    return high.astype(bf16), (values - high).astype(bf16)


def const_parts(table):
    table = np.asarray(table, np.float32)
    high = table.astype(jnp.bfloat16)
    low = (table - high.astype(np.float32)).astype(jnp.bfloat16)
    return high, low


def left_const(table):
    high, low = const_parts(table)
    return jnp.asarray(np.concatenate([high, high, low], axis=1))


def right_const(table):
    high, low = const_parts(table)
    return jnp.asarray(np.concatenate([high, high, low], axis=0))


def dot_left(table, values):
    high, low = split(values)
    return jnp.dot(
        table, jnp.concatenate([high, low, high], axis=0), preferred_element_type=f32
    )


def dot_right(values, table):
    high, low = split(values)
    return jnp.dot(
        jnp.concatenate([high, low, high], axis=1), table, preferred_element_type=f32
    )


def groups(count, width):
    size = max(1, 256 // width)
    return [list(range(i, min(i + size, count))) for i in range(0, count, size)]


def parts_in_lanes(values, span, width):
    items = values.shape[1] // width
    return jnp.concatenate(
        [
            jnp.concatenate(
                [values[:span, i * width : (i + 1) * width], values[span:, i * width : (i + 1) * width]],
                axis=1,
            )
            for i in range(items)
        ],
        axis=0,
    )


def to_rows_kernel(psi, y_table, out):
    _, _, planes, span_y, span_z = psi.shape
    devices, block_rows, _ = out.shape
    each = block_rows // planes
    for group in groups(planes, span_z):
        real = jnp.concatenate([psi[0, 0, p] - psi[1, 1, p] for p in group], axis=1)
        imag = jnp.concatenate([psi[0, 1, p] + psi[1, 0, p] for p in group], axis=1)
        along_y = dot_left(y_table[...], jnp.concatenate([real, imag], axis=0))
        for i, p in enumerate(group):
            out[:, p * each : (p + 1) * each, :] = along_y[
                :, i * span_z : (i + 1) * span_z
            ].reshape(devices, each, span_z)


def real_space_kernel(rows, planes, recv, pot, inverse, forward, inv_z, fwd_z, _, back, field):
    devices, size, span_z = recv.shape
    span_x = devices * planes
    arrived = recv.reshape(devices * size, span_z)
    leaving = back.reshape(devices * 2 * size, span_z)
    columns = [
        jnp.concatenate(
            [
                arrived[pl.ds((p * rows + r) * 2 + part, devices, stride=size), :]
                for part in range(2)
                for p in range(planes)
            ],
            axis=0,
        )
        for r in range(rows)
    ]
    along_x = dot_left(inverse[...], jnp.concatenate(columns, axis=1))
    spatial = dot_right(parts_in_lanes(along_x, span_x, span_z), inv_z[...])
    spectral = []
    for band in range(2):
        one = spatial[:, band * span_z : (band + 1) * span_z]
        field[band] = one
        product = one * pot[...]
        product = jnp.concatenate(
            [product[r * span_x : (r + 1) * span_x] for r in range(rows)], axis=1
        )
        spectral.append(parts_in_lanes(dot_left(forward[...], product), span_x, span_z))
    spectral = dot_right(jnp.concatenate(spectral, axis=0), fwd_z[...])
    for band in range(2):
        for r in range(rows):
            for p in range(planes):
                first = ((band * rows + r) * planes + p) * devices
                for part in range(2):
                    start = band * size + (p * rows + r) * 2 + part
                    leaving[pl.ds(start, devices, stride=2 * size), :] = spectral[
                        first : first + devices, part * span_z : (part + 1) * span_z
                    ]


def real_gram_kernel(bands, *refs):
    fields, (pot, out) = refs[:-2], refs[-2:]
    held = fields[0].shape[0]
    pairs = [(a, b) for a in range(bands) for b in range(a, bands)]
    for weighted in range(2):

        def step(i, sums):
            rows = pl.ds(pl.multiple_of(i * 8, 8), 8)
            values = [fields[a // held][a % held, rows, :] for a in range(bands)]
            other = [v * pot[rows, :] for v in values] if weighted else values
            result = []
            for (a, b), total in zip(pairs, sums):
                product = values[a] * other[b]
                lanes = product[:, :128]
                for c in range(128, product.shape[1], 128):
                    lanes = lanes + product[:, c : c + 128]
                result.append(total + lanes)
            return tuple(result)

        sums = lax.fori_loop(
            0, pot.shape[0] // 8, step, tuple(jnp.zeros((8, 128), f32) for _ in pairs)
        )
        for (a, b), total in zip(pairs, sums):
            line = jnp.sum(total, axis=0, keepdims=True)
            out[weighted, a, b : b + 1, :] = line
            out[weighted, b, a : a + 1, :] = line


def to_planes_kernel(recv, base, y_table, out):
    bands, _, planes, span_y, span_z = base.shape
    each = recv.shape[2] // planes
    for band in range(bands):
        for group in groups(planes, span_z):
            columns = [
                recv[:, band, p * each : (p + 1) * each, :].reshape(2 * span_y, span_z)
                for p in group
            ]
            along_y = dot_left(y_table[...], jnp.concatenate(columns, axis=1))
            for i, p in enumerate(group):
                for part in range(2):
                    out[band, part, p] = base[band, part, p] + (
                        along_y[part * span_y : (part + 1) * span_y, i * span_z : (i + 1) * span_z]
                    )


def last_sum_kernel(first, second, _, out):
    out[...] = first[...] + second[...]


def block_rows_of(psi, beta, slots):
    bands, _, span, span_z = psi.shape
    psi_flat = psi.reshape(bands * 2 * span, span_z)
    psi_rows = [psi_flat[pl.ds(y, 2 * bands, stride=span), :] for y in range(span)]
    beta_rows = [
        jnp.concatenate(
            [beta[pl.ds(2 * y + part, slots, stride=2 * span), :] for part in range(2)], axis=0
        )
        for y in range(span)
    ]
    return psi_rows, beta_rows


def project_kernel(slots, psi, beta, kinetic, out):
    bands, _, span, span_z = psi.shape
    psi_rows, beta_rows = block_rows_of(psi, beta, slots)
    kin_rows = [psi_rows[y] * kinetic[y : y + 1, :] for y in range(span)]
    right = jnp.concatenate(split(jnp.concatenate(psi_rows, axis=1)), axis=0)
    left = jnp.concatenate(
        split(jnp.concatenate(beta_rows, axis=1)) + split(jnp.concatenate(kin_rows, axis=1)), axis=0
    )
    full = lax.dot_general(left, right, (((1,), (1,)), ((), ())), preferred_element_type=f32)
    width, height = 2 * bands, 2 * slots
    full = full[:, :width] + full[:, width:]
    out[0:height] = full[0:height] + full[height : 2 * height]
    rest = full[2 * height :]
    out[height:] = rest[0:width] + rest[width:]


def base_kernel(slots, psi, beta, kinetic, coefs, out):
    bands, _, span, span_z = psi.shape
    psi_rows, beta_rows = block_rows_of(psi, beta, slots)
    values = jnp.concatenate(
        [jnp.concatenate(psi_rows, axis=1), jnp.concatenate(beta_rows, axis=1)], axis=0
    )
    high, low = split(coefs[...])
    summed = dot_left(jnp.concatenate([high, high, low], axis=1), values)
    flat = out.reshape(bands * 2 * span, span_z)
    for y in range(span):
        flat[pl.ds(y, 2 * bands, stride=span), :] = (
            psi_rows[y] * kinetic[y : y + 1, :] + summed[:, y * span_z : (y + 1) * span_z]
        )


def whole(shape):
    return pl.BlockSpec(shape, lambda *_: (0,) * len(shape))


def subspace_solve(s_real, h_real, h_imag):
    factor = jnp.linalg.cholesky(s_real)
    solved = jax.scipy.linalg.cho_solve((factor, True), jnp.concatenate([h_real, h_imag], axis=1))
    order_size = s_real.shape[0]
    return (solved[:, :order_size], solved[:, order_size:])


def tdot(pattern, left, right):
    return jnp.einsum(pattern, left, right, precision=highest, preferred_element_type=jnp.float32)


def partner(values, devices, k):
    return lax.ppermute(values, "ga", [(d, d ^ k) for d in range(devices)])


def sum_over(values, devices, after):
    if devices & (devices - 1) or devices < 2:
        return lax.psum(values, "ga")
    step = 1
    while step < devices // 2:
        values = values + partner(values, devices, step)
        step *= 2
    held = pl.BlockSpec(memory_space=pltpu.VMEM)
    return pl.pallas_call(
        last_sum_kernel,
        out_shape=jax.ShapeDtypeStruct(values.shape, f32),
        in_specs=[held] * 2 + [pl.BlockSpec(memory_space=pl.ANY)],
        out_specs=held,
        name="last_sum",
    )(values, partner(values, devices, step), after)


def on_device(devices, orbitals, plane_order, potential, projectors, slot_owner, strengths):
    bands = orbitals.shape[0]
    planes = orbitals.shape[2]
    span_y = orbitals.shape[3]
    span_z = orbitals.shape[4]
    span_x = plane_order.shape[0]
    blocks, slots = slot_owner.shape
    owners = strengths.shape[0] * strengths.shape[1]
    rows = span_y // devices
    block_rows = 2 * planes * rows
    pairs = bands // 2
    block_span = projectors.shape[3] // span_z
    per_plane = span_y // block_span
    grid_x = jnp.arange(span_x, dtype=jnp.int32)
    grid_y = jnp.arange(span_y, dtype=jnp.int32)
    grid_z = jnp.arange(span_z, dtype=jnp.int32)
    params = pltpu.CompilerParams(vmem_limit_bytes=vmem_limit)
    tail_params = pltpu.CompilerParams(vmem_limit_bytes=vmem_limit // 2)

    def cost(flops, moved):
        return pl.CostEstimate(flops=flops, bytes_accessed=moved, transcendentals=0)

    layers = 4 if devices % 4 == 0 else 1
    ranks = np.arange(devices).reshape(layers, -1).T
    if devices % 32 == 0:
        ranks = ranks.reshape(4, -1, layers)[[0, 1, 3, 2]]
    ranks = ranks.reshape(-1)
    order = np.arange(2 * span_y)
    order = (order % 2) * span_y + (ranks[:, None] * rows + np.arange(rows)).reshape(-1)[order // 2]

    def exchange(values):
        return lax.all_to_all(
            values,
            "ga",
            split_axis=0,
            concat_axis=0,
            axis_index_groups=[[int(rank) for rank in ranks]],
            tiled=True,
        )

    inv_y = left_const(left_table(span_y, 1.0)[order])
    fwd_y = left_const(left_table(span_y, -1.0)[:, order])
    inv_z = right_const(right_table(span_z, 1.0))
    fwd_z = right_const(right_table(span_z, -1.0))

    parts = 2 if pairs % 2 == 0 else 1
    share = pairs // parts
    arrived = []
    for c in range(parts):
        sent = pl.pallas_call(
            to_rows_kernel,
            out_shape=jax.ShapeDtypeStruct((devices, share, block_rows, span_z), f32),
            grid=(share,),
            in_specs=[
                pl.BlockSpec(
                    (2, 2, planes, span_y, span_z), lambda j, c=c: (c * share + j, 0, 0, 0, 0)
                ),
                whole(inv_y.shape),
            ],
            out_specs=pl.BlockSpec((devices, None, block_rows, span_z), lambda j: (0, j, 0, 0)),
            compiler_params=params,
            cost_estimate=cost(4 * 10**9, 3 * 10**6),
            name="to_rows",
        )(orbitals, inv_y)
        arrived.append(exchange(sent))

    stored = plane_order.reshape(devices, planes)[ranks].T.reshape(-1)
    phases = (stored[:, None] * grid_x[None, :]) % span_x
    angles = phases.astype(f32) * (2.0 * math.pi / span_x)
    factor = 1.0 / math.sqrt(span_x)
    cosine, sine = jnp.cos(angles) * factor, jnp.sin(angles) * factor
    fwd_x = jnp.concatenate([cosine, -sine], axis=0)
    inv_x = jnp.concatenate([fwd_x, jnp.concatenate([sine, cosine], axis=0)], axis=1).T
    high, low = split_outside(fwd_x)
    fwd_x = jnp.concatenate([high, high, low], axis=1)
    high, low = split_outside(inv_x)
    inv_x = jnp.concatenate([high, high, low], axis=1)
    pot = potential.transpose(1, 0, 2).reshape(rows * span_x, span_z)

    local_order = lax.dynamic_slice_in_dim(plane_order, lax.axis_index("ga") * planes, planes)
    freq_x = signed_index(local_order, span_x).astype(f32) / span_x
    freq_y = signed_index(grid_y, span_y).astype(f32) / span_y
    freq_z = signed_index(grid_z, span_z).astype(f32) / span_z
    kinetic = 2.0 * (
        freq_x[:, None, None] ** 2 + freq_y[None, :, None] ** 2 + freq_z[None, None, :] ** 2
    )
    beta = projectors.reshape(blocks, slots, 2, block_span, span_z)
    beta = beta.transpose(0, 1, 3, 2, 4).reshape(blocks, slots * block_span * 2, span_z)
    block_specs = [
        pl.BlockSpec(
            (bands, 2, None, block_span, span_z),
            lambda g: (0, 0, g // per_plane, g % per_plane, 0),
        ),
        pl.BlockSpec((None, slots * block_span * 2, span_z), lambda g: (g, 0, 0)),
        pl.BlockSpec((None, block_span, span_z), lambda g: (g // per_plane, g % per_plane, 0)),
    ]
    products = pl.pallas_call(
        functools.partial(project_kernel, slots),
        out_shape=jax.ShapeDtypeStruct((blocks, 2 * slots + 2 * bands, 2 * bands), f32),
        grid=(blocks,),
        in_specs=block_specs,
        out_specs=pl.BlockSpec((None, 2 * slots + 2 * bands, 2 * bands), lambda g: (g, 0, 0)),
        compiler_params=params,
        cost_estimate=cost(8 * 10**9, 8 * 10**6),
        name="project",
    )(orbitals, beta, kinetic)
    with_real = products[:, :slots].reshape(blocks, slots, bands, 2)
    with_imag = products[:, slots : 2 * slots].reshape(blocks, slots, bands, 2)
    proj = jnp.concatenate(
        [
            with_real[..., 0] + with_imag[..., 1],
            with_real[..., 1] - with_imag[..., 0],
        ],
        axis=-1,
    )
    owned = (
        slot_owner[:, :, None] == jnp.arange(owners, dtype=jnp.int32)[None, None, :]
    ).astype(f32)
    proj = tdot("gsj,gsc->jc", owned, proj)
    kin = jnp.sum(products[:, 2 * slots :], axis=0).reshape(bands, 2, bands, 2)
    kin = kin[:, 0, :, 0] + kin[:, 1, :, 1]

    returned, fields = [], []
    for c in range(parts):
        back, field = pl.pallas_call(
            functools.partial(real_space_kernel, rows, planes),
            out_shape=(
                jax.ShapeDtypeStruct((devices, 2 * share, block_rows, span_z), f32),
                jax.ShapeDtypeStruct((2 * share, rows * span_x, span_z), f32),
            ),
            grid=(share,),
            in_specs=[
                pl.BlockSpec((devices, None, block_rows, span_z), lambda j: (0, j, 0, 0)),
                whole(pot.shape),
                whole(inv_x.shape),
                whole(fwd_x.shape),
                whole(inv_z.shape),
                whole(fwd_z.shape),
                whole(proj.shape),
            ],
            out_specs=(
                pl.BlockSpec((devices, 2, block_rows, span_z), lambda j: (0, j, 0, 0)),
                pl.BlockSpec((2, rows * span_x, span_z), lambda j: (j, 0, 0)),
            ),
            compiler_params=params,
            cost_estimate=cost(4 * 10**9, 8 * 10**6),
            name="real_space",
        )(arrived[c], pot, inv_x, fwd_x, inv_z, fwd_z, proj)
        returned.append(exchange(back))
        fields.append(field)

    grams = pl.pallas_call(
        functools.partial(real_gram_kernel, bands),
        out_shape=jax.ShapeDtypeStruct((2, bands, bands, 128), f32),
        compiler_params=params,
        cost_estimate=cost(10**7, 2 * 10**6),
        name="real_gram",
    )(*fields, pot)
    grams = jnp.sum(grams, axis=-1)
    own = jnp.concatenate([proj, jnp.concatenate([grams[0], grams[1] + kin], axis=1)], axis=0)
    total = sum_over(own, devices, returned[0])
    proj, s_real, h_real = total[:owners], total[owners:, :bands], total[owners:, bands:]
    weighted = strengths.reshape(-1)[:, None] * proj
    p_real, p_imag = proj[:, :bands], proj[:, bands:]
    w_real, w_imag = weighted[:, :bands], weighted[:, bands:]
    h_real = h_real + tdot("ja,jb->ab", p_real, w_real) + tdot("ja,jb->ab", p_imag, w_imag)
    h_imag = tdot("ja,jb->ab", p_real, w_imag) - tdot("ja,jb->ab", p_imag, w_real)
    m_real, m_imag = subspace_solve(s_real, h_real, h_imag)

    coefs = tdot("gsj,jc->gcs", owned, weighted)
    c_real, c_imag = coefs[:, :bands], coefs[:, bands:]
    from_beta = jnp.stack(
        [
            jnp.concatenate([c_real, -c_imag], axis=2),
            jnp.concatenate([c_imag, c_real], axis=2),
        ],
        axis=2,
    ).reshape(blocks, 2 * bands, 2 * slots)
    from_psi = jnp.stack(
        [
            jnp.stack([-m_real.T, m_imag.T], axis=-1),
            jnp.stack([-m_imag.T, -m_real.T], axis=-1),
        ],
        axis=1,
    ).reshape(1, 2 * bands, 2 * bands)
    coefs = jnp.concatenate(
        [jnp.broadcast_to(from_psi, (blocks, 2 * bands, 2 * bands)), from_beta], axis=2
    )
    base = pl.pallas_call(
        functools.partial(base_kernel, slots),
        out_shape=jax.ShapeDtypeStruct(orbitals.shape, f32),
        grid=(blocks,),
        in_specs=block_specs
        + [pl.BlockSpec((None, 2 * bands, 2 * bands + 2 * slots), lambda g: (g, 0, 0))],
        out_specs=block_specs[0],
        compiler_params=tail_params,
        cost_estimate=cost(8 * 10**9, 12 * 10**6),
        name="base",
    )(orbitals, beta, kinetic, coefs)

    residual = base
    for c in range(parts):
        two_bands = pl.BlockSpec(
            (2, 2, planes, span_y, span_z), lambda j, c=c: (share * c + j, 0, 0, 0, 0)
        )
        residual = pl.pallas_call(
            to_planes_kernel,
            out_shape=jax.ShapeDtypeStruct(orbitals.shape, f32),
            grid=(share,),
            in_specs=[
                pl.BlockSpec((devices, 2, block_rows, span_z), lambda j: (0, j, 0, 0)),
                two_bands,
                whole(fwd_y.shape),
            ],
            out_specs=two_bands,
            input_output_aliases={1: 0},
            compiler_params=tail_params,
            cost_estimate=cost(8 * 10**9, 12 * 10**6),
            name="to_planes",
        )(returned[c], residual, fwd_y)
    return (residual, jnp.stack([m_real, m_imag]))


def solution(mesh):
    return jax.shard_map(
        functools.partial(on_device, mesh.shape["ga"]),
        mesh=mesh,
        in_specs=(
            P("rep", None, "ga", None, None),
            P("rep"),
            P("rep", "ga", None),
            P(("rep", "ga"), None, None, None),
            P(("rep", "ga"), None),
            P("rep", None),
        ),
        out_specs=(P("rep", None, "ga", None, None), P(None, "rep", None)),
        check_vma=False,
    )
```

```python
import functools
import math

import jax
import jax.numpy as jnp
import numpy as np
from jax import lax
from jax.experimental import pallas as pl
from jax.experimental.pallas import tpu as pltpu
from jax.sharding import PartitionSpec as P

highest = lax.Precision.HIGHEST
f32 = jnp.float32
bf16 = jnp.bfloat16
vmem_limit = 63 * 1024 * 1024


def signed_index(values, length):
    return jnp.where(values < length // 2, values, values - length)


def dft(length, orient):
    index = np.arange(length)
    angles = (index[:, None] * index[None, :] % length) * (2.0 * math.pi / length)
    factor = 1.0 / math.sqrt(length)
    return np.cos(angles) * factor, orient * np.sin(angles) * factor


def left_table(length, orient):
    cosine, sine = dft(length, orient)
    return np.block([[cosine, -sine], [sine, cosine]])


def right_table(length, orient):
    cosine, sine = dft(length, orient)
    return np.block([[cosine, sine], [-sine, cosine]])


def split(values):
    high = values.astype(bf16)
    low = (values - high.astype(f32)).astype(bf16)
    return high, low


def split_outside(values):
    high = lax.reduce_precision(values, exponent_bits=8, mantissa_bits=7)
    return high.astype(bf16), (values - high).astype(bf16)


def const_parts(table):
    table = np.asarray(table, np.float32)
    high = table.astype(jnp.bfloat16)
    low = (table - high.astype(np.float32)).astype(jnp.bfloat16)
    return high, low


def left_const(table):
    high, low = const_parts(table)
    return jnp.asarray(np.concatenate([high, high, low], axis=1))


def right_const(table):
    high, low = const_parts(table)
    return jnp.asarray(np.concatenate([high, high, low], axis=0))


def dot_left(table, values):
    high, low = split(values)
    return jnp.dot(
        table, jnp.concatenate([high, low, high], axis=0), preferred_element_type=f32
    )


def dot_right(values, table):
    high, low = split(values)
    return jnp.dot(
        jnp.concatenate([high, low, high], axis=1), table, preferred_element_type=f32
    )


def groups(count, width):
    size = max(1, 256 // width)
    return [list(range(i, min(i + size, count))) for i in range(0, count, size)]


def parts_in_lanes(values, span, width):
    items = values.shape[1] // width
    return jnp.concatenate(
        [
            jnp.concatenate(
                [values[:span, i * width : (i + 1) * width], values[span:, i * width : (i + 1) * width]],
                axis=1,
            )
            for i in range(items)
        ],
        axis=0,
    )


def to_rows_kernel(psi, y_table, out):
    _, _, planes, span_y, span_z = psi.shape
    devices, block_rows, _ = out.shape
    each = block_rows // planes
    for group in groups(planes, span_z):
        real = jnp.concatenate([psi[0, 0, p] - psi[1, 1, p] for p in group], axis=1)
        imag = jnp.concatenate([psi[0, 1, p] + psi[1, 0, p] for p in group], axis=1)
        along_y = dot_left(y_table[...], jnp.concatenate([real, imag], axis=0))
        for i, p in enumerate(group):
            out[:, p * each : (p + 1) * each, :] = along_y[
                :, i * span_z : (i + 1) * span_z
            ].reshape(devices, each, span_z)


def real_space_kernel(rows, planes, recv, pot, inverse, forward, inv_z, fwd_z, _, back, field):
    devices, size, span_z = recv.shape
    span_x = devices * planes
    arrived = recv.reshape(devices * size, span_z)
    leaving = back.reshape(devices * 2 * size, span_z)
    columns = [
        jnp.concatenate(
            [
                arrived[pl.ds((p * rows + r) * 2 + part, devices, stride=size), :]
                for part in range(2)
                for p in range(planes)
            ],
            axis=0,
        )
        for r in range(rows)
    ]
    along_x = dot_left(inverse[...], jnp.concatenate(columns, axis=1))
    spatial = dot_right(parts_in_lanes(along_x, span_x, span_z), inv_z[...])
    spectral = []
    for band in range(2):
        one = spatial[:, band * span_z : (band + 1) * span_z]
        field[band] = one
        product = one * pot[...]
        product = jnp.concatenate(
            [product[r * span_x : (r + 1) * span_x] for r in range(rows)], axis=1
        )
        spectral.append(parts_in_lanes(dot_left(forward[...], product), span_x, span_z))
    spectral = dot_right(jnp.concatenate(spectral, axis=0), fwd_z[...])
    for band in range(2):
        for r in range(rows):
            for p in range(planes):
                first = ((band * rows + r) * planes + p) * devices
                for part in range(2):
                    start = band * size + (p * rows + r) * 2 + part
                    leaving[pl.ds(start, devices, stride=2 * size), :] = spectral[
                        first : first + devices, part * span_z : (part + 1) * span_z
                    ]


def real_gram_kernel(bands, *refs):
    fields, (pot, out) = refs[:-2], refs[-2:]
    held = fields[0].shape[0]
    pairs = [(a, b) for a in range(bands) for b in range(a, bands)]
    for weighted in range(2):

        def step(i, sums):
            rows = pl.ds(pl.multiple_of(i * 8, 8), 8)
            values = [fields[a // held][a % held, rows, :] for a in range(bands)]
            other = [v * pot[rows, :] for v in values] if weighted else values
            result = []
            for (a, b), total in zip(pairs, sums):
                product = values[a] * other[b]
                lanes = product[:, :128]
                for c in range(128, product.shape[1], 128):
                    lanes = lanes + product[:, c : c + 128]
                result.append(total + lanes)
            return tuple(result)

        sums = lax.fori_loop(
            0, pot.shape[0] // 8, step, tuple(jnp.zeros((8, 128), f32) for _ in pairs)
        )
        for (a, b), total in zip(pairs, sums):
            line = jnp.sum(total, axis=0, keepdims=True)
            out[weighted, a, b : b + 1, :] = line
            out[weighted, b, a : a + 1, :] = line


def to_planes_kernel(recv, base, y_table, out):
    bands, _, planes, span_y, span_z = base.shape
    each = recv.shape[2] // planes
    for band in range(bands):
        for group in groups(planes, span_z):
            columns = [
                recv[:, band, p * each : (p + 1) * each, :].reshape(2 * span_y, span_z)
                for p in group
            ]
            along_y = dot_left(y_table[...], jnp.concatenate(columns, axis=1))
            for i, p in enumerate(group):
                for part in range(2):
                    out[band, part, p] = base[band, part, p] + (
                        along_y[part * span_y : (part + 1) * span_y, i * span_z : (i + 1) * span_z]
                    )


def last_sum_kernel(first, second, _, out):
    out[...] = first[...] + second[...]


def block_rows_of(psi, beta, slots):
    bands, _, span, span_z = psi.shape
    psi_flat = psi.reshape(bands * 2 * span, span_z)
    psi_rows = [psi_flat[pl.ds(y, 2 * bands, stride=span), :] for y in range(span)]
    beta_rows = [
        jnp.concatenate(
            [beta[pl.ds(2 * y + part, slots, stride=2 * span), :] for part in range(2)], axis=0
        )
        for y in range(span)
    ]
    return psi_rows, beta_rows


def project_kernel(slots, psi, beta, kinetic, out):
    bands, _, span, span_z = psi.shape
    psi_rows, beta_rows = block_rows_of(psi, beta, slots)
    kin_rows = [psi_rows[y] * kinetic[y : y + 1, :] for y in range(span)]
    right = jnp.concatenate(split(jnp.concatenate(psi_rows, axis=1)), axis=0)
    left = jnp.concatenate(
        split(jnp.concatenate(beta_rows, axis=1)) + split(jnp.concatenate(kin_rows, axis=1)), axis=0
    )
    full = lax.dot_general(left, right, (((1,), (1,)), ((), ())), preferred_element_type=f32)
    width, height = 2 * bands, 2 * slots
    full = full[:, :width] + full[:, width:]
    out[0:height] = full[0:height] + full[height : 2 * height]
    rest = full[2 * height :]
    out[height:] = rest[0:width] + rest[width:]


def base_kernel(slots, psi, beta, kinetic, coefs, out):
    bands, _, span, span_z = psi.shape
    psi_rows, beta_rows = block_rows_of(psi, beta, slots)
    values = jnp.concatenate(
        [jnp.concatenate(psi_rows, axis=1), jnp.concatenate(beta_rows, axis=1)], axis=0
    )
    high, low = split(coefs[...])
    summed = dot_left(jnp.concatenate([high, high, low], axis=1), values)
    flat = out.reshape(bands * 2 * span, span_z)
    for y in range(span):
        flat[pl.ds(y, 2 * bands, stride=span), :] = (
            psi_rows[y] * kinetic[y : y + 1, :] + summed[:, y * span_z : (y + 1) * span_z]
        )


def whole(shape):
    return pl.BlockSpec(shape, lambda *_: (0,) * len(shape))


def subspace_solve(s_real, h_real, h_imag):
    factor = jnp.linalg.cholesky(s_real)
    solved = jax.scipy.linalg.cho_solve((factor, True), jnp.concatenate([h_real, h_imag], axis=1))
    order_size = s_real.shape[0]
    return (solved[:, :order_size], solved[:, order_size:])


def tdot(pattern, left, right):
    return jnp.einsum(pattern, left, right, precision=highest, preferred_element_type=jnp.float32)


def partner(values, devices, k):
    return lax.ppermute(values, "ga", [(d, d ^ k) for d in range(devices)])


def sum_over(values, devices, after):
    if devices & (devices - 1) or devices < 2:
        return lax.psum(values, "ga")
    step = 1
    while step < devices // 2:
        values = values + partner(values, devices, step)
        step *= 2
    held = pl.BlockSpec(memory_space=pltpu.VMEM)
    return pl.pallas_call(
        last_sum_kernel,
        out_shape=jax.ShapeDtypeStruct(values.shape, f32),
        in_specs=[held] * 2 + [pl.BlockSpec(memory_space=pl.ANY)],
        out_specs=held,
        name="last_sum",
    )(values, partner(values, devices, step), after)


def on_device(devices, orbitals, plane_order, potential, projectors, slot_owner, strengths):
    bands = orbitals.shape[0]
    planes = orbitals.shape[2]
    span_y = orbitals.shape[3]
    span_z = orbitals.shape[4]
    span_x = plane_order.shape[0]
    blocks, slots = slot_owner.shape
    owners = strengths.shape[0] * strengths.shape[1]
    rows = span_y // devices
    block_rows = 2 * planes * rows
    pairs = bands // 2
    block_span = projectors.shape[3] // span_z
    per_plane = span_y // block_span
    grid_x = jnp.arange(span_x, dtype=jnp.int32)
    grid_y = jnp.arange(span_y, dtype=jnp.int32)
    grid_z = jnp.arange(span_z, dtype=jnp.int32)
    params = pltpu.CompilerParams(vmem_limit_bytes=vmem_limit)
    tail_params = pltpu.CompilerParams(vmem_limit_bytes=vmem_limit // 2)

    def cost(flops, moved):
        return pl.CostEstimate(flops=flops, bytes_accessed=moved, transcendentals=0)

    layers = 4 if devices % 4 == 0 else 1
    ranks = np.arange(devices).reshape(layers, -1).T
    if devices % 32 == 0:
        ranks = ranks.reshape(4, -1, layers)[[0, 1, 3, 2]]
    ranks = ranks.reshape(-1, layers)
    ranks = np.stack([np.roll(one, -i) for i, one in enumerate(ranks)]).reshape(-1)
    order = np.arange(2 * span_y)
    order = (order % 2) * span_y + (ranks[:, None] * rows + np.arange(rows)).reshape(-1)[order // 2]

    def exchange(values):
        return lax.all_to_all(
            values,
            "ga",
            split_axis=0,
            concat_axis=0,
            axis_index_groups=[[int(rank) for rank in ranks]],
            tiled=True,
        )

    inv_y = left_const(left_table(span_y, 1.0)[order])
    fwd_y = left_const(left_table(span_y, -1.0)[:, order])
    inv_z = right_const(right_table(span_z, 1.0))
    fwd_z = right_const(right_table(span_z, -1.0))

    parts = 2 if pairs % 2 == 0 else 1
    share = pairs // parts
    arrived = []
    for c in range(parts):
        sent = pl.pallas_call(
            to_rows_kernel,
            out_shape=jax.ShapeDtypeStruct((devices, share, block_rows, span_z), f32),
            grid=(share,),
            in_specs=[
                pl.BlockSpec(
                    (2, 2, planes, span_y, span_z), lambda j, c=c: (c * share + j, 0, 0, 0, 0)
                ),
                whole(inv_y.shape),
            ],
            out_specs=pl.BlockSpec((devices, None, block_rows, span_z), lambda j: (0, j, 0, 0)),
            compiler_params=params,
            cost_estimate=cost(4 * 10**9, 3 * 10**6),
            name="to_rows",
        )(orbitals, inv_y)
        arrived.append(exchange(sent))

    stored = plane_order.reshape(devices, planes)[ranks].T.reshape(-1)
    phases = (stored[:, None] * grid_x[None, :]) % span_x
    angles = phases.astype(f32) * (2.0 * math.pi / span_x)
    factor = 1.0 / math.sqrt(span_x)
    cosine, sine = jnp.cos(angles) * factor, jnp.sin(angles) * factor
    fwd_x = jnp.concatenate([cosine, -sine], axis=0)
    inv_x = jnp.concatenate([fwd_x, jnp.concatenate([sine, cosine], axis=0)], axis=1).T
    high, low = split_outside(fwd_x)
    fwd_x = jnp.concatenate([high, high, low], axis=1)
    high, low = split_outside(inv_x)
    inv_x = jnp.concatenate([high, high, low], axis=1)
    pot = potential.transpose(1, 0, 2).reshape(rows * span_x, span_z)

    local_order = lax.dynamic_slice_in_dim(plane_order, lax.axis_index("ga") * planes, planes)
    freq_x = signed_index(local_order, span_x).astype(f32) / span_x
    freq_y = signed_index(grid_y, span_y).astype(f32) / span_y
    freq_z = signed_index(grid_z, span_z).astype(f32) / span_z
    kinetic = 2.0 * (
        freq_x[:, None, None] ** 2 + freq_y[None, :, None] ** 2 + freq_z[None, None, :] ** 2
    )
    beta = projectors.reshape(blocks, slots, 2, block_span, span_z)
    beta = beta.transpose(0, 1, 3, 2, 4).reshape(blocks, slots * block_span * 2, span_z)
    block_specs = [
        pl.BlockSpec(
            (bands, 2, None, block_span, span_z),
            lambda g: (0, 0, g // per_plane, g % per_plane, 0),
        ),
        pl.BlockSpec((None, slots * block_span * 2, span_z), lambda g: (g, 0, 0)),
        pl.BlockSpec((None, block_span, span_z), lambda g: (g // per_plane, g % per_plane, 0)),
    ]
    products = pl.pallas_call(
        functools.partial(project_kernel, slots),
        out_shape=jax.ShapeDtypeStruct((blocks, 2 * slots + 2 * bands, 2 * bands), f32),
        grid=(blocks,),
        in_specs=block_specs,
        out_specs=pl.BlockSpec((None, 2 * slots + 2 * bands, 2 * bands), lambda g: (g, 0, 0)),
        compiler_params=params,
        cost_estimate=cost(8 * 10**9, 8 * 10**6),
        name="project",
    )(orbitals, beta, kinetic)
    with_real = products[:, :slots].reshape(blocks, slots, bands, 2)
    with_imag = products[:, slots : 2 * slots].reshape(blocks, slots, bands, 2)
    proj = jnp.concatenate(
        [
            with_real[..., 0] + with_imag[..., 1],
            with_real[..., 1] - with_imag[..., 0],
        ],
        axis=-1,
    )
    owned = (
        slot_owner[:, :, None] == jnp.arange(owners, dtype=jnp.int32)[None, None, :]
    ).astype(f32)
    proj = tdot("gsj,gsc->jc", owned, proj)
    kin = jnp.sum(products[:, 2 * slots :], axis=0).reshape(bands, 2, bands, 2)
    kin = kin[:, 0, :, 0] + kin[:, 1, :, 1]

    returned, fields = [], []
    for c in range(parts):
        back, field = pl.pallas_call(
            functools.partial(real_space_kernel, rows, planes),
            out_shape=(
                jax.ShapeDtypeStruct((devices, 2 * share, block_rows, span_z), f32),
                jax.ShapeDtypeStruct((2 * share, rows * span_x, span_z), f32),
            ),
            grid=(share,),
            in_specs=[
                pl.BlockSpec((devices, None, block_rows, span_z), lambda j: (0, j, 0, 0)),
                whole(pot.shape),
                whole(inv_x.shape),
                whole(fwd_x.shape),
                whole(inv_z.shape),
                whole(fwd_z.shape),
                whole(proj.shape),
            ],
            out_specs=(
                pl.BlockSpec((devices, 2, block_rows, span_z), lambda j: (0, j, 0, 0)),
                pl.BlockSpec((2, rows * span_x, span_z), lambda j: (j, 0, 0)),
            ),
            compiler_params=params,
            cost_estimate=cost(4 * 10**9, 8 * 10**6),
            name="real_space",
        )(arrived[c], pot, inv_x, fwd_x, inv_z, fwd_z, proj)
        returned.append(exchange(back))
        fields.append(field)

    grams = pl.pallas_call(
        functools.partial(real_gram_kernel, bands),
        out_shape=jax.ShapeDtypeStruct((2, bands, bands, 128), f32),
        compiler_params=params,
        cost_estimate=cost(10**7, 2 * 10**6),
        name="real_gram",
    )(*fields, pot)
    grams = jnp.sum(grams, axis=-1)
    own = jnp.concatenate([proj, jnp.concatenate([grams[0], grams[1] + kin], axis=1)], axis=0)
    total = sum_over(own, devices, returned[0])
    proj, s_real, h_real = total[:owners], total[owners:, :bands], total[owners:, bands:]
    weighted = strengths.reshape(-1)[:, None] * proj
    p_real, p_imag = proj[:, :bands], proj[:, bands:]
    w_real, w_imag = weighted[:, :bands], weighted[:, bands:]
    h_real = h_real + tdot("ja,jb->ab", p_real, w_real) + tdot("ja,jb->ab", p_imag, w_imag)
    h_imag = tdot("ja,jb->ab", p_real, w_imag) - tdot("ja,jb->ab", p_imag, w_real)
    m_real, m_imag = subspace_solve(s_real, h_real, h_imag)

    coefs = tdot("gsj,jc->gcs", owned, weighted)
    c_real, c_imag = coefs[:, :bands], coefs[:, bands:]
    from_beta = jnp.stack(
        [
            jnp.concatenate([c_real, -c_imag], axis=2),
            jnp.concatenate([c_imag, c_real], axis=2),
        ],
        axis=2,
    ).reshape(blocks, 2 * bands, 2 * slots)
    from_psi = jnp.stack(
        [
            jnp.stack([-m_real.T, m_imag.T], axis=-1),
            jnp.stack([-m_imag.T, -m_real.T], axis=-1),
        ],
        axis=1,
    ).reshape(1, 2 * bands, 2 * bands)
    coefs = jnp.concatenate(
        [jnp.broadcast_to(from_psi, (blocks, 2 * bands, 2 * bands)), from_beta], axis=2
    )
    base = pl.pallas_call(
        functools.partial(base_kernel, slots),
        out_shape=jax.ShapeDtypeStruct(orbitals.shape, f32),
        grid=(blocks,),
        in_specs=block_specs
        + [pl.BlockSpec((None, 2 * bands, 2 * bands + 2 * slots), lambda g: (g, 0, 0))],
        out_specs=block_specs[0],
        compiler_params=tail_params,
        cost_estimate=cost(8 * 10**9, 12 * 10**6),
        name="base",
    )(orbitals, beta, kinetic, coefs)

    residual = base
    for c in range(parts):
        two_bands = pl.BlockSpec(
            (2, 2, planes, span_y, span_z), lambda j, c=c: (share * c + j, 0, 0, 0, 0)
        )
        residual = pl.pallas_call(
            to_planes_kernel,
            out_shape=jax.ShapeDtypeStruct(orbitals.shape, f32),
            grid=(share,),
            in_specs=[
                pl.BlockSpec((devices, 2, block_rows, span_z), lambda j: (0, j, 0, 0)),
                two_bands,
                whole(fwd_y.shape),
            ],
            out_specs=two_bands,
            input_output_aliases={1: 0},
            compiler_params=tail_params,
            cost_estimate=cost(8 * 10**9, 12 * 10**6),
            name="to_planes",
        )(returned[c], residual, fwd_y)
    return (residual, jnp.stack([m_real, m_imag]))


def solution(mesh):
    return jax.shard_map(
        functools.partial(on_device, mesh.shape["ga"]),
        mesh=mesh,
        in_specs=(
            P("rep", None, "ga", None, None),
            P("rep"),
            P("rep", "ga", None),
            P(("rep", "ga"), None, None, None),
            P(("rep", "ga"), None),
            P("rep", None),
        ),
        out_specs=(P("rep", None, "ga", None, None), P(None, "rep", None)),
        check_vma=False,
    )
```

```python
import functools
import math

import jax
import jax.numpy as jnp
import numpy as np
from jax import lax
from jax.experimental import pallas as pl
from jax.experimental.pallas import tpu as pltpu
from jax.sharding import PartitionSpec as P

highest = lax.Precision.HIGHEST
f32 = jnp.float32
bf16 = jnp.bfloat16
vmem_limit = 63 * 1024 * 1024


def signed_index(values, length):
    return jnp.where(values < length // 2, values, values - length)


def dft(length, orient):
    index = np.arange(length)
    angles = (index[:, None] * index[None, :] % length) * (2.0 * math.pi / length)
    factor = 1.0 / math.sqrt(length)
    return np.cos(angles) * factor, orient * np.sin(angles) * factor


def left_table(length, orient):
    cosine, sine = dft(length, orient)
    return np.block([[cosine, -sine], [sine, cosine]])


def right_table(length, orient):
    cosine, sine = dft(length, orient)
    return np.block([[cosine, sine], [-sine, cosine]])


def split(values):
    high = values.astype(bf16)
    low = (values - high.astype(f32)).astype(bf16)
    return high, low


def split_outside(values):
    high = lax.reduce_precision(values, exponent_bits=8, mantissa_bits=7)
    return high.astype(bf16), (values - high).astype(bf16)


def const_parts(table):
    table = np.asarray(table, np.float32)
    high = table.astype(jnp.bfloat16)
    low = (table - high.astype(np.float32)).astype(jnp.bfloat16)
    return high, low


def left_const(table):
    high, low = const_parts(table)
    return jnp.asarray(np.concatenate([high, high, low], axis=1))


def right_const(table):
    high, low = const_parts(table)
    return jnp.asarray(np.concatenate([high, high, low], axis=0))


def dot_left(table, values):
    high, low = split(values)
    return jnp.dot(
        table, jnp.concatenate([high, low, high], axis=0), preferred_element_type=f32
    )


def dot_right(values, table):
    high, low = split(values)
    return jnp.dot(
        jnp.concatenate([high, low, high], axis=1), table, preferred_element_type=f32
    )


def groups(count, width):
    size = max(1, 256 // width)
    return [list(range(i, min(i + size, count))) for i in range(0, count, size)]


def parts_in_lanes(values, span, width):
    items = values.shape[1] // width
    return jnp.concatenate(
        [
            jnp.concatenate(
                [values[:span, i * width : (i + 1) * width], values[span:, i * width : (i + 1) * width]],
                axis=1,
            )
            for i in range(items)
        ],
        axis=0,
    )


def to_rows_kernel(psi, y_table, out):
    _, _, planes, span_y, span_z = psi.shape
    devices, block_rows, _ = out.shape
    each = block_rows // planes
    for group in groups(planes, span_z):
        real = jnp.concatenate([psi[0, 0, p] - psi[1, 1, p] for p in group], axis=1)
        imag = jnp.concatenate([psi[0, 1, p] + psi[1, 0, p] for p in group], axis=1)
        along_y = dot_left(y_table[...], jnp.concatenate([real, imag], axis=0))
        for i, p in enumerate(group):
            out[:, p * each : (p + 1) * each, :] = along_y[
                :, i * span_z : (i + 1) * span_z
            ].reshape(devices, each, span_z)


def real_space_kernel(rows, planes, recv, pot, inverse, forward, inv_z, fwd_z, _, back, field):
    devices, size, span_z = recv.shape
    span_x = devices * planes
    arrived = recv.reshape(devices * size, span_z)
    leaving = back.reshape(devices * 2 * size, span_z)
    columns = [
        jnp.concatenate(
            [
                arrived[pl.ds((p * rows + r) * 2 + part, devices, stride=size), :]
                for part in range(2)
                for p in range(planes)
            ],
            axis=0,
        )
        for r in range(rows)
    ]
    along_x = dot_left(inverse[...], jnp.concatenate(columns, axis=1))
    spatial = dot_right(parts_in_lanes(along_x, span_x, span_z), inv_z[...])
    spectral = []
    for band in range(2):
        one = spatial[:, band * span_z : (band + 1) * span_z]
        field[band] = one
        product = one * pot[...]
        product = jnp.concatenate(
            [product[r * span_x : (r + 1) * span_x] for r in range(rows)], axis=1
        )
        spectral.append(parts_in_lanes(dot_left(forward[...], product), span_x, span_z))
    spectral = dot_right(jnp.concatenate(spectral, axis=0), fwd_z[...])
    for band in range(2):
        for r in range(rows):
            for p in range(planes):
                first = ((band * rows + r) * planes + p) * devices
                for part in range(2):
                    start = band * size + (p * rows + r) * 2 + part
                    leaving[pl.ds(start, devices, stride=2 * size), :] = spectral[
                        first : first + devices, part * span_z : (part + 1) * span_z
                    ]


def real_gram_kernel(bands, *refs):
    fields, (pot, out) = refs[:-2], refs[-2:]
    held = fields[0].shape[0]
    pairs = [(a, b) for a in range(bands) for b in range(a, bands)]
    for weighted in range(2):

        def step(i, sums):
            rows = pl.ds(pl.multiple_of(i * 8, 8), 8)
            values = [fields[a // held][a % held, rows, :] for a in range(bands)]
            other = [v * pot[rows, :] for v in values] if weighted else values
            result = []
            for (a, b), total in zip(pairs, sums):
                product = values[a] * other[b]
                lanes = product[:, :128]
                for c in range(128, product.shape[1], 128):
                    lanes = lanes + product[:, c : c + 128]
                result.append(total + lanes)
            return tuple(result)

        sums = lax.fori_loop(
            0, pot.shape[0] // 8, step, tuple(jnp.zeros((8, 128), f32) for _ in pairs)
        )
        for (a, b), total in zip(pairs, sums):
            line = jnp.sum(total, axis=0, keepdims=True)
            out[weighted, a, b : b + 1, :] = line
            out[weighted, b, a : a + 1, :] = line


def to_planes_kernel(recv, base, y_table, out):
    bands, _, planes, span_y, span_z = base.shape
    each = recv.shape[2] // planes
    for band in range(bands):
        for group in groups(planes, span_z):
            columns = [
                recv[:, band, p * each : (p + 1) * each, :].reshape(2 * span_y, span_z)
                for p in group
            ]
            along_y = dot_left(y_table[...], jnp.concatenate(columns, axis=1))
            for i, p in enumerate(group):
                for part in range(2):
                    out[band, part, p] = base[band, part, p] + (
                        along_y[part * span_y : (part + 1) * span_y, i * span_z : (i + 1) * span_z]
                    )


def last_sum_kernel(first, second, _, out):
    out[...] = first[...] + second[...]


def block_rows_of(psi, beta, slots):
    bands, _, span, span_z = psi.shape
    psi_flat = psi.reshape(bands * 2 * span, span_z)
    psi_rows = [psi_flat[pl.ds(y, 2 * bands, stride=span), :] for y in range(span)]
    beta_rows = [
        jnp.concatenate(
            [beta[pl.ds(2 * y + part, slots, stride=2 * span), :] for part in range(2)], axis=0
        )
        for y in range(span)
    ]
    return psi_rows, beta_rows


def project_kernel(slots, psi, beta, kinetic, out):
    bands, _, span, span_z = psi.shape
    psi_rows, beta_rows = block_rows_of(psi, beta, slots)
    kin_rows = [psi_rows[y] * kinetic[y : y + 1, :] for y in range(span)]
    right = jnp.concatenate(split(jnp.concatenate(psi_rows, axis=1)), axis=0)
    left = jnp.concatenate(
        split(jnp.concatenate(beta_rows, axis=1)) + split(jnp.concatenate(kin_rows, axis=1)), axis=0
    )
    full = lax.dot_general(left, right, (((1,), (1,)), ((), ())), preferred_element_type=f32)
    width, height = 2 * bands, 2 * slots
    full = full[:, :width] + full[:, width:]
    out[0:height] = full[0:height] + full[height : 2 * height]
    rest = full[2 * height :]
    out[height:] = rest[0:width] + rest[width:]


def base_kernel(slots, psi, beta, kinetic, coefs, out):
    bands, _, span, span_z = psi.shape
    psi_rows, beta_rows = block_rows_of(psi, beta, slots)
    values = jnp.concatenate(
        [jnp.concatenate(psi_rows, axis=1), jnp.concatenate(beta_rows, axis=1)], axis=0
    )
    high, low = split(coefs[...])
    summed = dot_left(jnp.concatenate([high, high, low], axis=1), values)
    flat = out.reshape(bands * 2 * span, span_z)
    for y in range(span):
        flat[pl.ds(y, 2 * bands, stride=span), :] = (
            psi_rows[y] * kinetic[y : y + 1, :] + summed[:, y * span_z : (y + 1) * span_z]
        )


def whole(shape):
    return pl.BlockSpec(shape, lambda *_: (0,) * len(shape))


def subspace_solve(s_real, h_real, h_imag):
    factor = jnp.linalg.cholesky(s_real)
    solved = jax.scipy.linalg.cho_solve((factor, True), jnp.concatenate([h_real, h_imag], axis=1))
    order_size = s_real.shape[0]
    return (solved[:, :order_size], solved[:, order_size:])


def tdot(pattern, left, right):
    return jnp.einsum(pattern, left, right, precision=highest, preferred_element_type=jnp.float32)


def partner(values, devices, k):
    return lax.ppermute(values, "ga", [(d, d ^ k) for d in range(devices)])


def sum_over(values, devices, after):
    if devices & (devices - 1) or devices < 2:
        return lax.psum(values, "ga")
    step = 1
    while step < devices // 2:
        values = values + partner(values, devices, step)
        step *= 2
    held = pl.BlockSpec(memory_space=pltpu.VMEM)
    return pl.pallas_call(
        last_sum_kernel,
        out_shape=jax.ShapeDtypeStruct(values.shape, f32),
        in_specs=[held] * 2 + [pl.BlockSpec(memory_space=pl.ANY)],
        out_specs=held,
        name="last_sum",
    )(values, partner(values, devices, step), after)


def on_device(devices, orbitals, plane_order, potential, projectors, slot_owner, strengths):
    bands = orbitals.shape[0]
    planes = orbitals.shape[2]
    span_y = orbitals.shape[3]
    span_z = orbitals.shape[4]
    span_x = plane_order.shape[0]
    blocks, slots = slot_owner.shape
    owners = strengths.shape[0] * strengths.shape[1]
    rows = span_y // devices
    block_rows = 2 * planes * rows
    pairs = bands // 2
    block_span = projectors.shape[3] // span_z
    per_plane = span_y // block_span
    grid_x = jnp.arange(span_x, dtype=jnp.int32)
    grid_y = jnp.arange(span_y, dtype=jnp.int32)
    grid_z = jnp.arange(span_z, dtype=jnp.int32)
    params = pltpu.CompilerParams(vmem_limit_bytes=vmem_limit)
    tail_params = pltpu.CompilerParams(vmem_limit_bytes=vmem_limit // 2)

    def cost(flops, moved):
        return pl.CostEstimate(flops=flops, bytes_accessed=moved, transcendentals=0)

    layers = 4 if devices % 4 == 0 else 1
    ranks = np.arange(devices).reshape(layers, -1).T
    if devices % 32 == 0:
        ranks = ranks.reshape(4, -1, layers)[[0, 1, 3, 2]].transpose(1, 0, 2)
    ranks = ranks.reshape(-1)
    order = np.arange(2 * span_y)
    order = (order % 2) * span_y + (ranks[:, None] * rows + np.arange(rows)).reshape(-1)[order // 2]

    def exchange(values):
        return lax.all_to_all(
            values,
            "ga",
            split_axis=0,
            concat_axis=0,
            axis_index_groups=[[int(rank) for rank in ranks]],
            tiled=True,
        )

    inv_y = left_const(left_table(span_y, 1.0)[order])
    fwd_y = left_const(left_table(span_y, -1.0)[:, order])
    inv_z = right_const(right_table(span_z, 1.0))
    fwd_z = right_const(right_table(span_z, -1.0))

    parts = 2 if pairs % 2 == 0 else 1
    share = pairs // parts
    arrived = []
    for c in range(parts):
        sent = pl.pallas_call(
            to_rows_kernel,
            out_shape=jax.ShapeDtypeStruct((devices, share, block_rows, span_z), f32),
            grid=(share,),
            in_specs=[
                pl.BlockSpec(
                    (2, 2, planes, span_y, span_z), lambda j, c=c: (c * share + j, 0, 0, 0, 0)
                ),
                whole(inv_y.shape),
            ],
            out_specs=pl.BlockSpec((devices, None, block_rows, span_z), lambda j: (0, j, 0, 0)),
            compiler_params=params,
            cost_estimate=cost(4 * 10**9, 3 * 10**6),
            name="to_rows",
        )(orbitals, inv_y)
        arrived.append(exchange(sent))

    stored = plane_order.reshape(devices, planes)[ranks].T.reshape(-1)
    phases = (stored[:, None] * grid_x[None, :]) % span_x
    angles = phases.astype(f32) * (2.0 * math.pi / span_x)
    factor = 1.0 / math.sqrt(span_x)
    cosine, sine = jnp.cos(angles) * factor, jnp.sin(angles) * factor
    fwd_x = jnp.concatenate([cosine, -sine], axis=0)
    inv_x = jnp.concatenate([fwd_x, jnp.concatenate([sine, cosine], axis=0)], axis=1).T
    high, low = split_outside(fwd_x)
    fwd_x = jnp.concatenate([high, high, low], axis=1)
    high, low = split_outside(inv_x)
    inv_x = jnp.concatenate([high, high, low], axis=1)
    pot = potential.transpose(1, 0, 2).reshape(rows * span_x, span_z)

    local_order = lax.dynamic_slice_in_dim(plane_order, lax.axis_index("ga") * planes, planes)
    freq_x = signed_index(local_order, span_x).astype(f32) / span_x
    freq_y = signed_index(grid_y, span_y).astype(f32) / span_y
    freq_z = signed_index(grid_z, span_z).astype(f32) / span_z
    kinetic = 2.0 * (
        freq_x[:, None, None] ** 2 + freq_y[None, :, None] ** 2 + freq_z[None, None, :] ** 2
    )
    beta = projectors.reshape(blocks, slots, 2, block_span, span_z)
    beta = beta.transpose(0, 1, 3, 2, 4).reshape(blocks, slots * block_span * 2, span_z)
    block_specs = [
        pl.BlockSpec(
            (bands, 2, None, block_span, span_z),
            lambda g: (0, 0, g // per_plane, g % per_plane, 0),
        ),
        pl.BlockSpec((None, slots * block_span * 2, span_z), lambda g: (g, 0, 0)),
        pl.BlockSpec((None, block_span, span_z), lambda g: (g // per_plane, g % per_plane, 0)),
    ]
    products = pl.pallas_call(
        functools.partial(project_kernel, slots),
        out_shape=jax.ShapeDtypeStruct((blocks, 2 * slots + 2 * bands, 2 * bands), f32),
        grid=(blocks,),
        in_specs=block_specs,
        out_specs=pl.BlockSpec((None, 2 * slots + 2 * bands, 2 * bands), lambda g: (g, 0, 0)),
        compiler_params=params,
        cost_estimate=cost(8 * 10**9, 8 * 10**6),
        name="project",
    )(orbitals, beta, kinetic)
    with_real = products[:, :slots].reshape(blocks, slots, bands, 2)
    with_imag = products[:, slots : 2 * slots].reshape(blocks, slots, bands, 2)
    proj = jnp.concatenate(
        [
            with_real[..., 0] + with_imag[..., 1],
            with_real[..., 1] - with_imag[..., 0],
        ],
        axis=-1,
    )
    owned = (
        slot_owner[:, :, None] == jnp.arange(owners, dtype=jnp.int32)[None, None, :]
    ).astype(f32)
    proj = tdot("gsj,gsc->jc", owned, proj)
    kin = jnp.sum(products[:, 2 * slots :], axis=0).reshape(bands, 2, bands, 2)
    kin = kin[:, 0, :, 0] + kin[:, 1, :, 1]

    returned, fields = [], []
    for c in range(parts):
        back, field = pl.pallas_call(
            functools.partial(real_space_kernel, rows, planes),
            out_shape=(
                jax.ShapeDtypeStruct((devices, 2 * share, block_rows, span_z), f32),
                jax.ShapeDtypeStruct((2 * share, rows * span_x, span_z), f32),
            ),
            grid=(share,),
            in_specs=[
                pl.BlockSpec((devices, None, block_rows, span_z), lambda j: (0, j, 0, 0)),
                whole(pot.shape),
                whole(inv_x.shape),
                whole(fwd_x.shape),
                whole(inv_z.shape),
                whole(fwd_z.shape),
                whole(proj.shape),
            ],
            out_specs=(
                pl.BlockSpec((devices, 2, block_rows, span_z), lambda j: (0, j, 0, 0)),
                pl.BlockSpec((2, rows * span_x, span_z), lambda j: (j, 0, 0)),
            ),
            compiler_params=params,
            cost_estimate=cost(4 * 10**9, 8 * 10**6),
            name="real_space",
        )(arrived[c], pot, inv_x, fwd_x, inv_z, fwd_z, proj)
        returned.append(exchange(back))
        fields.append(field)

    grams = pl.pallas_call(
        functools.partial(real_gram_kernel, bands),
        out_shape=jax.ShapeDtypeStruct((2, bands, bands, 128), f32),
        compiler_params=params,
        cost_estimate=cost(10**7, 2 * 10**6),
        name="real_gram",
    )(*fields, pot)
    grams = jnp.sum(grams, axis=-1)
    own = jnp.concatenate([proj, jnp.concatenate([grams[0], grams[1] + kin], axis=1)], axis=0)
    total = sum_over(own, devices, returned[0])
    proj, s_real, h_real = total[:owners], total[owners:, :bands], total[owners:, bands:]
    weighted = strengths.reshape(-1)[:, None] * proj
    p_real, p_imag = proj[:, :bands], proj[:, bands:]
    w_real, w_imag = weighted[:, :bands], weighted[:, bands:]
    h_real = h_real + tdot("ja,jb->ab", p_real, w_real) + tdot("ja,jb->ab", p_imag, w_imag)
    h_imag = tdot("ja,jb->ab", p_real, w_imag) - tdot("ja,jb->ab", p_imag, w_real)
    m_real, m_imag = subspace_solve(s_real, h_real, h_imag)

    coefs = tdot("gsj,jc->gcs", owned, weighted)
    c_real, c_imag = coefs[:, :bands], coefs[:, bands:]
    from_beta = jnp.stack(
        [
            jnp.concatenate([c_real, -c_imag], axis=2),
            jnp.concatenate([c_imag, c_real], axis=2),
        ],
        axis=2,
    ).reshape(blocks, 2 * bands, 2 * slots)
    from_psi = jnp.stack(
        [
            jnp.stack([-m_real.T, m_imag.T], axis=-1),
            jnp.stack([-m_imag.T, -m_real.T], axis=-1),
        ],
        axis=1,
    ).reshape(1, 2 * bands, 2 * bands)
    coefs = jnp.concatenate(
        [jnp.broadcast_to(from_psi, (blocks, 2 * bands, 2 * bands)), from_beta], axis=2
    )
    base = pl.pallas_call(
        functools.partial(base_kernel, slots),
        out_shape=jax.ShapeDtypeStruct(orbitals.shape, f32),
        grid=(blocks,),
        in_specs=block_specs
        + [pl.BlockSpec((None, 2 * bands, 2 * bands + 2 * slots), lambda g: (g, 0, 0))],
        out_specs=block_specs[0],
        compiler_params=tail_params,
        cost_estimate=cost(8 * 10**9, 12 * 10**6),
        name="base",
    )(orbitals, beta, kinetic, coefs)

    residual = base
    for c in range(parts):
        two_bands = pl.BlockSpec(
            (2, 2, planes, span_y, span_z), lambda j, c=c: (share * c + j, 0, 0, 0, 0)
        )
        residual = pl.pallas_call(
            to_planes_kernel,
            out_shape=jax.ShapeDtypeStruct(orbitals.shape, f32),
            grid=(share,),
            in_specs=[
                pl.BlockSpec((devices, 2, block_rows, span_z), lambda j: (0, j, 0, 0)),
                two_bands,
                whole(fwd_y.shape),
            ],
            out_specs=two_bands,
            input_output_aliases={1: 0},
            compiler_params=tail_params,
            cost_estimate=cost(8 * 10**9, 12 * 10**6),
            name="to_planes",
        )(returned[c], residual, fwd_y)
    return (residual, jnp.stack([m_real, m_imag]))


def solution(mesh):
    return jax.shard_map(
        functools.partial(on_device, mesh.shape["ga"]),
        mesh=mesh,
        in_specs=(
            P("rep", None, "ga", None, None),
            P("rep"),
            P("rep", "ga", None),
            P(("rep", "ga"), None, None, None),
            P(("rep", "ga"), None),
            P("rep", None),
        ),
        out_specs=(P("rep", None, "ga", None, None), P(None, "rep", None)),
        check_vma=False,
    )
```
